32 devices in a mesh: wide: 8 (over z, x), narrow: 4 (over y, core).
Axes of the slice: x: 2, y: 2, z: 4, core: 2. Of those that a mesh axis runs over, the one named last changes fastest.
Arguments:
- layer_argument: bfloat16 [20480, 768], P('wide'), may hold values from -6 to 6
- document_extents: int32 [8, 4], P('wide'), may hold values from 1 to 1024, as said below
- distance_bin_lookup: int32 [2047], replicated, may hold values from 0 to 31, as said below
- tile_location: int32 [13], replicated, may hold values from 0 to 15, as said below
- precise_parameter_blocks: float32 [16, 768, 768], P('wide', 'narrow'), may hold values from -0.21875 to 0.21875
- precise_mean_est: float32 [16, 768, 768], P('wide', 'narrow'), may hold values from -2.2888184e-05 to 2.2888184e-05
- precise_variance_est: float32 [16, 768, 768], P('wide', 'narrow'), may hold values from 1.30417e-11 to 5.21668e-11
- rescaling_coefficients: float32 [3, 768], replicated, may hold values from 0.5 to 1.5
- norm_scale_mean_est: float32 [3, 768], replicated, may hold values from -9.1552734e-05 to 9.1552734e-05
- norm_scale_variance_est: float32 [3, 768], replicated, may hold values from 2.086672e-10 to 8.346688e-10
- distance_bias_table: float32 [32, 12], P(None, 'narrow'), may hold values from -6 to 6
- offset_bias_mean_est: float32 [32, 12], P(None, 'narrow'), may hold values from -3.0517578e-05 to 3.0517578e-05
- offset_bias_variance_est: float32 [32, 12], P(None, 'narrow'), may hold values from 1.30417e-11 to 5.21668e-11
- sharpness_exponent: float32 [1], replicated, may hold values from 3 to 3.7
- sharpness_mean_est: float32 [1], replicated, may hold values from -0.03125 to 0.03125
- sharpness_variance_est: float32 [1], replicated, may hold values from 2.5e-05 to 0.0001
Outputs:
- loss: float32 [], replicated
- layer_result: float32 [20480, 768], P('wide')
- input_grad: float32 [20480, 768], P('wide')
- grad_norm: float32 [], replicated
- slot_first: float32 [16, 768, 768], P('wide', 'narrow')
- slot_second: float32 [16, 768, 768], P('wide', 'narrow')
- slot_weight: float32 [16, 768, 768], P('wide', 'narrow')
- gain_first: float32 [3, 768], replicated
- gain_second: float32 [3, 768], replicated
- gain_new: float32 [3, 768], replicated
- bias_first: float32 [32, 12], P(None, 'narrow')
- bias_second: float32 [32, 12], P(None, 'narrow')
- bias_new: float32 [32, 12], P(None, 'narrow')
- sharpness_mean_fresh: float32 [1], replicated
- sharpness_variance_fresh: float32 [1], replicated
- sharpness_exponent_fresh: float32 [1], replicated
The draws below stay inside these ranges and needn't reach their ends.
Inputs may be any that keep to these rules, and one draw needn't show every extreme that they name: `distance_bin_lookup`: bucket of a relative offset: offsets of size under 32 // 4 have their own buckets, larger ones share buckets that never fall with the offset's size; offsets above zero have 32 // 2 added. Distinct slots; block u belongs to index tile_location[u] // 2 of wide; some index of wide owns 2 blocks. `document_extents`: the lengths of a row add up to 2560.
All inputs are finite; a program needn't handle non-finite values.
Results may differ from the reference program's by a relative error of at most 0.03.
Values may be sent and summed in bfloat16 or wider, within the bound.
No kernel may reach another device: no remote copies, remote signals or barrier semaphores. Data moves between devices by JAX's collectives and lax.ppermute only.
A program may use at most 320 MiB of HBM per device.

```python
import math
import jax
import jax.numpy as jnp
from jax import lax

D = 768
HEADS = 12
HEAD_DIM = 64
FF = 3072
BUCKETS = 32
TOK_DEV = 2560
SEQS_DEV = 4
DOCLEN = 1024
QBLOCK = 512
CAP = 2
STEP = 10
UNITS = 13
TOKENS = 20480
SEQS = 32
N_WIDE = 8
N_NARROW = 4


def draw_document_extents(key, part):
    key = jax.random.fold_in(key, 37)
    shift_key, place_key = jax.random.split(key)
    others = SEQS_DEV - 1
    rest = TOK_DEV - DOCLEN
    base = rest // others
    reach = base // 4
    lifts = jax.random.randint(shift_key, (N_WIDE, others), 0, reach + 1).astype(jnp.int32)
    moves = lifts - jnp.roll(lifts, 1, axis=1)
    extra = jnp.zeros((others,), jnp.int32).at[0].set(rest - base * others)
    spread = (base + moves + extra[None, :]).astype(jnp.int32)
    rows = jnp.concatenate([jnp.full((N_WIDE, 1), DOCLEN, jnp.int32), spread], axis=1)
    row_keys = jax.random.split(place_key, N_WIDE)
    orders = jax.vmap(lambda one_key: jax.random.permutation(one_key, SEQS_DEV))(row_keys).astype(jnp.int32)
    return jnp.take_along_axis(rows, orders, axis=1).astype(jnp.int32)


def draw_distance_bin_lookup(key, part):
    key = jax.random.fold_in(key, 11)
    half_count = BUCKETS // 2
    exact_count = half_count // 2
    breaks = jax.random.randint(key, (half_count - exact_count - 1,), exact_count + 1, DOCLEN)
    offsets = jnp.arange(2 * DOCLEN - 1, dtype=jnp.int32) - (DOCLEN - 1)
    distance = jnp.abs(offsets)
    coarse = exact_count + jnp.sum((breaks[None, :] <= distance[:, None]).astype(jnp.int32), axis=1)
    within = jnp.where(distance < exact_count, distance, coarse)
    return (within + jnp.where(offsets > 0, half_count, 0)).astype(jnp.int32)


def draw_tile_location(key, part):
    key = jax.random.fold_in(key, 23)
    owner_key, order_key, unit_key = jax.random.split(key, 3)
    full_owner = jax.random.randint(owner_key, (), 0, N_WIDE)
    full_slots = full_owner * CAP + jnp.arange(CAP, dtype=jnp.int32)
    pool_top = (N_WIDE - 1) * CAP - 1
    inner = (jax.random.permutation(order_key, pool_top - 1) + 1)[:UNITS - CAP - 2].astype(jnp.int32)
    others = jnp.concatenate([jnp.zeros((1,), jnp.int32), jnp.full((1,), pool_top, jnp.int32), inner])
    others = jnp.where(others >= full_owner * CAP, others + CAP, others)
    every_slot = jnp.concatenate([full_slots.astype(jnp.int32), others.astype(jnp.int32)])
    return every_slot[jax.random.permutation(unit_key, UNITS)].astype(jnp.int32)


def block_levels(rng, extent, shards, low, high):
    def one(axis_at, blocks):
        draws = jax.random.uniform(jax.random.fold_in(jax.random.fold_in(rng, 6), axis_at), (blocks,), jnp.float32, low / len(shards), high / len(shards))
        return jnp.repeat(jnp.exp(draws), extent[axis_at] // blocks).reshape((-1,) + (1,) * (len(extent) - axis_at - 1))

    loudness = one(*shards[0])
    for cut in shards[1:]:
        loudness = loudness * one(*cut)
    return loudness


def gaussian(rng, extent, width, most, cuts=(), held_as=jnp.bfloat16):
    entries = jax.random.normal(rng, extent, jnp.float32) * width
    if len(cuts) > 0:
        entries = block_levels(rng, extent, cuts, -0.22, 0.18) * entries
    return jnp.clip(entries, min=-most, max=most).astype(held_as)


def setup_inputs(seed: int = 0) -> dict:
    key_list = jax.random.split(jax.random.key(seed), 17)
    layer_argument = gaussian(key_list[0], (TOKENS, D), 1.0, 6.0, ((0, 8),))
    document_extents = draw_document_extents(jax.random.fold_in(key_list[16], 71), 0)
    distance_bin_lookup = draw_distance_bin_lookup(jax.random.fold_in(key_list[16], 71), 0)
    tile_location = draw_tile_location(jax.random.fold_in(key_list[16], 71), 0)
    precise_parameter_blocks = gaussian(key_list[4], (N_WIDE * CAP, D, D), D ** -0.5, 0.21875, ((0, 8), (1, 4)), jnp.float32)
    precise_mean_est = gaussian(key_list[5], (N_WIDE * CAP, D, D), (0.01 / (UNITS * D * D) ** 0.5), 2.288818359375e-05, ((0, 8), (1, 4)), jnp.float32)
    precise_variance_est = jnp.clip(jnp.exp(math.log(5.216679865860385e-11) - 1.3862944 * jax.random.uniform(key_list[6], (N_WIDE * CAP, D, D), jnp.float32) ** block_levels(key_list[6], (N_WIDE * CAP, D, D), ((0, 8), (1, 4)), -0.2, 0.2)), 1.3041699664650963e-11, 5.216679865860385e-11)
    rescaling_coefficients = jnp.clip(1.0 + 0.1 * jax.random.normal(key_list[7], (3, D), jnp.float32), 0.5, 1.5)
    norm_scale_mean_est = gaussian(key_list[8], (3, D), (0.04 / (UNITS * D * D) ** 0.5), 9.1552734375e-05, (), jnp.float32)
    norm_scale_variance_est = jnp.clip(jnp.exp(jax.random.uniform(key_list[9], (3, D), jnp.float32, math.log(2.086671946344154e-10), math.log(8.346687785376616e-10))), 2.086671946344154e-10, 8.346687785376616e-10)
    distance_bias_table = gaussian(key_list[10], (BUCKETS, HEADS), 1.0, 6.0, ((1, 4),), jnp.float32)
    offset_bias_mean_est = gaussian(key_list[11], (BUCKETS, HEADS), (0.015 / (UNITS * D * D) ** 0.5), 3.0517578125e-05, ((1, 4),), jnp.float32)
    offset_bias_variance_est = jnp.clip(jnp.exp(math.log(5.216679865860385e-11) - 1.3862944 * jax.random.uniform(key_list[12], (BUCKETS, HEADS), jnp.float32) ** block_levels(key_list[12], (BUCKETS, HEADS), ((1, 4),), -0.2, 0.2)), 1.3041699664650963e-11, 5.216679865860385e-11)
    sharpness_exponent = jnp.clip(jax.random.uniform(key_list[13], (1,), jnp.float32, 3.0, 3.7), 3.0, 3.7)
    sharpness_mean_est = gaussian(key_list[14], (1,), 0.005, 0.03125, (), jnp.float32)
    sharpness_variance_est = jnp.clip(jnp.exp(jax.random.uniform(key_list[15], (1,), jnp.float32, math.log(2.499999936844688e-05), math.log(0.0001))), 2.499999936844688e-05, 0.0001)
    return dict(layer_argument=layer_argument, document_extents=document_extents, distance_bin_lookup=distance_bin_lookup, tile_location=tile_location, precise_parameter_blocks=precise_parameter_blocks, precise_mean_est=precise_mean_est, precise_variance_est=precise_variance_est, rescaling_coefficients=rescaling_coefficients, norm_scale_mean_est=norm_scale_mean_est, norm_scale_variance_est=norm_scale_variance_est, distance_bias_table=distance_bias_table, offset_bias_mean_est=offset_bias_mean_est, offset_bias_variance_est=offset_bias_variance_est, sharpness_exponent=sharpness_exponent, sharpness_mean_est=sharpness_mean_est, sharpness_variance_est=sharpness_variance_est)


norm_eps = 1e-06
clip_limit = 0.01
learn_rate = 0.01
side_rate = 0.5
beta_one = 0.5
beta_two = 0.5
adam_eps = 1e-08
decay_rate = 0.01
score_scale = 0.125
masked_score = -1e+30

@jax.custom_vjp
def low(v):
    return lax.optimization_barrier(v.astype(jnp.bfloat16)).astype(jnp.float32)

@jax.custom_vjp
def low_back(v):
    return v

def low_keep(v):
    return (low(v), None)

def low_pass(kept, grad):
    return (grad,)

def back_keep(v):
    return (v, None)

def back_low(kept, grad):
    return (low(grad),)
low.defvjp(low_keep, low_pass)
low_back.defvjp(back_keep, back_low)

def round_both(values):
    return low(low_back(values))

def multiply_matrices(left_side, right_side):
    return jnp.dot(left_side, right_side, precision=lax.Precision.HIGHEST)

def rms_scale(values):
    return lax.rsqrt(lax.optimization_barrier(jnp.mean(values * values, axis=-1, keepdims=True)) + norm_eps)

def arrange(pieces):
    split_pieces = pieces.reshape(FF // D, N_NARROW, D // N_NARROW, D)
    return jnp.transpose(split_pieces, (1, 0, 2, 3)).reshape(FF, D)

def attention_group(queries, keys_all, values_all, segment_ids, bias_block):
    window = QBLOCK + 2 * DOCLEN
    key_padded = jnp.pad(keys_all, ((DOCLEN, DOCLEN), (0, 0), (0, 0)))
    value_padded = jnp.pad(values_all, ((DOCLEN, DOCLEN), (0, 0), (0, 0)))
    segment_padded = jnp.pad(segment_ids, (DOCLEN, DOCLEN), constant_values=-1)

    def one_block(block_start):
        query_block = lax.dynamic_slice_in_dim(queries, block_start, QBLOCK, 0)
        key_block = lax.dynamic_slice_in_dim(key_padded, block_start, window, 0)
        value_block = lax.dynamic_slice_in_dim(value_padded, block_start, window, 0)
        query_segments = lax.dynamic_slice_in_dim(segment_ids, block_start, QBLOCK, 0)
        key_segments = lax.dynamic_slice_in_dim(segment_padded, block_start, window, 0)
        scores = jnp.einsum('qhd,khd->hqk', query_block, key_block, precision=lax.Precision.HIGHEST) * score_scale + bias_block
        scores = low_back(scores)
        allowed = query_segments[:, None] == key_segments[None, :]
        scores = jnp.where(allowed[None, :, :], scores, masked_score)
        row_top = lax.optimization_barrier(jnp.max(scores, axis=-1, keepdims=True))
        weights = jnp.exp(scores - row_top)
        probabilities = weights / lax.optimization_barrier(jnp.sum(weights, axis=-1, keepdims=True))
        return jnp.einsum('hqk,khd->qhd', low(probabilities), value_block, precision=lax.Precision.HIGHEST)
    starts = (jnp.arange(TOK_DEV // QBLOCK) * QBLOCK).astype(jnp.int32)
    blocks = lax.map(jax.checkpoint(one_block), starts)
    return blocks.reshape(TOK_DEV, D)

def group_forward(group_rows, lengths, layer_weights, rescaling_coefficients, bias_block):
    query_weight, key_weight, value_weight, out_weight, inner_weight, outer_weight = layer_weights
    seq_ends = jnp.cumsum(lengths).astype(jnp.int32)
    positions = jnp.arange(TOK_DEV, dtype=jnp.int32)
    segment_ids = lax.optimization_barrier(jnp.sum((seq_ends[None, :] <= positions[:, None]).astype(jnp.int32), axis=1)).astype(jnp.int32)
    normed_one = low(group_rows * rms_scale(group_rows) * rescaling_coefficients[0])
    queries = round_both(multiply_matrices(normed_one, query_weight.T)).reshape(TOK_DEV, HEADS, HEAD_DIM)
    keys_all = round_both(multiply_matrices(normed_one, key_weight.T)).reshape(TOK_DEV, HEADS, HEAD_DIM)
    values_all = round_both(multiply_matrices(normed_one, value_weight.T)).reshape(TOK_DEV, HEADS, HEAD_DIM)
    context = round_both(attention_group(queries, keys_all, values_all, segment_ids, bias_block))
    residual_mid = group_rows + low_back(multiply_matrices(context, out_weight))
    normed_two = low(residual_mid * rms_scale(residual_mid) * rescaling_coefficients[1])
    gate_pre = low_back(multiply_matrices(normed_two, inner_weight.T))
    hidden_act = low(jax.nn.gelu(gate_pre))
    layer_result = residual_mid + low_back(multiply_matrices(hidden_act, outer_weight))
    final_rows = layer_result * rms_scale(layer_result) * rescaling_coefficients[2]
    member = (segment_ids[None, :] == jnp.arange(SEQS_DEV, dtype=jnp.int32)[:, None]).astype(jnp.float32)
    pooled = multiply_matrices(member, final_rows) / lengths[:, None].astype(jnp.float32)
    return (layer_result, pooled)

def evaluate_layer(arguments_list, parameter_tiles, rescaling_coefficients, distance_bias_table, sharpness_exponent, document_extents, distance_bin_lookup):
    rounded = low(parameter_tiles)
    ffn_units = FF // D
    layer_weights = (rounded[0], rounded[1], rounded[2], rounded[3], arrange(rounded[5:5 + ffn_units]), arrange(rounded[5 + ffn_units:]))
    proj_weight = rounded[4]
    bucket_onehot = (distance_bin_lookup[:, None] == jnp.arange(BUCKETS, dtype=jnp.int32)[None, :]).astype(jnp.float32)
    rel_values = multiply_matrices(bucket_onehot, distance_bias_table).T
    row_offsets = jnp.arange(QBLOCK, dtype=jnp.int32)
    column_offsets = jnp.arange(QBLOCK + 2 * DOCLEN, dtype=jnp.int32)
    table_index = jnp.clip(column_offsets[None, :] - row_offsets[:, None] - 1, 0, 2 * DOCLEN - 2)
    bias_block = rel_values[:, table_index]

    def per_group(state_in, group_inputs):
        group_rows, lengths = group_inputs
        layer_result, pooled = group_forward(group_rows, lengths, layer_weights, rescaling_coefficients, bias_block)
        return (state_in, (layer_result, pooled))
    stacked = (arguments_list.reshape(N_WIDE, TOK_DEV, D), document_extents)
    state_out, (encoded_all, pooled_all) = lax.scan(jax.checkpoint(per_group), jnp.zeros((), jnp.float32), stacked)
    pooled_flat = pooled_all.reshape(SEQS, D)
    projected = round_both(multiply_matrices(low(pooled_flat), proj_weight.T))
    inverse = lax.rsqrt(lax.optimization_barrier(jnp.sum(projected * projected, axis=1, keepdims=True)) + norm_eps)
    vectorized_text = low(projected * inverse)
    sharpened_agreement = jnp.exp(sharpness_exponent[0]) * multiply_matrices(vectorized_text, vectorized_text.T)
    seq_index = jnp.arange(SEQS, dtype=jnp.int32)
    sharpened_agreement = jnp.where(seq_index[:, None] == seq_index[None, :], masked_score, sharpened_agreement)
    row_top = lax.optimization_barrier(jnp.max(sharpened_agreement, axis=1, keepdims=True))
    log_total = row_top[:, 0] + jnp.log(lax.optimization_barrier(jnp.sum(jnp.exp(sharpened_agreement - row_top), axis=1)))
    partner = jnp.bitwise_xor(seq_index, 1)
    positive = lax.optimization_barrier(jnp.sum(jnp.where(seq_index[None, :] == partner[:, None], sharpened_agreement, 0.0), axis=1))
    penalty_amount = jnp.mean(log_total - positive)
    return (penalty_amount, encoded_all.reshape(TOKENS, D))

def decoupled_decay_step(gradient, first_moment, second_moment, weight, multiplier, step_rate):
    clipped = gradient * multiplier
    first_new = beta_one * first_moment + (1.0 - beta_one) * clipped
    second_new = beta_two * second_moment + (1.0 - beta_two) * clipped * clipped
    first_hat = first_new / (1.0 - beta_one ** STEP)
    second_hat = second_new / (1.0 - beta_two ** STEP)
    weight_new = weight - step_rate * (first_hat / (jnp.sqrt(second_hat) + adam_eps) + decay_rate * weight)
    return (first_new, second_new, weight_new)

def reference(layer_argument, document_extents, distance_bin_lookup, tile_location, precise_parameter_blocks, precise_mean_est, precise_variance_est, rescaling_coefficients, norm_scale_mean_est, norm_scale_variance_est, distance_bias_table, offset_bias_mean_est, offset_bias_variance_est, sharpness_exponent, sharpness_mean_est, sharpness_variance_est):
    parameter_tiles = jnp.take(precise_parameter_blocks, tile_location, axis=0)
    arguments_list = layer_argument.astype(jnp.float32)

    def training_criterion(layer_in, block_values, gain_values, bias_values, temp_values):
        return evaluate_layer(layer_in, block_values, gain_values, bias_values, temp_values, document_extents, distance_bin_lookup)
    (penalty_amount, layer_result), adjoint_mapping = jax.vjp(training_criterion, arguments_list, parameter_tiles, rescaling_coefficients, distance_bias_table, sharpness_exponent)
    input_grad, unit_grads, norm_scale_slopes, bias_grads, sharpness_slopes = adjoint_mapping((jnp.ones_like(penalty_amount), jnp.zeros_like(layer_result)))
    square_total = jnp.sum(unit_grads * unit_grads) + jnp.sum(norm_scale_slopes * norm_scale_slopes) + jnp.sum(bias_grads * bias_grads) + jnp.sum(sharpness_slopes * sharpness_slopes)
    grad_norm = jnp.sqrt(square_total)
    multiplier = jnp.minimum(1.0, clip_limit / grad_norm)
    slot_grads = jnp.zeros_like(precise_parameter_blocks).at[tile_location].set(unit_grads)
    slot_first, slot_second, slot_weight = decoupled_decay_step(slot_grads, precise_mean_est, precise_variance_est, precise_parameter_blocks, multiplier, learn_rate)
    gain_first, gain_second, gain_new = decoupled_decay_step(norm_scale_slopes, norm_scale_mean_est, norm_scale_variance_est, rescaling_coefficients, multiplier, side_rate)
    bias_first, bias_second, bias_new = decoupled_decay_step(bias_grads, offset_bias_mean_est, offset_bias_variance_est, distance_bias_table, multiplier, side_rate)
    sharpness_mean_fresh, sharpness_variance_fresh, sharpness_exponent_fresh = decoupled_decay_step(sharpness_slopes, sharpness_mean_est, sharpness_variance_est, sharpness_exponent, multiplier, learn_rate)
    return (penalty_amount, layer_result, input_grad, grad_norm, slot_first, slot_second, slot_weight, gain_first, gain_second, gain_new, bias_first, bias_second, bias_new, sharpness_mean_fresh, sharpness_variance_fresh, sharpness_exponent_fresh)
```

```python
import jax
import jax.numpy as jnp
from jax import lax
from jax.experimental import pallas as pl
from jax.experimental.pallas import tpu as pltpu
from jax.sharding import PartitionSpec as P

D = 768
FF = 3072
BUCKETS = 32
TOK_DEV = 2560
SEQS_DEV = 4
DOCLEN = 1024
CAP = 2
STEP = 10
LANE = 128
BQ = 512
BK = 512
REACH = DOCLEN // LANE
OFF = REACH + (BQ + BK) // LANE
SPAN = 2 * OFF + 1
LINES = 2 * REACH + 2
VMEM_LIMIT = 56 * 1024 * 1024


norm_eps = 1e-06
clip_limit = 0.01
learn_rate = 0.01
side_rate = 0.5
beta_one = 0.5
beta_two = 0.5
adam_eps = 1e-08
decay_rate = 0.01
score_scale = 0.125
masked_score = -1e30


def times_transposed(left_side, right_side):
    return lax.dot_general(
        left_side, right_side, (((1,), (1,)), ((), ())), preferred_element_type=jnp.float32
    )


def plain_product(left_side, right_side):
    return jnp.dot(left_side, right_side, preferred_element_type=jnp.float32)


def outer_product(left_side, right_side):
    return lax.dot_general(
        left_side, right_side, (((0,), (0,)), ((), ())), preferred_element_type=jnp.float32
    )


def rms_scale(values):
    return lax.rsqrt(jnp.mean(values * values, axis=-1, keepdims=True) + norm_eps)


def norm_backward(values, row_scale, gain_row, grad_out):
    weighted = grad_out * gain_row
    gain_grad = jnp.sum(grad_out * values * row_scale, axis=0)
    inner_mean = jnp.mean(weighted * values, axis=-1, keepdims=True)
    value_grad = row_scale * weighted - values * row_scale * row_scale * row_scale * inner_mean
    return (value_grad, gain_grad)


def nn(a,b): return lax.dot_general(a,b,(((1,),(0,)),((),())),preferred_element_type=jnp.float32)
def nt(a,b): return lax.dot_general(a,b,(((1,),(1,)),((),())),preferred_element_type=jnp.float32)

def bias_kernel(chunks, tiles):
    heads=tiles.shape[0]
    tiles[...]=jnp.zeros_like(tiles)
    for h in range(heads):
        for d in range(-REACH,REACH+1):
            left=chunks[h,REACH+1-d:REACH+2-d,:]
            right=chunks[h,REACH-d:REACH+1-d,:]
            line=jnp.concatenate([left,right],axis=1)
            rolled=pltpu.roll(jnp.broadcast_to(line,(LANE,2*LANE)),0,1,stride=1,stride_axis=0)
            tiles[h,pl.ds((d+OFF)*LANE,LANE),:]=rolled[:,:LANE]

def bias_tiles(rel_chunks):
    heads=rel_chunks.shape[0]
    return pl.pallas_call(bias_kernel,
        out_shape=jax.ShapeDtypeStruct((heads,SPAN*LANE,LANE),jnp.float32),
        compiler_params=pltpu.CompilerParams(vmem_limit_bytes=VMEM_LIMIT),
        name="bias_tiles")(rel_chunks)

def key_range(lengths, first, last):
    start=jnp.int32(0); end=jnp.int32(0); low=jnp.int32(0); high=jnp.int32(0)
    found=jnp.int32(0)
    for s in range(lengths.shape[0]):
        end=start+lengths[s]
        low=jnp.where(start<=first,start,low)
        high=jnp.where(start<=last,end,high)
        start=end
    return low//BK,(high+BK-1)//BK

def bias_part(bias,h,i,j):
    row=(j*(BK//LANE)-i*(BQ//LANE)+OFF)*LANE
    return jnp.concatenate([bias[h,pl.ds(pl.multiple_of(row-b*LANE,LANE),BK),:] for b in range(BQ//LANE)],axis=1)

def forward_kernel(lengths,qT,kn,vT,exq,bias,ctx_o,ctxT_o,lse_o,qa,acc):
    tokens=qT.shape[1]
    heads=bias.shape[0]
    hs=qT.shape[0]//heads
    qa[...]=jnp.zeros_like(qa)
    @pl.loop(0,tokens//BQ)
    def _(i):
        q0=pl.multiple_of(i*BQ,BQ)
        for h in range(heads):
            qa[h*LANE:h*LANE+hs,:]=qT[h*hs:(h+1)*hs,pl.ds(q0,BQ)]
            qa[h*LANE+hs:h*LANE+hs+16,:]=exq[:,pl.ds(q0,BQ)]
        acc[...]=jnp.zeros_like(acc)
        low,high=key_range(lengths,q0,q0+BQ-1)
        def step(j,carry):
            k0=pl.multiple_of(j*BK,BK)
            out=[]
            for h in range(heads):
                top,total=carry[2*h],carry[2*h+1]
                s=nn(kn[pl.ds(k0,BK),h*LANE:(h+1)*LANE],qa[h*LANE:(h+1)*LANE,:])
                s=s+bias_part(bias,h,i,j)
                new_top=jnp.maximum(top,jnp.max(s,axis=0,keepdims=True))
                fade=jnp.exp(top-new_top)
                p=jnp.exp(s-new_top)
                total=total*fade+jnp.sum(p,axis=0,keepdims=True)
                rows=slice(h*hs,(h+1)*hs)
                acc[rows,:]=acc[rows,:]*fade+nn(vT[rows,pl.ds(k0,BK)],p.astype(jnp.bfloat16))
                out+=[new_top,total]
            return tuple(out)
        init=tuple(jnp.full((1,BQ),2.0*masked_score if n%2==0 else 0.0,jnp.float32) for n in range(2*heads))
        done=lax.fori_loop(low,high,step,init)
        lse=[]
        for h in range(heads):
            rows=slice(h*hs,(h+1)*hs)
            acc[rows,:]=acc[rows,:]/done[2*h+1]
            lse_o[h:h+1,pl.ds(q0,BQ)]=done[2*h]+jnp.log(done[2*h+1])
        ctxT_o[:,pl.ds(q0,BQ)]=acc[...]
        ctx_o[pl.ds(q0,BQ),:]=acc[...].T.astype(jnp.bfloat16)

def smem(): return pl.BlockSpec(memory_space=pltpu.SMEM)
def vmem(): return pl.BlockSpec(memory_space=pltpu.VMEM)

def attention_forward(lengths,qT,kn,vT,exq,bias):
    width,tokens=qT.shape
    heads=bias.shape[0]
    return pl.pallas_call(forward_kernel,
        out_shape=(jax.ShapeDtypeStruct((tokens,width),jnp.bfloat16),jax.ShapeDtypeStruct((width,tokens),jnp.float32),jax.ShapeDtypeStruct((heads,tokens),jnp.float32)),
        in_specs=[smem()]+[vmem()]*5, out_specs=(vmem(),)*3,
        scratch_shapes=[pltpu.VMEM((heads*LANE,BQ),jnp.bfloat16),pltpu.VMEM((width,BQ),jnp.float32)],
        compiler_params=pltpu.CompilerParams(vmem_limit_bytes=VMEM_LIMIT),
        name="attention_forward")(lengths,qT,kn,vT,exq,bias)

def split3(v):
    a=v.astype(jnp.bfloat16); r=v-a.astype(jnp.float32)
    b=r.astype(jnp.bfloat16); c=r-b.astype(jnp.float32)
    return a.astype(jnp.float32),b.astype(jnp.float32),c

def backward_kernel(lengths,qT,kn,vn,kT,dcT,ctxT,lse,exq,bias,dT_o,dn_o,lines_o,qa,da,dq,dk,dv,tiles):
    width,tokens=qT.shape
    heads=bias.shape[0]
    hs=width//heads
    qa[...]=jnp.zeros_like(qa)
    da[...]=jnp.zeros_like(da)
    dk[...]=jnp.zeros_like(dk)
    dv[...]=jnp.zeros_like(dv)
    tiles[...]=jnp.zeros_like(tiles)
    place=lax.broadcasted_iota(jnp.int32,(16,BQ),0)
    def pieces(v):
        a,b,c=split3(v)
        return jnp.where(place==4,a,jnp.where(place==5,b,jnp.where(place==6,c,0.0)))
    @pl.loop(0,tokens//BQ)
    def _(i):
        q0=pl.multiple_of(i*BQ,BQ)
        for h in range(heads):
            rows=slice(h*hs,(h+1)*hs)
            qa[h*LANE:h*LANE+hs,:]=qT[rows,pl.ds(q0,BQ)]
            qa[h*LANE+hs:h*LANE+hs+16,:]=(exq[:,pl.ds(q0,BQ)].astype(jnp.float32)+pieces(-lse[h:h+1,pl.ds(q0,BQ)])).astype(jnp.bfloat16)
            dc=dcT[rows,pl.ds(q0,BQ)]
            delta=jnp.sum(dc.astype(jnp.float32)*ctxT[rows,pl.ds(q0,BQ)],axis=0,keepdims=True)
            da[h*LANE:h*LANE+hs,:]=dc
            da[h*LANE+hs:h*LANE+hs+16,:]=pieces(-delta).astype(jnp.bfloat16)
        dq[...]=jnp.zeros_like(dq)
        low,high=key_range(lengths,q0,q0+BQ-1)
        @pl.loop(low,high)
        def _(j):
            k0=pl.multiple_of(j*BK,BK)
            base=(j*(BK//LANE)-i*(BQ//LANE)+OFF)*LANE
            for h in range(heads):
                rows=slice(h*hs,(h+1)*hs)
                own=slice(h*LANE,(h+1)*LANE)
                s=nn(kn[pl.ds(k0,BK),own],qa[own,:])
                p=jnp.exp(s+bias_part(bias,h,i,j))
                dp=nn(vn[pl.ds(k0,BK),own],da[own,:])
                ds=p*dp
                for b in range(BQ//LANE):
                    at=pl.ds(pl.multiple_of(base-b*LANE,LANE),BK)
                    tiles[h,at,:]=tiles[h,at,:]+ds[:,b*LANE:(b+1)*LANE]
                pb=p.astype(jnp.bfloat16)
                db=ds.astype(jnp.bfloat16)
                dv[rows,pl.ds(k0,BK)]=dv[rows,pl.ds(k0,BK)]+nt(da[h*LANE:h*LANE+hs,:],pb)
                dk[rows,pl.ds(k0,BK)]=dk[rows,pl.ds(k0,BK)]+nt(qa[h*LANE:h*LANE+hs,:],db)
                dq[rows,:]=dq[rows,:]+nn(kT[rows,pl.ds(k0,BK)],db)
        grad=dq[...]*0.125
        dT_o[0:width,pl.ds(q0,BQ)]=grad.astype(jnp.bfloat16)
        dn_o[pl.ds(q0,BQ),0:width]=grad.T.astype(jnp.bfloat16)
    @pl.loop(0,tokens//BQ)
    def _(i):
        q0=pl.multiple_of(i*BQ,BQ)
        both=jnp.concatenate([dk[:,pl.ds(q0,BQ)],dv[:,pl.ds(q0,BQ)]],axis=0)
        dT_o[width:3*width,pl.ds(q0,BQ)]=both.astype(jnp.bfloat16)
        dn_o[pl.ds(q0,BQ),width:3*width]=both.T.astype(jnp.bfloat16)
    over=lax.broadcasted_iota(jnp.int32,(LANE,LANE),1)>=lax.broadcasted_iota(jnp.int32,(LANE,LANE),0)
    sub=lax.broadcasted_iota(jnp.int32,(8,LANE),0)
    for h in range(heads):
        for d in range(-REACH,REACH+2):
            here=tiles[h,(d+OFF)*LANE:(d+OFF+1)*LANE,:]
            below=tiles[h,(d+OFF-1)*LANE:(d+OFF)*LANE,:]
            mixed=jnp.where(over,here,below)
            line=mixed[LANE-8:,:]
            for g in range(LANE//8-2,-1,-1):
                line=mixed[8*g:8*g+8,:]+pltpu.roll(line,LANE-8,1)
            for bit in (1,2,4):
                line=jnp.where((sub&bit)!=0,pltpu.roll(line,LANE-bit,1),line)
            lines_o[h,REACH+1-d:REACH+2-d,:]=jnp.sum(line,axis=0,keepdims=True)

def attention_backward(lengths,qT,kn,vn,kT,dcT,ctxT,lse,exq,bias):
    width,tokens=qT.shape
    heads=bias.shape[0]
    return pl.pallas_call(backward_kernel,
        out_shape=(jax.ShapeDtypeStruct((3*width,tokens),jnp.bfloat16),jax.ShapeDtypeStruct((tokens,3*width),jnp.bfloat16),jax.ShapeDtypeStruct((heads,2*REACH+2,LANE),jnp.float32)),
        in_specs=[smem()]+[vmem()]*9, out_specs=(vmem(),)*3,
        scratch_shapes=[pltpu.VMEM((heads*LANE,BQ),jnp.bfloat16),pltpu.VMEM((heads*LANE,BQ),jnp.bfloat16),
            pltpu.VMEM((width,BQ),jnp.float32),pltpu.VMEM((width,tokens),jnp.float32),pltpu.VMEM((width,tokens),jnp.float32),
            pltpu.VMEM((heads,SPAN*LANE,LANE),jnp.float32)],
        compiler_params=pltpu.CompilerParams(vmem_limit_bytes=VMEM_LIMIT),
        name="attention_backward")(lengths,qT,kn,vn,kT,dcT,ctxT,lse,exq,bias)


def decoupled_decay_step(gradient, first_moment, second_moment, weight, multiplier, step_rate):
    clipped = gradient * multiplier
    first_new = beta_one * first_moment + (1.0 - beta_one) * clipped
    second_new = beta_two * second_moment + (1.0 - beta_two) * clipped * clipped
    first_hat = first_new / (1.0 - beta_one**STEP)
    second_hat = second_new / (1.0 - beta_two**STEP)
    weight_new = weight - step_rate * (
        first_hat / (jnp.sqrt(second_hat) + adam_eps) + decay_rate * weight
    )
    return (first_new, second_new, weight_new)


def on_device(
    layer_argument,
    document_extents,
    distance_bin_lookup,
    tile_location,
    precise_parameter_blocks,
    precise_mean_est,
    precise_variance_est,
    rescaling_coefficients,
    norm_scale_mean_est,
    norm_scale_variance_est,
    distance_bias_table,
    offset_bias_mean_est,
    offset_bias_variance_est,
    sharpness_exponent,
    sharpness_mean_est,
    sharpness_variance_est,
):
    wide_count = lax.axis_size("wide")
    wide_index = lax.axis_index("wide")
    narrow_index = lax.axis_index("narrow")
    unit_rows = precise_parameter_blocks.shape[1]
    heads_here = distance_bias_table.shape[1]
    head_size = unit_rows // heads_here
    ffn_units = FF // D
    every_slot = lax.all_gather(
        precise_parameter_blocks.astype(jnp.bfloat16), "wide", axis=0, tiled=True
    ).astype(precise_parameter_blocks.dtype)
    unit_weights = jnp.take(every_slot, tile_location, axis=0)
    weights_low = unit_weights.astype(jnp.bfloat16)
    qkv_weight = weights_low[0:3].reshape(3 * unit_rows, D)
    out_weight = weights_low[3]
    proj_weight = weights_low[4]
    inner_weight = weights_low[5 : 5 + ffn_units].reshape(ffn_units * unit_rows, D)
    outer_weight = weights_low[5 + ffn_units :].reshape(ffn_units * unit_rows, D)
    arguments_list = layer_argument.astype(jnp.float32)
    lengths = document_extents[0]
    seq_ends = jnp.cumsum(lengths)
    positions = jnp.arange(TOK_DEV, dtype=jnp.int32)
    segment_ids = jnp.sum((seq_ends[None, :] <= positions[:, None]).astype(jnp.int32), axis=1)
    beyond = LINES * LANE - LANE - 1 - distance_bin_lookup.shape[0]
    offsets_down = jnp.pad(distance_bin_lookup[::-1], (LANE + 1, beyond), constant_values=-1)
    bucket_onehot = (
        offsets_down[:, None] == jnp.arange(BUCKETS, dtype=jnp.int32)[None, :]
    ).astype(jnp.float32)
    rel_values = jnp.dot(bucket_onehot, distance_bias_table, precision=lax.Precision.HIGHEST).T
    tiles_bias = bias_tiles(rel_values.reshape(heads_here, LINES, LANE))
    scale_one = rms_scale(arguments_list)
    normed_one = (arguments_list * scale_one * rescaling_coefficients[0]).astype(jnp.bfloat16)
    transposed_rows = times_transposed(qkv_weight, normed_one)
    query_cols = (transposed_rows[:unit_rows] * score_scale).astype(jnp.bfloat16)
    key_cols = transposed_rows[unit_rows : 2 * unit_rows].astype(jnp.bfloat16)
    value_cols = transposed_rows[2 * unit_rows :].astype(jnp.bfloat16)
    spread_weight = jnp.pad(
        weights_low[1:3].reshape(2 * heads_here, head_size, D),
        ((0, 0), (0, LANE - head_size), (0, 0)),
    ).reshape(2 * heads_here * LANE, D)
    lane_place = jnp.arange(2 * heads_here * LANE, dtype=jnp.int32) % LANE - head_size
    marks = jnp.logical_or(
        lane_place[None, :] == segment_ids[:, None],
        jnp.logical_and(lane_place >= SEQS_DEV, lane_place < SEQS_DEV + 3)[None, :],
    )
    key_value_rows = (
        times_transposed(normed_one, spread_weight) + marks.astype(jnp.float32)
    ).astype(jnp.bfloat16)
    key_rows = key_value_rows[:, : heads_here * LANE]
    value_rows = key_value_rows[:, heads_here * LANE :]
    row_place = jnp.arange(16, dtype=jnp.int32)[:, None]
    apart = jnp.where(
        jnp.logical_and(row_place < SEQS_DEV, row_place != segment_ids[None, :]), masked_score, 0.0
    ).astype(jnp.bfloat16)
    context, context_cols, log_rows = attention_forward(
        lengths, query_cols, key_rows, value_cols, apart, tiles_bias
    )
    attn_total = lax.psum(plain_product(context, out_weight), "narrow")
    residual_mid = arguments_list + attn_total
    scale_two = rms_scale(residual_mid)
    normed_two = (residual_mid * scale_two * rescaling_coefficients[1]).astype(jnp.bfloat16)
    gate_pre = times_transposed(normed_two, inner_weight)
    hidden_act, gelu_back = jax.vjp(jax.nn.gelu, gate_pre)
    hidden_low = hidden_act.astype(jnp.bfloat16)
    ffn_total = lax.psum(plain_product(hidden_low, outer_weight), "narrow")
    layer_result = residual_mid + ffn_total
    scale_three = rms_scale(layer_result)
    final_rows = layer_result * scale_three * rescaling_coefficients[2]
    member = (segment_ids[None, :] == jnp.arange(SEQS_DEV, dtype=jnp.int32)[:, None]).astype(
        jnp.float32
    )
    length_values = lengths.astype(jnp.float32)[:, None]
    pooled = jnp.dot(member, final_rows, precision=lax.Precision.HIGHEST) / length_values
    pooled_low = pooled.astype(jnp.bfloat16)
    proj_part = times_transposed(pooled_low, proj_weight).astype(jnp.bfloat16)
    projected = lax.all_gather(proj_part, "narrow", axis=1, tiled=True).astype(jnp.float32)
    inverse = lax.rsqrt(jnp.sum(projected * projected, axis=1, keepdims=True) + norm_eps)
    embed_low = (projected * inverse).astype(jnp.bfloat16)
    every_low = lax.all_gather(embed_low, "wide", axis=0, tiled=True)
    gathered_embeddings = every_low.astype(jnp.float32)
    embed_own = embed_low.astype(jnp.float32)
    sharpness_factor = jnp.exp(sharpness_exponent[0])
    angular_agreement = times_transposed(embed_low, every_low)
    sharpened_agreement = sharpness_factor * angular_agreement
    global_rows = wide_index * SEQS_DEV + jnp.arange(SEQS_DEV, dtype=jnp.int32)
    columns = jnp.arange(gathered_embeddings.shape[0], dtype=jnp.int32)
    sharpened_agreement = jnp.where(
        columns[None, :] == global_rows[:, None], masked_score, sharpened_agreement
    )
    row_top = jnp.max(sharpened_agreement, axis=1, keepdims=True)
    log_total = row_top + jnp.log(
        jnp.sum(jnp.exp(sharpened_agreement - row_top), axis=1, keepdims=True)
    )
    partner = jnp.bitwise_xor(global_rows, 1)
    positive_mask = (columns[None, :] == partner[:, None]).astype(jnp.float32)
    positive = jnp.sum(
        positive_mask * jnp.where(positive_mask > 0.0, sharpened_agreement, 0.0), axis=1
    )
    total_seqs = gathered_embeddings.shape[0]
    penalty_piece = jnp.sum(log_total[:, 0] - positive) / total_seqs
    softmax_rows = jnp.exp(sharpened_agreement - log_total)
    raw_score_slope = (softmax_rows - positive_mask) / total_seqs
    sharpness_derivative = sharpness_factor * jnp.sum(raw_score_slope * angular_agreement)
    horizontal_penalty_slope = sharpness_factor * jnp.dot(
        raw_score_slope, gathered_embeddings, precision=lax.Precision.HIGHEST
    )
    vertical_penalty_piece = sharpness_factor * lax.dot_general(
        raw_score_slope, embed_own, (((0,), (0,)), ((), ())), precision=lax.Precision.HIGHEST
    )
    embed_grad = horizontal_penalty_slope + lax.psum_scatter(
        vertical_penalty_piece, "wide", scatter_dimension=0, tiled=True
    )
    along = jnp.sum(projected * embed_grad, axis=1, keepdims=True)
    proj_grad = inverse * embed_grad - projected * inverse * inverse * inverse * along
    proj_grad_low = lax.dynamic_slice_in_dim(
        proj_grad, narrow_index * unit_rows, unit_rows, 1
    ).astype(jnp.bfloat16)
    proj_weight_grad = outer_product(proj_grad_low, pooled_low)
    pooled_grad = lax.psum(plain_product(proj_grad_low, proj_weight), "narrow")
    final_grad = lax.dot_general(
        member,
        pooled_grad / length_values,
        (((0,), (0,)), ((), ())),
        precision=lax.Precision.HIGHEST,
    )
    encoded_grad, final_gain_grad = norm_backward(
        layer_result, scale_three, rescaling_coefficients[2], final_grad
    )
    ffn_grad_low = encoded_grad.astype(jnp.bfloat16)
    hidden_grad = times_transposed(ffn_grad_low, outer_weight)
    outer_grad = outer_product(hidden_low, ffn_grad_low)
    (pre_grad,) = gelu_back(hidden_grad)
    pre_low = pre_grad.astype(jnp.bfloat16)
    inner_grad = outer_product(pre_low, normed_two)
    normed_two_grad = lax.psum(plain_product(pre_low, inner_weight), "narrow")
    mid_norm_grad, ffn_gain_grad = norm_backward(
        residual_mid, scale_two, rescaling_coefficients[1], normed_two_grad
    )
    mid_grad = encoded_grad + mid_norm_grad
    attn_grad_low = mid_grad.astype(jnp.bfloat16)
    context_grad = times_transposed(out_weight, attn_grad_low).astype(jnp.bfloat16)
    out_grad = outer_product(context, attn_grad_low)

    qkv_cols, qkv_rows, bias_lines = attention_backward(
        lengths,
        query_cols,
        key_rows,
        value_rows,
        key_cols,
        context_grad,
        context_cols,
        log_rows,
        apart,
        tiles_bias,
    )
    offset_bias_slope = lax.dot_general(
        bucket_onehot,
        bias_lines.reshape(heads_here, LINES * LANE),
        (((0,), (1,)), ((), ())),
        precision=lax.Precision.HIGHEST,
    )
    qkv_weight_grad = plain_product(qkv_cols, normed_one)
    normed_one_grad = lax.psum(plain_product(qkv_rows, qkv_weight), "narrow")
    input_norm_grad, attn_gain_grad = norm_backward(
        arguments_list, scale_one, rescaling_coefficients[0], normed_one_grad
    )
    input_grad = mid_grad + input_norm_grad
    unit_grads = jnp.concatenate(
        [
            qkv_weight_grad.reshape(3, unit_rows, D),
            out_grad[None],
            proj_weight_grad[None],
            inner_grad.reshape(ffn_units, unit_rows, D),
            outer_grad.reshape(ffn_units, unit_rows, D),
        ],
        axis=0,
    )
    norm_scale_slopes = jnp.stack([attn_gain_grad, ffn_gain_grad, final_gain_grad])
    gain_total, bias_total, sharpness_slope_overall, loss_total = lax.psum(
        (
            norm_scale_slopes,
            offset_bias_slope,
            sharpness_derivative.reshape(1),
            penalty_piece.reshape(1),
        ),
        "wide",
    )
    placed = (
        jnp.zeros((wide_count * CAP,) + precise_parameter_blocks.shape[1:], jnp.float32)
        .at[tile_location]
        .set(unit_grads)
    )
    slot_grads = lax.psum_scatter(placed, "wide", scatter_dimension=0, tiled=True)
    first_wide = (wide_index == 0).astype(jnp.float32)
    first_both = first_wide * (narrow_index == 0).astype(jnp.float32)
    local_squares = (
        jnp.sum(slot_grads * slot_grads)
        + first_wide * jnp.sum(bias_total * bias_total)
        + first_both
        * (
            jnp.sum(gain_total * gain_total)
            + jnp.sum(sharpness_slope_overall * sharpness_slope_overall)
        )
    )
    grad_norm = jnp.sqrt(lax.psum(local_squares, ("wide", "narrow")))
    multiplier = jnp.minimum(1.0, clip_limit / grad_norm)
    slot_first, slot_second, slot_weight = decoupled_decay_step(
        slot_grads,
        precise_mean_est,
        precise_variance_est,
        precise_parameter_blocks,
        multiplier,
        learn_rate,
    )
    gain_first, gain_second, gain_new = decoupled_decay_step(
        gain_total,
        norm_scale_mean_est,
        norm_scale_variance_est,
        rescaling_coefficients,
        multiplier,
        side_rate,
    )
    bias_first, bias_second, bias_new = decoupled_decay_step(
        bias_total,
        offset_bias_mean_est,
        offset_bias_variance_est,
        distance_bias_table,
        multiplier,
        side_rate,
    )
    sharpness_mean_fresh, sharpness_variance_fresh, sharpness_exponent_fresh = decoupled_decay_step(
        sharpness_slope_overall,
        sharpness_mean_est,
        sharpness_variance_est,
        sharpness_exponent,
        multiplier,
        learn_rate,
    )
    return (
        loss_total[0],
        layer_result,
        input_grad,
        grad_norm,
        slot_first,
        slot_second,
        slot_weight,
        gain_first,
        gain_second,
        gain_new,
        bias_first,
        bias_second,
        bias_new,
        sharpness_mean_fresh,
        sharpness_variance_fresh,
        sharpness_exponent_fresh,
    )


def solution(mesh):
    placed = (
        P("wide", None),
        P("wide", None),
        P(),
        P(),
        P("wide", "narrow", None),
        P("wide", "narrow", None),
        P("wide", "narrow", None),
        P(),
        P(),
        P(),
        P(None, "narrow"),
        P(None, "narrow"),
        P(None, "narrow"),
        P(),
        P(),
        P(),
    )
    return jax.shard_map(
        on_device,
        mesh=mesh,
        in_specs=placed,
        out_specs=(
            P(),
            P("wide", None),
            P("wide", None),
            P(),
            P("wide", "narrow", None),
            P("wide", "narrow", None),
            P("wide", "narrow", None),
            P(),
            P(),
            P(),
            P(None, "narrow"),
            P(None, "narrow"),
            P(None, "narrow"),
            P(),
            P(),
            P(),
        ),
        check_vma=False,
    )
```

```python
import jax
import jax.numpy as jnp
from jax import lax
from jax.experimental import pallas as pl
from jax.experimental.pallas import tpu as pltpu
from jax.sharding import PartitionSpec as P

D = 768
FF = 3072
BUCKETS = 32
TOK_DEV = 2560
SEQS_DEV = 4
DOCLEN = 1024
CAP = 2
STEP = 10
LANE = 128
BQ = 512
BK = 512
REACH = DOCLEN // LANE
OFF = REACH + (BQ + BK) // LANE
SPAN = 2 * OFF + 1
LINES = 2 * REACH + 2
VMEM_LIMIT = 56 * 1024 * 1024

norm_eps = 1e-06
clip_limit = 0.01
learn_rate = 0.01
side_rate = 0.5
beta_one = 0.5
beta_two = 0.5
adam_eps = 1e-08
decay_rate = 0.01
score_scale = 0.125
masked_score = -1e30
low_type = jnp.bfloat16


def times_transposed(left_side, right_side):
    return lax.dot_general(
        left_side, right_side, (((1,), (1,)), ((), ())), preferred_element_type=jnp.float32
    )


def plain_product(left_side, right_side):
    return jnp.dot(left_side, right_side, preferred_element_type=jnp.float32)


def outer_product(left_side, right_side):
    return lax.dot_general(
        left_side, right_side, (((0,), (0,)), ((), ())), preferred_element_type=jnp.float32
    )


def rms_scale(values):
    return lax.rsqrt(jnp.mean(values * values, axis=-1, keepdims=True) + norm_eps)


def norm_backward(values, row_scale, gain_row, grad_out):
    weighted = grad_out * gain_row
    gain_grad = jnp.sum(grad_out * values * row_scale, axis=0)
    inner_mean = jnp.mean(weighted * values, axis=-1, keepdims=True)
    value_grad = row_scale * weighted - values * row_scale * row_scale * row_scale * inner_mean
    return (value_grad, gain_grad)


def decoupled_decay_step(gradient, first_moment, second_moment, weight, multiplier, step_rate):
    clipped = gradient * multiplier
    first_new = beta_one * first_moment + (1.0 - beta_one) * clipped
    second_new = beta_two * second_moment + (1.0 - beta_two) * clipped * clipped
    first_hat = first_new / (1.0 - beta_one**STEP)
    second_hat = second_new / (1.0 - beta_two**STEP)
    weight_new = weight - step_rate * (
        first_hat / (jnp.sqrt(second_hat) + adam_eps) + decay_rate * weight
    )
    return (first_new, second_new, weight_new)


def swap(values, bit):
    count = lax.axis_size("narrow")
    return lax.ppermute(values, "narrow", [(i, i ^ bit) for i in range(count)])


def narrow_bits():
    count = lax.axis_size("narrow")
    return [1 << s for s in range(count.bit_length() - 1)]


def peer_order():
    order = [0]
    for bit in reversed(narrow_bits()):
        order = order + [peer ^ bit for peer in order]
    return order


def join_rows(values):
    for bit in reversed(narrow_bits()):
        values = jnp.concatenate([values, swap(values, bit)], axis=0)
    return values


def add_rows(values):
    for bit in narrow_bits():
        half = values.shape[0] // 2
        came = swap(values[half:].astype(low_type), bit)
        values = values[:half].astype(jnp.float32) + came.astype(jnp.float32)
    return values


def product_add_rows(left_side, right_side):
    bits = narrow_bits()
    half = left_side.shape[0] // 2
    sent = plain_product(left_side[half:], right_side).astype(low_type)
    came = swap(sent, bits[0])
    values = plain_product(left_side[:half], right_side) + came.astype(jnp.float32)
    for bit in bits[1:]:
        half = values.shape[0] // 2
        came = swap(values[half:].astype(low_type), bit)
        values = values[:half] + came.astype(jnp.float32)
    return values


def natural_rows(joined, narrow_index):
    order = peer_order()
    group = joined.shape[0] // len(order)
    place = jnp.array([order.index(peer) for peer in range(len(order))], jnp.int32)
    return jnp.concatenate(
        [
            lax.dynamic_slice_in_dim(joined, place[g ^ narrow_index] * group, group, 0)
            for g in range(len(order))
        ],
        axis=0,
    )


def spread(values):
    count = lax.axis_size("wide") * lax.axis_size("narrow")
    copies = jnp.broadcast_to(values[None], (count,) + values.shape)
    return lax.all_to_all(copies, ("wide", "narrow"), split_axis=0, concat_axis=0, tiled=True)


def smem():
    return pl.BlockSpec(memory_space=pltpu.SMEM)


def vmem():
    return pl.BlockSpec(memory_space=pltpu.VMEM)


def bias_kernel(chunks, tiles):
    heads = tiles.shape[0]
    tiles[...] = jnp.zeros_like(tiles)
    for h in range(heads):
        for d in range(-REACH, REACH + 1):
            left = chunks[h, REACH + 1 - d : REACH + 2 - d, :]
            right = chunks[h, REACH - d : REACH + 1 - d, :]
            line = jnp.broadcast_to(jnp.concatenate([left, right], axis=1), (LANE, 2 * LANE))
            rolled = pltpu.roll(line, 0, 1, stride=1, stride_axis=0)
            tiles[h, (d + OFF) * LANE : (d + OFF + 1) * LANE, :] = rolled[:, :LANE]


def bias_tiles(rel_chunks):
    heads = rel_chunks.shape[0]
    return pl.pallas_call(
        bias_kernel,
        out_shape=jax.ShapeDtypeStruct((heads, SPAN * LANE, LANE), jnp.float32),
        compiler_params=pltpu.CompilerParams(vmem_limit_bytes=VMEM_LIMIT),
        name="bias_tiles",
    )(rel_chunks)


def key_range(lengths, first, last):
    start = jnp.int32(0)
    low = jnp.int32(0)
    high = jnp.int32(0)
    for s in range(SEQS_DEV):
        end = start + lengths[s]
        low = jnp.where(start <= first, start, low)
        high = jnp.where(start <= last, end, high)
        start = end
    return low // BK, (high + BK - 1) // BK


def bias_part(bias, h, row):
    return jnp.concatenate(
        [
            bias[h, pl.ds(pl.multiple_of(row - b * LANE, LANE), BK), :]
            for b in range(BQ // LANE)
        ],
        axis=1,
    )


def forward_kernel(first_row, lengths, origin, qT, kn, vT, apart, bias, ctx_o, ctxT_o, lse_o, qa, acc):
    width, rows_here = qT.shape
    heads = bias.shape[0]
    size = width // heads
    qa[...] = jnp.zeros_like(qa)

    @pl.loop(0, rows_here // BQ)
    def _(i):
        q0 = pl.multiple_of(i * BQ, BQ)
        here = pl.ds(q0, BQ)
        for h in range(heads):
            qa[h * LANE : h * LANE + size, :] = qT[h * size : (h + 1) * size, here]
            qa[h * LANE + size : h * LANE + size + 16, :] = apart[:, here]
        acc[...] = jnp.zeros_like(acc)
        low, high = key_range(lengths, first_row + q0, first_row + q0 + BQ - 1)

        def step(j, carry):
            k0 = pl.multiple_of(j * BK, BK)
            row = (j * (BK // LANE) - i * (BQ // LANE) - first_row // LANE + OFF) * LANE
            out = []
            for h in range(heads):
                top, total = carry[2 * h], carry[2 * h + 1]
                own = slice(h * LANE, (h + 1) * LANE)
                rows = slice(h * size, (h + 1) * size)
                s = plain_product(kn[pl.ds(k0, BK), own], qa[own, :]) + bias_part(bias, h, row)
                new_top = jnp.maximum(top, jnp.max(s, axis=0, keepdims=True))
                fade = jnp.exp(top - new_top)
                p = jnp.exp(s - new_top)
                total = total * fade + jnp.sum(p, axis=0, keepdims=True)
                acc[rows, :] = acc[rows, :] * fade + plain_product(
                    vT[rows, pl.ds(k0, BK)], p.astype(low_type)
                )
                out += [new_top, total]
            return tuple(out)

        init = tuple(
            jnp.full((1, BQ), 2.0 * masked_score if n % 2 == 0 else 0.0, jnp.float32)
            for n in range(2 * heads)
        )
        done = lax.fori_loop(low, high, step, init)
        for h in range(heads):
            rows = slice(h * size, (h + 1) * size)
            acc[rows, :] = acc[rows, :] / done[2 * h + 1]
            lse_o[h : h + 1, here] = done[2 * h] + jnp.log(done[2 * h + 1])
        ctxT_o[:, here] = acc[...]
        turned = acc[...].T.astype(low_type)
        for b in range(BQ // LANE):
            at = pl.multiple_of(origin[i * (BQ // LANE) + b], LANE)
            ctx_o[pl.ds(at, LANE), :] = turned[b * LANE : (b + 1) * LANE, :]


def attention_forward(first_row, lengths, origin, qT, kn, vT, apart, bias):
    width, rows_here = qT.shape
    heads = bias.shape[0]

    def body(*refs):
        forward_kernel(first_row, *refs)

    return pl.pallas_call(
        body,
        out_shape=(
            jax.ShapeDtypeStruct((rows_here, width), low_type),
            jax.ShapeDtypeStruct((width, rows_here), jnp.float32),
            jax.ShapeDtypeStruct((heads, rows_here), jnp.float32),
        ),
        in_specs=[smem()] * 2 + [vmem()] * 5,
        out_specs=(vmem(),) * 3,
        scratch_shapes=[
            pltpu.VMEM((heads * LANE, BQ), low_type),
            pltpu.VMEM((width, BQ), jnp.float32),
        ],
        compiler_params=pltpu.CompilerParams(vmem_limit_bytes=VMEM_LIMIT),
        cost_estimate=pl.CostEstimate(
            flops=8 * rows_here * TOK_DEV * width,
            bytes_accessed=12 * width * TOK_DEV,
            transcendentals=rows_here * TOK_DEV * heads,
        ),
        name="attention_forward",
    )(lengths, origin, qT, kn, vT, apart, bias)


def three_parts(values):
    first = values.astype(low_type).astype(jnp.float32)
    rest = values - first
    second = rest.astype(low_type).astype(jnp.float32)
    return first, second, rest - second


def backward_kernel(
    lengths, origin, qT, kn, vn, kT, dcn, ctxT, lse, apart, bias,
    dT_o, dn_o, lines_o, qa, da, dq, dk, dv, tiles,
):
    width, tokens = qT.shape
    heads = bias.shape[0]
    size = width // heads
    for ref in (qa, da, dk, dv, tiles):
        ref[...] = jnp.zeros_like(ref)
    place = lax.broadcasted_iota(jnp.int32, (16, BQ), 0) - SEQS_DEV

    def in_depth(values):
        a, b, c = three_parts(values)
        return jnp.where(place == 0, a, jnp.where(place == 1, b, jnp.where(place == 2, c, 0.0)))

    @pl.loop(0, tokens // BQ)
    def _(i):
        q0 = pl.multiple_of(i * BQ, BQ)
        here = pl.ds(q0, BQ)
        at = [pl.multiple_of(origin[i * (BQ // LANE) + b], LANE) for b in range(BQ // LANE)]
        dcT = jnp.concatenate(
            [dcn[pl.ds(at[b], LANE), :].astype(jnp.float32) for b in range(BQ // LANE)], axis=0
        ).T
        for h in range(heads):
            rows = slice(h * size, (h + 1) * size)
            top = h * LANE
            qa[top : top + size, :] = qT[rows, here]
            extra = apart[:, here].astype(jnp.float32) + in_depth(-lse[h : h + 1, here])
            qa[top + size : top + size + 16, :] = extra.astype(low_type)
            da[top : top + size, :] = dcT[rows, :].astype(low_type)
            delta = jnp.sum(dcT[rows, :] * ctxT[rows, here], axis=0, keepdims=True)
            da[top + size : top + size + 16, :] = in_depth(-delta).astype(low_type)
        dq[...] = jnp.zeros_like(dq)
        low, high = key_range(lengths, q0, q0 + BQ - 1)

        @pl.loop(low, high)
        def _(j):
            k0 = pl.multiple_of(j * BK, BK)
            there = pl.ds(k0, BK)
            row = (j * (BK // LANE) - i * (BQ // LANE) + OFF) * LANE
            for h in range(heads):
                rows = slice(h * size, (h + 1) * size)
                own = slice(h * LANE, (h + 1) * LANE)
                flat = slice(h * LANE, h * LANE + size)
                s = plain_product(kn[there, own], qa[own, :])
                p = jnp.exp(s + bias_part(bias, h, row))
                ds = p * plain_product(vn[there, own], da[own, :])
                for b in range(BQ // LANE):
                    window = pl.ds(pl.multiple_of(row - b * LANE, LANE), BK)
                    tiles[h, window, :] = (
                        tiles[h, window, :] + ds[:, b * LANE : (b + 1) * LANE]
                    )
                p_low = p.astype(low_type)
                ds_low = ds.astype(low_type)
                dv[rows, there] = dv[rows, there] + times_transposed(da[flat, :], p_low)
                dk[rows, there] = dk[rows, there] + times_transposed(qa[flat, :], ds_low)
                dq[rows, :] = dq[rows, :] + plain_product(kT[rows, there], ds_low)

        grad = dq[...] * score_scale
        dT_o[0:width, here] = grad.astype(low_type)
        turned = grad.T.astype(low_type)
        for b in range(BQ // LANE):
            dn_o[pl.ds(at[b], LANE), 0:width] = turned[b * LANE : (b + 1) * LANE, :]

    @pl.loop(0, tokens // BQ)
    def _(i):
        here = pl.ds(pl.multiple_of(i * BQ, BQ), BQ)
        both = jnp.concatenate([dk[:, here], dv[:, here]], axis=0)
        dT_o[width : 3 * width, here] = both.astype(low_type)
        turned = both.T.astype(low_type)
        for b in range(BQ // LANE):
            at = pl.multiple_of(origin[i * (BQ // LANE) + b], LANE)
            dn_o[pl.ds(at, LANE), width : 3 * width] = turned[b * LANE : (b + 1) * LANE, :]

    across = lax.broadcasted_iota(jnp.int32, (LANE, LANE), 1)
    over = across >= lax.broadcasted_iota(jnp.int32, (LANE, LANE), 0)
    sub = lax.broadcasted_iota(jnp.int32, (8, LANE), 0)
    for h in range(heads):
        for d in range(-REACH, REACH + 2):
            here = tiles[h, (d + OFF) * LANE : (d + OFF + 1) * LANE, :]
            below = tiles[h, (d + OFF - 1) * LANE : (d + OFF) * LANE, :]
            mixed = jnp.where(over, here, below)
            line = mixed[LANE - 8 :, :]
            for g in range(LANE // 8 - 2, -1, -1):
                line = mixed[8 * g : 8 * g + 8, :] + pltpu.roll(line, LANE - 8, 1)
            for bit in (1, 2, 4):
                line = jnp.where((sub & bit) != 0, pltpu.roll(line, LANE - bit, 1), line)
            lines_o[h, REACH + 1 - d : REACH + 2 - d, :] = jnp.sum(line, axis=0, keepdims=True)


def attention_backward(lengths, origin, qT, kn, vn, kT, dcn, ctxT, lse, apart, bias):
    width, tokens = qT.shape
    heads = bias.shape[0]
    return pl.pallas_call(
        backward_kernel,
        out_shape=(
            jax.ShapeDtypeStruct((3 * width, tokens), low_type),
            jax.ShapeDtypeStruct((tokens, 3 * width), low_type),
            jax.ShapeDtypeStruct((heads, LINES, LANE), jnp.float32),
        ),
        in_specs=[smem()] * 2 + [vmem()] * 9,
        out_specs=(vmem(),) * 3,
        scratch_shapes=[
            pltpu.VMEM((heads * LANE, BQ), low_type),
            pltpu.VMEM((heads * LANE, BQ), low_type),
            pltpu.VMEM((width, BQ), jnp.float32),
            pltpu.VMEM((width, tokens), jnp.float32),
            pltpu.VMEM((width, tokens), jnp.float32),
            pltpu.VMEM((heads, SPAN * LANE, LANE), jnp.float32),
        ],
        compiler_params=pltpu.CompilerParams(vmem_limit_bytes=VMEM_LIMIT),
        cost_estimate=pl.CostEstimate(
            flops=20 * tokens * TOK_DEV * width,
            bytes_accessed=30 * width * TOK_DEV,
            transcendentals=tokens * TOK_DEV * heads,
        ),
        name="attention_backward",
    )(lengths, origin, qT, kn, vn, kT, dcn, ctxT, lse, apart, bias)


def on_device(
    layer_argument,
    document_extents,
    distance_bin_lookup,
    tile_location,
    precise_parameter_blocks,
    precise_mean_est,
    precise_variance_est,
    rescaling_coefficients,
    norm_scale_mean_est,
    norm_scale_variance_est,
    distance_bias_table,
    offset_bias_mean_est,
    offset_bias_variance_est,
    sharpness_exponent,
    sharpness_mean_est,
    sharpness_variance_est,
):
    wide_count = lax.axis_size("wide")
    narrow_count = lax.axis_size("narrow")
    wide_index = lax.axis_index("wide")
    narrow_index = lax.axis_index("narrow")
    order = peer_order()
    place_of = jnp.array([order.index(peer) for peer in range(narrow_count)], jnp.int32)
    unit_rows = precise_parameter_blocks.shape[1]
    heads_here = distance_bias_table.shape[1]
    head_size = unit_rows // heads_here
    ffn_units = FF // D
    group = TOK_DEV // narrow_count
    own_slots = wide_index * CAP + jnp.arange(CAP, dtype=jnp.int32)

    every_slot = lax.all_gather(
        precise_parameter_blocks.astype(low_type), "wide", axis=0, tiled=True
    )

    def block(u):
        return lax.dynamic_index_in_dim(every_slot, tile_location[u], 0, keepdims=False)

    qkv_weight = jnp.concatenate([block(u) for u in range(3)], axis=0)
    inner_weight = jnp.concatenate([block(5 + k) for k in range(ffn_units)], axis=0)
    outer_weight = jnp.concatenate([block(5 + ffn_units + k) for k in range(ffn_units)], axis=0)
    both_joined = join_rows(jnp.stack([block(3), block(4)])[None])
    out_joined = both_joined[:, 0].reshape(D, D)
    proj_weight = natural_rows(both_joined[:, 1].reshape(D, D), narrow_index)

    lengths = document_extents[0]
    seq_ends = jnp.cumsum(lengths)
    positions = jnp.arange(TOK_DEV, dtype=jnp.int32)

    def segments_of(where):
        return jnp.sum((seq_ends[None, :] <= where[:, None]).astype(jnp.int32), axis=1)

    segment_ids = segments_of(positions)
    peers = jnp.array(order, jnp.int32)[positions // group]
    joined_segments = segments_of((peers ^ narrow_index) * group + positions % group)
    own_segments = joined_segments[:group]
    tile_starts = jnp.arange(TOK_DEV // LANE, dtype=jnp.int32) * LANE
    origin = place_of[(tile_starts // group) ^ narrow_index] * group + tile_starts % group

    beyond = LINES * LANE - LANE - 1 - distance_bin_lookup.shape[0]
    offsets_down = jnp.pad(distance_bin_lookup[::-1], (LANE + 1, beyond), constant_values=-1)
    bucket_onehot = (
        offsets_down[:, None] == jnp.arange(BUCKETS, dtype=jnp.int32)[None, :]
    ).astype(jnp.float32)
    rel_values = jnp.dot(bucket_onehot, distance_bias_table, precision=lax.Precision.HIGHEST).T
    tiles_bias = bias_tiles(rel_values.reshape(heads_here, LINES, LANE))

    all_rows = layer_argument.astype(jnp.float32)
    normed_one = (all_rows * rms_scale(all_rows) * rescaling_coefficients[0]).astype(low_type)
    transposed_rows = times_transposed(qkv_weight, normed_one)
    query_cols = (transposed_rows[:unit_rows] * score_scale).astype(low_type)
    key_cols = transposed_rows[unit_rows : 2 * unit_rows].astype(low_type)
    value_cols = transposed_rows[2 * unit_rows :].astype(low_type)
    spread_weight = jnp.pad(
        qkv_weight[unit_rows:].reshape(2 * heads_here, head_size, D),
        ((0, 0), (0, LANE - head_size), (0, 0)),
    ).reshape(2 * heads_here * LANE, D)
    lane_place = jnp.arange(2 * heads_here * LANE, dtype=jnp.int32) % LANE - head_size
    marks = jnp.logical_or(
        lane_place[None, :] == segment_ids[:, None],
        jnp.logical_and(lane_place >= SEQS_DEV, lane_place < SEQS_DEV + 3)[None, :],
    )
    key_value_rows = (
        times_transposed(normed_one, spread_weight) + marks.astype(jnp.float32)
    ).astype(low_type)
    key_rows = key_value_rows[:, : heads_here * LANE]
    value_rows = key_value_rows[:, heads_here * LANE :]
    row_place = jnp.arange(16, dtype=jnp.int32)[:, None]
    apart = jnp.where(
        jnp.logical_and(row_place < SEQS_DEV, row_place != segment_ids[None, :]), masked_score, 0.0
    ).astype(low_type)
    context, context_cols, log_rows = attention_forward(
        0, lengths, origin, query_cols, key_rows, value_cols, apart, tiles_bias
    )

    def to_peer(values, peer):
        if peer == 0:
            return values
        pairs = [(i, i ^ peer) for i in range(narrow_count)]
        return lax.ppermute(values, "narrow", pairs)

    context_own = jnp.concatenate(
        [
            to_peer(context[s * group : (s + 1) * group], peer)
            for s, peer in enumerate(order)
        ],
        axis=1,
    )
    own_rows = lax.dynamic_slice_in_dim(layer_argument, narrow_index * group, group, 0).astype(
        jnp.float32
    )
    scale_one = rms_scale(own_rows)
    residual_mid = own_rows + plain_product(context_own, out_joined)
    scale_two = rms_scale(residual_mid)
    normed_two_own = (residual_mid * scale_two * rescaling_coefficients[1]).astype(low_type)
    normed_two = join_rows(normed_two_own)

    gate_pre = times_transposed(normed_two, inner_weight)
    hidden_act, gelu_back = jax.vjp(jax.nn.gelu, gate_pre)
    hidden_low = hidden_act.astype(low_type)
    result_own = residual_mid + product_add_rows(hidden_low, outer_weight)
    result_joined = join_rows(result_own.astype(low_type))
    layer_result = natural_rows(result_joined, narrow_index).astype(jnp.float32)

    scale_three = rms_scale(result_own)
    member = (
        own_segments[None, :] == jnp.arange(SEQS_DEV, dtype=jnp.int32)[:, None]
    ).astype(jnp.float32)
    length_values = lengths.astype(jnp.float32)[:, None]
    unscaled_part = (
        jnp.dot(member, result_own * scale_three, precision=lax.Precision.HIGHEST) / length_values
    )
    total_seqs = wide_count * SEQS_DEV
    unscaled = jnp.sum(
        spread(unscaled_part).reshape(wide_count, narrow_count, SEQS_DEV, D), axis=1
    ).reshape(total_seqs, D)
    pooled_low = (unscaled * rescaling_coefficients[2]).astype(low_type)
    projected = times_transposed(pooled_low, proj_weight).astype(low_type).astype(jnp.float32)
    inverse = lax.rsqrt(jnp.sum(projected * projected, axis=1, keepdims=True) + norm_eps)
    embed_low = (projected * inverse).astype(low_type)
    embeddings = embed_low.astype(jnp.float32)
    sharpness_factor = jnp.exp(sharpness_exponent[0])
    angular_agreement = times_transposed(embed_low, embed_low)
    seq_index = jnp.arange(total_seqs, dtype=jnp.int32)
    sharpened_agreement = jnp.where(
        seq_index[None, :] == seq_index[:, None],
        masked_score,
        sharpness_factor * angular_agreement,
    )
    row_top = jnp.max(sharpened_agreement, axis=1, keepdims=True)
    log_total = row_top + jnp.log(
        jnp.sum(jnp.exp(sharpened_agreement - row_top), axis=1, keepdims=True)
    )
    partner = seq_index[None, :] == jnp.bitwise_xor(seq_index, 1)[:, None]
    positive = jnp.sum(jnp.where(partner, sharpened_agreement, 0.0), axis=1)
    loss = jnp.mean(log_total[:, 0] - positive)
    raw_score_slope = (
        jnp.exp(sharpened_agreement - log_total) - partner.astype(jnp.float32)
    ) / total_seqs
    sharpness_slope = sharpness_factor * jnp.sum(raw_score_slope * angular_agreement)
    embed_grad = sharpness_factor * jnp.dot(
        raw_score_slope + raw_score_slope.T, embeddings, precision=lax.Precision.HIGHEST
    )
    along = jnp.sum(projected * embed_grad, axis=1, keepdims=True)
    proj_grad_low = (
        inverse * embed_grad - projected * inverse * inverse * inverse * along
    ).astype(low_type)
    proj_weight_grad = outer_product(
        lax.dynamic_slice_in_dim(proj_grad_low, narrow_index * unit_rows, unit_rows, 1), pooled_low
    )
    pooled_grad = plain_product(proj_grad_low, proj_weight)
    final_gain_grad = jnp.sum(pooled_grad * unscaled, axis=0)
    own_pooled_grad = lax.dynamic_slice_in_dim(
        pooled_grad, wide_index * SEQS_DEV, SEQS_DEV, 0
    ) * (rescaling_coefficients[2] / length_values)

    def final_backward(values, segments):
        weighted = own_pooled_grad[SEQS_DEV - 1]
        for s in range(SEQS_DEV - 2, -1, -1):
            weighted = jnp.where((segments == s)[:, None], own_pooled_grad[s], weighted)
        row_scale = rms_scale(values)
        inner_mean = jnp.mean(weighted * values, axis=-1, keepdims=True)
        return row_scale * weighted - values * (row_scale * row_scale * row_scale * inner_mean)

    encoded_grad = final_backward(result_own, own_segments)
    ffn_grad_low = final_backward(result_joined.astype(jnp.float32), joined_segments).astype(
        low_type
    )
    hidden_grad = times_transposed(ffn_grad_low, outer_weight)
    outer_grad = outer_product(hidden_low, ffn_grad_low)
    (pre_grad,) = gelu_back(hidden_grad)
    pre_low = pre_grad.astype(low_type)
    inner_grad = outer_product(pre_low, normed_two)
    normed_two_grad = product_add_rows(pre_low, inner_weight)
    mid_norm_grad, ffn_gain_grad = norm_backward(
        residual_mid, scale_two, rescaling_coefficients[1], normed_two_grad
    )
    mid_grad = encoded_grad + mid_norm_grad
    attn_grad_low = mid_grad.astype(low_type)
    out_grad = add_rows(outer_product(context_own, attn_grad_low))

    context_grad = jnp.concatenate(
        [
            to_peer(
                times_transposed(
                    attn_grad_low, out_joined[s * unit_rows : (s + 1) * unit_rows]
                ).astype(low_type),
                peer,
            )
            for s, peer in enumerate(order)
        ],
        axis=0,
    )
    qkv_cols, qkv_rows, bias_lines = attention_backward(
        lengths,
        origin,
        query_cols,
        key_rows,
        value_rows,
        key_cols,
        context_grad,
        context_cols,
        log_rows,
        apart,
        tiles_bias,
    )
    offset_bias_slope = lax.dot_general(
        bucket_onehot,
        bias_lines.reshape(heads_here, LINES * LANE),
        (((0,), (1,)), ((), ())),
        precision=lax.Precision.HIGHEST,
    )

    early = {3: out_grad}
    for k in range(ffn_units):
        rows = slice(k * unit_rows, (k + 1) * unit_rows)
        early[5 + k] = inner_grad[rows]
        early[5 + ffn_units + k] = outer_grad[rows]
    early_units = sorted(early)
    stacked = jnp.stack([early[u].astype(low_type) for u in early_units])
    slots = jnp.arange(wide_count * CAP, dtype=jnp.int32)
    held = slots[:, None] == tile_location[jnp.array(early_units)][None, :]
    source = jnp.sum(held * jnp.arange(len(early_units), dtype=jnp.int32)[None, :], axis=1)
    placed = jnp.where(
        jnp.any(held, axis=1)[:, None, None], stacked[source], jnp.zeros((), low_type)
    )
    slot_grads = lax.psum_scatter(placed, "wide", scatter_dimension=0, tiled=True).astype(
        jnp.float32
    )
    proj_here = (own_slots == tile_location[4]).astype(jnp.float32)
    slot_grads = slot_grads + proj_here[:, None, None] * proj_weight_grad[None]

    qkv_weight_grad = plain_product(qkv_cols, normed_one).astype(low_type)
    parts = lax.all_to_all(
        qkv_weight_grad.reshape(wide_count, 3 * unit_rows // wide_count, D),
        "wide",
        split_axis=0,
        concat_axis=0,
        tiled=True,
    )
    qkv_part = jnp.sum(parts.astype(jnp.float32), axis=0)
    qkv_whole = lax.all_gather(qkv_part.astype(low_type), "wide", axis=0, tiled=True).reshape(
        3, unit_rows, D
    )
    normed_one_grad = product_add_rows(qkv_rows, qkv_weight)
    input_norm_grad, attn_gain_grad = norm_backward(
        own_rows, scale_one, rescaling_coefficients[0], normed_one_grad
    )
    input_own = mid_grad + input_norm_grad
    input_grad = natural_rows(join_rows(input_own.astype(low_type)), narrow_index).astype(
        jnp.float32
    )

    bias_size = offset_bias_slope.size
    small = jnp.stack(
        [
            ffn_gain_grad,
            attn_gain_grad,
            jnp.pad(offset_bias_slope.reshape(bias_size), (0, D - bias_size)),
        ]
    )
    small_all = spread(small).reshape(wide_count, narrow_count, 3, D)
    gain_sums = jnp.sum(small_all[:, :, :2], axis=(0, 1))
    gain_total = jnp.stack([gain_sums[1], gain_sums[0], final_gain_grad])
    bias_all = jnp.sum(small_all[:, :, 2], axis=0)
    bias_total = lax.dynamic_index_in_dim(bias_all, narrow_index, 0, keepdims=False)[
        :bias_size
    ].reshape(offset_bias_slope.shape)
    sharpness_total = sharpness_slope.reshape(1)
    local_squares = jnp.sum(slot_grads * slot_grads) + jnp.sum(qkv_part * qkv_part)
    square_terms = spread(jnp.broadcast_to(local_squares, (8, LANE)))[:, 0, 0]
    grad_norm = jnp.sqrt(
        jnp.sum(square_terms)
        + jnp.sum(gain_total * gain_total)
        + jnp.sum(bias_all * bias_all)
        + sharpness_slope * sharpness_slope
    )
    multiplier = jnp.minimum(1.0, clip_limit / grad_norm)
    for u in range(3):
        here = (own_slots == tile_location[u])[:, None, None]
        slot_grads = jnp.where(here, qkv_whole[u].astype(jnp.float32)[None], slot_grads)
    slot_first, slot_second, slot_weight = decoupled_decay_step(
        slot_grads,
        precise_mean_est,
        precise_variance_est,
        precise_parameter_blocks,
        multiplier,
        learn_rate,
    )
    gain_first, gain_second, gain_new = decoupled_decay_step(
        gain_total,
        norm_scale_mean_est,
        norm_scale_variance_est,
        rescaling_coefficients,
        multiplier,
        side_rate,
    )
    bias_first, bias_second, bias_new = decoupled_decay_step(
        bias_total,
        offset_bias_mean_est,
        offset_bias_variance_est,
        distance_bias_table,
        multiplier,
        side_rate,
    )
    sharpness_mean_fresh, sharpness_variance_fresh, sharpness_exponent_fresh = decoupled_decay_step(
        sharpness_total,
        sharpness_mean_est,
        sharpness_variance_est,
        sharpness_exponent,
        multiplier,
        learn_rate,
    )
    return (
        loss,
        layer_result,
        input_grad,
        grad_norm,
        slot_first,
        slot_second,
        slot_weight,
        gain_first,
        gain_second,
        gain_new,
        bias_first,
        bias_second,
        bias_new,
        sharpness_mean_fresh,
        sharpness_variance_fresh,
        sharpness_exponent_fresh,
    )


def solution(mesh):
    placed = (
        P("wide", None),
        P("wide", None),
        P(),
        P(),
        P("wide", "narrow", None),
        P("wide", "narrow", None),
        P("wide", "narrow", None),
        P(),
        P(),
        P(),
        P(None, "narrow"),
        P(None, "narrow"),
        P(None, "narrow"),
        P(),
        P(),
        P(),
    )
    return jax.shard_map(
        on_device,
        mesh=mesh,
        in_specs=placed,
        out_specs=(
            P(),
            P("wide", None),
            P("wide", None),
            P(),
            P("wide", "narrow", None),
            P("wide", "narrow", None),
            P("wide", "narrow", None),
            P(),
            P(),
            P(),
            P(None, "narrow"),
            P(None, "narrow"),
            P(None, "narrow"),
            P(),
            P(),
            P(),
        ),
        check_vma=False,
    )
```

```python
import jax
import jax.numpy as jnp
from jax import lax
from jax.experimental import pallas as pl
from jax.experimental.pallas import tpu as pltpu
from jax.sharding import PartitionSpec as P

D = 768
FF = 3072
BUCKETS = 32
TOK_DEV = 2560
SEQS_DEV = 4
DOCLEN = 1024
CAP = 2
STEP = 10
LANE = 128
BQ = 512
BK = 512
REACH = DOCLEN // LANE
OFF = REACH + (BQ + BK) // LANE
SPAN = 2 * OFF + 1
LINES = 2 * REACH + 2
VMEM_LIMIT = 56 * 1024 * 1024

norm_eps = 1e-06
clip_limit = 0.01
learn_rate = 0.01
side_rate = 0.5
beta_one = 0.5
beta_two = 0.5
adam_eps = 1e-08
decay_rate = 0.01
score_scale = 0.125
masked_score = -1e30
low_type = jnp.bfloat16


def times_transposed(left_side, right_side):
    return lax.dot_general(
        left_side, right_side, (((1,), (1,)), ((), ())), preferred_element_type=jnp.float32
    )


def plain_product(left_side, right_side):
    return jnp.dot(left_side, right_side, preferred_element_type=jnp.float32)


def outer_product(left_side, right_side):
    return lax.dot_general(
        left_side, right_side, (((0,), (0,)), ((), ())), preferred_element_type=jnp.float32
    )


def rms_scale(values):
    return lax.rsqrt(jnp.mean(values * values, axis=-1, keepdims=True) + norm_eps)


def norm_backward(values, row_scale, gain_row, grad_out):
    weighted = grad_out * gain_row
    gain_grad = jnp.sum(grad_out * values * row_scale, axis=0)
    inner_mean = jnp.mean(weighted * values, axis=-1, keepdims=True)
    value_grad = row_scale * weighted - values * row_scale * row_scale * row_scale * inner_mean
    return (value_grad, gain_grad)


def decoupled_decay_step(gradient, first_moment, second_moment, weight, multiplier, step_rate):
    clipped = gradient * multiplier
    first_new = beta_one * first_moment + (1.0 - beta_one) * clipped
    second_new = beta_two * second_moment + (1.0 - beta_two) * clipped * clipped
    first_hat = first_new / (1.0 - beta_one**STEP)
    second_hat = second_new / (1.0 - beta_two**STEP)
    weight_new = weight - step_rate * (
        first_hat / (jnp.sqrt(second_hat) + adam_eps) + decay_rate * weight
    )
    return (first_new, second_new, weight_new)


def swap(values, bit):
    count = lax.axis_size("narrow")
    return lax.ppermute(values, "narrow", [(i, i ^ bit) for i in range(count)])


def narrow_bits():
    count = lax.axis_size("narrow")
    return [1 << s for s in range(count.bit_length() - 1)]


def peer_order():
    order = [0]
    for bit in reversed(narrow_bits()):
        order = order + [peer ^ bit for peer in order]
    return order


def join_rows(values):
    for bit in reversed(narrow_bits()):
        values = jnp.concatenate([values, swap(values, bit)], axis=0)
    return values


def add_rows(values):
    for bit in narrow_bits():
        half = values.shape[0] // 2
        came = swap(values[half:].astype(low_type), bit)
        values = values[:half].astype(jnp.float32) + came.astype(jnp.float32)
    return values


def product_add_rows(left_side, right_side):
    bits = narrow_bits()
    half = left_side.shape[0] // 2
    sent = plain_product(left_side[half:], right_side).astype(low_type)
    came = swap(sent, bits[0])
    values = plain_product(left_side[:half], right_side) + came.astype(jnp.float32)
    for bit in bits[1:]:
        half = values.shape[0] // 2
        came = swap(values[half:].astype(low_type), bit)
        values = values[:half] + came.astype(jnp.float32)
    return values


def natural_rows(joined, narrow_index):
    order = peer_order()
    group = joined.shape[0] // len(order)
    place = jnp.array([order.index(peer) for peer in range(len(order))], jnp.int32)
    return jnp.concatenate(
        [
            lax.dynamic_slice_in_dim(joined, place[g ^ narrow_index] * group, group, 0)
            for g in range(len(order))
        ],
        axis=0,
    )


def spread(values):
    count = lax.axis_size("wide") * lax.axis_size("narrow")
    copies = jnp.broadcast_to(values[None], (count,) + values.shape)
    return lax.all_to_all(copies, ("wide", "narrow"), split_axis=0, concat_axis=0, tiled=True)


def smem():
    return pl.BlockSpec(memory_space=pltpu.SMEM)


def vmem():
    return pl.BlockSpec(memory_space=pltpu.VMEM)


def bias_kernel(chunks, tiles):
    heads = tiles.shape[0]
    tiles[...] = jnp.zeros_like(tiles)
    for h in range(heads):
        for d in range(-REACH, REACH + 1):
            left = chunks[h, REACH + 1 - d : REACH + 2 - d, :]
            right = chunks[h, REACH - d : REACH + 1 - d, :]
            line = jnp.broadcast_to(jnp.concatenate([left, right], axis=1), (LANE, 2 * LANE))
            rolled = pltpu.roll(line, 0, 1, stride=1, stride_axis=0)
            tiles[h, (d + OFF) * LANE : (d + OFF + 1) * LANE, :] = rolled[:, :LANE]


def bias_tiles(rel_chunks):
    heads = rel_chunks.shape[0]
    return pl.pallas_call(
        bias_kernel,
        out_shape=jax.ShapeDtypeStruct((heads, SPAN * LANE, LANE), jnp.float32),
        compiler_params=pltpu.CompilerParams(vmem_limit_bytes=VMEM_LIMIT),
        name="bias_tiles",
    )(rel_chunks)


def key_range(lengths, first, last):
    start = jnp.int32(0)
    low = jnp.int32(0)
    high = jnp.int32(0)
    for s in range(SEQS_DEV):
        end = start + lengths[s]
        low = jnp.where(start <= first, start, low)
        high = jnp.where(start <= last, end, high)
        start = end
    return low // BK, (high + BK - 1) // BK


def bias_part(bias, h, row):
    return jnp.concatenate(
        [
            bias[h, pl.ds(pl.multiple_of(row - b * LANE, LANE), BK), :]
            for b in range(BQ // LANE)
        ],
        axis=1,
    )


def forward_kernel(first_row, lengths, origin, qT, kn, vT, apart, bias, ctx_o, ctxT_o, lse_o, qa, acc):
    width, rows_here = qT.shape
    heads = bias.shape[0]
    size = width // heads
    qa[...] = jnp.zeros_like(qa)

    @pl.loop(0, rows_here // BQ)
    def _(i):
        q0 = pl.multiple_of(i * BQ, BQ)
        here = pl.ds(q0, BQ)
        for h in range(heads):
            qa[h * LANE : h * LANE + size, :] = qT[h * size : (h + 1) * size, here]
            qa[h * LANE + size : h * LANE + size + 16, :] = apart[:, here]
        acc[...] = jnp.zeros_like(acc)
        low, high = key_range(lengths, first_row + q0, first_row + q0 + BQ - 1)

        def step(j, carry):
            k0 = pl.multiple_of(j * BK, BK)
            row = (j * (BK // LANE) - i * (BQ // LANE) - first_row // LANE + OFF) * LANE
            out = []
            for h in range(heads):
                top, total = carry[2 * h], carry[2 * h + 1]
                own = slice(h * LANE, (h + 1) * LANE)
                rows = slice(h * size, (h + 1) * size)
                s = plain_product(kn[pl.ds(k0, BK), own], qa[own, :]) + bias_part(bias, h, row)
                new_top = jnp.maximum(top, jnp.max(s, axis=0, keepdims=True))
                fade = jnp.exp(top - new_top)
                p = jnp.exp(s - new_top)
                total = total * fade + jnp.sum(p, axis=0, keepdims=True)
                acc[rows, :] = acc[rows, :] * fade + plain_product(
                    vT[rows, pl.ds(k0, BK)], p.astype(low_type)
                )
                out += [new_top, total]
            return tuple(out)

        init = tuple(
            jnp.full((1, BQ), 2.0 * masked_score if n % 2 == 0 else 0.0, jnp.float32)
            for n in range(2 * heads)
        )
        done = lax.fori_loop(low, high, step, init)
        for h in range(heads):
            rows = slice(h * size, (h + 1) * size)
            acc[rows, :] = acc[rows, :] / done[2 * h + 1]
            lse_o[h : h + 1, here] = done[2 * h] + jnp.log(done[2 * h + 1])
        ctxT_o[:, here] = acc[...]
        turned = acc[...].T.astype(low_type)
        for b in range(BQ // LANE):
            at = pl.multiple_of(origin[i * (BQ // LANE) + b], LANE)
            ctx_o[pl.ds(at, LANE), :] = turned[b * LANE : (b + 1) * LANE, :]


def attention_forward(first_row, lengths, origin, qT, kn, vT, apart, bias):
    width, rows_here = qT.shape
    heads = bias.shape[0]

    def body(*refs):
        forward_kernel(first_row, *refs)

    return pl.pallas_call(
        body,
        out_shape=(
            jax.ShapeDtypeStruct((rows_here, width), low_type),
            jax.ShapeDtypeStruct((width, rows_here), jnp.float32),
            jax.ShapeDtypeStruct((heads, rows_here), jnp.float32),
        ),
        in_specs=[smem()] * 2 + [vmem()] * 5,
        out_specs=(vmem(),) * 3,
        scratch_shapes=[
            pltpu.VMEM((heads * LANE, BQ), low_type),
            pltpu.VMEM((width, BQ), jnp.float32),
        ],
        compiler_params=pltpu.CompilerParams(vmem_limit_bytes=VMEM_LIMIT),
        cost_estimate=pl.CostEstimate(
            flops=8 * rows_here * TOK_DEV * width,
            bytes_accessed=12 * width * TOK_DEV,
            transcendentals=rows_here * TOK_DEV * heads,
        ),
        name="attention_forward",
    )(lengths, origin, qT, kn, vT, apart, bias)


def three_parts(values):
    first = values.astype(low_type).astype(jnp.float32)
    rest = values - first
    second = rest.astype(low_type).astype(jnp.float32)
    return first, second, rest - second


def backward_kernel(
    lengths, origin, qT, kn, vn, kT, dcn, ctxT, lse, apart, bias,
    dT_o, dn_o, lines_o, qa, da, dq, dk, dv, tiles,
):
    width, tokens = qT.shape
    heads = bias.shape[0]
    size = width // heads
    for ref in (qa, da, dk, dv, tiles):
        ref[...] = jnp.zeros_like(ref)
    place = lax.broadcasted_iota(jnp.int32, (16, BQ), 0) - SEQS_DEV

    def in_depth(values):
        a, b, c = three_parts(values)
        return jnp.where(place == 0, a, jnp.where(place == 1, b, jnp.where(place == 2, c, 0.0)))

    @pl.loop(0, tokens // BQ)
    def _(i):
        q0 = pl.multiple_of(i * BQ, BQ)
        here = pl.ds(q0, BQ)
        at = [pl.multiple_of(origin[i * (BQ // LANE) + b], LANE) for b in range(BQ // LANE)]
        dcT = jnp.concatenate(
            [dcn[pl.ds(at[b], LANE), :].astype(jnp.float32) for b in range(BQ // LANE)], axis=0
        ).T
        for h in range(heads):
            rows = slice(h * size, (h + 1) * size)
            top = h * LANE
            qa[top : top + size, :] = qT[rows, here]
            extra = apart[:, here].astype(jnp.float32) + in_depth(-lse[h : h + 1, here])
            qa[top + size : top + size + 16, :] = extra.astype(low_type)
            da[top : top + size, :] = dcT[rows, :].astype(low_type)
            delta = jnp.sum(dcT[rows, :] * ctxT[rows, here], axis=0, keepdims=True)
            da[top + size : top + size + 16, :] = in_depth(-delta).astype(low_type)
        dq[...] = jnp.zeros_like(dq)
        low, high = key_range(lengths, q0, q0 + BQ - 1)

        @pl.loop(low, high)
        def _(j):
            k0 = pl.multiple_of(j * BK, BK)
            there = pl.ds(k0, BK)
            row = (j * (BK // LANE) - i * (BQ // LANE) + OFF) * LANE
            for h in range(heads):
                rows = slice(h * size, (h + 1) * size)
                own = slice(h * LANE, (h + 1) * LANE)
                flat = slice(h * LANE, h * LANE + size)
                s = plain_product(kn[there, own], qa[own, :])
                p = jnp.exp(s + bias_part(bias, h, row))
                ds = p * plain_product(vn[there, own], da[own, :])
                for b in range(BQ // LANE):
                    window = pl.ds(pl.multiple_of(row - b * LANE, LANE), BK)
                    tiles[h, window, :] = (
                        tiles[h, window, :] + ds[:, b * LANE : (b + 1) * LANE]
                    )
                p_low = p.astype(low_type)
                ds_low = ds.astype(low_type)
                dv[rows, there] = dv[rows, there] + times_transposed(da[flat, :], p_low)
                dk[rows, there] = dk[rows, there] + times_transposed(qa[flat, :], ds_low)
                dq[rows, :] = dq[rows, :] + plain_product(kT[rows, there], ds_low)

        grad = dq[...] * score_scale
        dT_o[0:width, here] = grad.astype(low_type)
        turned = grad.T.astype(low_type)
        for b in range(BQ // LANE):
            dn_o[pl.ds(at[b], LANE), 0:width] = turned[b * LANE : (b + 1) * LANE, :]

    @pl.loop(0, tokens // BQ)
    def _(i):
        here = pl.ds(pl.multiple_of(i * BQ, BQ), BQ)
        both = jnp.concatenate([dk[:, here], dv[:, here]], axis=0)
        dT_o[width : 3 * width, here] = both.astype(low_type)
        turned = both.T.astype(low_type)
        for b in range(BQ // LANE):
            at = pl.multiple_of(origin[i * (BQ // LANE) + b], LANE)
            dn_o[pl.ds(at, LANE), width : 3 * width] = turned[b * LANE : (b + 1) * LANE, :]

    across = lax.broadcasted_iota(jnp.int32, (LANE, LANE), 1)
    over = across >= lax.broadcasted_iota(jnp.int32, (LANE, LANE), 0)
    sub = lax.broadcasted_iota(jnp.int32, (8, LANE), 0)
    for h in range(heads):
        for d in range(-REACH, REACH + 2):
            here = tiles[h, (d + OFF) * LANE : (d + OFF + 1) * LANE, :]
            below = tiles[h, (d + OFF - 1) * LANE : (d + OFF) * LANE, :]
            mixed = jnp.where(over, here, below)
            line = mixed[LANE - 8 :, :]
            for g in range(LANE // 8 - 2, -1, -1):
                line = mixed[8 * g : 8 * g + 8, :] + pltpu.roll(line, LANE - 8, 1)
            for bit in (1, 2, 4):
                line = jnp.where((sub & bit) != 0, pltpu.roll(line, LANE - bit, 1), line)
            lines_o[h, REACH + 1 - d : REACH + 2 - d, :] = jnp.sum(line, axis=0, keepdims=True)


def attention_backward(lengths, origin, qT, kn, vn, kT, dcn, ctxT, lse, apart, bias):
    width, tokens = qT.shape
    heads = bias.shape[0]
    return pl.pallas_call(
        backward_kernel,
        out_shape=(
            jax.ShapeDtypeStruct((3 * width, tokens), low_type),
            jax.ShapeDtypeStruct((tokens, 3 * width), low_type),
            jax.ShapeDtypeStruct((heads, LINES, LANE), jnp.float32),
        ),
        in_specs=[smem()] * 2 + [vmem()] * 9,
        out_specs=(vmem(),) * 3,
        scratch_shapes=[
            pltpu.VMEM((heads * LANE, BQ), low_type),
            pltpu.VMEM((heads * LANE, BQ), low_type),
            pltpu.VMEM((width, BQ), jnp.float32),
            pltpu.VMEM((width, tokens), jnp.float32),
            pltpu.VMEM((width, tokens), jnp.float32),
            pltpu.VMEM((heads, SPAN * LANE, LANE), jnp.float32),
        ],
        compiler_params=pltpu.CompilerParams(vmem_limit_bytes=VMEM_LIMIT),
        cost_estimate=pl.CostEstimate(
            flops=20 * tokens * TOK_DEV * width,
            bytes_accessed=30 * width * TOK_DEV,
            transcendentals=tokens * TOK_DEV * heads,
        ),
        name="attention_backward",
    )(lengths, origin, qT, kn, vn, kT, dcn, ctxT, lse, apart, bias)


def loss_kernel(place, numbers, parts, proj_weight, gain, out_slope, out_low, out_row, out_gain):
    total_seqs = out_low.shape[0] // 2
    terms = parts.shape[0] // total_seqs
    exact = dict(precision=lax.Precision.HIGHEST, preferred_element_type=jnp.float32)
    seq = lax.broadcasted_iota(jnp.int32, (total_seqs, parts.shape[0]), 0)
    part = lax.broadcasted_iota(jnp.int32, (total_seqs, parts.shape[0]), 1)
    joins = jnp.logical_and(
        seq // SEQS_DEV == part // (SEQS_DEV * terms), seq % SEQS_DEV == part % SEQS_DEV
    )
    unscaled = jnp.dot(joins.astype(jnp.float32), parts[...], **exact)
    pooled_low = (unscaled * gain[...]).astype(low_type)
    projected = times_transposed(pooled_low, proj_weight[...]).astype(low_type).astype(jnp.float32)
    inverse = lax.rsqrt(jnp.sum(projected * projected, axis=1, keepdims=True) + norm_eps)
    embed_low = (projected * inverse).astype(low_type)
    sharpness_factor = jnp.exp(jnp.full((1, 1), numbers[0], jnp.float32))
    agreement = times_transposed(embed_low, embed_low)
    row = lax.broadcasted_iota(jnp.int32, (total_seqs, total_seqs), 0)
    column = lax.broadcasted_iota(jnp.int32, (total_seqs, total_seqs), 1)
    logits = jnp.where(row == column, masked_score, sharpness_factor * agreement)
    partner = (row ^ 1) == column

    def log_sum(axis):
        top = jnp.max(logits, axis=axis, keepdims=True)
        return top + jnp.log(jnp.sum(jnp.exp(logits - top), axis=axis, keepdims=True))

    log_rows = log_sum(1)
    positive = jnp.where(partner, 1.0, 0.0)
    slope = (jnp.exp(logits - log_rows) - positive) / total_seqs
    slope_turned = (jnp.exp(logits - log_sum(0)) - positive) / total_seqs
    embed_grad = sharpness_factor * jnp.dot(
        slope + slope_turned, embed_low.astype(jnp.float32), **exact
    )
    along = jnp.sum(projected * embed_grad, axis=1, keepdims=True)
    proj_grad_low = (
        inverse * embed_grad - projected * inverse * inverse * inverse * along
    ).astype(low_type)
    pooled_grad = plain_product(proj_grad_low, proj_weight[...])
    out_low[0:total_seqs, :] = proj_grad_low
    out_low[total_seqs : 2 * total_seqs, :] = pooled_low
    out_gain[...] = jnp.sum(pooled_grad * unscaled, axis=0, keepdims=True)
    loss = jnp.sum(
        log_rows - jnp.sum(positive * jnp.where(partner, logits, 0.0), axis=1, keepdims=True),
        axis=0,
        keepdims=True,
    ) / total_seqs
    temperature = sharpness_factor * jnp.sum(
        jnp.sum(slope * agreement, axis=1, keepdims=True), axis=0, keepdims=True
    )
    lane = lax.broadcasted_iota(jnp.int32, (1, LANE), 1)
    out_row[...] = jnp.where(lane == 0, loss, jnp.where(lane == 1, temperature, 0.0))
    mine = lax.broadcasted_iota(jnp.int32, (8, total_seqs), 0)
    seq_of = lax.broadcasted_iota(jnp.int32, (8, total_seqs), 1) - place[0] * SEQS_DEV
    picks = jnp.logical_and(mine == seq_of, mine < SEQS_DEV).astype(jnp.float32)
    own = jnp.dot(picks, pooled_grad, **exact)
    index = lax.broadcasted_iota(jnp.int32, (8, 1), 0)
    extent = jnp.ones((8, 1), jnp.float32)
    for s in range(SEQS_DEV):
        extent = jnp.where(index == s, place[1 + s].astype(jnp.float32), extent)
    out_slope[...] = own * gain[...] / extent


def contrastive(place, numbers, parts, proj_weight, gain, total_seqs):
    return pl.pallas_call(
        loss_kernel,
        out_shape=(
            jax.ShapeDtypeStruct((8, D), jnp.float32),
            jax.ShapeDtypeStruct((2 * total_seqs, D), low_type),
            jax.ShapeDtypeStruct((1, LANE), jnp.float32),
            jax.ShapeDtypeStruct((1, D), jnp.float32),
        ),
        in_specs=[smem()] * 2 + [vmem()] * 3,
        out_specs=(vmem(),) * 4,
        compiler_params=pltpu.CompilerParams(vmem_limit_bytes=VMEM_LIMIT),
        cost_estimate=pl.CostEstimate(
            flops=4 * total_seqs * D * D, bytes_accessed=4 * D * D, transcendentals=total_seqs
        ),
        name="contrastive",
    )(place, numbers, parts, proj_weight, gain)


def on_device(
    layer_argument,
    document_extents,
    distance_bin_lookup,
    tile_location,
    precise_parameter_blocks,
    precise_mean_est,
    precise_variance_est,
    rescaling_coefficients,
    norm_scale_mean_est,
    norm_scale_variance_est,
    distance_bias_table,
    offset_bias_mean_est,
    offset_bias_variance_est,
    sharpness_exponent,
    sharpness_mean_est,
    sharpness_variance_est,
):
    wide_count = lax.axis_size("wide")
    narrow_count = lax.axis_size("narrow")
    wide_index = lax.axis_index("wide")
    narrow_index = lax.axis_index("narrow")
    order = peer_order()
    place_of = jnp.array([order.index(peer) for peer in range(narrow_count)], jnp.int32)
    unit_rows = precise_parameter_blocks.shape[1]
    heads_here = distance_bias_table.shape[1]
    head_size = unit_rows // heads_here
    ffn_units = FF // D
    group = TOK_DEV // narrow_count
    own_slots = wide_index * CAP + jnp.arange(CAP, dtype=jnp.int32)

    every_slot = lax.all_gather(
        precise_parameter_blocks.astype(low_type), "wide", axis=0, tiled=True
    )

    def block(u):
        return lax.dynamic_index_in_dim(every_slot, tile_location[u], 0, keepdims=False)

    qkv_weight = jnp.concatenate([block(u) for u in range(3)], axis=0)
    crossing = [
        jnp.concatenate([block(u) for u in units], axis=0)
        for units in ((3, 4), range(5, 5 + ffn_units), range(5 + ffn_units, 5 + 2 * ffn_units))
    ]
    bits = narrow_bits()
    for bit in reversed(bits[1:]):
        crossing = [jnp.concatenate([rows, swap(rows, bit)], axis=0) for rows in crossing]

    lengths = document_extents[0]
    seq_ends = jnp.cumsum(lengths)
    positions = jnp.arange(TOK_DEV, dtype=jnp.int32)

    def segments_of(where):
        return jnp.sum((seq_ends[None, :] <= where[:, None]).astype(jnp.int32), axis=1)

    segment_ids = segments_of(positions)
    own_segments = segments_of(narrow_index * group + positions[:group])
    tile_starts = jnp.arange(TOK_DEV // LANE, dtype=jnp.int32) * LANE
    origin = place_of[(tile_starts // group) ^ narrow_index] * group + tile_starts % group

    beyond = LINES * LANE - LANE - 1 - distance_bin_lookup.shape[0]
    offsets_down = jnp.pad(distance_bin_lookup[::-1], (LANE + 1, beyond), constant_values=-1)
    bucket_onehot = (
        offsets_down[:, None] == jnp.arange(BUCKETS, dtype=jnp.int32)[None, :]
    ).astype(jnp.float32)
    rel_values = jnp.dot(bucket_onehot, distance_bias_table, precision=lax.Precision.HIGHEST).T
    tiles_bias = bias_tiles(rel_values.reshape(heads_here, LINES, LANE))

    all_rows = layer_argument.astype(jnp.float32)
    normed_one = (all_rows * rms_scale(all_rows) * rescaling_coefficients[0]).astype(low_type)
    transposed_rows = times_transposed(qkv_weight, normed_one)
    query_cols = (transposed_rows[:unit_rows] * score_scale).astype(low_type)
    key_cols = transposed_rows[unit_rows : 2 * unit_rows].astype(low_type)
    value_cols = transposed_rows[2 * unit_rows :].astype(low_type)
    spread_weight = jnp.pad(
        qkv_weight[unit_rows:].reshape(2 * heads_here, head_size, D),
        ((0, 0), (0, LANE - head_size), (0, 0)),
    ).reshape(2 * heads_here * LANE, D)
    lane_place = jnp.arange(2 * heads_here * LANE, dtype=jnp.int32) % LANE - head_size
    marks = jnp.logical_or(
        lane_place[None, :] == segment_ids[:, None],
        jnp.logical_and(lane_place >= SEQS_DEV, lane_place < SEQS_DEV + 3)[None, :],
    )
    key_value_rows = (
        times_transposed(normed_one, spread_weight) + marks.astype(jnp.float32)
    ).astype(low_type)
    key_rows = key_value_rows[:, : heads_here * LANE]
    value_rows = key_value_rows[:, heads_here * LANE :]
    row_place = jnp.arange(16, dtype=jnp.int32)[:, None]
    apart = jnp.where(
        jnp.logical_and(row_place < SEQS_DEV, row_place != segment_ids[None, :]), masked_score, 0.0
    ).astype(low_type)
    context, context_cols, log_rows = attention_forward(
        0, lengths, origin, query_cols, key_rows, value_cols, apart, tiles_bias
    )

    context, *crossing = lax.optimization_barrier((context, *crossing))
    both_joined, inner_joined, outer_joined = [
        jnp.concatenate([rows, swap(rows, bits[0])], axis=0) for rows in crossing
    ]
    both_joined = both_joined.reshape(narrow_count, 2, unit_rows, D)
    out_joined = both_joined[:, 0].reshape(D, D)
    proj_weight = natural_rows(both_joined[:, 1].reshape(D, D), narrow_index)

    def to_peer(values, peer):
        if peer == 0:
            return values
        pairs = [(i, i ^ peer) for i in range(narrow_count)]
        return lax.ppermute(values, "narrow", pairs)

    context_own = jnp.concatenate(
        [
            to_peer(context[s * group : (s + 1) * group], peer)
            for s, peer in enumerate(order)
        ],
        axis=1,
    )
    own_rows = lax.dynamic_slice_in_dim(layer_argument, narrow_index * group, group, 0).astype(
        jnp.float32
    )
    scale_one = rms_scale(own_rows)
    residual_mid = own_rows + plain_product(context_own, out_joined)
    scale_two = rms_scale(residual_mid)
    normed_two = (residual_mid * scale_two * rescaling_coefficients[1]).astype(low_type)

    gate_pre = times_transposed(normed_two, inner_joined)
    hidden_act, gelu_back = jax.vjp(jax.nn.gelu, gate_pre)
    hidden_low = hidden_act.astype(low_type)
    result_own = residual_mid + plain_product(hidden_low, outer_joined)
    layer_result = natural_rows(join_rows(result_own.astype(low_type)), narrow_index).astype(
        jnp.float32
    )

    scale_three = rms_scale(result_own)
    member = (
        own_segments[None, :] == jnp.arange(SEQS_DEV, dtype=jnp.int32)[:, None]
    ).astype(jnp.float32)
    length_values = lengths.astype(jnp.float32)[:, None]
    unscaled_part = (
        jnp.dot(member, result_own * scale_three, precision=lax.Precision.HIGHEST) / length_values
    )
    total_seqs = wide_count * SEQS_DEV
    own_pooled_grad, loss_low, loss_row, final_gain_grad = contrastive(
        jnp.concatenate([wide_index.reshape(1), lengths]),
        sharpness_exponent,
        spread(unscaled_part).reshape(total_seqs * narrow_count, D),
        proj_weight,
        rescaling_coefficients[2:3],
        total_seqs,
    )
    loss = loss_row[0, 0]
    sharpness_total = loss_row[0, 1:2]
    proj_grad_own = lax.dynamic_slice_in_dim(
        loss_low[:total_seqs], narrow_index * unit_rows, unit_rows, 1
    )
    proj_weight_grad = outer_product(proj_grad_own, loss_low[total_seqs:])

    weighted = own_pooled_grad[SEQS_DEV - 1]
    for s in range(SEQS_DEV - 2, -1, -1):
        weighted = jnp.where((own_segments == s)[:, None], own_pooled_grad[s], weighted)
    inner_mean = jnp.mean(weighted * result_own, axis=-1, keepdims=True)
    encoded_grad = scale_three * weighted - result_own * (
        scale_three * scale_three * scale_three * inner_mean
    )
    ffn_grad_low = encoded_grad.astype(low_type)
    outer_grad = add_rows(outer_product(hidden_low, ffn_grad_low).astype(low_type))
    hidden_grad = times_transposed(ffn_grad_low, outer_joined)
    (pre_grad,) = gelu_back(hidden_grad)
    pre_low = pre_grad.astype(low_type)
    inner_grad = add_rows(outer_product(pre_low, normed_two).astype(low_type))
    normed_two_grad = plain_product(pre_low, inner_joined)
    mid_norm_grad, ffn_gain_grad = norm_backward(
        residual_mid, scale_two, rescaling_coefficients[1], normed_two_grad
    )
    mid_grad = encoded_grad + mid_norm_grad
    attn_grad_low = mid_grad.astype(low_type)
    out_grad = add_rows(outer_product(context_own, attn_grad_low))

    context_grad = jnp.concatenate(
        [
            to_peer(
                times_transposed(
                    attn_grad_low, out_joined[s * unit_rows : (s + 1) * unit_rows]
                ).astype(low_type),
                peer,
            )
            for s, peer in enumerate(order)
        ],
        axis=0,
    )
    context_grad, layer_result = lax.optimization_barrier((context_grad, layer_result))
    qkv_cols, qkv_rows, bias_lines = attention_backward(
        lengths,
        origin,
        query_cols,
        key_rows,
        value_rows,
        key_cols,
        context_grad,
        context_cols,
        log_rows,
        apart,
        tiles_bias,
    )
    offset_bias_slope = lax.dot_general(
        bucket_onehot,
        bias_lines.reshape(heads_here, LINES * LANE),
        (((0,), (1,)), ((), ())),
        precision=lax.Precision.HIGHEST,
    )

    early = {3: out_grad}
    for k in range(ffn_units):
        rows = slice(k * unit_rows, (k + 1) * unit_rows)
        early[5 + k] = inner_grad[rows]
        early[5 + ffn_units + k] = outer_grad[rows]
    early_units = sorted(early)
    stacked = jnp.stack(
        [early[u].astype(low_type) for u in early_units] + [jnp.zeros((unit_rows, D), low_type)]
    )
    slots = jnp.arange(wide_count * CAP, dtype=jnp.int32)
    held = slots[:, None] == tile_location[jnp.array(early_units)][None, :]
    steps = jnp.arange(len(early_units), dtype=jnp.int32) - len(early_units)
    source = len(early_units) + jnp.sum(held * steps[None, :], axis=1)
    placed = jnp.take(stacked, source, axis=0, mode="clip")
    slot_grads = lax.psum_scatter(placed, "wide", scatter_dimension=0, tiled=True).astype(
        jnp.float32
    )
    proj_here = (own_slots == tile_location[4]).astype(jnp.float32)
    slot_grads = slot_grads + proj_here[:, None, None] * proj_weight_grad[None]

    qkv_weight_grad = plain_product(qkv_cols, normed_one).astype(low_type)
    parts = lax.all_to_all(
        qkv_weight_grad.reshape(wide_count, 3 * unit_rows // wide_count, D),
        "wide",
        split_axis=0,
        concat_axis=0,
        tiled=True,
    )
    qkv_part = jnp.sum(parts.astype(jnp.float32), axis=0)
    copies = jnp.broadcast_to(qkv_part.astype(low_type)[None], (wide_count,) + qkv_part.shape)
    qkv_whole = lax.all_to_all(
        copies, "wide", split_axis=0, concat_axis=0, tiled=True
    ).reshape(3, unit_rows, D)
    normed_one_grad = product_add_rows(qkv_rows, qkv_weight)
    input_norm_grad, attn_gain_grad = norm_backward(
        own_rows, scale_one, rescaling_coefficients[0], normed_one_grad
    )
    input_own = mid_grad + input_norm_grad
    input_grad = natural_rows(join_rows(input_own.astype(low_type)), narrow_index).astype(
        jnp.float32
    )

    bias_size = offset_bias_slope.size
    small = jnp.stack(
        [
            ffn_gain_grad,
            attn_gain_grad,
            jnp.pad(offset_bias_slope.reshape(bias_size), (0, D - bias_size)),
        ]
    )
    small_all = spread(small).reshape(wide_count, narrow_count, 3, D)
    gain_sums = jnp.sum(small_all[:, :, :2], axis=(0, 1))
    gain_total = jnp.stack([gain_sums[1], gain_sums[0], final_gain_grad[0]])
    bias_all = jnp.sum(small_all[:, :, 2], axis=0)
    bias_total = lax.dynamic_index_in_dim(bias_all, narrow_index, 0, keepdims=False)[
        :bias_size
    ].reshape(offset_bias_slope.shape)
    local_squares = jnp.sum(slot_grads * slot_grads) + jnp.sum(qkv_part * qkv_part)
    square_terms = spread(jnp.broadcast_to(local_squares, (8, LANE)))[:, 0, 0]
    grad_norm = jnp.sqrt(
        jnp.sum(square_terms)
        + jnp.sum(gain_total * gain_total)
        + jnp.sum(bias_all * bias_all)
        + jnp.sum(sharpness_total * sharpness_total)
    )
    multiplier = jnp.minimum(1.0, clip_limit / grad_norm)
    for u in range(3):
        here = (own_slots == tile_location[u])[:, None, None]
        slot_grads = jnp.where(here, qkv_whole[u].astype(jnp.float32)[None], slot_grads)
    slot_first, slot_second, slot_weight = decoupled_decay_step(
        slot_grads,
        precise_mean_est,
        precise_variance_est,
        precise_parameter_blocks,
        multiplier,
        learn_rate,
    )
    gain_first, gain_second, gain_new = decoupled_decay_step(
        gain_total,
        norm_scale_mean_est,
        norm_scale_variance_est,
        rescaling_coefficients,
        multiplier,
        side_rate,
    )
    bias_first, bias_second, bias_new = decoupled_decay_step(
        bias_total,
        offset_bias_mean_est,
        offset_bias_variance_est,
        distance_bias_table,
        multiplier,
        side_rate,
    )
    sharpness_mean_fresh, sharpness_variance_fresh, sharpness_exponent_fresh = decoupled_decay_step(
        sharpness_total,
        sharpness_mean_est,
        sharpness_variance_est,
        sharpness_exponent,
        multiplier,
        learn_rate,
    )
    return (
        loss,
        layer_result,
        input_grad,
        grad_norm,
        slot_first,
        slot_second,
        slot_weight,
        gain_first,
        gain_second,
        gain_new,
        bias_first,
        bias_second,
        bias_new,
        sharpness_mean_fresh,
        sharpness_variance_fresh,
        sharpness_exponent_fresh,
    )


def solution(mesh):
    placed = (
        P("wide", None),
        P("wide", None),
        P(),
        P(),
        P("wide", "narrow", None),
        P("wide", "narrow", None),
        P("wide", "narrow", None),
        P(),
        P(),
        P(),
        P(None, "narrow"),
        P(None, "narrow"),
        P(None, "narrow"),
        P(),
        P(),
        P(),
    )
    return jax.shard_map(
        on_device,
        mesh=mesh,
        in_specs=placed,
        out_specs=(
            P(),
            P("wide", None),
            P("wide", None),
            P(),
            P("wide", "narrow", None),
            P("wide", "narrow", None),
            P("wide", "narrow", None),
            P(),
            P(),
            P(),
            P(None, "narrow"),
            P(None, "narrow"),
            P(None, "narrow"),
            P(),
            P(),
            P(),
        ),
        check_vma=False,
    )
```

```python
import jax
import jax.numpy as jnp
from jax import lax
from jax.experimental import pallas as pl
from jax.experimental.pallas import tpu as pltpu
from jax.sharding import PartitionSpec as P

D = 768
FF = 3072
BUCKETS = 32
TOK_DEV = 2560
SEQS_DEV = 4
DOCLEN = 1024
CAP = 2
STEP = 10
LANE = 128
BQ = 512
BK = 512
REACH = DOCLEN // LANE
OFF = REACH + (BQ + BK) // LANE
SPAN = 2 * OFF + 1
LINES = 2 * REACH + 2
VMEM_LIMIT = 56 * 1024 * 1024

norm_eps = 1e-06
clip_limit = 0.01
learn_rate = 0.01
side_rate = 0.5
beta_one = 0.5
beta_two = 0.5
adam_eps = 1e-08
decay_rate = 0.01
score_scale = 0.125
masked_score = -1e30
low_type = jnp.bfloat16


def times_transposed(left_side, right_side):
    return lax.dot_general(
        left_side, right_side, (((1,), (1,)), ((), ())), preferred_element_type=jnp.float32
    )


def plain_product(left_side, right_side):
    return jnp.dot(left_side, right_side, preferred_element_type=jnp.float32)


def outer_product(left_side, right_side):
    return lax.dot_general(
        left_side, right_side, (((0,), (0,)), ((), ())), preferred_element_type=jnp.float32
    )


def rms_scale(values):
    return lax.rsqrt(jnp.mean(values * values, axis=-1, keepdims=True) + norm_eps)


def norm_backward(values, row_scale, gain_row, grad_out):
    weighted = grad_out * gain_row
    gain_grad = jnp.sum(grad_out * values * row_scale, axis=0)
    inner_mean = jnp.mean(weighted * values, axis=-1, keepdims=True)
    value_grad = row_scale * weighted - values * row_scale * row_scale * row_scale * inner_mean
    return (value_grad, gain_grad)


def decoupled_decay_step(gradient, first_moment, second_moment, weight, multiplier, step_rate):
    clipped = gradient * multiplier
    first_new = beta_one * first_moment + (1.0 - beta_one) * clipped
    second_new = beta_two * second_moment + (1.0 - beta_two) * clipped * clipped
    first_hat = first_new / (1.0 - beta_one**STEP)
    second_hat = second_new / (1.0 - beta_two**STEP)
    weight_new = weight - step_rate * (
        first_hat / (jnp.sqrt(second_hat) + adam_eps) + decay_rate * weight
    )
    return (first_new, second_new, weight_new)


def swap(values, bit):
    count = lax.axis_size("narrow")
    return lax.ppermute(values, "narrow", [(i, i ^ bit) for i in range(count)])


def narrow_bits():
    count = lax.axis_size("narrow")
    return [1 << s for s in range(count.bit_length() - 1)]


def peer_order():
    order = [0]
    for bit in reversed(narrow_bits()):
        order = order + [peer ^ bit for peer in order]
    return order


def join_rows(values):
    for bit in reversed(narrow_bits()):
        values = jnp.concatenate([values, swap(values, bit)], axis=0)
    return values


def after(values, other):
    return lax.optimization_barrier((values, other))[0]


def first_add(values):
    bit = narrow_bits()[0]
    half = values.shape[0] // 2
    came = swap(values[half:], bit)
    values = (values[:half].astype(jnp.float32) + came.astype(jnp.float32)).astype(low_type)
    return values[: half // 2], values[half // 2 :]


def gelu_and_slope(values):
    rate = 0.7978845608028654
    cubic = 0.044715
    squares = values * values
    turn = jnp.tanh(rate * values * (1.0 + cubic * squares))
    half = 0.5 * (1.0 + turn)
    slope = half + 0.5 * values * (1.0 - turn * turn) * (rate * (1.0 + 3.0 * cubic * squares))
    return (values * half).astype(low_type), slope.astype(low_type)


def product_add_rows(left_side, right_side):
    bits = narrow_bits()
    half = left_side.shape[0] // 2
    sent = plain_product(left_side[half:], right_side).astype(low_type)
    came = swap(sent, bits[0])
    values = plain_product(left_side[:half], right_side) + came.astype(jnp.float32)
    for bit in bits[1:]:
        half = values.shape[0] // 2
        came = swap(values[half:].astype(low_type), bit)
        values = values[:half] + came.astype(jnp.float32)
    return values


def natural_rows(joined, narrow_index):
    order = peer_order()
    group = joined.shape[0] // len(order)
    place = jnp.array([order.index(peer) for peer in range(len(order))], jnp.int32)
    return jnp.concatenate(
        [
            lax.dynamic_slice_in_dim(joined, place[g ^ narrow_index] * group, group, 0)
            for g in range(len(order))
        ],
        axis=0,
    )


def spread(values):
    count = lax.axis_size("wide") * lax.axis_size("narrow")
    copies = jnp.broadcast_to(values[None], (count,) + values.shape)
    return lax.all_to_all(copies, ("wide", "narrow"), split_axis=0, concat_axis=0, tiled=True)


def smem():
    return pl.BlockSpec(memory_space=pltpu.SMEM)


def vmem():
    return pl.BlockSpec(memory_space=pltpu.VMEM)


def bias_kernel(chunks, tiles):
    heads = tiles.shape[0]
    tiles[...] = jnp.zeros_like(tiles)
    for h in range(heads):
        for d in range(-REACH, REACH + 1):
            left = chunks[h, REACH + 1 - d : REACH + 2 - d, :]
            right = chunks[h, REACH - d : REACH + 1 - d, :]
            line = jnp.broadcast_to(jnp.concatenate([left, right], axis=1), (LANE, 2 * LANE))
            rolled = pltpu.roll(line, 0, 1, stride=1, stride_axis=0)
            tiles[h, (d + OFF) * LANE : (d + OFF + 1) * LANE, :] = rolled[:, :LANE]


def bias_tiles(rel_chunks):
    heads = rel_chunks.shape[0]
    return pl.pallas_call(
        bias_kernel,
        out_shape=jax.ShapeDtypeStruct((heads, SPAN * LANE, LANE), jnp.float32),
        compiler_params=pltpu.CompilerParams(vmem_limit_bytes=VMEM_LIMIT),
        name="bias_tiles",
    )(rel_chunks)


def key_range(lengths, first, last):
    start = jnp.int32(0)
    low = jnp.int32(0)
    high = jnp.int32(0)
    for s in range(SEQS_DEV):
        end = start + lengths[s]
        low = jnp.where(start <= first, start, low)
        high = jnp.where(start <= last, end, high)
        start = end
    return low // BK, (high + BK - 1) // BK


def bias_part(bias, h, row):
    return jnp.concatenate(
        [
            bias[h, pl.ds(pl.multiple_of(row - b * LANE, LANE), BK), :]
            for b in range(BQ // LANE)
        ],
        axis=1,
    )


def forward_kernel(first_row, lengths, origin, qT, kn, vT, apart, bias, ctx_o, ctxT_o, lse_o, qa, acc):
    width, rows_here = qT.shape
    heads = bias.shape[0]
    size = width // heads
    qa[...] = jnp.zeros_like(qa)

    @pl.loop(0, rows_here // BQ)
    def _(i):
        q0 = pl.multiple_of(i * BQ, BQ)
        here = pl.ds(q0, BQ)
        for h in range(heads):
            qa[h * LANE : h * LANE + size, :] = qT[h * size : (h + 1) * size, here]
            qa[h * LANE + size : h * LANE + size + 16, :] = apart[:, here]
        acc[...] = jnp.zeros_like(acc)
        low, high = key_range(lengths, first_row + q0, first_row + q0 + BQ - 1)

        def step(j, carry):
            k0 = pl.multiple_of(j * BK, BK)
            row = (j * (BK // LANE) - i * (BQ // LANE) - first_row // LANE + OFF) * LANE
            out = []
            for h in range(heads):
                top, total = carry[2 * h], carry[2 * h + 1]
                own = slice(h * LANE, (h + 1) * LANE)
                rows = slice(h * size, (h + 1) * size)
                s = plain_product(kn[pl.ds(k0, BK), own], qa[own, :]) + bias_part(bias, h, row)
                new_top = jnp.maximum(top, jnp.max(s, axis=0, keepdims=True))
                fade = jnp.exp(top - new_top)
                p = jnp.exp(s - new_top)
                total = total * fade + jnp.sum(p, axis=0, keepdims=True)
                acc[rows, :] = acc[rows, :] * fade + plain_product(
                    vT[rows, pl.ds(k0, BK)], p.astype(low_type)
                )
                out += [new_top, total]
            return tuple(out)

        init = tuple(
            jnp.full((1, BQ), 2.0 * masked_score if n % 2 == 0 else 0.0, jnp.float32)
            for n in range(2 * heads)
        )
        done = lax.fori_loop(low, high, step, init)
        for h in range(heads):
            rows = slice(h * size, (h + 1) * size)
            acc[rows, :] = acc[rows, :] / done[2 * h + 1]
            lse_o[h : h + 1, here] = done[2 * h] + jnp.log(done[2 * h + 1])
        ctxT_o[:, here] = acc[...]
        turned = acc[...].T.astype(low_type)
        for b in range(BQ // LANE):
            at = pl.multiple_of(origin[i * (BQ // LANE) + b], LANE)
            ctx_o[pl.ds(at, LANE), :] = turned[b * LANE : (b + 1) * LANE, :]


def attention_forward(first_row, lengths, origin, qT, kn, vT, apart, bias):
    width, rows_here = qT.shape
    heads = bias.shape[0]

    def body(*refs):
        forward_kernel(first_row, *refs)

    return pl.pallas_call(
        body,
        out_shape=(
            jax.ShapeDtypeStruct((rows_here, width), low_type),
            jax.ShapeDtypeStruct((width, rows_here), jnp.float32),
            jax.ShapeDtypeStruct((heads, rows_here), jnp.float32),
        ),
        in_specs=[smem()] * 2 + [vmem()] * 5,
        out_specs=(vmem(),) * 3,
        scratch_shapes=[
            pltpu.VMEM((heads * LANE, BQ), low_type),
            pltpu.VMEM((width, BQ), jnp.float32),
        ],
        compiler_params=pltpu.CompilerParams(vmem_limit_bytes=VMEM_LIMIT),
        cost_estimate=pl.CostEstimate(
            flops=8 * rows_here * TOK_DEV * width,
            bytes_accessed=12 * width * TOK_DEV,
            transcendentals=rows_here * TOK_DEV * heads,
        ),
        name="attention_forward",
    )(lengths, origin, qT, kn, vT, apart, bias)


def three_parts(values):
    first = values.astype(low_type).astype(jnp.float32)
    rest = values - first
    second = rest.astype(low_type).astype(jnp.float32)
    return first, second, rest - second


def backward_kernel(
    lengths, origin, qT, kn, vn, kT, dcn, ctxT, lse, apart, bias,
    dT_o, dn_o, lines_o, qa, da, dq, dk, dv, tiles,
):
    width, tokens = qT.shape
    heads = bias.shape[0]
    size = width // heads
    for ref in (qa, da, dk, dv, tiles):
        ref[...] = jnp.zeros_like(ref)
    place = lax.broadcasted_iota(jnp.int32, (16, BQ), 0) - SEQS_DEV

    def in_depth(values):
        a, b, c = three_parts(values)
        return jnp.where(place == 0, a, jnp.where(place == 1, b, jnp.where(place == 2, c, 0.0)))

    @pl.loop(0, tokens // BQ)
    def _(i):
        q0 = pl.multiple_of(i * BQ, BQ)
        here = pl.ds(q0, BQ)
        at = [pl.multiple_of(origin[i * (BQ // LANE) + b], LANE) for b in range(BQ // LANE)]
        dcT = jnp.concatenate(
            [dcn[pl.ds(at[b], LANE), :].astype(jnp.float32) for b in range(BQ // LANE)], axis=0
        ).T
        for h in range(heads):
            rows = slice(h * size, (h + 1) * size)
            top = h * LANE
            qa[top : top + size, :] = qT[rows, here]
            extra = apart[:, here].astype(jnp.float32) + in_depth(-lse[h : h + 1, here])
            qa[top + size : top + size + 16, :] = extra.astype(low_type)
            da[top : top + size, :] = dcT[rows, :].astype(low_type)
            delta = jnp.sum(dcT[rows, :] * ctxT[rows, here], axis=0, keepdims=True)
            da[top + size : top + size + 16, :] = in_depth(-delta).astype(low_type)
        dq[...] = jnp.zeros_like(dq)
        low, high = key_range(lengths, q0, q0 + BQ - 1)

        @pl.loop(low, high)
        def _(j):
            k0 = pl.multiple_of(j * BK, BK)
            there = pl.ds(k0, BK)
            row = (j * (BK // LANE) - i * (BQ // LANE) + OFF) * LANE
            for h in range(heads):
                rows = slice(h * size, (h + 1) * size)
                own = slice(h * LANE, (h + 1) * LANE)
                flat = slice(h * LANE, h * LANE + size)
                s = plain_product(kn[there, own], qa[own, :])
                p = jnp.exp(s + bias_part(bias, h, row))
                ds = p * plain_product(vn[there, own], da[own, :])
                for b in range(BQ // LANE):
                    window = pl.ds(pl.multiple_of(row - b * LANE, LANE), BK)
                    tiles[h, window, :] = (
                        tiles[h, window, :] + ds[:, b * LANE : (b + 1) * LANE]
                    )
                p_low = p.astype(low_type)
                ds_low = ds.astype(low_type)
                dv[rows, there] = dv[rows, there] + times_transposed(da[flat, :], p_low)
                dk[rows, there] = dk[rows, there] + times_transposed(qa[flat, :], ds_low)
                dq[rows, :] = dq[rows, :] + plain_product(kT[rows, there], ds_low)

        grad = dq[...] * score_scale
        dT_o[0:width, here] = grad.astype(low_type)
        turned = grad.T.astype(low_type)
        for b in range(BQ // LANE):
            dn_o[pl.ds(at[b], LANE), 0:width] = turned[b * LANE : (b + 1) * LANE, :]

    @pl.loop(0, tokens // BQ)
    def _(i):
        here = pl.ds(pl.multiple_of(i * BQ, BQ), BQ)
        both = jnp.concatenate([dk[:, here], dv[:, here]], axis=0)
        dT_o[width : 3 * width, here] = both.astype(low_type)
        turned = both.T.astype(low_type)
        for b in range(BQ // LANE):
            at = pl.multiple_of(origin[i * (BQ // LANE) + b], LANE)
            dn_o[pl.ds(at, LANE), width : 3 * width] = turned[b * LANE : (b + 1) * LANE, :]

    across = lax.broadcasted_iota(jnp.int32, (LANE, LANE), 1)
    over = across >= lax.broadcasted_iota(jnp.int32, (LANE, LANE), 0)
    sub = lax.broadcasted_iota(jnp.int32, (8, LANE), 0)
    for h in range(heads):
        for d in range(-REACH, REACH + 2):
            here = tiles[h, (d + OFF) * LANE : (d + OFF + 1) * LANE, :]
            below = tiles[h, (d + OFF - 1) * LANE : (d + OFF) * LANE, :]
            mixed = jnp.where(over, here, below)
            line = mixed[LANE - 8 :, :]
            for g in range(LANE // 8 - 2, -1, -1):
                line = mixed[8 * g : 8 * g + 8, :] + pltpu.roll(line, LANE - 8, 1)
            for bit in (1, 2, 4):
                line = jnp.where((sub & bit) != 0, pltpu.roll(line, LANE - bit, 1), line)
            lines_o[h, REACH + 1 - d : REACH + 2 - d, :] = jnp.sum(line, axis=0, keepdims=True)


def attention_backward(lengths, origin, qT, kn, vn, kT, dcn, ctxT, lse, apart, bias):
    width, tokens = qT.shape
    heads = bias.shape[0]
    return pl.pallas_call(
        backward_kernel,
        out_shape=(
            jax.ShapeDtypeStruct((3 * width, tokens), low_type),
            jax.ShapeDtypeStruct((tokens, 3 * width), low_type),
            jax.ShapeDtypeStruct((heads, LINES, LANE), jnp.float32),
        ),
        in_specs=[smem()] * 2 + [vmem()] * 9,
        out_specs=(vmem(),) * 3,
        scratch_shapes=[
            pltpu.VMEM((heads * LANE, BQ), low_type),
            pltpu.VMEM((heads * LANE, BQ), low_type),
            pltpu.VMEM((width, BQ), jnp.float32),
            pltpu.VMEM((width, tokens), jnp.float32),
            pltpu.VMEM((width, tokens), jnp.float32),
            pltpu.VMEM((heads, SPAN * LANE, LANE), jnp.float32),
        ],
        compiler_params=pltpu.CompilerParams(vmem_limit_bytes=VMEM_LIMIT),
        cost_estimate=pl.CostEstimate(
            flops=20 * tokens * TOK_DEV * width,
            bytes_accessed=30 * width * TOK_DEV,
            transcendentals=tokens * TOK_DEV * heads,
        ),
        name="attention_backward",
    )(lengths, origin, qT, kn, vn, kT, dcn, ctxT, lse, apart, bias)


def loss_kernel(place, numbers, parts, proj_weight, gain, out_slope, out_low, out_row, out_gain):
    total_seqs = out_low.shape[0] // 2
    terms = parts.shape[0] // total_seqs
    exact = dict(precision=lax.Precision.HIGHEST, preferred_element_type=jnp.float32)
    seq = lax.broadcasted_iota(jnp.int32, (total_seqs, parts.shape[0]), 0)
    part = lax.broadcasted_iota(jnp.int32, (total_seqs, parts.shape[0]), 1)
    joins = jnp.logical_and(
        seq // SEQS_DEV == part // (SEQS_DEV * terms), seq % SEQS_DEV == part % SEQS_DEV
    )
    unscaled = jnp.dot(joins.astype(jnp.float32), parts[...], **exact)
    pooled_low = (unscaled * gain[...]).astype(low_type)
    projected = times_transposed(pooled_low, proj_weight[...]).astype(low_type).astype(jnp.float32)
    inverse = lax.rsqrt(jnp.sum(projected * projected, axis=1, keepdims=True) + norm_eps)
    embed_low = (projected * inverse).astype(low_type)
    sharpness_factor = jnp.exp(jnp.full((1, 1), numbers[0], jnp.float32))
    agreement = times_transposed(embed_low, embed_low)
    row = lax.broadcasted_iota(jnp.int32, (total_seqs, total_seqs), 0)
    column = lax.broadcasted_iota(jnp.int32, (total_seqs, total_seqs), 1)
    logits = jnp.where(row == column, masked_score, sharpness_factor * agreement)
    partner = (row ^ 1) == column

    def log_sum(axis):
        top = jnp.max(logits, axis=axis, keepdims=True)
        return top + jnp.log(jnp.sum(jnp.exp(logits - top), axis=axis, keepdims=True))

    log_rows = log_sum(1)
    positive = jnp.where(partner, 1.0, 0.0)
    slope = (jnp.exp(logits - log_rows) - positive) / total_seqs
    slope_turned = (jnp.exp(logits - log_sum(0)) - positive) / total_seqs
    embed_grad = sharpness_factor * jnp.dot(
        slope + slope_turned, embed_low.astype(jnp.float32), **exact
    )
    along = jnp.sum(projected * embed_grad, axis=1, keepdims=True)
    proj_grad_low = (
        inverse * embed_grad - projected * inverse * inverse * inverse * along
    ).astype(low_type)
    pooled_grad = plain_product(proj_grad_low, proj_weight[...])
    out_low[0:total_seqs, :] = proj_grad_low
    out_low[total_seqs : 2 * total_seqs, :] = pooled_low
    out_gain[...] = jnp.sum(pooled_grad * unscaled, axis=0, keepdims=True)
    loss = jnp.sum(
        log_rows - jnp.sum(positive * jnp.where(partner, logits, 0.0), axis=1, keepdims=True),
        axis=0,
        keepdims=True,
    ) / total_seqs
    temperature = sharpness_factor * jnp.sum(
        jnp.sum(slope * agreement, axis=1, keepdims=True), axis=0, keepdims=True
    )
    lane = lax.broadcasted_iota(jnp.int32, (1, LANE), 1)
    out_row[...] = jnp.where(lane == 0, loss, jnp.where(lane == 1, temperature, 0.0))
    mine = lax.broadcasted_iota(jnp.int32, (8, total_seqs), 0)
    seq_of = lax.broadcasted_iota(jnp.int32, (8, total_seqs), 1) - place[0] * SEQS_DEV
    picks = jnp.logical_and(mine == seq_of, mine < SEQS_DEV).astype(jnp.float32)
    own = jnp.dot(picks, pooled_grad, **exact)
    index = lax.broadcasted_iota(jnp.int32, (8, 1), 0)
    extent = jnp.ones((8, 1), jnp.float32)
    for s in range(SEQS_DEV):
        extent = jnp.where(index == s, place[1 + s].astype(jnp.float32), extent)
    out_slope[...] = own * gain[...] / extent


def contrastive(place, numbers, parts, proj_weight, gain, total_seqs):
    return pl.pallas_call(
        loss_kernel,
        out_shape=(
            jax.ShapeDtypeStruct((8, D), jnp.float32),
            jax.ShapeDtypeStruct((2 * total_seqs, D), low_type),
            jax.ShapeDtypeStruct((1, LANE), jnp.float32),
            jax.ShapeDtypeStruct((1, D), jnp.float32),
        ),
        in_specs=[smem()] * 2 + [vmem()] * 3,
        out_specs=(vmem(),) * 4,
        compiler_params=pltpu.CompilerParams(vmem_limit_bytes=VMEM_LIMIT),
        cost_estimate=pl.CostEstimate(
            flops=4 * total_seqs * D * D, bytes_accessed=4 * D * D, transcendentals=total_seqs
        ),
        name="contrastive",
    )(place, numbers, parts, proj_weight, gain)


def on_device(
    layer_argument,
    document_extents,
    distance_bin_lookup,
    tile_location,
    precise_parameter_blocks,
    precise_mean_est,
    precise_variance_est,
    rescaling_coefficients,
    norm_scale_mean_est,
    norm_scale_variance_est,
    distance_bias_table,
    offset_bias_mean_est,
    offset_bias_variance_est,
    sharpness_exponent,
    sharpness_mean_est,
    sharpness_variance_est,
):
    wide_count = lax.axis_size("wide")
    narrow_count = lax.axis_size("narrow")
    wide_index = lax.axis_index("wide")
    narrow_index = lax.axis_index("narrow")
    order = peer_order()
    place_of = jnp.array([order.index(peer) for peer in range(narrow_count)], jnp.int32)
    unit_rows = precise_parameter_blocks.shape[1]
    heads_here = distance_bias_table.shape[1]
    head_size = unit_rows // heads_here
    ffn_units = FF // D
    group = TOK_DEV // narrow_count
    own_slots = wide_index * CAP + jnp.arange(CAP, dtype=jnp.int32)

    every_slot = lax.all_gather(
        precise_parameter_blocks.astype(low_type), "wide", axis=0, tiled=True
    )

    def block(u):
        return lax.dynamic_index_in_dim(every_slot, tile_location[u], 0, keepdims=False)

    qkv_weight = jnp.concatenate([block(u) for u in range(3)], axis=0)
    crossing = [
        jnp.concatenate([block(u) for u in units], axis=0)
        for units in ((3, 4), range(5, 5 + ffn_units), range(5 + ffn_units, 5 + 2 * ffn_units))
    ]
    qkv_weight = after(qkv_weight, crossing[0])
    bits = narrow_bits()
    for bit in reversed(bits[1:]):
        crossing = [jnp.concatenate([rows, swap(rows, bit)], axis=0) for rows in crossing]

    lengths = document_extents[0]
    seq_ends = jnp.cumsum(lengths)
    positions = jnp.arange(TOK_DEV, dtype=jnp.int32)

    def segments_of(where):
        return jnp.sum((seq_ends[None, :] <= where[:, None]).astype(jnp.int32), axis=1)

    segment_ids = segments_of(positions)
    own_segments = segments_of(narrow_index * group + positions[:group])
    tile_starts = jnp.arange(TOK_DEV // LANE, dtype=jnp.int32) * LANE
    origin = place_of[(tile_starts // group) ^ narrow_index] * group + tile_starts % group

    beyond = LINES * LANE - LANE - 1 - distance_bin_lookup.shape[0]
    offsets_down = jnp.pad(distance_bin_lookup[::-1], (LANE + 1, beyond), constant_values=-1)
    bucket_onehot = (
        offsets_down[:, None] == jnp.arange(BUCKETS, dtype=jnp.int32)[None, :]
    ).astype(jnp.float32)
    rel_values = jnp.dot(bucket_onehot, distance_bias_table, precision=lax.Precision.HIGHEST).T
    tiles_bias = bias_tiles(rel_values.reshape(heads_here, LINES, LANE))

    all_rows = layer_argument.astype(jnp.float32)
    normed_one = (all_rows * rms_scale(all_rows) * rescaling_coefficients[0]).astype(low_type)
    transposed_rows = times_transposed(qkv_weight, normed_one)
    query_cols = (transposed_rows[:unit_rows] * score_scale).astype(low_type)
    key_cols = transposed_rows[unit_rows : 2 * unit_rows].astype(low_type)
    value_cols = transposed_rows[2 * unit_rows :].astype(low_type)
    spread_weight = jnp.pad(
        qkv_weight[unit_rows:].reshape(2 * heads_here, head_size, D),
        ((0, 0), (0, LANE - head_size), (0, 0)),
    ).reshape(2 * heads_here * LANE, D)
    lane_place = jnp.arange(2 * heads_here * LANE, dtype=jnp.int32) % LANE - head_size
    marks = jnp.logical_or(
        lane_place[None, :] == segment_ids[:, None],
        jnp.logical_and(lane_place >= SEQS_DEV, lane_place < SEQS_DEV + 3)[None, :],
    )
    key_value_rows = (
        times_transposed(normed_one, spread_weight) + marks.astype(jnp.float32)
    ).astype(low_type)
    key_rows = key_value_rows[:, : heads_here * LANE]
    value_rows = key_value_rows[:, heads_here * LANE :]
    row_place = jnp.arange(16, dtype=jnp.int32)[:, None]
    apart = jnp.where(
        jnp.logical_and(row_place < SEQS_DEV, row_place != segment_ids[None, :]), masked_score, 0.0
    ).astype(low_type)
    context, context_cols, log_rows = attention_forward(
        0, lengths, origin, query_cols, key_rows, value_cols, apart, tiles_bias
    )

    crossing = [after(rows, context) for rows in crossing]
    both_joined, inner_joined, outer_joined = [
        jnp.concatenate([rows, swap(rows, bits[0])], axis=0) for rows in crossing
    ]
    both_joined = both_joined.reshape(narrow_count, 2, unit_rows, D)
    out_joined = both_joined[:, 0].reshape(D, D)
    proj_weight = natural_rows(both_joined[:, 1].reshape(D, D), narrow_index)

    def to_peer(values, peer):
        if peer == 0:
            return values
        pairs = [(i, i ^ peer) for i in range(narrow_count)]
        return lax.ppermute(values, "narrow", pairs)

    context_own = jnp.concatenate(
        [
            to_peer(context[s * group : (s + 1) * group], peer)
            for s, peer in enumerate(order)
        ],
        axis=1,
    )
    own_rows = lax.dynamic_slice_in_dim(layer_argument, narrow_index * group, group, 0).astype(
        jnp.float32
    )
    scale_one = rms_scale(own_rows)
    residual_mid = own_rows + plain_product(context_own, out_joined)
    scale_two = rms_scale(residual_mid)
    normed_two = (residual_mid * scale_two * rescaling_coefficients[1]).astype(low_type)

    hidden_low, hidden_slope = gelu_and_slope(times_transposed(normed_two, inner_joined))
    result_own = residual_mid + plain_product(hidden_low, outer_joined)
    layer_result = natural_rows(join_rows(result_own.astype(low_type)), narrow_index).astype(
        jnp.float32
    )

    scale_three = rms_scale(result_own)
    member = (
        own_segments[None, :] == jnp.arange(SEQS_DEV, dtype=jnp.int32)[:, None]
    ).astype(jnp.float32)
    length_values = lengths.astype(jnp.float32)[:, None]
    unscaled_part = (
        jnp.dot(member, result_own * scale_three, precision=lax.Precision.HIGHEST) / length_values
    )
    total_seqs = wide_count * SEQS_DEV
    own_pooled_grad, loss_low, loss_row, final_gain_grad = contrastive(
        jnp.concatenate([wide_index.reshape(1), lengths]),
        sharpness_exponent,
        spread(unscaled_part).reshape(total_seqs * narrow_count, D),
        proj_weight,
        rescaling_coefficients[2:3],
        total_seqs,
    )
    loss = loss_row[0, 0]
    sharpness_total = loss_row[0, 1:2]
    proj_grad_own = lax.dynamic_slice_in_dim(
        loss_low[:total_seqs], narrow_index * unit_rows, unit_rows, 1
    )
    proj_weight_grad = outer_product(proj_grad_own, loss_low[total_seqs:])

    weighted = own_pooled_grad[SEQS_DEV - 1]
    for s in range(SEQS_DEV - 2, -1, -1):
        weighted = jnp.where((own_segments == s)[:, None], own_pooled_grad[s], weighted)
    inner_mean = jnp.mean(weighted * result_own, axis=-1, keepdims=True)
    encoded_grad = scale_three * weighted - result_own * (
        scale_three * scale_three * scale_three * inner_mean
    )
    ffn_grad_low = encoded_grad.astype(low_type)
    outer_grad = outer_product(hidden_low, ffn_grad_low).astype(low_type)
    outer_kept, outer_sent = first_add(outer_grad)
    pre_low = (
        times_transposed(after(ffn_grad_low, outer_grad), outer_joined) * hidden_slope
    ).astype(low_type)
    normed_two_grad = plain_product(pre_low, inner_joined)
    mid_norm_grad, ffn_gain_grad = norm_backward(
        residual_mid, scale_two, rescaling_coefficients[1], normed_two_grad
    )
    mid_grad = encoded_grad + mid_norm_grad
    attn_grad_low = mid_grad.astype(low_type)

    context_grad = times_transposed(attn_grad_low, out_joined).astype(low_type)
    context_grad = [
        to_peer(context_grad[:, s * unit_rows : (s + 1) * unit_rows], peer)
        for s, peer in enumerate(order)
    ]
    inner_grad = outer_product(after(pre_low, attn_grad_low), normed_two).astype(low_type)
    inner_kept, inner_sent = first_add(inner_grad)
    out_kept, out_sent = first_add(outer_product(context_own, attn_grad_low).astype(low_type))
    context_grad, layer_result, outer_sent, inner_sent, out_sent = lax.optimization_barrier(
        (jnp.concatenate(context_grad, axis=0), layer_result, outer_sent, inner_sent, out_sent)
    )
    qkv_cols, qkv_rows, bias_lines = attention_backward(
        lengths,
        origin,
        query_cols,
        key_rows,
        value_rows,
        key_cols,
        context_grad,
        context_cols,
        log_rows,
        apart,
        tiles_bias,
    )
    offset_bias_slope = lax.dot_general(
        bucket_onehot,
        bias_lines.reshape(heads_here, LINES * LANE),
        (((0,), (1,)), ((), ())),
        precision=lax.Precision.HIGHEST,
    )

    qkv_weight_grad = plain_product(qkv_cols, normed_one).astype(low_type)
    placed = jnp.zeros((wide_count * CAP, unit_rows, D), low_type)
    for kept, sent, first_unit in (
        (out_kept, out_sent, 3),
        (outer_kept, outer_sent, 5 + ffn_units),
        (inner_kept, inner_sent, 5),
    ):
        came = after(swap(sent, bits[1]), qkv_weight_grad)
        for k in range(kept.shape[0] // unit_rows):
            rows = slice(k * unit_rows, (k + 1) * unit_rows)
            total = kept[rows].astype(jnp.float32) + came[rows].astype(jnp.float32)
            placed = lax.dynamic_update_index_in_dim(
                placed, total.astype(low_type), tile_location[first_unit + k], 0
            )
    slot_grads = lax.psum_scatter(placed, "wide", scatter_dimension=0, tiled=True).astype(
        jnp.float32
    )
    proj_here = (own_slots == tile_location[4]).astype(jnp.float32)
    slot_grads = slot_grads + proj_here[:, None, None] * proj_weight_grad[None]

    parts = lax.all_to_all(
        qkv_weight_grad.reshape(wide_count, 3 * unit_rows // wide_count, D),
        "wide",
        split_axis=0,
        concat_axis=0,
        tiled=True,
    )
    qkv_part = jnp.sum(parts.astype(jnp.float32), axis=0)
    copies = jnp.broadcast_to(qkv_part.astype(low_type)[None], (wide_count,) + qkv_part.shape)
    qkv_whole = lax.all_to_all(
        copies, "wide", split_axis=0, concat_axis=0, tiled=True
    ).reshape(3, unit_rows, D)
    normed_one_grad = product_add_rows(qkv_rows, qkv_weight)
    input_norm_grad, attn_gain_grad = norm_backward(
        own_rows, scale_one, rescaling_coefficients[0], normed_one_grad
    )
    input_own = mid_grad + input_norm_grad
    input_grad = natural_rows(join_rows(input_own.astype(low_type)), narrow_index).astype(
        jnp.float32
    )

    bias_size = offset_bias_slope.size
    small = jnp.stack(
        [
            ffn_gain_grad,
            attn_gain_grad,
            jnp.pad(offset_bias_slope.reshape(bias_size), (0, D - bias_size)),
        ]
    )
    small_all = spread(small).reshape(wide_count, narrow_count, 3, D)
    gain_sums = jnp.sum(small_all[:, :, :2], axis=(0, 1))
    gain_total = jnp.stack([gain_sums[1], gain_sums[0], final_gain_grad[0]])
    bias_all = jnp.sum(small_all[:, :, 2], axis=0)
    bias_total = lax.dynamic_index_in_dim(bias_all, narrow_index, 0, keepdims=False)[
        :bias_size
    ].reshape(offset_bias_slope.shape)
    local_squares = jnp.sum(slot_grads * slot_grads) + jnp.sum(qkv_part * qkv_part)
    square_terms = spread(jnp.broadcast_to(local_squares, (8, LANE)))[:, 0, 0]
    grad_norm = jnp.sqrt(
        jnp.sum(square_terms)
        + jnp.sum(gain_total * gain_total)
        + jnp.sum(bias_all * bias_all)
        + jnp.sum(sharpness_total * sharpness_total)
    )
    multiplier = jnp.minimum(1.0, clip_limit / grad_norm)
    for u in range(3):
        here = (own_slots == tile_location[u])[:, None, None]
        slot_grads = jnp.where(here, qkv_whole[u].astype(jnp.float32)[None], slot_grads)
    slot_first, slot_second, slot_weight = decoupled_decay_step(
        slot_grads,
        precise_mean_est,
        precise_variance_est,
        precise_parameter_blocks,
        multiplier,
        learn_rate,
    )
    gain_first, gain_second, gain_new = decoupled_decay_step(
        gain_total,
        norm_scale_mean_est,
        norm_scale_variance_est,
        rescaling_coefficients,
        multiplier,
        side_rate,
    )
    bias_first, bias_second, bias_new = decoupled_decay_step(
        bias_total,
        offset_bias_mean_est,
        offset_bias_variance_est,
        distance_bias_table,
        multiplier,
        side_rate,
    )
    sharpness_mean_fresh, sharpness_variance_fresh, sharpness_exponent_fresh = decoupled_decay_step(
        sharpness_total,
        sharpness_mean_est,
        sharpness_variance_est,
        sharpness_exponent,
        multiplier,
        learn_rate,
    )
    return (
        loss,
        layer_result,
        input_grad,
        grad_norm,
        slot_first,
        slot_second,
        slot_weight,
        gain_first,
        gain_second,
        gain_new,
        bias_first,
        bias_second,
        bias_new,
        sharpness_mean_fresh,
        sharpness_variance_fresh,
        sharpness_exponent_fresh,
    )


def solution(mesh):
    placed = (
        P("wide", None),
        P("wide", None),
        P(),
        P(),
        P("wide", "narrow", None),
        P("wide", "narrow", None),
        P("wide", "narrow", None),
        P(),
        P(),
        P(),
        P(None, "narrow"),
        P(None, "narrow"),
        P(None, "narrow"),
        P(),
        P(),
        P(),
    )
    return jax.shard_map(
        on_device,
        mesh=mesh,
        in_specs=placed,
        out_specs=(
            P(),
            P("wide", None),
            P("wide", None),
            P(),
            P("wide", "narrow", None),
            P("wide", "narrow", None),
            P("wide", "narrow", None),
            P(),
            P(),
            P(),
            P(None, "narrow"),
            P(None, "narrow"),
            P(None, "narrow"),
            P(),
            P(),
            P(),
        ),
        check_vma=False,
    )
```

```python
import jax
import jax.numpy as jnp
from jax import lax
from jax.experimental import pallas as pl
from jax.experimental.pallas import tpu as pltpu
from jax.sharding import Mesh
from jax.sharding import PartitionSpec as P

D = 768
FF = 3072
BUCKETS = 32
TOK_DEV = 2560
SEQS_DEV = 4
DOCLEN = 1024
CAP = 2
STEP = 10
LANE = 128
BQ = 512
BK = 512
UNIT_BLOCK = 768
REACH = DOCLEN // LANE
OFF = REACH + (BQ + BK) // LANE
SPAN = 2 * OFF + 1
LINES = 2 * REACH + 2
VMEM_LIMIT = 56 * 1024 * 1024

norm_eps = 1e-06
clip_limit = 0.01
learn_rate = 0.01
side_rate = 0.5
beta_one = 0.5
beta_two = 0.5
adam_eps = 1e-08
decay_rate = 0.01
score_scale = 0.125
masked_score = -1e30
low_type = jnp.bfloat16


def times_transposed(left_side, right_side):
    return lax.dot_general(
        left_side, right_side, (((1,), (1,)), ((), ())), preferred_element_type=jnp.float32
    )


def plain_product(left_side, right_side):
    return jnp.dot(left_side, right_side, preferred_element_type=jnp.float32)


def outer_product(left_side, right_side):
    return lax.dot_general(
        left_side, right_side, (((0,), (0,)), ((), ())), preferred_element_type=jnp.float32
    )


def rms_scale(values):
    return lax.rsqrt(jnp.mean(values * values, axis=-1, keepdims=True) + norm_eps)


def norm_backward(values, row_scale, gain_row, grad_out):
    weighted = grad_out * gain_row
    gain_grad = jnp.sum(grad_out * values * row_scale, axis=0)
    inner_mean = jnp.mean(weighted * values, axis=-1, keepdims=True)
    value_grad = row_scale * weighted - values * row_scale * row_scale * row_scale * inner_mean
    return (value_grad, gain_grad)


def decoupled_decay_step(gradient, first_moment, second_moment, weight, multiplier, step_rate):
    clipped = gradient * multiplier
    first_new = beta_one * first_moment + (1.0 - beta_one) * clipped
    second_new = beta_two * second_moment + (1.0 - beta_two) * clipped * clipped
    first_hat = first_new / (1.0 - beta_one**STEP)
    second_hat = second_new / (1.0 - beta_two**STEP)
    weight_new = weight - step_rate * (
        first_hat / (jnp.sqrt(second_hat) + adam_eps) + decay_rate * weight
    )
    return (first_new, second_new, weight_new)


def swap(values, axes, bit):
    count = lax.axis_size(axes)
    return lax.ppermute(values, axes, [(i, i ^ bit) for i in range(count)])


def sum_low(left, right):
    return (left.astype(jnp.float32) + right.astype(jnp.float32)).astype(low_type)


def narrow_bits(count):
    return [1 << s for s in range(count.bit_length() - 1)]


def peer_order(count):
    order = [0]
    for bit in reversed(narrow_bits(count)):
        order = order + [peer ^ bit for peer in order]
    return order


def join_rows(values, axes):
    for bit in reversed(narrow_bits(lax.axis_size(axes))):
        values = jnp.concatenate([values, swap(values, axes, bit)], axis=0)
    return values


def add_rows(values, axes):
    for bit in narrow_bits(lax.axis_size(axes)):
        half = values.shape[0] // 2
        came = swap(values[half:].astype(low_type), axes, bit)
        values = values[:half].astype(jnp.float32) + came.astype(jnp.float32)
    return values


def product_add_rows(left_side, right_side, axes):
    bits = narrow_bits(lax.axis_size(axes))
    half = left_side.shape[0] // 2
    sent = plain_product(left_side[half:], right_side).astype(low_type)
    came = swap(sent, axes, bits[0])
    values = plain_product(left_side[:half], right_side) + came.astype(jnp.float32)
    for bit in bits[1:]:
        half = values.shape[0] // 2
        came = swap(values[half:].astype(low_type), axes, bit)
        values = values[:half] + came.astype(jnp.float32)
    return values


def natural_rows(joined, index, count):
    order = peer_order(count)
    group = joined.shape[0] // count
    place = jnp.array([order.index(peer) for peer in range(count)], jnp.int32)
    return jnp.concatenate(
        [
            lax.dynamic_slice_in_dim(joined, place[g ^ index] * group, group, 0)
            for g in range(count)
        ],
        axis=0,
    )


def spread(values, axes):
    copies = jnp.broadcast_to(values[None], (lax.axis_size(axes),) + values.shape)
    return lax.all_to_all(copies, axes, split_axis=0, concat_axis=0, tiled=True)


def after(values, other):
    return lax.optimization_barrier((values, other))[0]


def gelu_and_slope(values):
    rate = 0.7978845608028654
    cubic = 0.044715
    squares = values * values
    turn = jnp.tanh(rate * values * (1.0 + cubic * squares))
    half = 0.5 * (1.0 + turn)
    slope = half + 0.5 * values * (1.0 - turn * turn) * (rate * (1.0 + 3.0 * cubic * squares))
    return (values * half).astype(low_type), slope.astype(low_type)


def smem():
    return pl.BlockSpec(memory_space=pltpu.SMEM)


def vmem():
    return pl.BlockSpec(memory_space=pltpu.VMEM)


def bias_kernel(chunks, tiles):
    heads = tiles.shape[0]
    tiles[...] = jnp.zeros_like(tiles)
    for h in range(heads):
        for d in range(-REACH, REACH + 1):
            left = chunks[h, REACH + 1 - d : REACH + 2 - d, :]
            right = chunks[h, REACH - d : REACH + 1 - d, :]
            line = jnp.broadcast_to(jnp.concatenate([left, right], axis=1), (LANE, 2 * LANE))
            rolled = pltpu.roll(line, 0, 1, stride=1, stride_axis=0)
            tiles[h, (d + OFF) * LANE : (d + OFF + 1) * LANE, :] = rolled[:, :LANE]


def bias_tiles(rel_chunks):
    heads = rel_chunks.shape[0]
    return pl.pallas_call(
        bias_kernel,
        out_shape=jax.ShapeDtypeStruct((heads, SPAN * LANE, LANE), jnp.float32),
        compiler_params=pltpu.CompilerParams(vmem_limit_bytes=VMEM_LIMIT),
        name="bias_tiles",
    )(rel_chunks)


def key_range(lengths, first, last):
    start = jnp.int32(0)
    low = jnp.int32(0)
    high = jnp.int32(0)
    for s in range(SEQS_DEV):
        end = start + lengths[s]
        low = jnp.where(start <= first, start, low)
        high = jnp.where(start <= last, end, high)
        start = end
    return low // BK, (high + BK - 1) // BK


def bias_part(bias, h, row):
    return jnp.concatenate(
        [
            bias[h, pl.ds(pl.multiple_of(row - b * LANE, LANE), BK), :]
            for b in range(BQ // LANE)
        ],
        axis=1,
    )


def forward_kernel(first_row, lengths, origin, qT, kn, vT, apart, bias, ctx_o, ctxT_o, lse_o, qa, acc):
    width, rows_here = qT.shape
    heads = bias.shape[0]
    size = width // heads
    qa[...] = jnp.zeros_like(qa)

    @pl.loop(0, rows_here // BQ)
    def _(i):
        q0 = pl.multiple_of(i * BQ, BQ)
        here = pl.ds(q0, BQ)
        for h in range(heads):
            qa[h * LANE : h * LANE + size, :] = qT[h * size : (h + 1) * size, here]
            qa[h * LANE + size : h * LANE + size + 16, :] = apart[:, here]
        acc[...] = jnp.zeros_like(acc)
        low, high = key_range(lengths, first_row + q0, first_row + q0 + BQ - 1)

        def step(j, carry):
            k0 = pl.multiple_of(j * BK, BK)
            row = (j * (BK // LANE) - i * (BQ // LANE) - first_row // LANE + OFF) * LANE
            out = []
            for h in range(heads):
                top, total = carry[2 * h], carry[2 * h + 1]
                own = slice(h * LANE, (h + 1) * LANE)
                rows = slice(h * size, (h + 1) * size)
                s = plain_product(kn[pl.ds(k0, BK), own], qa[own, :]) + bias_part(bias, h, row)
                new_top = jnp.maximum(top, jnp.max(s, axis=0, keepdims=True))
                fade = jnp.exp(top - new_top)
                p = jnp.exp(s - new_top)
                total = total * fade + jnp.sum(p, axis=0, keepdims=True)
                acc[rows, :] = acc[rows, :] * fade + plain_product(
                    vT[rows, pl.ds(k0, BK)], p.astype(low_type)
                )
                out += [new_top, total]
            return tuple(out)

        init = tuple(
            jnp.full((1, BQ), 2.0 * masked_score if n % 2 == 0 else 0.0, jnp.float32)
            for n in range(2 * heads)
        )
        done = lax.fori_loop(low, high, step, init)
        for h in range(heads):
            rows = slice(h * size, (h + 1) * size)
            acc[rows, :] = acc[rows, :] / done[2 * h + 1]
            lse_o[h : h + 1, here] = done[2 * h] + jnp.log(done[2 * h + 1])
        ctxT_o[:, here] = acc[...]
        turned = acc[...].T.astype(low_type)
        for b in range(BQ // LANE):
            at = pl.multiple_of(origin[i * (BQ // LANE) + b], LANE)
            ctx_o[pl.ds(at, LANE), :] = turned[b * LANE : (b + 1) * LANE, :]


def attention_forward(first_row, lengths, origin, qT, kn, vT, apart, bias):
    width, rows_here = qT.shape
    heads = bias.shape[0]

    def body(*refs):
        forward_kernel(first_row, *refs)

    return pl.pallas_call(
        body,
        out_shape=(
            jax.ShapeDtypeStruct((rows_here, width), low_type),
            jax.ShapeDtypeStruct((width, rows_here), jnp.float32),
            jax.ShapeDtypeStruct((heads, rows_here), jnp.float32),
        ),
        in_specs=[smem()] * 2 + [vmem()] * 5,
        out_specs=(vmem(),) * 3,
        scratch_shapes=[
            pltpu.VMEM((heads * LANE, BQ), low_type),
            pltpu.VMEM((width, BQ), jnp.float32),
        ],
        compiler_params=pltpu.CompilerParams(vmem_limit_bytes=VMEM_LIMIT),
        cost_estimate=pl.CostEstimate(
            flops=rows_here * width, bytes_accessed=width * TOK_DEV, transcendentals=0
        ),
        name="attention_forward",
    )(lengths, origin, qT, kn, vT, apart, bias)


def three_parts(values):
    first = values.astype(low_type).astype(jnp.float32)
    rest = values - first
    second = rest.astype(low_type).astype(jnp.float32)
    return first, second, rest - second


def backward_kernel(
    lengths, origin, qT, kn, vn, kT, dcn, ctxT, lse, apart, bias,
    dT_o, dn_o, lines_o, qa, da, dq, dk, dv, tiles,
):
    width, tokens = qT.shape
    heads = bias.shape[0]
    size = width // heads
    for ref in (qa, da, dk, dv, tiles):
        ref[...] = jnp.zeros_like(ref)
    place = lax.broadcasted_iota(jnp.int32, (16, BQ), 0) - SEQS_DEV

    def in_depth(values):
        a, b, c = three_parts(values)
        return jnp.where(place == 0, a, jnp.where(place == 1, b, jnp.where(place == 2, c, 0.0)))

    @pl.loop(0, tokens // BQ)
    def _(i):
        q0 = pl.multiple_of(i * BQ, BQ)
        here = pl.ds(q0, BQ)
        at = [pl.multiple_of(origin[i * (BQ // LANE) + b], LANE) for b in range(BQ // LANE)]
        dcT = jnp.concatenate(
            [dcn[pl.ds(at[b], LANE), :].astype(jnp.float32) for b in range(BQ // LANE)], axis=0
        ).T
        for h in range(heads):
            rows = slice(h * size, (h + 1) * size)
            top = h * LANE
            qa[top : top + size, :] = qT[rows, here]
            extra = apart[:, here].astype(jnp.float32) + in_depth(-lse[h : h + 1, here])
            qa[top + size : top + size + 16, :] = extra.astype(low_type)
            da[top : top + size, :] = dcT[rows, :].astype(low_type)
            delta = jnp.sum(dcT[rows, :] * ctxT[rows, here], axis=0, keepdims=True)
            da[top + size : top + size + 16, :] = in_depth(-delta).astype(low_type)
        dq[...] = jnp.zeros_like(dq)
        low, high = key_range(lengths, q0, q0 + BQ - 1)

        @pl.loop(low, high)
        def _(j):
            k0 = pl.multiple_of(j * BK, BK)
            there = pl.ds(k0, BK)
            row = (j * (BK // LANE) - i * (BQ // LANE) + OFF) * LANE
            for h in range(heads):
                rows = slice(h * size, (h + 1) * size)
                own = slice(h * LANE, (h + 1) * LANE)
                flat = slice(h * LANE, h * LANE + size)
                s = plain_product(kn[there, own], qa[own, :])
                p = jnp.exp(s + bias_part(bias, h, row))
                ds = p * plain_product(vn[there, own], da[own, :])
                for b in range(BQ // LANE):
                    window = pl.ds(pl.multiple_of(row - b * LANE, LANE), BK)
                    tiles[h, window, :] = (
                        tiles[h, window, :] + ds[:, b * LANE : (b + 1) * LANE]
                    )
                p_low = p.astype(low_type)
                ds_low = ds.astype(low_type)
                dv[rows, there] = dv[rows, there] + times_transposed(da[flat, :], p_low)
                dk[rows, there] = dk[rows, there] + times_transposed(qa[flat, :], ds_low)
                dq[rows, :] = dq[rows, :] + plain_product(kT[rows, there], ds_low)

        grad = dq[...] * score_scale
        dT_o[0:width, here] = grad.astype(low_type)
        turned = grad.T.astype(low_type)
        for b in range(BQ // LANE):
            dn_o[pl.ds(at[b], LANE), 0:width] = turned[b * LANE : (b + 1) * LANE, :]

    @pl.loop(0, tokens // BQ)
    def _(i):
        here = pl.ds(pl.multiple_of(i * BQ, BQ), BQ)
        both = jnp.concatenate([dk[:, here], dv[:, here]], axis=0)
        dT_o[width : 3 * width, here] = both.astype(low_type)
        turned = both.T.astype(low_type)
        for b in range(BQ // LANE):
            at = pl.multiple_of(origin[i * (BQ // LANE) + b], LANE)
            dn_o[pl.ds(at, LANE), width : 3 * width] = turned[b * LANE : (b + 1) * LANE, :]

    across = lax.broadcasted_iota(jnp.int32, (LANE, LANE), 1)
    over = across >= lax.broadcasted_iota(jnp.int32, (LANE, LANE), 0)
    sub = lax.broadcasted_iota(jnp.int32, (8, LANE), 0)
    for h in range(heads):
        for d in range(-REACH, REACH + 2):
            here = tiles[h, (d + OFF) * LANE : (d + OFF + 1) * LANE, :]
            below = tiles[h, (d + OFF - 1) * LANE : (d + OFF) * LANE, :]
            mixed = jnp.where(over, here, below)
            line = mixed[LANE - 8 :, :]
            for g in range(LANE // 8 - 2, -1, -1):
                line = mixed[8 * g : 8 * g + 8, :] + pltpu.roll(line, LANE - 8, 1)
            for bit in (1, 2, 4):
                line = jnp.where((sub & bit) != 0, pltpu.roll(line, LANE - bit, 1), line)
            lines_o[h, REACH + 1 - d : REACH + 2 - d, :] = jnp.sum(line, axis=0, keepdims=True)


def attention_backward(lengths, origin, qT, kn, vn, kT, dcn, ctxT, lse, apart, bias):
    width, tokens = qT.shape
    heads = bias.shape[0]
    return pl.pallas_call(
        backward_kernel,
        out_shape=(
            jax.ShapeDtypeStruct((3 * width, tokens), low_type),
            jax.ShapeDtypeStruct((tokens, 3 * width), low_type),
            jax.ShapeDtypeStruct((heads, LINES, LANE), jnp.float32),
        ),
        in_specs=[smem()] * 2 + [vmem()] * 9,
        out_specs=(vmem(),) * 3,
        scratch_shapes=[
            pltpu.VMEM((heads * LANE, BQ), low_type),
            pltpu.VMEM((heads * LANE, BQ), low_type),
            pltpu.VMEM((width, BQ), jnp.float32),
            pltpu.VMEM((width, tokens), jnp.float32),
            pltpu.VMEM((width, tokens), jnp.float32),
            pltpu.VMEM((heads, SPAN * LANE, LANE), jnp.float32),
        ],
        compiler_params=pltpu.CompilerParams(vmem_limit_bytes=VMEM_LIMIT),
        cost_estimate=pl.CostEstimate(
            flops=tokens * width, bytes_accessed=width * TOK_DEV, transcendentals=0
        ),
        name="attention_backward",
    )(lengths, origin, qT, kn, vn, kT, dcn, ctxT, lse, apart, bias)


def feed_forward_backward_kernel(
    grad, rows, hidden, slope, inner, outer, weight_grads, rows_grad
):
    groups, _, size, width = weight_grads.shape

    @pl.when(pl.program_id(0) == 0)
    def _():
        rows_grad[...] = jnp.zeros_like(rows_grad)

    outer_grad = outer_product(hidden[...], grad[...]).astype(low_type)
    weight_grads[:, 0] = outer_grad.reshape(groups, size, width)
    pre = (
        times_transposed(grad[...], outer[...]) * slope[...].astype(jnp.float32)
    ).astype(low_type)
    inner_grad = outer_product(pre, rows[...]).astype(low_type)
    weight_grads[:, 1] = inner_grad.reshape(groups, size, width)
    rows_grad[...] += plain_product(pre, inner[...])


def feed_forward_backward(grad, rows, hidden, slope, inner, outer, size):
    count = grad.shape[0]
    groups = UNIT_BLOCK // size
    every = pl.BlockSpec((count, D), lambda i: (0, 0))
    units = pl.BlockSpec((count, UNIT_BLOCK), lambda i: (0, i))
    weight = pl.BlockSpec((UNIT_BLOCK, D), lambda i: (i, 0))
    return pl.pallas_call(
        feed_forward_backward_kernel,
        grid=(FF // UNIT_BLOCK,),
        out_shape=(
            jax.ShapeDtypeStruct((FF // size, 2, size, D), low_type),
            jax.ShapeDtypeStruct((count, D), jnp.float32),
        ),
        in_specs=[every, every, units, units, weight, weight],
        out_specs=(pl.BlockSpec((groups, 2, size, D), lambda i: (i, 0, 0, 0)), every),
        compiler_params=pltpu.CompilerParams(vmem_limit_bytes=VMEM_LIMIT),
        cost_estimate=pl.CostEstimate(flops=FF * D, bytes_accessed=FF * D, transcendentals=0),
        name="feed_forward_backward",
    )(grad, rows, hidden, slope, inner, outer)


def loss_kernel(place, numbers, parts, proj_weight, gain, out_slope, out_low, out_row, out_gain):
    total_seqs = out_low.shape[0] // 2
    terms = parts.shape[0] // total_seqs
    exact = dict(precision=lax.Precision.HIGHEST, preferred_element_type=jnp.float32)
    seq = lax.broadcasted_iota(jnp.int32, (total_seqs, parts.shape[0]), 0)
    part = lax.broadcasted_iota(jnp.int32, (total_seqs, parts.shape[0]), 1)
    joins = jnp.logical_and(
        seq // SEQS_DEV == part // (SEQS_DEV * terms), seq % SEQS_DEV == part % SEQS_DEV
    )
    unscaled = jnp.dot(joins.astype(jnp.float32), parts[...], **exact)
    pooled_low = (unscaled * gain[...]).astype(low_type)
    projected = times_transposed(pooled_low, proj_weight[...]).astype(low_type).astype(jnp.float32)
    inverse = lax.rsqrt(jnp.sum(projected * projected, axis=1, keepdims=True) + norm_eps)
    embed_low = (projected * inverse).astype(low_type)
    sharpness_factor = jnp.exp(jnp.full((1, 1), numbers[0], jnp.float32))
    agreement = times_transposed(embed_low, embed_low)
    row = lax.broadcasted_iota(jnp.int32, (total_seqs, total_seqs), 0)
    column = lax.broadcasted_iota(jnp.int32, (total_seqs, total_seqs), 1)
    logits = jnp.where(row == column, masked_score, sharpness_factor * agreement)
    partner = (row ^ 1) == column

    def log_sum(axis):
        top = jnp.max(logits, axis=axis, keepdims=True)
        return top + jnp.log(jnp.sum(jnp.exp(logits - top), axis=axis, keepdims=True))

    log_rows = log_sum(1)
    positive = jnp.where(partner, 1.0, 0.0)
    slope = (jnp.exp(logits - log_rows) - positive) / total_seqs
    slope_turned = (jnp.exp(logits - log_sum(0)) - positive) / total_seqs
    embed_grad = sharpness_factor * jnp.dot(
        slope + slope_turned, embed_low.astype(jnp.float32), **exact
    )
    along = jnp.sum(projected * embed_grad, axis=1, keepdims=True)
    proj_grad_low = (
        inverse * embed_grad - projected * inverse * inverse * inverse * along
    ).astype(low_type)
    pooled_grad = plain_product(proj_grad_low, proj_weight[...])
    out_low[0:total_seqs, :] = proj_grad_low
    out_low[total_seqs : 2 * total_seqs, :] = pooled_low
    out_gain[...] = jnp.sum(pooled_grad * unscaled, axis=0, keepdims=True)
    loss = jnp.sum(
        log_rows - jnp.sum(positive * jnp.where(partner, logits, 0.0), axis=1, keepdims=True),
        axis=0,
        keepdims=True,
    ) / total_seqs
    temperature = sharpness_factor * jnp.sum(
        jnp.sum(slope * agreement, axis=1, keepdims=True), axis=0, keepdims=True
    )
    lane = lax.broadcasted_iota(jnp.int32, (1, LANE), 1)
    out_row[...] = jnp.where(lane == 0, loss, jnp.where(lane == 1, temperature, 0.0))
    mine = lax.broadcasted_iota(jnp.int32, (8, total_seqs), 0)
    seq_of = lax.broadcasted_iota(jnp.int32, (8, total_seqs), 1) - place[0] * SEQS_DEV
    picks = jnp.logical_and(mine == seq_of, mine < SEQS_DEV).astype(jnp.float32)
    own = jnp.dot(picks, pooled_grad, **exact)
    index = lax.broadcasted_iota(jnp.int32, (8, 1), 0)
    extent = jnp.ones((8, 1), jnp.float32)
    for s in range(SEQS_DEV):
        extent = jnp.where(index == s, place[1 + s].astype(jnp.float32), extent)
    out_slope[...] = own * gain[...] / extent


def contrastive(place, numbers, parts, proj_weight, gain, total_seqs):
    return pl.pallas_call(
        loss_kernel,
        out_shape=(
            jax.ShapeDtypeStruct((8, D), jnp.float32),
            jax.ShapeDtypeStruct((2 * total_seqs, D), low_type),
            jax.ShapeDtypeStruct((1, LANE), jnp.float32),
            jax.ShapeDtypeStruct((1, D), jnp.float32),
        ),
        in_specs=[smem()] * 2 + [vmem()] * 3,
        out_specs=(vmem(),) * 4,
        compiler_params=pltpu.CompilerParams(vmem_limit_bytes=VMEM_LIMIT),
        cost_estimate=pl.CostEstimate(
            flops=4 * total_seqs * D * D, bytes_accessed=4 * D * D, transcendentals=total_seqs
        ),
        name="contrastive",
    )(place, numbers, parts, proj_weight, gain)


def on_device(
    axes,
    layer_argument,
    document_extents,
    distance_bin_lookup,
    tile_location,
    precise_parameter_blocks,
    precise_mean_est,
    precise_variance_est,
    rescaling_coefficients,
    norm_scale_mean_est,
    norm_scale_variance_est,
    distance_bias_table,
    offset_bias_mean_est,
    offset_bias_variance_est,
    sharpness_exponent,
    sharpness_mean_est,
    sharpness_variance_est,
):
    wide, narrow, far, near = axes
    everyone = wide + narrow
    near_axes = near + narrow
    wide_count = lax.axis_size(wide)
    narrow_count = lax.axis_size(narrow)
    far_count = lax.axis_size(far)
    near_count = wide_count // far_count
    wide_index = lax.axis_index(wide)
    narrow_index = lax.axis_index(narrow)
    bits = narrow_bits(narrow_count)
    order = peer_order(narrow_count)
    place_of = jnp.array([order.index(peer) for peer in range(narrow_count)], jnp.int32)
    unit_rows = precise_parameter_blocks.shape[1]
    heads_here = distance_bias_table.shape[1]
    head_size = unit_rows // heads_here
    ffn_units = FF // D
    group = TOK_DEV // narrow_count
    own_slots = wide_index * CAP + jnp.arange(CAP, dtype=jnp.int32)

    every_slot = lax.all_gather(
        precise_parameter_blocks.astype(low_type), wide, axis=0, tiled=True
    )

    def block(u):
        return lax.dynamic_index_in_dim(every_slot, tile_location[u], 0, keepdims=False)

    qkv_weight = jnp.concatenate([block(u) for u in range(3)], axis=0)

    part_rows = D // wide_count

    def unit_order(first_unit):
        rows = jnp.concatenate([block(first_unit + k) for k in range(ffn_units)], axis=0)
        rows = rows.reshape(far_count, near_count, part_rows, D)
        return jnp.swapaxes(rows, 0, 1).reshape(near_count, far_count * part_rows, D)

    crossing = [
        jnp.concatenate([block(3), block(4)], axis=0),
        unit_order(5),
        unit_order(5 + ffn_units),
    ]
    for rows in crossing:
        qkv_weight = after(qkv_weight, rows)
    crossed = [[rows] + [swap(rows, narrow, peer) for peer in bits[1:]] for rows in crossing]

    lengths = document_extents[0]
    seq_ends = jnp.cumsum(lengths)
    positions = jnp.arange(TOK_DEV, dtype=jnp.int32)

    def segments_of(where):
        return jnp.sum((seq_ends[None, :] <= where[:, None]).astype(jnp.int32), axis=1)

    segment_ids = segments_of(positions)
    own_segments = segments_of(narrow_index * group + positions[:group])
    tile_starts = jnp.arange(TOK_DEV // LANE, dtype=jnp.int32) * LANE
    origin = place_of[(tile_starts // group) ^ narrow_index] * group + tile_starts % group

    beyond = LINES * LANE - LANE - 1 - distance_bin_lookup.shape[0]
    offsets_down = jnp.pad(distance_bin_lookup[::-1], (LANE + 1, beyond), constant_values=-1)
    bucket_onehot = (
        offsets_down[:, None] == jnp.arange(BUCKETS, dtype=jnp.int32)[None, :]
    ).astype(jnp.float32)
    rel_values = jnp.dot(bucket_onehot, distance_bias_table, precision=lax.Precision.HIGHEST).T
    tiles_bias = bias_tiles(rel_values.reshape(heads_here, LINES, LANE))

    all_rows = layer_argument.astype(jnp.float32)
    normed_one = (all_rows * rms_scale(all_rows) * rescaling_coefficients[0]).astype(low_type)
    transposed_rows = times_transposed(qkv_weight, normed_one)
    query_cols = (transposed_rows[:unit_rows] * score_scale).astype(low_type)
    key_cols = transposed_rows[unit_rows : 2 * unit_rows].astype(low_type)
    value_cols = transposed_rows[2 * unit_rows :].astype(low_type)
    spread_weight = jnp.pad(
        qkv_weight[unit_rows:].reshape(2 * heads_here, head_size, D),
        ((0, 0), (0, LANE - head_size), (0, 0)),
    ).reshape(2 * heads_here * LANE, D)
    lane_place = jnp.arange(2 * heads_here * LANE, dtype=jnp.int32) % LANE - head_size
    marks = jnp.logical_or(
        lane_place[None, :] == segment_ids[:, None],
        jnp.logical_and(lane_place >= SEQS_DEV, lane_place < SEQS_DEV + 3)[None, :],
    )
    key_value_rows = (
        times_transposed(normed_one, spread_weight) + marks.astype(jnp.float32)
    ).astype(low_type)
    key_rows = key_value_rows[:, : heads_here * LANE]
    value_rows = key_value_rows[:, heads_here * LANE :]
    row_place = jnp.arange(16, dtype=jnp.int32)[:, None]
    apart = jnp.where(
        jnp.logical_and(row_place < SEQS_DEV, row_place != segment_ids[None, :]), masked_score, 0.0
    ).astype(low_type)
    context, context_cols, log_rows = attention_forward(
        0, lengths, origin, query_cols, key_rows, value_cols, apart, tiles_bias
    )

    def all_peers(pieces):
        own, *even = pieces
        even = [after(rows, context) for rows in even]
        peers = [(0, own), (1, swap(own, narrow, 1))]
        for bit, rows in zip(bits[1:], even):
            peers += [(bit, rows), (bit + 1, swap(rows, narrow, 1))]
        return peers

    def in_unit_order(pieces):
        whole = jnp.zeros((near_count, narrow_count, far_count * part_rows, D), low_type)
        for peer, rows in all_peers(pieces):
            start = (0, narrow_index ^ peer, 0, 0)
            whole = lax.dynamic_update_slice(whole, rows[:, None], start)
        return whole.reshape(FF, D)

    both = dict(all_peers(crossed[0]))
    out_joined = jnp.concatenate([both[peer][:unit_rows] for peer in order], axis=0)
    proj_weight = natural_rows(
        jnp.concatenate([both[peer][unit_rows:] for peer in order], axis=0),
        narrow_index,
        narrow_count,
    )
    inner_joined = in_unit_order(crossed[1])
    outer_joined = in_unit_order(crossed[2])

    def to_peer(values, peer):
        if peer == 0:
            return values
        return swap(values, narrow, peer)

    context_own = jnp.concatenate(
        [
            to_peer(context[s * group : (s + 1) * group], peer)
            for s, peer in enumerate(order)
        ],
        axis=1,
    )
    own_rows = lax.dynamic_slice_in_dim(layer_argument, narrow_index * group, group, 0).astype(
        jnp.float32
    )
    scale_one = rms_scale(own_rows)
    residual_mid = own_rows + plain_product(context_own, out_joined)
    scale_two = rms_scale(residual_mid)
    normed_two = (residual_mid * scale_two * rescaling_coefficients[1]).astype(low_type)

    hidden_low, hidden_slope = gelu_and_slope(times_transposed(normed_two, inner_joined))
    result_own = residual_mid + plain_product(hidden_low, outer_joined)
    result_low = result_own.astype(low_type)
    result_even = [result_low] + [swap(result_low, narrow, peer) for peer in bits[1:]]

    scale_three = rms_scale(result_own)
    member = (
        own_segments[None, :] == jnp.arange(SEQS_DEV, dtype=jnp.int32)[:, None]
    ).astype(jnp.float32)
    length_values = lengths.astype(jnp.float32)[:, None]
    unscaled_part = (
        jnp.dot(member, result_own * scale_three, precision=lax.Precision.HIGHEST) / length_values
    )
    total_seqs = wide_count * SEQS_DEV
    own_pooled_grad, loss_low, loss_row, final_gain_grad = contrastive(
        jnp.concatenate([wide_index.reshape(1), lengths]),
        sharpness_exponent,
        spread(unscaled_part, everyone).reshape(total_seqs * narrow_count, D),
        proj_weight,
        rescaling_coefficients[2:3],
        total_seqs,
    )
    loss = loss_row[0, 0]
    sharpness_total = loss_row[0, 1:2]
    proj_grad_own = lax.dynamic_slice_in_dim(
        loss_low[:total_seqs], narrow_index * unit_rows, unit_rows, 1
    )
    proj_weight_grad = outer_product(proj_grad_own, loss_low[total_seqs:])

    weighted = own_pooled_grad[SEQS_DEV - 1]
    for s in range(SEQS_DEV - 2, -1, -1):
        weighted = jnp.where((own_segments == s)[:, None], own_pooled_grad[s], weighted)
    inner_mean = jnp.mean(weighted * result_own, axis=-1, keepdims=True)
    encoded_grad = scale_three * weighted - result_own * (
        scale_three * scale_three * scale_three * inner_mean
    )
    ffn_grad_low = encoded_grad.astype(low_type)
    group_rows = part_rows if part_rows % 16 == 0 else D
    weight_grads, normed_two_grad = feed_forward_backward(
        ffn_grad_low,
        normed_two,
        hidden_low,
        hidden_slope,
        inner_joined,
        outer_joined,
        group_rows,
    )
    near_part = lax.psum_scatter(
        weight_grads.reshape(2 * FF, D), near_axes, scatter_dimension=0, tiled=True
    )
    mid_norm_grad, ffn_gain_grad = norm_backward(
        residual_mid, scale_two, rescaling_coefficients[1], normed_two_grad
    )
    mid_grad = encoded_grad + mid_norm_grad
    attn_grad_low = mid_grad.astype(low_type)

    context_grad_own = times_transposed(attn_grad_low, out_joined).astype(low_type)
    context_grad = [
        to_peer(context_grad_own[:, s * unit_rows : (s + 1) * unit_rows], peer)
        for s, peer in enumerate(order)
    ]
    attn_grad_low = after(attn_grad_low, context_grad_own)
    out_grad = add_rows(outer_product(context_own, attn_grad_low).astype(low_type), narrow)
    context_grad, out_grad = lax.optimization_barrier(
        (jnp.concatenate(context_grad, axis=0), out_grad)
    )
    qkv_cols, qkv_rows, bias_lines = attention_backward(
        lengths,
        origin,
        query_cols,
        key_rows,
        value_rows,
        key_cols,
        context_grad,
        context_cols,
        log_rows,
        apart,
        tiles_bias,
    )
    offset_bias_slope = lax.dot_general(
        bucket_onehot,
        bias_lines.reshape(heads_here, LINES * LANE),
        (((0,), (1,)), ((), ())),
        precision=lax.Precision.HIGHEST,
    )

    late = jnp.concatenate(
        [plain_product(qkv_cols, normed_one).astype(low_type), out_grad.astype(low_type)], axis=0
    )
    early = after(near_part, late).reshape(-1, 2, group_rows // part_rows, part_rows, D)
    early = jnp.swapaxes(early, 1, 2).reshape(far_count * 2 * part_rows, D)
    early_part = lax.psum_scatter(early, far, scatter_dimension=0, tiled=True)
    late_rows = late.shape[0] // wide_count
    late_terms = lax.all_to_all(
        late.reshape(wide_count, late_rows, D), wide, split_axis=0, concat_axis=0, tiled=True
    )
    late_part = jnp.sum(late_terms.astype(jnp.float32), axis=0)
    late_sums = spread(late_part.astype(low_type), wide).reshape(4, unit_rows, D)
    early_sums = lax.all_gather(early_part, wide, axis=0, tiled=True).reshape(
        ffn_units, wide_count // ffn_units, 2, part_rows, D
    )
    squares = (
        jnp.sum(jnp.square(early_sums.astype(jnp.float32)))
        + jnp.sum(jnp.square(late_sums.astype(jnp.float32)))
        + jnp.sum(jnp.square(proj_weight_grad))
    )
    slot_grads = []
    for slot in range(CAP):
        here = tile_location == own_slots[slot]
        unit = jnp.sum(jnp.where(here, jnp.arange(here.shape[0], dtype=jnp.int32), 0))
        early_unit = jnp.clip(unit - 5, 0, 2 * ffn_units - 1)
        early_sum = lax.dynamic_slice(
            early_sums,
            (early_unit % ffn_units, 0, 1 - early_unit // ffn_units, 0, 0),
            (1, wide_count // ffn_units, 1, part_rows, D),
        ).reshape(unit_rows, D)
        late_sum = lax.dynamic_index_in_dim(late_sums, jnp.clip(unit, 0, 3), 0, keepdims=False)
        low_sum = jnp.where(unit >= 5, early_sum, late_sum).astype(jnp.float32)
        low_sum = jnp.where(unit == 4, proj_weight_grad, low_sum)
        slot_grads.append(jnp.where(jnp.any(here), low_sum, 0.0))
    slot_grads = jnp.stack(slot_grads)
    normed_one_grad = product_add_rows(qkv_rows, qkv_weight, narrow)
    input_norm_grad, attn_gain_grad = norm_backward(
        own_rows, scale_one, rescaling_coefficients[0], normed_one_grad
    )
    input_own = mid_grad + input_norm_grad
    input_grad = natural_rows(
        join_rows(input_own.astype(low_type), narrow), narrow_index, narrow_count
    ).astype(jnp.float32)

    result_pieces = {}
    for peer, rows in zip([0] + bits[1:], result_even):
        rows = after(rows, qkv_cols)
        result_pieces[peer], result_pieces[peer + 1] = rows, swap(rows, narrow, 1)
    layer_result = natural_rows(
        jnp.concatenate([result_pieces[peer] for peer in order], axis=0),
        narrow_index,
        narrow_count,
    ).astype(jnp.float32)

    bias_size = offset_bias_slope.size
    small = jnp.stack(
        [
            ffn_gain_grad,
            attn_gain_grad,
            jnp.pad(offset_bias_slope.reshape(bias_size), (0, D - bias_size)),
        ]
    )
    small_all = spread(small, everyone).reshape(wide_count, narrow_count, 3, D)
    gain_sums = jnp.sum(small_all[:, :, :2], axis=(0, 1))
    gain_total = jnp.stack([gain_sums[1], gain_sums[0], final_gain_grad[0]])
    bias_all = jnp.sum(small_all[:, :, 2], axis=0)
    bias_total = lax.dynamic_index_in_dim(bias_all, narrow_index, 0, keepdims=False)[
        :bias_size
    ].reshape(offset_bias_slope.shape)
    square_terms = lax.all_gather(
        jnp.broadcast_to(squares, (8, LANE)), narrow, axis=0, tiled=True
    )[::8, 0]
    grad_norm = jnp.sqrt(
        jnp.sum(square_terms)
        + jnp.sum(gain_total * gain_total)
        + jnp.sum(bias_all * bias_all)
        + jnp.sum(sharpness_total * sharpness_total)
    )
    multiplier = jnp.minimum(1.0, clip_limit / grad_norm)
    slot_first, slot_second, slot_weight = decoupled_decay_step(
        slot_grads,
        precise_mean_est,
        precise_variance_est,
        precise_parameter_blocks,
        multiplier,
        learn_rate,
    )
    gain_first, gain_second, gain_new = decoupled_decay_step(
        gain_total,
        norm_scale_mean_est,
        norm_scale_variance_est,
        rescaling_coefficients,
        multiplier,
        side_rate,
    )
    bias_first, bias_second, bias_new = decoupled_decay_step(
        bias_total,
        offset_bias_mean_est,
        offset_bias_variance_est,
        distance_bias_table,
        multiplier,
        side_rate,
    )
    sharpness_mean_fresh, sharpness_variance_fresh, sharpness_exponent_fresh = decoupled_decay_step(
        sharpness_total,
        sharpness_mean_est,
        sharpness_variance_est,
        sharpness_exponent,
        multiplier,
        learn_rate,
    )
    return (
        loss,
        layer_result,
        input_grad,
        grad_norm,
        slot_first,
        slot_second,
        slot_weight,
        gain_first,
        gain_second,
        gain_new,
        bias_first,
        bias_second,
        bias_new,
        sharpness_mean_fresh,
        sharpness_variance_fresh,
        sharpness_exponent_fresh,
    )


def solution(mesh):
    wide, narrow, far, near = ("wide",), ("narrow",), ("wide",), ()
    if dict(mesh.shape) == {"wide": 8, "narrow": 4}:
        mesh = Mesh(mesh.devices.reshape(4, 2, 2, 2), ("line", "pair", "side", "core"))
        wide, narrow, far, near = ("line", "pair"), ("side", "core"), ("line",), ("pair",)
    whole, rows, blocks, heads = P(), P(wide, None), P(wide, narrow, None), P(None, narrow)
    arguments = (rows, rows, whole, whole, blocks, blocks, blocks, whole, whole, whole)
    arguments += (heads, heads, heads, whole, whole, whole)
    results = (whole, rows, rows, whole, blocks, blocks, blocks, whole, whole, whole)
    results += (heads, heads, heads, whole, whole, whole)

    def body(*arrays):
        return on_device((wide, narrow, far, near), *arrays)

    return jax.shard_map(
        body, mesh=mesh, in_specs=arguments, out_specs=results, check_vma=False
    )
```

```python
import jax
import jax.numpy as jnp
from jax import lax
from jax.experimental import pallas as pl
from jax.experimental.pallas import tpu as pltpu
from jax.sharding import Mesh
from jax.sharding import PartitionSpec as P

D = 768
FF = 3072
BUCKETS = 32
TOK_DEV = 2560
SEQS_DEV = 4
DOCLEN = 1024
CAP = 2
STEP = 10
LANE = 128
BQ = 512
BK = 512
UNIT_BLOCK = 768
REACH = DOCLEN // LANE
OFF = REACH + (BQ + BK) // LANE
SPAN = 2 * OFF + 1
LINES = 2 * REACH + 2
VMEM_LIMIT = 56 * 1024 * 1024

norm_eps = 1e-06
clip_limit = 0.01
learn_rate = 0.01
side_rate = 0.5
beta_one = 0.5
beta_two = 0.5
adam_eps = 1e-08
decay_rate = 0.01
score_scale = 0.125
masked_score = -1e30
low_type = jnp.bfloat16


def times_transposed(left_side, right_side):
    return lax.dot_general(
        left_side, right_side, (((1,), (1,)), ((), ())), preferred_element_type=jnp.float32
    )


def plain_product(left_side, right_side):
    return jnp.dot(left_side, right_side, preferred_element_type=jnp.float32)


def outer_product(left_side, right_side):
    return lax.dot_general(
        left_side, right_side, (((0,), (0,)), ((), ())), preferred_element_type=jnp.float32
    )


def rms_scale(values):
    return lax.rsqrt(jnp.mean(values * values, axis=-1, keepdims=True) + norm_eps)


def norm_backward(values, row_scale, gain_row, grad_out):
    weighted = grad_out * gain_row
    gain_grad = jnp.sum(grad_out * values * row_scale, axis=0)
    inner_mean = jnp.mean(weighted * values, axis=-1, keepdims=True)
    value_grad = row_scale * weighted - values * row_scale * row_scale * row_scale * inner_mean
    return (value_grad, gain_grad)


def decoupled_decay_step(gradient, first_moment, second_moment, weight, multiplier, step_rate):
    clipped = gradient * multiplier
    first_new = beta_one * first_moment + (1.0 - beta_one) * clipped
    second_new = beta_two * second_moment + (1.0 - beta_two) * clipped * clipped
    first_hat = first_new / (1.0 - beta_one**STEP)
    second_hat = second_new / (1.0 - beta_two**STEP)
    weight_new = weight - step_rate * (
        first_hat / (jnp.sqrt(second_hat) + adam_eps) + decay_rate * weight
    )
    return (first_new, second_new, weight_new)


def swap(values, axes, bit):
    count = lax.axis_size(axes)
    return lax.ppermute(values, axes, [(i, i ^ bit) for i in range(count)])


def sum_low(left, right):
    return (left.astype(jnp.float32) + right.astype(jnp.float32)).astype(low_type)


def narrow_bits(count):
    return [1 << s for s in range(count.bit_length() - 1)]


def peer_order(count):
    order = [0]
    for bit in reversed(narrow_bits(count)):
        order = order + [peer ^ bit for peer in order]
    return order


def join_rows(values, axes):
    for bit in reversed(narrow_bits(lax.axis_size(axes))):
        values = jnp.concatenate([values, swap(values, axes, bit)], axis=0)
    return values


def add_rows(values, axes):
    for bit in narrow_bits(lax.axis_size(axes)):
        half = values.shape[0] // 2
        came = swap(values[half:].astype(low_type), axes, bit)
        values = values[:half].astype(jnp.float32) + came.astype(jnp.float32)
    return values


def product_add_rows(left_side, right_side, axes):
    bits = narrow_bits(lax.axis_size(axes))
    half = left_side.shape[0] // 2
    sent = plain_product(left_side[half:], right_side).astype(low_type)
    came = swap(sent, axes, bits[0])
    values = plain_product(left_side[:half], right_side) + came.astype(jnp.float32)
    for bit in bits[1:]:
        half = values.shape[0] // 2
        came = swap(values[half:].astype(low_type), axes, bit)
        values = values[:half] + came.astype(jnp.float32)
    return values


def natural_rows(joined, index, count):
    order = peer_order(count)
    group = joined.shape[0] // count
    place = jnp.array([order.index(peer) for peer in range(count)], jnp.int32)
    return jnp.concatenate(
        [
            lax.dynamic_slice_in_dim(joined, place[g ^ index] * group, group, 0)
            for g in range(count)
        ],
        axis=0,
    )


def spread(values, axes):
    copies = jnp.broadcast_to(values[None], (lax.axis_size(axes),) + values.shape)
    return lax.all_to_all(copies, axes, split_axis=0, concat_axis=0, tiled=True)


def after(values, other):
    return lax.optimization_barrier((values, other))[0]


def gelu_and_slope(values):
    rate = 0.7978845608028654
    cubic = 0.044715
    squares = values * values
    turn = jnp.tanh(rate * values * (1.0 + cubic * squares))
    half = 0.5 * (1.0 + turn)
    slope = half + 0.5 * values * (1.0 - turn * turn) * (rate * (1.0 + 3.0 * cubic * squares))
    return (values * half).astype(low_type), slope.astype(low_type)


def smem():
    return pl.BlockSpec(memory_space=pltpu.SMEM)


def vmem():
    return pl.BlockSpec(memory_space=pltpu.VMEM)


def bias_kernel(chunks, tiles):
    heads = tiles.shape[0]
    tiles[...] = jnp.zeros_like(tiles)
    for h in range(heads):
        for d in range(-REACH, REACH + 1):
            left = chunks[h, REACH + 1 - d : REACH + 2 - d, :]
            right = chunks[h, REACH - d : REACH + 1 - d, :]
            line = jnp.broadcast_to(jnp.concatenate([left, right], axis=1), (LANE, 2 * LANE))
            rolled = pltpu.roll(line, 0, 1, stride=1, stride_axis=0)
            tiles[h, (d + OFF) * LANE : (d + OFF + 1) * LANE, :] = rolled[:, :LANE]


def bias_tiles(rel_chunks):
    heads = rel_chunks.shape[0]
    return pl.pallas_call(
        bias_kernel,
        out_shape=jax.ShapeDtypeStruct((heads, SPAN * LANE, LANE), jnp.float32),
        compiler_params=pltpu.CompilerParams(vmem_limit_bytes=VMEM_LIMIT),
        name="bias_tiles",
    )(rel_chunks)


def key_range(lengths, first, last):
    start = jnp.int32(0)
    low = jnp.int32(0)
    high = jnp.int32(0)
    for s in range(SEQS_DEV):
        end = start + lengths[s]
        low = jnp.where(start <= first, start, low)
        high = jnp.where(start <= last, end, high)
        start = end
    return low // BK, (high + BK - 1) // BK


def bias_part(bias, h, row):
    return jnp.concatenate(
        [
            bias[h, pl.ds(pl.multiple_of(row - b * LANE, LANE), BK), :]
            for b in range(BQ // LANE)
        ],
        axis=1,
    )


def forward_kernel(first_row, lengths, origin, qT, kn, vT, apart, bias, ctx_o, ctxT_o, lse_o, qa, acc):
    width, rows_here = qT.shape
    heads = bias.shape[0]
    size = width // heads
    qa[...] = jnp.zeros_like(qa)

    @pl.loop(0, rows_here // BQ)
    def _(i):
        q0 = pl.multiple_of(i * BQ, BQ)
        here = pl.ds(q0, BQ)
        for h in range(heads):
            qa[h * LANE : h * LANE + size, :] = qT[h * size : (h + 1) * size, here]
            qa[h * LANE + size : h * LANE + size + 16, :] = apart[:, here]
        acc[...] = jnp.zeros_like(acc)
        low, high = key_range(lengths, first_row + q0, first_row + q0 + BQ - 1)

        def step(j, carry):
            k0 = pl.multiple_of(j * BK, BK)
            row = (j * (BK // LANE) - i * (BQ // LANE) - first_row // LANE + OFF) * LANE
            out = []
            for h in range(heads):
                top, total = carry[2 * h], carry[2 * h + 1]
                own = slice(h * LANE, (h + 1) * LANE)
                rows = slice(h * size, (h + 1) * size)
                s = plain_product(kn[pl.ds(k0, BK), own], qa[own, :]) + bias_part(bias, h, row)
                new_top = jnp.maximum(top, jnp.max(s, axis=0, keepdims=True))
                fade = jnp.exp(top - new_top)
                p = jnp.exp(s - new_top)
                total = total * fade + jnp.sum(p, axis=0, keepdims=True)
                acc[rows, :] = acc[rows, :] * fade + plain_product(
                    vT[rows, pl.ds(k0, BK)], p.astype(low_type)
                )
                out += [new_top, total]
            return tuple(out)

        init = tuple(
            jnp.full((1, BQ), 2.0 * masked_score if n % 2 == 0 else 0.0, jnp.float32)
            for n in range(2 * heads)
        )
        done = lax.fori_loop(low, high, step, init)
        for h in range(heads):
            rows = slice(h * size, (h + 1) * size)
            acc[rows, :] = acc[rows, :] / done[2 * h + 1]
            lse_o[h : h + 1, here] = done[2 * h] + jnp.log(done[2 * h + 1])
        ctxT_o[:, here] = acc[...]
        turned = acc[...].T.astype(low_type)
        for b in range(BQ // LANE):
            at = pl.multiple_of(origin[i * (BQ // LANE) + b], LANE)
            ctx_o[pl.ds(at, LANE), :] = turned[b * LANE : (b + 1) * LANE, :]


def attention_forward(first_row, lengths, origin, qT, kn, vT, apart, bias):
    width, rows_here = qT.shape
    heads = bias.shape[0]

    def body(*refs):
        forward_kernel(first_row, *refs)

    return pl.pallas_call(
        body,
        out_shape=(
            jax.ShapeDtypeStruct((rows_here, width), low_type),
            jax.ShapeDtypeStruct((width, rows_here), jnp.float32),
            jax.ShapeDtypeStruct((heads, rows_here), jnp.float32),
        ),
        in_specs=[smem()] * 2 + [vmem()] * 5,
        out_specs=(vmem(),) * 3,
        scratch_shapes=[
            pltpu.VMEM((heads * LANE, BQ), low_type),
            pltpu.VMEM((width, BQ), jnp.float32),
        ],
        compiler_params=pltpu.CompilerParams(vmem_limit_bytes=VMEM_LIMIT),
        cost_estimate=pl.CostEstimate(
            flops=rows_here * width, bytes_accessed=width * TOK_DEV, transcendentals=0
        ),
        name="attention_forward",
    )(lengths, origin, qT, kn, vT, apart, bias)


def three_parts(values):
    first = values.astype(low_type).astype(jnp.float32)
    rest = values - first
    second = rest.astype(low_type).astype(jnp.float32)
    return first, second, rest - second


def backward_kernel(
    lengths, origin, qT, kn, vn, kT, dcn, ctxT, lse, apart, bias,
    dT_o, dn_o, lines_o, qa, da, dq, dk, dv, tiles,
):
    width, tokens = qT.shape
    heads = bias.shape[0]
    size = width // heads
    for ref in (qa, da, dk, dv, tiles):
        ref[...] = jnp.zeros_like(ref)
    place = lax.broadcasted_iota(jnp.int32, (16, BQ), 0) - SEQS_DEV

    def in_depth(values):
        a, b, c = three_parts(values)
        return jnp.where(place == 0, a, jnp.where(place == 1, b, jnp.where(place == 2, c, 0.0)))

    @pl.loop(0, tokens // BQ)
    def _(i):
        q0 = pl.multiple_of(i * BQ, BQ)
        here = pl.ds(q0, BQ)
        at = [pl.multiple_of(origin[i * (BQ // LANE) + b], LANE) for b in range(BQ // LANE)]
        dcT = jnp.concatenate(
            [dcn[pl.ds(at[b], LANE), :].astype(jnp.float32) for b in range(BQ // LANE)], axis=0
        ).T
        for h in range(heads):
            rows = slice(h * size, (h + 1) * size)
            top = h * LANE
            qa[top : top + size, :] = qT[rows, here]
            extra = apart[:, here].astype(jnp.float32) + in_depth(-lse[h : h + 1, here])
            qa[top + size : top + size + 16, :] = extra.astype(low_type)
            da[top : top + size, :] = dcT[rows, :].astype(low_type)
            delta = jnp.sum(dcT[rows, :] * ctxT[rows, here], axis=0, keepdims=True)
            da[top + size : top + size + 16, :] = in_depth(-delta).astype(low_type)
        dq[...] = jnp.zeros_like(dq)
        low, high = key_range(lengths, q0, q0 + BQ - 1)

        @pl.loop(low, high)
        def _(j):
            k0 = pl.multiple_of(j * BK, BK)
            there = pl.ds(k0, BK)
            row = (j * (BK // LANE) - i * (BQ // LANE) + OFF) * LANE
            for h in range(heads):
                rows = slice(h * size, (h + 1) * size)
                own = slice(h * LANE, (h + 1) * LANE)
                flat = slice(h * LANE, h * LANE + size)
                s = plain_product(kn[there, own], qa[own, :])
                p = jnp.exp(s + bias_part(bias, h, row))
                ds = p * plain_product(vn[there, own], da[own, :])
                for b in range(BQ // LANE):
                    window = pl.ds(pl.multiple_of(row - b * LANE, LANE), BK)
                    tiles[h, window, :] = (
                        tiles[h, window, :] + ds[:, b * LANE : (b + 1) * LANE]
                    )
                p_low = p.astype(low_type)
                ds_low = ds.astype(low_type)
                dv[rows, there] = dv[rows, there] + times_transposed(da[flat, :], p_low)
                dk[rows, there] = dk[rows, there] + times_transposed(qa[flat, :], ds_low)
                dq[rows, :] = dq[rows, :] + plain_product(kT[rows, there], ds_low)

        grad = dq[...] * score_scale
        dT_o[0:width, here] = grad.astype(low_type)
        turned = grad.T.astype(low_type)
        for b in range(BQ // LANE):
            dn_o[pl.ds(at[b], LANE), 0:width] = turned[b * LANE : (b + 1) * LANE, :]

    @pl.loop(0, tokens // BQ)
    def _(i):
        here = pl.ds(pl.multiple_of(i * BQ, BQ), BQ)
        both = jnp.concatenate([dk[:, here], dv[:, here]], axis=0)
        dT_o[width : 3 * width, here] = both.astype(low_type)
        turned = both.T.astype(low_type)
        for b in range(BQ // LANE):
            at = pl.multiple_of(origin[i * (BQ // LANE) + b], LANE)
            dn_o[pl.ds(at, LANE), width : 3 * width] = turned[b * LANE : (b + 1) * LANE, :]

    across = lax.broadcasted_iota(jnp.int32, (LANE, LANE), 1)
    over = across >= lax.broadcasted_iota(jnp.int32, (LANE, LANE), 0)
    sub = lax.broadcasted_iota(jnp.int32, (8, LANE), 0)
    for h in range(heads):
        for d in range(-REACH, REACH + 2):
            here = tiles[h, (d + OFF) * LANE : (d + OFF + 1) * LANE, :]
            below = tiles[h, (d + OFF - 1) * LANE : (d + OFF) * LANE, :]
            mixed = jnp.where(over, here, below)
            line = mixed[LANE - 8 :, :]
            for g in range(LANE // 8 - 2, -1, -1):
                line = mixed[8 * g : 8 * g + 8, :] + pltpu.roll(line, LANE - 8, 1)
            for bit in (1, 2, 4):
                line = jnp.where((sub & bit) != 0, pltpu.roll(line, LANE - bit, 1), line)
            lines_o[h, REACH + 1 - d : REACH + 2 - d, :] = jnp.sum(line, axis=0, keepdims=True)


def attention_backward(lengths, origin, qT, kn, vn, kT, dcn, ctxT, lse, apart, bias):
    width, tokens = qT.shape
    heads = bias.shape[0]
    return pl.pallas_call(
        backward_kernel,
        out_shape=(
            jax.ShapeDtypeStruct((3 * width, tokens), low_type),
            jax.ShapeDtypeStruct((tokens, 3 * width), low_type),
            jax.ShapeDtypeStruct((heads, LINES, LANE), jnp.float32),
        ),
        in_specs=[smem()] * 2 + [vmem()] * 9,
        out_specs=(vmem(),) * 3,
        scratch_shapes=[
            pltpu.VMEM((heads * LANE, BQ), low_type),
            pltpu.VMEM((heads * LANE, BQ), low_type),
            pltpu.VMEM((width, BQ), jnp.float32),
            pltpu.VMEM((width, tokens), jnp.float32),
            pltpu.VMEM((width, tokens), jnp.float32),
            pltpu.VMEM((heads, SPAN * LANE, LANE), jnp.float32),
        ],
        compiler_params=pltpu.CompilerParams(vmem_limit_bytes=VMEM_LIMIT),
        cost_estimate=pl.CostEstimate(
            flops=tokens * width, bytes_accessed=width * TOK_DEV, transcendentals=0
        ),
        name="attention_backward",
    )(lengths, origin, qT, kn, vn, kT, dcn, ctxT, lse, apart, bias)


def feed_forward_backward_kernel(
    grad, rows, hidden, slope, inner, outer, weight_grads, rows_grad
):
    groups, _, size, width = weight_grads.shape

    @pl.when(pl.program_id(0) == 0)
    def _():
        rows_grad[...] = jnp.zeros_like(rows_grad)

    outer_grad = outer_product(hidden[...], grad[...]).astype(low_type)
    weight_grads[:, 0] = outer_grad.reshape(groups, size, width)
    pre = (
        times_transposed(grad[...], outer[...]) * slope[...].astype(jnp.float32)
    ).astype(low_type)
    inner_grad = outer_product(pre, rows[...]).astype(low_type)
    weight_grads[:, 1] = inner_grad.reshape(groups, size, width)
    rows_grad[...] += plain_product(pre, inner[...])


def feed_forward_backward(grad, rows, hidden, slope, inner, outer, size):
    count = grad.shape[0]
    groups = UNIT_BLOCK // size
    every = pl.BlockSpec((count, D), lambda i: (0, 0))
    units = pl.BlockSpec((count, UNIT_BLOCK), lambda i: (0, i))
    weight = pl.BlockSpec((UNIT_BLOCK, D), lambda i: (i, 0))
    return pl.pallas_call(
        feed_forward_backward_kernel,
        grid=(FF // UNIT_BLOCK,),
        out_shape=(
            jax.ShapeDtypeStruct((FF // size, 2, size, D), low_type),
            jax.ShapeDtypeStruct((count, D), jnp.float32),
        ),
        in_specs=[every, every, units, units, weight, weight],
        out_specs=(pl.BlockSpec((groups, 2, size, D), lambda i: (i, 0, 0, 0)), every),
        compiler_params=pltpu.CompilerParams(vmem_limit_bytes=VMEM_LIMIT),
        cost_estimate=pl.CostEstimate(flops=FF * D, bytes_accessed=FF * D, transcendentals=0),
        name="feed_forward_backward",
    )(grad, rows, hidden, slope, inner, outer)


def loss_kernel(place, numbers, parts, proj_weight, gain, out_slope, out_low, out_row, out_gain):
    total_seqs = out_low.shape[0] // 2
    terms = parts.shape[0] // total_seqs
    exact = dict(precision=lax.Precision.HIGHEST, preferred_element_type=jnp.float32)
    seq = lax.broadcasted_iota(jnp.int32, (total_seqs, parts.shape[0]), 0)
    part = lax.broadcasted_iota(jnp.int32, (total_seqs, parts.shape[0]), 1)
    joins = jnp.logical_and(
        seq // SEQS_DEV == part // (SEQS_DEV * terms), seq % SEQS_DEV == part % SEQS_DEV
    )
    unscaled = jnp.dot(joins.astype(jnp.float32), parts[...], **exact)
    pooled_low = (unscaled * gain[...]).astype(low_type)
    projected = times_transposed(pooled_low, proj_weight[...]).astype(low_type).astype(jnp.float32)
    inverse = lax.rsqrt(jnp.sum(projected * projected, axis=1, keepdims=True) + norm_eps)
    embed_low = (projected * inverse).astype(low_type)
    sharpness_factor = jnp.exp(jnp.full((1, 1), numbers[0], jnp.float32))
    agreement = times_transposed(embed_low, embed_low)
    row = lax.broadcasted_iota(jnp.int32, (total_seqs, total_seqs), 0)
    column = lax.broadcasted_iota(jnp.int32, (total_seqs, total_seqs), 1)
    logits = jnp.where(row == column, masked_score, sharpness_factor * agreement)
    partner = (row ^ 1) == column

    def log_sum(axis):
        top = jnp.max(logits, axis=axis, keepdims=True)
        return top + jnp.log(jnp.sum(jnp.exp(logits - top), axis=axis, keepdims=True))

    log_rows = log_sum(1)
    positive = jnp.where(partner, 1.0, 0.0)
    slope = (jnp.exp(logits - log_rows) - positive) / total_seqs
    slope_turned = (jnp.exp(logits - log_sum(0)) - positive) / total_seqs
    embed_grad = sharpness_factor * jnp.dot(
        slope + slope_turned, embed_low.astype(jnp.float32), **exact
    )
    along = jnp.sum(projected * embed_grad, axis=1, keepdims=True)
    proj_grad_low = (
        inverse * embed_grad - projected * inverse * inverse * inverse * along
    ).astype(low_type)
    pooled_grad = plain_product(proj_grad_low, proj_weight[...])
    out_low[0:total_seqs, :] = proj_grad_low
    out_low[total_seqs : 2 * total_seqs, :] = pooled_low
    out_gain[...] = jnp.sum(pooled_grad * unscaled, axis=0, keepdims=True)
    loss = jnp.sum(
        log_rows - jnp.sum(positive * jnp.where(partner, logits, 0.0), axis=1, keepdims=True),
        axis=0,
        keepdims=True,
    ) / total_seqs
    temperature = sharpness_factor * jnp.sum(
        jnp.sum(slope * agreement, axis=1, keepdims=True), axis=0, keepdims=True
    )
    lane = lax.broadcasted_iota(jnp.int32, (1, LANE), 1)
    out_row[...] = jnp.where(lane == 0, loss, jnp.where(lane == 1, temperature, 0.0))
    mine = lax.broadcasted_iota(jnp.int32, (8, total_seqs), 0)
    seq_of = lax.broadcasted_iota(jnp.int32, (8, total_seqs), 1) - place[0] * SEQS_DEV
    picks = jnp.logical_and(mine == seq_of, mine < SEQS_DEV).astype(jnp.float32)
    own = jnp.dot(picks, pooled_grad, **exact)
    index = lax.broadcasted_iota(jnp.int32, (8, 1), 0)
    extent = jnp.ones((8, 1), jnp.float32)
    for s in range(SEQS_DEV):
        extent = jnp.where(index == s, place[1 + s].astype(jnp.float32), extent)
    out_slope[...] = own * gain[...] / extent


def contrastive(place, numbers, parts, proj_weight, gain, total_seqs):
    return pl.pallas_call(
        loss_kernel,
        out_shape=(
            jax.ShapeDtypeStruct((8, D), jnp.float32),
            jax.ShapeDtypeStruct((2 * total_seqs, D), low_type),
            jax.ShapeDtypeStruct((1, LANE), jnp.float32),
            jax.ShapeDtypeStruct((1, D), jnp.float32),
        ),
        in_specs=[smem()] * 2 + [vmem()] * 3,
        out_specs=(vmem(),) * 4,
        compiler_params=pltpu.CompilerParams(vmem_limit_bytes=VMEM_LIMIT),
        cost_estimate=pl.CostEstimate(
            flops=4 * total_seqs * D * D, bytes_accessed=4 * D * D, transcendentals=total_seqs
        ),
        name="contrastive",
    )(place, numbers, parts, proj_weight, gain)


def on_device(
    axes,
    layer_argument,
    document_extents,
    distance_bin_lookup,
    tile_location,
    precise_parameter_blocks,
    precise_mean_est,
    precise_variance_est,
    rescaling_coefficients,
    norm_scale_mean_est,
    norm_scale_variance_est,
    distance_bias_table,
    offset_bias_mean_est,
    offset_bias_variance_est,
    sharpness_exponent,
    sharpness_mean_est,
    sharpness_variance_est,
):
    wide, narrow, far, near = axes
    everyone = wide + narrow
    near_axes = near + narrow
    wide_count = lax.axis_size(wide)
    narrow_count = lax.axis_size(narrow)
    far_count = lax.axis_size(far)
    near_count = wide_count // far_count
    wide_index = lax.axis_index(wide)
    narrow_index = lax.axis_index(narrow)
    bits = narrow_bits(narrow_count)
    order = peer_order(narrow_count)
    place_of = jnp.array([order.index(peer) for peer in range(narrow_count)], jnp.int32)
    unit_rows = precise_parameter_blocks.shape[1]
    heads_here = distance_bias_table.shape[1]
    head_size = unit_rows // heads_here
    ffn_units = FF // D
    group = TOK_DEV // narrow_count
    own_slots = wide_index * CAP + jnp.arange(CAP, dtype=jnp.int32)

    every_slot = lax.all_gather(
        precise_parameter_blocks.astype(low_type), wide, axis=0, tiled=True
    )

    def block(u):
        return lax.dynamic_index_in_dim(every_slot, tile_location[u], 0, keepdims=False)

    qkv_weight = jnp.concatenate([block(u) for u in range(3)], axis=0)

    part_rows = D // wide_count

    def unit_order(first_unit):
        rows = jnp.concatenate([block(first_unit + k) for k in range(ffn_units)], axis=0)
        rows = rows.reshape(far_count, near_count, part_rows, D)
        return jnp.swapaxes(rows, 0, 1).reshape(near_count, far_count * part_rows, D)

    crossing = [
        jnp.concatenate([block(3), block(4)], axis=0),
        unit_order(5),
        unit_order(5 + ffn_units),
    ]
    for rows in crossing:
        qkv_weight = after(qkv_weight, rows)
    crossed = [[rows] + [swap(rows, narrow, peer) for peer in bits[1:]] for rows in crossing]

    lengths = document_extents[0]
    seq_ends = jnp.cumsum(lengths)
    positions = jnp.arange(TOK_DEV, dtype=jnp.int32)

    def segments_of(where):
        return jnp.sum((seq_ends[None, :] <= where[:, None]).astype(jnp.int32), axis=1)

    segment_ids = segments_of(positions)
    own_segments = segments_of(narrow_index * group + positions[:group])
    tile_starts = jnp.arange(TOK_DEV // LANE, dtype=jnp.int32) * LANE
    origin = place_of[(tile_starts // group) ^ narrow_index] * group + tile_starts % group

    beyond = LINES * LANE - LANE - 1 - distance_bin_lookup.shape[0]
    offsets_down = jnp.pad(distance_bin_lookup[::-1], (LANE + 1, beyond), constant_values=-1)
    bucket_onehot = (
        offsets_down[:, None] == jnp.arange(BUCKETS, dtype=jnp.int32)[None, :]
    ).astype(jnp.float32)
    rel_values = jnp.dot(bucket_onehot, distance_bias_table, precision=lax.Precision.HIGHEST).T
    tiles_bias = bias_tiles(rel_values.reshape(heads_here, LINES, LANE))

    all_rows = layer_argument.astype(jnp.float32)
    normed_one = (all_rows * rms_scale(all_rows) * rescaling_coefficients[0]).astype(low_type)
    transposed_rows = times_transposed(qkv_weight, normed_one)
    query_cols = (transposed_rows[:unit_rows] * score_scale).astype(low_type)
    key_cols = transposed_rows[unit_rows : 2 * unit_rows].astype(low_type)
    value_cols = transposed_rows[2 * unit_rows :].astype(low_type)
    spread_weight = jnp.pad(
        qkv_weight[unit_rows:].reshape(2 * heads_here, head_size, D),
        ((0, 0), (0, LANE - head_size), (0, 0)),
    ).reshape(2 * heads_here * LANE, D)
    lane_place = jnp.arange(2 * heads_here * LANE, dtype=jnp.int32) % LANE - head_size
    marks = jnp.logical_or(
        lane_place[None, :] == segment_ids[:, None],
        jnp.logical_and(lane_place >= SEQS_DEV, lane_place < SEQS_DEV + 3)[None, :],
    )
    key_value_rows = (
        times_transposed(normed_one, spread_weight) + marks.astype(jnp.float32)
    ).astype(low_type)
    key_rows = key_value_rows[:, : heads_here * LANE]
    value_rows = key_value_rows[:, heads_here * LANE :]
    row_place = jnp.arange(16, dtype=jnp.int32)[:, None]
    apart = jnp.where(
        jnp.logical_and(row_place < SEQS_DEV, row_place != segment_ids[None, :]), masked_score, 0.0
    ).astype(low_type)
    context, context_cols, log_rows = attention_forward(
        0, lengths, origin, query_cols, key_rows, value_cols, apart, tiles_bias
    )

    def all_peers(pieces):
        own, *even = pieces
        even = [after(rows, context) for rows in even]
        peers = [(0, own), (1, swap(own, narrow, 1))]
        for bit, rows in zip(bits[1:], even):
            peers += [(bit, rows), (bit + 1, swap(rows, narrow, 1))]
        return peers

    def in_unit_order(pieces):
        whole = jnp.zeros((near_count, narrow_count, far_count * part_rows, D), low_type)
        for peer, rows in all_peers(pieces):
            start = (0, narrow_index ^ peer, 0, 0)
            whole = lax.dynamic_update_slice(whole, rows[:, None], start)
        return whole.reshape(FF, D)

    both = dict(all_peers(crossed[0]))
    out_joined = jnp.concatenate([both[peer][:unit_rows] for peer in order], axis=0)
    proj_weight = natural_rows(
        jnp.concatenate([both[peer][unit_rows:] for peer in order], axis=0),
        narrow_index,
        narrow_count,
    )
    inner_joined = in_unit_order(crossed[1])
    outer_joined = in_unit_order(crossed[2])

    def to_peer(values, peer):
        if peer == 0:
            return values
        return swap(values, narrow, peer)

    context_own = jnp.concatenate(
        [
            to_peer(context[s * group : (s + 1) * group], peer)
            for s, peer in enumerate(order)
        ],
        axis=1,
    )
    own_rows = lax.dynamic_slice_in_dim(layer_argument, narrow_index * group, group, 0).astype(
        jnp.float32
    )
    scale_one = rms_scale(own_rows)
    residual_mid = own_rows + plain_product(context_own, out_joined)
    scale_two = rms_scale(residual_mid)
    normed_two = (residual_mid * scale_two * rescaling_coefficients[1]).astype(low_type)

    hidden_low, hidden_slope = gelu_and_slope(times_transposed(normed_two, inner_joined))
    result_own = residual_mid + plain_product(hidden_low, outer_joined)
    result_low = result_own.astype(low_type)
    result_even = [result_low] + [swap(result_low, narrow, peer) for peer in bits[1:]]

    scale_three = rms_scale(result_own)
    member = (
        own_segments[None, :] == jnp.arange(SEQS_DEV, dtype=jnp.int32)[:, None]
    ).astype(jnp.float32)
    length_values = lengths.astype(jnp.float32)[:, None]
    unscaled_part = (
        jnp.dot(member, result_own * scale_three, precision=lax.Precision.HIGHEST) / length_values
    )
    total_seqs = wide_count * SEQS_DEV
    own_pooled_grad, loss_low, loss_row, final_gain_grad = contrastive(
        jnp.concatenate([wide_index.reshape(1), lengths]),
        sharpness_exponent,
        spread(unscaled_part, everyone).reshape(total_seqs * narrow_count, D),
        proj_weight,
        rescaling_coefficients[2:3],
        total_seqs,
    )
    loss = loss_row[0, 0]
    sharpness_total = loss_row[0, 1:2]
    proj_grad_own = lax.dynamic_slice_in_dim(
        loss_low[:total_seqs], narrow_index * unit_rows, unit_rows, 1
    )
    proj_weight_grad = outer_product(proj_grad_own, loss_low[total_seqs:])

    weighted = own_pooled_grad[SEQS_DEV - 1]
    for s in range(SEQS_DEV - 2, -1, -1):
        weighted = jnp.where((own_segments == s)[:, None], own_pooled_grad[s], weighted)
    inner_mean = jnp.mean(weighted * result_own, axis=-1, keepdims=True)
    encoded_grad = scale_three * weighted - result_own * (
        scale_three * scale_three * scale_three * inner_mean
    )
    ffn_grad_low = encoded_grad.astype(low_type)
    group_rows = part_rows if part_rows % 16 == 0 else D
    weight_grads, normed_two_grad = feed_forward_backward(
        ffn_grad_low,
        normed_two,
        hidden_low,
        hidden_slope,
        inner_joined,
        outer_joined,
        group_rows,
    )
    near_part = lax.psum_scatter(
        weight_grads.reshape(2 * FF, D), near_axes, scatter_dimension=0, tiled=True
    )
    mid_norm_grad, ffn_gain_grad = norm_backward(
        residual_mid, scale_two, rescaling_coefficients[1], normed_two_grad
    )
    mid_grad = encoded_grad + mid_norm_grad
    attn_grad_low = mid_grad.astype(low_type)

    context_grad_own = times_transposed(attn_grad_low, out_joined).astype(low_type)
    context_grad = [
        to_peer(context_grad_own[:, s * unit_rows : (s + 1) * unit_rows], peer)
        for s, peer in enumerate(order)
    ]
    attn_grad_low = after(attn_grad_low, context_grad_own)
    out_kept = outer_product(context_own, attn_grad_low).astype(low_type)
    for bit in bits:
        half = out_kept.shape[0] // 2
        out_came = swap(out_kept[half:], narrow, bit)
        if bit == bits[-1]:
            break
        out_kept = sum_low(out_kept[:half], out_came)
    context_grad = after(jnp.concatenate(context_grad, axis=0), out_kept)
    qkv_cols, qkv_rows, bias_lines = attention_backward(
        lengths,
        origin,
        query_cols,
        key_rows,
        value_rows,
        key_cols,
        context_grad,
        context_cols,
        log_rows,
        apart,
        tiles_bias,
    )
    qkv_cols, qkv_rows, out_came = lax.optimization_barrier((qkv_cols, qkv_rows, out_came))
    out_grad = sum_low(out_kept[: out_came.shape[0]], out_came)
    offset_bias_slope = lax.dot_general(
        bucket_onehot,
        bias_lines.reshape(heads_here, LINES * LANE),
        (((0,), (1,)), ((), ())),
        precision=lax.Precision.HIGHEST,
    )

    late = jnp.concatenate(
        [plain_product(qkv_cols, normed_one).astype(low_type), out_grad], axis=0
    )
    early = after(near_part, late).reshape(-1, 2, group_rows // part_rows, part_rows, D)
    early = jnp.swapaxes(early, 1, 2).reshape(far_count * 2 * part_rows, D)
    early_part = lax.psum_scatter(early, far, scatter_dimension=0, tiled=True)
    late_rows = late.shape[0] // wide_count
    late_terms = lax.all_to_all(
        late.reshape(wide_count, late_rows, D), wide, split_axis=0, concat_axis=0, tiled=True
    )
    late_part = jnp.sum(late_terms.astype(jnp.float32), axis=0)
    late_low = late_part.astype(low_type)
    late_sums = spread(late_low, wide).reshape(4, unit_rows, D)
    early_sums = lax.all_gather(early_part, wide, axis=0, tiled=True).reshape(
        ffn_units, wide_count // ffn_units, 2, part_rows, D
    )
    normed_one_grad = product_add_rows(qkv_rows, qkv_weight, narrow)
    input_norm_grad, attn_gain_grad = norm_backward(
        own_rows, scale_one, rescaling_coefficients[0], normed_one_grad
    )
    input_own = mid_grad + input_norm_grad
    input_grad = natural_rows(
        join_rows(input_own.astype(low_type), narrow), narrow_index, narrow_count
    ).astype(jnp.float32)

    result_pieces = {}
    for peer, rows in zip([0] + bits[1:], result_even):
        rows = after(rows, qkv_cols)
        result_pieces[peer], result_pieces[peer + 1] = rows, swap(rows, narrow, 1)
    layer_result = natural_rows(
        jnp.concatenate([result_pieces[peer] for peer in order], axis=0),
        narrow_index,
        narrow_count,
    ).astype(jnp.float32)

    bias_size = offset_bias_slope.size
    small = jnp.stack(
        [
            ffn_gain_grad,
            attn_gain_grad,
            jnp.pad(offset_bias_slope.reshape(bias_size), (0, D - bias_size)),
        ]
    )
    small_all = spread(after(small, late_sums), everyone).reshape(wide_count, narrow_count, 3, D)
    gain_sums = jnp.sum(small_all[:, :, :2], axis=(0, 1))
    gain_total = jnp.stack([gain_sums[1], gain_sums[0], final_gain_grad[0]])
    bias_all = jnp.sum(small_all[:, :, 2], axis=0)
    bias_total = lax.dynamic_index_in_dim(bias_all, narrow_index, 0, keepdims=False)[
        :bias_size
    ].reshape(offset_bias_slope.shape)
    early_sums, late_sums, *_ = lax.optimization_barrier(
        (early_sums, late_sums, input_grad, layer_result, gain_total, bias_all, bias_total)
    )
    squares = (
        jnp.sum(jnp.square(early_sums.astype(jnp.float32)))
        + jnp.sum(jnp.square(late_sums.astype(jnp.float32)))
        + jnp.sum(jnp.square(proj_weight_grad))
    )
    slot_grads = []
    for slot in range(CAP):
        here = tile_location == own_slots[slot]
        unit = jnp.sum(jnp.where(here, jnp.arange(here.shape[0], dtype=jnp.int32), 0))
        early_unit = jnp.clip(unit - 5, 0, 2 * ffn_units - 1)
        early_sum = lax.dynamic_slice(
            early_sums,
            (early_unit % ffn_units, 0, 1 - early_unit // ffn_units, 0, 0),
            (1, wide_count // ffn_units, 1, part_rows, D),
        ).reshape(unit_rows, D)
        late_sum = lax.dynamic_index_in_dim(late_sums, jnp.clip(unit, 0, 3), 0, keepdims=False)
        low_sum = jnp.where(unit >= 5, early_sum, late_sum).astype(jnp.float32)
        low_sum = jnp.where(unit == 4, proj_weight_grad, low_sum)
        slot_grads.append(jnp.where(jnp.any(here), low_sum, 0.0))
    slot_grads = jnp.stack(slot_grads)
    square_terms = lax.all_gather(
        jnp.broadcast_to(squares, (8, LANE)), narrow, axis=0, tiled=True
    )[::8, 0]
    grad_norm = jnp.sqrt(
        jnp.sum(square_terms)
        + jnp.sum(gain_total * gain_total)
        + jnp.sum(bias_all * bias_all)
        + jnp.sum(sharpness_total * sharpness_total)
    )
    multiplier = jnp.minimum(1.0, clip_limit / grad_norm)
    slot_first, slot_second, slot_weight = decoupled_decay_step(
        slot_grads,
        precise_mean_est,
        precise_variance_est,
        precise_parameter_blocks,
        multiplier,
        learn_rate,
    )
    gain_first, gain_second, gain_new = decoupled_decay_step(
        gain_total,
        norm_scale_mean_est,
        norm_scale_variance_est,
        rescaling_coefficients,
        multiplier,
        side_rate,
    )
    bias_first, bias_second, bias_new = decoupled_decay_step(
        bias_total,
        offset_bias_mean_est,
        offset_bias_variance_est,
        distance_bias_table,
        multiplier,
        side_rate,
    )
    sharpness_mean_fresh, sharpness_variance_fresh, sharpness_exponent_fresh = decoupled_decay_step(
        sharpness_total,
        sharpness_mean_est,
        sharpness_variance_est,
        sharpness_exponent,
        multiplier,
        learn_rate,
    )
    return (
        loss,
        layer_result,
        input_grad,
        grad_norm,
        slot_first,
        slot_second,
        slot_weight,
        gain_first,
        gain_second,
        gain_new,
        bias_first,
        bias_second,
        bias_new,
        sharpness_mean_fresh,
        sharpness_variance_fresh,
        sharpness_exponent_fresh,
    )


def solution(mesh):
    wide, narrow, far, near = ("wide",), ("narrow",), ("wide",), ()
    if dict(mesh.shape) == {"wide": 8, "narrow": 4}:
        mesh = Mesh(mesh.devices.reshape(4, 2, 2, 2), ("line", "pair", "side", "core"))
        wide, narrow, far, near = ("line", "pair"), ("side", "core"), ("line",), ("pair",)
    whole, rows, blocks, heads = P(), P(wide, None), P(wide, narrow, None), P(None, narrow)
    arguments = (rows, rows, whole, whole, blocks, blocks, blocks, whole, whole, whole)
    arguments += (heads, heads, heads, whole, whole, whole)
    results = (whole, rows, rows, whole, blocks, blocks, blocks, whole, whole, whole)
    results += (heads, heads, heads, whole, whole, whole)

    def body(*arrays):
        return on_device((wide, narrow, far, near), *arrays)

    return jax.shard_map(
        body, mesh=mesh, in_specs=arguments, out_specs=results, check_vma=False
    )
```

```python
import jax
import jax.numpy as jnp
from jax import lax
from jax.experimental import pallas as pl
from jax.experimental.pallas import tpu as pltpu
from jax.sharding import Mesh
from jax.sharding import PartitionSpec as P

D = 768
FF = 3072
BUCKETS = 32
TOK_DEV = 2560
SEQS_DEV = 4
DOCLEN = 1024
CAP = 2
STEP = 10
LANE = 128
BQ = 512
BK = 512
UNIT_BLOCK = 768
REACH = DOCLEN // LANE
OFF = REACH + (BQ + BK) // LANE
SPAN = 2 * OFF + 1
LINES = 2 * REACH + 2
VMEM_LIMIT = 56 * 1024 * 1024

norm_eps = 1e-06
clip_limit = 0.01
learn_rate = 0.01
side_rate = 0.5
beta_one = 0.5
beta_two = 0.5
adam_eps = 1e-08
decay_rate = 0.01
score_scale = 0.125
masked_score = -1e30
low_type = jnp.bfloat16


def times_transposed(left_side, right_side):
    return lax.dot_general(
        left_side, right_side, (((1,), (1,)), ((), ())), preferred_element_type=jnp.float32
    )


def plain_product(left_side, right_side):
    return jnp.dot(left_side, right_side, preferred_element_type=jnp.float32)


def outer_product(left_side, right_side):
    return lax.dot_general(
        left_side, right_side, (((0,), (0,)), ((), ())), preferred_element_type=jnp.float32
    )


def rms_scale(values):
    return lax.rsqrt(jnp.mean(values * values, axis=-1, keepdims=True) + norm_eps)


def norm_backward(values, row_scale, gain_row, grad_out):
    weighted = grad_out * gain_row
    gain_grad = jnp.sum(grad_out * values * row_scale, axis=0)
    inner_mean = jnp.mean(weighted * values, axis=-1, keepdims=True)
    value_grad = row_scale * weighted - values * row_scale * row_scale * row_scale * inner_mean
    return (value_grad, gain_grad)


def decoupled_decay_step(gradient, first_moment, second_moment, weight, multiplier, step_rate):
    clipped = gradient * multiplier
    first_new = beta_one * first_moment + (1.0 - beta_one) * clipped
    second_new = beta_two * second_moment + (1.0 - beta_two) * clipped * clipped
    first_hat = first_new / (1.0 - beta_one**STEP)
    second_hat = second_new / (1.0 - beta_two**STEP)
    weight_new = weight - step_rate * (
        first_hat / (jnp.sqrt(second_hat) + adam_eps) + decay_rate * weight
    )
    return (first_new, second_new, weight_new)


def swap(values, axes, bit):
    count = lax.axis_size(axes)
    return lax.ppermute(values, axes, [(i, i ^ bit) for i in range(count)])


def sum_low(left, right):
    return (left.astype(jnp.float32) + right.astype(jnp.float32)).astype(low_type)


def narrow_bits(count):
    return [1 << s for s in range(count.bit_length() - 1)]


def peer_order(count):
    order = [0]
    for bit in reversed(narrow_bits(count)):
        order = order + [peer ^ bit for peer in order]
    return order


def join_rows(values, axes):
    for bit in reversed(narrow_bits(lax.axis_size(axes))):
        values = jnp.concatenate([values, swap(values, axes, bit)], axis=0)
    return values


def add_rows(values, axes):
    for bit in narrow_bits(lax.axis_size(axes)):
        half = values.shape[0] // 2
        came = swap(values[half:].astype(low_type), axes, bit)
        values = values[:half].astype(jnp.float32) + came.astype(jnp.float32)
    return values


def product_add_rows(left_side, right_side, axes):
    bits = narrow_bits(lax.axis_size(axes))
    half = left_side.shape[0] // 2
    sent = plain_product(left_side[half:], right_side).astype(low_type)
    came = swap(sent, axes, bits[0])
    values = plain_product(left_side[:half], right_side) + came.astype(jnp.float32)
    for bit in bits[1:]:
        half = values.shape[0] // 2
        came = swap(values[half:].astype(low_type), axes, bit)
        values = values[:half] + came.astype(jnp.float32)
    return values


def natural_rows(joined, index, count):
    order = peer_order(count)
    group = joined.shape[0] // count
    place = jnp.array([order.index(peer) for peer in range(count)], jnp.int32)
    return jnp.concatenate(
        [
            lax.dynamic_slice_in_dim(joined, place[g ^ index] * group, group, 0)
            for g in range(count)
        ],
        axis=0,
    )


def spread(values, axes):
    copies = jnp.broadcast_to(values[None], (lax.axis_size(axes),) + values.shape)
    return lax.all_to_all(copies, axes, split_axis=0, concat_axis=0, tiled=True)


def after(values, other):
    return lax.optimization_barrier((values, other))[0]


def gelu_and_slope(values):
    rate = 0.7978845608028654
    cubic = 0.044715
    squares = values * values
    turn = jnp.tanh(rate * values * (1.0 + cubic * squares))
    half = 0.5 * (1.0 + turn)
    slope = half + 0.5 * values * (1.0 - turn * turn) * (rate * (1.0 + 3.0 * cubic * squares))
    return (values * half).astype(low_type), slope.astype(low_type)


def smem():
    return pl.BlockSpec(memory_space=pltpu.SMEM)


def vmem():
    return pl.BlockSpec(memory_space=pltpu.VMEM)


def bias_kernel(chunks, tiles):
    heads = tiles.shape[0]
    tiles[...] = jnp.zeros_like(tiles)
    for h in range(heads):
        for d in range(-REACH, REACH + 1):
            left = chunks[h, REACH + 1 - d : REACH + 2 - d, :]
            right = chunks[h, REACH - d : REACH + 1 - d, :]
            line = jnp.broadcast_to(jnp.concatenate([left, right], axis=1), (LANE, 2 * LANE))
            rolled = pltpu.roll(line, 0, 1, stride=1, stride_axis=0)
            tiles[h, (d + OFF) * LANE : (d + OFF + 1) * LANE, :] = rolled[:, :LANE]


def bias_tiles(rel_chunks):
    heads = rel_chunks.shape[0]
    return pl.pallas_call(
        bias_kernel,
        out_shape=jax.ShapeDtypeStruct((heads, SPAN * LANE, LANE), jnp.float32),
        compiler_params=pltpu.CompilerParams(vmem_limit_bytes=VMEM_LIMIT),
        name="bias_tiles",
    )(rel_chunks)


def key_range(lengths, first, last):
    start = jnp.int32(0)
    low = jnp.int32(0)
    high = jnp.int32(0)
    for s in range(SEQS_DEV):
        end = start + lengths[s]
        low = jnp.where(start <= first, start, low)
        high = jnp.where(start <= last, end, high)
        start = end
    return low // BK, (high + BK - 1) // BK


def bias_part(bias, h, row):
    return jnp.concatenate(
        [
            bias[h, pl.ds(pl.multiple_of(row - b * LANE, LANE), BK), :]
            for b in range(BQ // LANE)
        ],
        axis=1,
    )


def forward_kernel(first_row, lengths, origin, qT, kn, vT, apart, bias, ctx_o, ctxT_o, lse_o, qa, acc):
    width, rows_here = qT.shape
    heads = bias.shape[0]
    size = width // heads
    qa[...] = jnp.zeros_like(qa)

    @pl.loop(0, rows_here // BQ)
    def _(i):
        q0 = pl.multiple_of(i * BQ, BQ)
        here = pl.ds(q0, BQ)
        for h in range(heads):
            qa[h * LANE : h * LANE + size, :] = qT[h * size : (h + 1) * size, here]
            qa[h * LANE + size : h * LANE + size + 16, :] = apart[:, here]
        acc[...] = jnp.zeros_like(acc)
        low, high = key_range(lengths, first_row + q0, first_row + q0 + BQ - 1)

        def step(j, carry):
            k0 = pl.multiple_of(j * BK, BK)
            row = (j * (BK // LANE) - i * (BQ // LANE) - first_row // LANE + OFF) * LANE
            out = []
            for h in range(heads):
                top, total = carry[2 * h], carry[2 * h + 1]
                own = slice(h * LANE, (h + 1) * LANE)
                rows = slice(h * size, (h + 1) * size)
                s = plain_product(kn[pl.ds(k0, BK), own], qa[own, :]) + bias_part(bias, h, row)
                new_top = jnp.maximum(top, jnp.max(s, axis=0, keepdims=True))
                fade = jnp.exp(top - new_top)
                p = jnp.exp(s - new_top)
                total = total * fade + jnp.sum(p, axis=0, keepdims=True)
                acc[rows, :] = acc[rows, :] * fade + plain_product(
                    vT[rows, pl.ds(k0, BK)], p.astype(low_type)
                )
                out += [new_top, total]
            return tuple(out)

        init = tuple(
            jnp.full((1, BQ), 2.0 * masked_score if n % 2 == 0 else 0.0, jnp.float32)
            for n in range(2 * heads)
        )
        done = lax.fori_loop(low, high, step, init)
        for h in range(heads):
            rows = slice(h * size, (h + 1) * size)
            acc[rows, :] = acc[rows, :] / done[2 * h + 1]
            lse_o[h : h + 1, here] = done[2 * h] + jnp.log(done[2 * h + 1])
        ctxT_o[:, here] = acc[...]
        turned = acc[...].T.astype(low_type)
        for b in range(BQ // LANE):
            at = pl.multiple_of(origin[i * (BQ // LANE) + b], LANE)
            ctx_o[pl.ds(at, LANE), :] = turned[b * LANE : (b + 1) * LANE, :]


def attention_forward(first_row, lengths, origin, qT, kn, vT, apart, bias):
    width, rows_here = qT.shape
    heads = bias.shape[0]

    def body(*refs):
        forward_kernel(first_row, *refs)

    return pl.pallas_call(
        body,
        out_shape=(
            jax.ShapeDtypeStruct((rows_here, width), low_type),
            jax.ShapeDtypeStruct((width, rows_here), jnp.float32),
            jax.ShapeDtypeStruct((heads, rows_here), jnp.float32),
        ),
        in_specs=[smem()] * 2 + [vmem()] * 5,
        out_specs=(vmem(),) * 3,
        scratch_shapes=[
            pltpu.VMEM((heads * LANE, BQ), low_type),
            pltpu.VMEM((width, BQ), jnp.float32),
        ],
        compiler_params=pltpu.CompilerParams(vmem_limit_bytes=VMEM_LIMIT),
        cost_estimate=pl.CostEstimate(
            flops=rows_here * width, bytes_accessed=width * TOK_DEV, transcendentals=0
        ),
        name="attention_forward",
    )(lengths, origin, qT, kn, vT, apart, bias)


def three_parts(values):
    first = values.astype(low_type).astype(jnp.float32)
    rest = values - first
    second = rest.astype(low_type).astype(jnp.float32)
    return first, second, rest - second


def backward_kernel(
    lengths, origin, qT, kn, vn, kT, dcn, ctxT, lse, apart, bias,
    dT_o, dn_o, lines_o, qa, da, dq, dk, dv, tiles,
):
    width, tokens = qT.shape
    heads = bias.shape[0]
    size = width // heads
    for ref in (qa, da, dk, dv, tiles):
        ref[...] = jnp.zeros_like(ref)
    place = lax.broadcasted_iota(jnp.int32, (16, BQ), 0) - SEQS_DEV

    def in_depth(values):
        a, b, c = three_parts(values)
        return jnp.where(place == 0, a, jnp.where(place == 1, b, jnp.where(place == 2, c, 0.0)))

    @pl.loop(0, tokens // BQ)
    def _(i):
        q0 = pl.multiple_of(i * BQ, BQ)
        here = pl.ds(q0, BQ)
        at = [pl.multiple_of(origin[i * (BQ // LANE) + b], LANE) for b in range(BQ // LANE)]
        dcT = jnp.concatenate(
            [dcn[pl.ds(at[b], LANE), :].astype(jnp.float32) for b in range(BQ // LANE)], axis=0
        ).T
        for h in range(heads):
            rows = slice(h * size, (h + 1) * size)
            top = h * LANE
            qa[top : top + size, :] = qT[rows, here]
            extra = apart[:, here].astype(jnp.float32) + in_depth(-lse[h : h + 1, here])
            qa[top + size : top + size + 16, :] = extra.astype(low_type)
            da[top : top + size, :] = dcT[rows, :].astype(low_type)
            delta = jnp.sum(dcT[rows, :] * ctxT[rows, here], axis=0, keepdims=True)
            da[top + size : top + size + 16, :] = in_depth(-delta).astype(low_type)
        dq[...] = jnp.zeros_like(dq)
        low, high = key_range(lengths, q0, q0 + BQ - 1)

        @pl.loop(low, high)
        def _(j):
            k0 = pl.multiple_of(j * BK, BK)
            there = pl.ds(k0, BK)
            row = (j * (BK // LANE) - i * (BQ // LANE) + OFF) * LANE
            for h in range(heads):
                rows = slice(h * size, (h + 1) * size)
                own = slice(h * LANE, (h + 1) * LANE)
                flat = slice(h * LANE, h * LANE + size)
                s = plain_product(kn[there, own], qa[own, :])
                p = jnp.exp(s + bias_part(bias, h, row))
                ds = p * plain_product(vn[there, own], da[own, :])
                for b in range(BQ // LANE):
                    window = pl.ds(pl.multiple_of(row - b * LANE, LANE), BK)
                    tiles[h, window, :] = (
                        tiles[h, window, :] + ds[:, b * LANE : (b + 1) * LANE]
                    )
                p_low = p.astype(low_type)
                ds_low = ds.astype(low_type)
                dv[rows, there] = dv[rows, there] + times_transposed(da[flat, :], p_low)
                dk[rows, there] = dk[rows, there] + times_transposed(qa[flat, :], ds_low)
                dq[rows, :] = dq[rows, :] + plain_product(kT[rows, there], ds_low)

        grad = dq[...] * score_scale
        dT_o[0:width, here] = grad.astype(low_type)
        turned = grad.T.astype(low_type)
        for b in range(BQ // LANE):
            dn_o[pl.ds(at[b], LANE), 0:width] = turned[b * LANE : (b + 1) * LANE, :]

    @pl.loop(0, tokens // BQ)
    def _(i):
        here = pl.ds(pl.multiple_of(i * BQ, BQ), BQ)
        both = jnp.concatenate([dk[:, here], dv[:, here]], axis=0)
        dT_o[width : 3 * width, here] = both.astype(low_type)
        turned = both.T.astype(low_type)
        for b in range(BQ // LANE):
            at = pl.multiple_of(origin[i * (BQ // LANE) + b], LANE)
            dn_o[pl.ds(at, LANE), width : 3 * width] = turned[b * LANE : (b + 1) * LANE, :]

    across = lax.broadcasted_iota(jnp.int32, (LANE, LANE), 1)
    over = across >= lax.broadcasted_iota(jnp.int32, (LANE, LANE), 0)
    sub = lax.broadcasted_iota(jnp.int32, (8, LANE), 0)
    for h in range(heads):
        for d in range(-REACH, REACH + 2):
            here = tiles[h, (d + OFF) * LANE : (d + OFF + 1) * LANE, :]
            below = tiles[h, (d + OFF - 1) * LANE : (d + OFF) * LANE, :]
            mixed = jnp.where(over, here, below)
            line = mixed[LANE - 8 :, :]
            for g in range(LANE // 8 - 2, -1, -1):
                line = mixed[8 * g : 8 * g + 8, :] + pltpu.roll(line, LANE - 8, 1)
            for bit in (1, 2, 4):
                line = jnp.where((sub & bit) != 0, pltpu.roll(line, LANE - bit, 1), line)
            lines_o[h, REACH + 1 - d : REACH + 2 - d, :] = jnp.sum(line, axis=0, keepdims=True)


def attention_backward(lengths, origin, qT, kn, vn, kT, dcn, ctxT, lse, apart, bias):
    width, tokens = qT.shape
    heads = bias.shape[0]
    return pl.pallas_call(
        backward_kernel,
        out_shape=(
            jax.ShapeDtypeStruct((3 * width, tokens), low_type),
            jax.ShapeDtypeStruct((tokens, 3 * width), low_type),
            jax.ShapeDtypeStruct((heads, LINES, LANE), jnp.float32),
        ),
        in_specs=[smem()] * 2 + [vmem()] * 9,
        out_specs=(vmem(),) * 3,
        scratch_shapes=[
            pltpu.VMEM((heads * LANE, BQ), low_type),
            pltpu.VMEM((heads * LANE, BQ), low_type),
            pltpu.VMEM((width, BQ), jnp.float32),
            pltpu.VMEM((width, tokens), jnp.float32),
            pltpu.VMEM((width, tokens), jnp.float32),
            pltpu.VMEM((heads, SPAN * LANE, LANE), jnp.float32),
        ],
        compiler_params=pltpu.CompilerParams(vmem_limit_bytes=VMEM_LIMIT),
        cost_estimate=pl.CostEstimate(
            flops=tokens * width, bytes_accessed=width * TOK_DEV, transcendentals=0
        ),
        name="attention_backward",
    )(lengths, origin, qT, kn, vn, kT, dcn, ctxT, lse, apart, bias)


def feed_forward_backward_kernel(
    grad, rows, hidden, slope, inner, outer, weight_grads, rows_grad
):
    groups, _, size, width = weight_grads.shape

    @pl.when(pl.program_id(0) == 0)
    def _():
        rows_grad[...] = jnp.zeros_like(rows_grad)

    outer_grad = outer_product(hidden[...], grad[...]).astype(low_type)
    weight_grads[:, 0] = outer_grad.reshape(groups, size, width)
    pre = (
        times_transposed(grad[...], outer[...]) * slope[...].astype(jnp.float32)
    ).astype(low_type)
    inner_grad = outer_product(pre, rows[...]).astype(low_type)
    weight_grads[:, 1] = inner_grad.reshape(groups, size, width)
    rows_grad[...] += plain_product(pre, inner[...])


def feed_forward_backward(grad, rows, hidden, slope, inner, outer, size):
    count = grad.shape[0]
    groups = UNIT_BLOCK // size
    every = pl.BlockSpec((count, D), lambda i: (0, 0))
    units = pl.BlockSpec((count, UNIT_BLOCK), lambda i: (0, i))
    weight = pl.BlockSpec((UNIT_BLOCK, D), lambda i: (i, 0))
    return pl.pallas_call(
        feed_forward_backward_kernel,
        grid=(FF // UNIT_BLOCK,),
        out_shape=(
            jax.ShapeDtypeStruct((FF // size, 2, size, D), low_type),
            jax.ShapeDtypeStruct((count, D), jnp.float32),
        ),
        in_specs=[every, every, units, units, weight, weight],
        out_specs=(pl.BlockSpec((groups, 2, size, D), lambda i: (i, 0, 0, 0)), every),
        compiler_params=pltpu.CompilerParams(vmem_limit_bytes=VMEM_LIMIT),
        cost_estimate=pl.CostEstimate(flops=FF * D, bytes_accessed=FF * D, transcendentals=0),
        name="feed_forward_backward",
    )(grad, rows, hidden, slope, inner, outer)


def loss_kernel(place, numbers, parts, proj_weight, gain, out_slope, out_low, out_row, out_gain):
    total_seqs = out_low.shape[0] // 2
    terms = parts.shape[0] // total_seqs
    exact = dict(precision=lax.Precision.HIGHEST, preferred_element_type=jnp.float32)
    seq = lax.broadcasted_iota(jnp.int32, (total_seqs, parts.shape[0]), 0)
    part = lax.broadcasted_iota(jnp.int32, (total_seqs, parts.shape[0]), 1)
    joins = jnp.logical_and(
        seq // SEQS_DEV == part // (SEQS_DEV * terms), seq % SEQS_DEV == part % SEQS_DEV
    )
    unscaled = jnp.dot(joins.astype(jnp.float32), parts[...], **exact)
    pooled_low = (unscaled * gain[...]).astype(low_type)
    projected = times_transposed(pooled_low, proj_weight[...]).astype(low_type).astype(jnp.float32)
    inverse = lax.rsqrt(jnp.sum(projected * projected, axis=1, keepdims=True) + norm_eps)
    embed_low = (projected * inverse).astype(low_type)
    sharpness_factor = jnp.exp(jnp.full((1, 1), numbers[0], jnp.float32))
    agreement = times_transposed(embed_low, embed_low)
    row = lax.broadcasted_iota(jnp.int32, (total_seqs, total_seqs), 0)
    column = lax.broadcasted_iota(jnp.int32, (total_seqs, total_seqs), 1)
    logits = jnp.where(row == column, masked_score, sharpness_factor * agreement)
    partner = (row ^ 1) == column

    def log_sum(axis):
        top = jnp.max(logits, axis=axis, keepdims=True)
        return top + jnp.log(jnp.sum(jnp.exp(logits - top), axis=axis, keepdims=True))

    log_rows = log_sum(1)
    positive = jnp.where(partner, 1.0, 0.0)
    slope = (jnp.exp(logits - log_rows) - positive) / total_seqs
    slope_turned = (jnp.exp(logits - log_sum(0)) - positive) / total_seqs
    embed_grad = sharpness_factor * jnp.dot(
        slope + slope_turned, embed_low.astype(jnp.float32), **exact
    )
    along = jnp.sum(projected * embed_grad, axis=1, keepdims=True)
    proj_grad_low = (
        inverse * embed_grad - projected * inverse * inverse * inverse * along
    ).astype(low_type)
    pooled_grad = plain_product(proj_grad_low, proj_weight[...])
    out_low[0:total_seqs, :] = proj_grad_low
    out_low[total_seqs : 2 * total_seqs, :] = pooled_low
    out_gain[...] = jnp.sum(pooled_grad * unscaled, axis=0, keepdims=True)
    loss = jnp.sum(
        log_rows - jnp.sum(positive * jnp.where(partner, logits, 0.0), axis=1, keepdims=True),
        axis=0,
        keepdims=True,
    ) / total_seqs
    temperature = sharpness_factor * jnp.sum(
        jnp.sum(slope * agreement, axis=1, keepdims=True), axis=0, keepdims=True
    )
    lane = lax.broadcasted_iota(jnp.int32, (1, LANE), 1)
    out_row[...] = jnp.where(lane == 0, loss, jnp.where(lane == 1, temperature, 0.0))
    mine = lax.broadcasted_iota(jnp.int32, (8, total_seqs), 0)
    seq_of = lax.broadcasted_iota(jnp.int32, (8, total_seqs), 1) - place[0] * SEQS_DEV
    picks = jnp.logical_and(mine == seq_of, mine < SEQS_DEV).astype(jnp.float32)
    own = jnp.dot(picks, pooled_grad, **exact)
    index = lax.broadcasted_iota(jnp.int32, (8, 1), 0)
    extent = jnp.ones((8, 1), jnp.float32)
    for s in range(SEQS_DEV):
        extent = jnp.where(index == s, place[1 + s].astype(jnp.float32), extent)
    out_slope[...] = own * gain[...] / extent


def contrastive(place, numbers, parts, proj_weight, gain, total_seqs):
    return pl.pallas_call(
        loss_kernel,
        out_shape=(
            jax.ShapeDtypeStruct((8, D), jnp.float32),
            jax.ShapeDtypeStruct((2 * total_seqs, D), low_type),
            jax.ShapeDtypeStruct((1, LANE), jnp.float32),
            jax.ShapeDtypeStruct((1, D), jnp.float32),
        ),
        in_specs=[smem()] * 2 + [vmem()] * 3,
        out_specs=(vmem(),) * 4,
        compiler_params=pltpu.CompilerParams(vmem_limit_bytes=VMEM_LIMIT),
        cost_estimate=pl.CostEstimate(
            flops=4 * total_seqs * D * D, bytes_accessed=4 * D * D, transcendentals=total_seqs
        ),
        name="contrastive",
    )(place, numbers, parts, proj_weight, gain)


def on_device(
    axes,
    layer_argument,
    document_extents,
    distance_bin_lookup,
    tile_location,
    precise_parameter_blocks,
    precise_mean_est,
    precise_variance_est,
    rescaling_coefficients,
    norm_scale_mean_est,
    norm_scale_variance_est,
    distance_bias_table,
    offset_bias_mean_est,
    offset_bias_variance_est,
    sharpness_exponent,
    sharpness_mean_est,
    sharpness_variance_est,
):
    wide, narrow, far, near = axes
    everyone = wide + narrow
    near_axes = near + narrow
    wide_count = lax.axis_size(wide)
    narrow_count = lax.axis_size(narrow)
    far_count = lax.axis_size(far)
    near_count = wide_count // far_count
    wide_index = lax.axis_index(wide)
    narrow_index = lax.axis_index(narrow)
    bits = narrow_bits(narrow_count)
    order = peer_order(narrow_count)
    place_of = jnp.array([order.index(peer) for peer in range(narrow_count)], jnp.int32)
    unit_rows = precise_parameter_blocks.shape[1]
    heads_here = distance_bias_table.shape[1]
    head_size = unit_rows // heads_here
    ffn_units = FF // D
    group = TOK_DEV // narrow_count
    own_slots = wide_index * CAP + jnp.arange(CAP, dtype=jnp.int32)

    every_slot = lax.all_gather(
        precise_parameter_blocks.astype(low_type), wide, axis=0, tiled=True
    )

    def block(u):
        return lax.dynamic_index_in_dim(every_slot, tile_location[u], 0, keepdims=False)

    qkv_weight = jnp.concatenate([block(u) for u in range(3)], axis=0)

    part_rows = D // wide_count

    def unit_order(first_unit):
        rows = jnp.concatenate([block(first_unit + k) for k in range(ffn_units)], axis=0)
        rows = rows.reshape(far_count, near_count, part_rows, D)
        return jnp.swapaxes(rows, 0, 1).reshape(near_count, far_count * part_rows, D)

    crossing = [block(3), unit_order(5), unit_order(5 + ffn_units)]
    for rows in crossing:
        qkv_weight = after(qkv_weight, rows)
    crossed = [[rows] + [swap(rows, narrow, peer) for peer in bits[1:]] for rows in crossing]

    lengths = document_extents[0]
    seq_ends = jnp.cumsum(lengths)
    positions = jnp.arange(TOK_DEV, dtype=jnp.int32)

    def segments_of(where):
        return jnp.sum((seq_ends[None, :] <= where[:, None]).astype(jnp.int32), axis=1)

    segment_ids = segments_of(positions)
    own_segments = segments_of(narrow_index * group + positions[:group])
    tile_starts = jnp.arange(TOK_DEV // LANE, dtype=jnp.int32) * LANE
    origin = place_of[(tile_starts // group) ^ narrow_index] * group + tile_starts % group

    beyond = LINES * LANE - LANE - 1 - distance_bin_lookup.shape[0]
    offsets_down = jnp.pad(distance_bin_lookup[::-1], (LANE + 1, beyond), constant_values=-1)
    bucket_onehot = (
        offsets_down[:, None] == jnp.arange(BUCKETS, dtype=jnp.int32)[None, :]
    ).astype(jnp.float32)
    rel_values = jnp.dot(bucket_onehot, distance_bias_table, precision=lax.Precision.HIGHEST).T
    tiles_bias = bias_tiles(rel_values.reshape(heads_here, LINES, LANE))

    all_rows = layer_argument.astype(jnp.float32)
    normed_one = (all_rows * rms_scale(all_rows) * rescaling_coefficients[0]).astype(low_type)
    transposed_rows = times_transposed(qkv_weight, normed_one)
    query_cols = (transposed_rows[:unit_rows] * score_scale).astype(low_type)
    key_cols = transposed_rows[unit_rows : 2 * unit_rows].astype(low_type)
    value_cols = transposed_rows[2 * unit_rows :].astype(low_type)
    spread_weight = jnp.pad(
        qkv_weight[unit_rows:].reshape(2 * heads_here, head_size, D),
        ((0, 0), (0, LANE - head_size), (0, 0)),
    ).reshape(2 * heads_here * LANE, D)
    lane_place = jnp.arange(2 * heads_here * LANE, dtype=jnp.int32) % LANE - head_size
    marks = jnp.logical_or(
        lane_place[None, :] == segment_ids[:, None],
        jnp.logical_and(lane_place >= SEQS_DEV, lane_place < SEQS_DEV + 3)[None, :],
    )
    key_value_rows = (
        times_transposed(normed_one, spread_weight) + marks.astype(jnp.float32)
    ).astype(low_type)
    key_rows = key_value_rows[:, : heads_here * LANE]
    value_rows = key_value_rows[:, heads_here * LANE :]
    row_place = jnp.arange(16, dtype=jnp.int32)[:, None]
    apart = jnp.where(
        jnp.logical_and(row_place < SEQS_DEV, row_place != segment_ids[None, :]), masked_score, 0.0
    ).astype(low_type)
    context, context_cols, log_rows = attention_forward(
        0, lengths, origin, query_cols, key_rows, value_cols, apart, tiles_bias
    )

    flat = [rows for pieces in crossed for rows in pieces[1:]]
    context, *flat = lax.optimization_barrier((context, *flat))
    evens = len(bits) - 1
    crossed = [
        [pieces[0]] + flat[n * evens : (n + 1) * evens] for n, pieces in enumerate(crossed)
    ]
    def all_peers(pieces):
        own, *even = pieces
        peers = [(0, own), (1, swap(own, narrow, 1))]
        for bit, rows in zip(bits[1:], even):
            peers += [(bit, rows), (bit + 1, swap(rows, narrow, 1))]
        return peers

    def in_unit_order(pieces):
        whole = jnp.zeros((near_count, narrow_count, far_count * part_rows, D), low_type)
        for peer, rows in all_peers(pieces):
            start = (0, narrow_index ^ peer, 0, 0)
            whole = lax.dynamic_update_slice(whole, rows[:, None], start)
        return whole.reshape(FF, D)

    out_pieces = dict(all_peers(crossed[0]))
    out_joined = jnp.concatenate([out_pieces[peer] for peer in order], axis=0)
    inner_joined = in_unit_order(crossed[1])
    outer_joined = in_unit_order(crossed[2])

    def to_peer(values, peer):
        if peer == 0:
            return values
        return swap(values, narrow, peer)

    context_own = jnp.concatenate(
        [
            to_peer(context[s * group : (s + 1) * group], peer)
            for s, peer in enumerate(order)
        ],
        axis=1,
    )
    own_rows = lax.dynamic_slice_in_dim(layer_argument, narrow_index * group, group, 0).astype(
        jnp.float32
    )
    scale_one = rms_scale(own_rows)
    residual_mid = own_rows + plain_product(context_own, out_joined)
    scale_two = rms_scale(residual_mid)
    normed_two = (residual_mid * scale_two * rescaling_coefficients[1]).astype(low_type)

    proj_weight = natural_rows(
        join_rows(after(block(4), normed_two), narrow), narrow_index, narrow_count
    )

    hidden_low, hidden_slope = gelu_and_slope(times_transposed(normed_two, inner_joined))
    result_own = residual_mid + plain_product(hidden_low, outer_joined)
    result_low = result_own.astype(low_type)
    result_even = [result_low] + [swap(result_low, narrow, peer) for peer in bits[1:]]

    scale_three = rms_scale(result_own)
    member = (
        own_segments[None, :] == jnp.arange(SEQS_DEV, dtype=jnp.int32)[:, None]
    ).astype(jnp.float32)
    length_values = lengths.astype(jnp.float32)[:, None]
    unscaled_part = (
        jnp.dot(member, result_own * scale_three, precision=lax.Precision.HIGHEST) / length_values
    )
    total_seqs = wide_count * SEQS_DEV
    own_pooled_grad, loss_low, loss_row, final_gain_grad = contrastive(
        jnp.concatenate([wide_index.reshape(1), lengths]),
        sharpness_exponent,
        spread(unscaled_part, everyone).reshape(total_seqs * narrow_count, D),
        proj_weight,
        rescaling_coefficients[2:3],
        total_seqs,
    )
    loss = loss_row[0, 0]
    sharpness_total = loss_row[0, 1:2]
    proj_grad_own = lax.dynamic_slice_in_dim(
        loss_low[:total_seqs], narrow_index * unit_rows, unit_rows, 1
    )
    proj_weight_grad = outer_product(proj_grad_own, loss_low[total_seqs:])

    weighted = own_pooled_grad[SEQS_DEV - 1]
    for s in range(SEQS_DEV - 2, -1, -1):
        weighted = jnp.where((own_segments == s)[:, None], own_pooled_grad[s], weighted)
    inner_mean = jnp.mean(weighted * result_own, axis=-1, keepdims=True)
    encoded_grad = scale_three * weighted - result_own * (
        scale_three * scale_three * scale_three * inner_mean
    )
    ffn_grad_low = encoded_grad.astype(low_type)
    group_rows = part_rows if part_rows % 16 == 0 else D
    weight_grads, normed_two_grad = feed_forward_backward(
        ffn_grad_low,
        normed_two,
        hidden_low,
        hidden_slope,
        inner_joined,
        outer_joined,
        group_rows,
    )
    near_part = lax.psum_scatter(
        weight_grads.reshape(2 * FF, D), near_axes, scatter_dimension=0, tiled=True
    )
    mid_norm_grad, ffn_gain_grad = norm_backward(
        residual_mid, scale_two, rescaling_coefficients[1], normed_two_grad
    )
    mid_grad = encoded_grad + mid_norm_grad
    attn_grad_low = mid_grad.astype(low_type)

    context_grad_own = times_transposed(attn_grad_low, out_joined).astype(low_type)
    context_grad = [
        to_peer(context_grad_own[:, s * unit_rows : (s + 1) * unit_rows], peer)
        for s, peer in enumerate(order)
    ]
    attn_grad_low = after(attn_grad_low, context_grad_own)
    out_kept = outer_product(context_own, attn_grad_low).astype(low_type)
    for bit in bits:
        half = out_kept.shape[0] // 2
        out_came = swap(out_kept[half:], narrow, bit)
        if bit == bits[-1]:
            break
        out_kept = sum_low(out_kept[:half], out_came)
    context_grad = after(jnp.concatenate(context_grad, axis=0), out_kept)
    qkv_cols, qkv_rows, bias_lines = attention_backward(
        lengths,
        origin,
        query_cols,
        key_rows,
        value_rows,
        key_cols,
        context_grad,
        context_cols,
        log_rows,
        apart,
        tiles_bias,
    )
    qkv_cols, qkv_rows, out_came = lax.optimization_barrier((qkv_cols, qkv_rows, out_came))
    out_grad = sum_low(out_kept[: out_came.shape[0]], out_came)
    offset_bias_slope = lax.dot_general(
        bucket_onehot,
        bias_lines.reshape(heads_here, LINES * LANE),
        (((0,), (1,)), ((), ())),
        precision=lax.Precision.HIGHEST,
    )

    late = jnp.concatenate(
        [plain_product(qkv_cols, normed_one).astype(low_type), out_grad], axis=0
    ).reshape(far_count, near_count, part_rows, D)
    half = qkv_rows.shape[0] // 2
    rows_sent = plain_product(qkv_rows[half:], qkv_weight).astype(low_type)
    rows_kept = plain_product(qkv_rows[:half], after(qkv_weight, rows_sent))
    near_index = wide_index % near_count
    late_sum = lax.dynamic_index_in_dim(late, near_index, 1, keepdims=False)
    for peer in range(1, near_count):
        sent = lax.dynamic_index_in_dim(late, near_index ^ peer, 1, keepdims=False)
        late_sum = sum_low(late_sum, after(swap(sent, near, peer), rows_kept))
    early = after(near_part, late).reshape(-1, 2, group_rows // part_rows, part_rows, D)
    early = jnp.swapaxes(early, 1, 2).reshape(far_count, 2, part_rows, D)
    terms = jnp.concatenate([early, late_sum[:, None]], axis=1)
    own_part = lax.psum_scatter(
        terms.reshape(far_count * 3 * part_rows, D), far, scatter_dimension=0, tiled=True
    )
    sums = lax.all_gather(own_part, wide, axis=0, tiled=True)
    normed_one_grad = rows_kept + swap(rows_sent, narrow, bits[0]).astype(jnp.float32)
    for bit in bits[1:]:
        half = normed_one_grad.shape[0] // 2
        came = swap(normed_one_grad[half:].astype(low_type), narrow, bit)
        normed_one_grad = normed_one_grad[:half] + came.astype(jnp.float32)
    input_norm_grad, attn_gain_grad = norm_backward(
        own_rows, scale_one, rescaling_coefficients[0], normed_one_grad
    )
    input_own = mid_grad + input_norm_grad
    input_grad = natural_rows(
        join_rows(input_own.astype(low_type), narrow), narrow_index, narrow_count
    ).astype(jnp.float32)

    result_pieces = {}
    for peer, rows in zip([0] + bits[1:], result_even):
        rows = after(rows, qkv_cols)
        result_pieces[peer], result_pieces[peer + 1] = rows, swap(rows, narrow, 1)
    layer_result = natural_rows(
        jnp.concatenate([result_pieces[peer] for peer in order], axis=0),
        narrow_index,
        narrow_count,
    ).astype(jnp.float32)

    bias_size = offset_bias_slope.size
    small = jnp.stack(
        [
            ffn_gain_grad,
            attn_gain_grad,
            jnp.pad(offset_bias_slope.reshape(bias_size), (0, D - bias_size)),
        ]
    )
    small_all = spread(small, everyone).reshape(wide_count, narrow_count, 3, D)
    gain_sums = jnp.sum(small_all[:, :, :2], axis=(0, 1))
    gain_total = jnp.stack([gain_sums[1], gain_sums[0], final_gain_grad[0]])
    bias_all = jnp.sum(small_all[:, :, 2], axis=0)
    bias_total = lax.dynamic_index_in_dim(bias_all, narrow_index, 0, keepdims=False)[
        :bias_size
    ].reshape(offset_bias_slope.shape)
    squares = jnp.sum(jnp.square(own_part.astype(jnp.float32))) + jnp.where(
        tile_location[4] // CAP == wide_index, jnp.sum(jnp.square(proj_weight_grad)), 0.0
    )
    square_terms = spread(jnp.broadcast_to(squares, (8, LANE)), everyone)[:, 0, 0]
    sums, proj_weight_grad, square_terms, *_ = lax.optimization_barrier(
        (sums, proj_weight_grad, square_terms, input_grad, layer_result, gain_total, bias_total)
    )
    sums = sums.reshape(ffn_units, wide_count // ffn_units, 3, part_rows, D)
    slot_grads = []
    for slot in range(CAP):
        here = tile_location == own_slots[slot]
        unit = jnp.sum(jnp.where(here, jnp.arange(here.shape[0], dtype=jnp.int32), 0))
        row = jnp.where(unit >= 5, (unit - 5) % ffn_units, jnp.minimum(unit, ffn_units - 1))
        column = jnp.where(unit >= 5, 1 - (unit - 5) // ffn_units, 2)
        low_sum = lax.dynamic_slice(
            sums, (row, 0, column, 0, 0), (1, wide_count // ffn_units, 1, part_rows, D)
        ).reshape(unit_rows, D)
        low_sum = jnp.where(unit == 4, proj_weight_grad, low_sum.astype(jnp.float32))
        slot_grads.append(jnp.where(jnp.any(here), low_sum, 0.0))
    slot_grads = jnp.stack(slot_grads)
    grad_norm = jnp.sqrt(
        jnp.sum(square_terms)
        + jnp.sum(gain_total * gain_total)
        + jnp.sum(bias_all * bias_all)
        + jnp.sum(sharpness_total * sharpness_total)
    )
    multiplier = jnp.minimum(1.0, clip_limit / grad_norm)
    slot_first, slot_second, slot_weight = decoupled_decay_step(
        slot_grads,
        precise_mean_est,
        precise_variance_est,
        precise_parameter_blocks,
        multiplier,
        learn_rate,
    )
    gain_first, gain_second, gain_new = decoupled_decay_step(
        gain_total,
        norm_scale_mean_est,
        norm_scale_variance_est,
        rescaling_coefficients,
        multiplier,
        side_rate,
    )
    bias_first, bias_second, bias_new = decoupled_decay_step(
        bias_total,
        offset_bias_mean_est,
        offset_bias_variance_est,
        distance_bias_table,
        multiplier,
        side_rate,
    )
    sharpness_mean_fresh, sharpness_variance_fresh, sharpness_exponent_fresh = decoupled_decay_step(
        sharpness_total,
        sharpness_mean_est,
        sharpness_variance_est,
        sharpness_exponent,
        multiplier,
        learn_rate,
    )
    return (
        loss,
        layer_result,
        input_grad,
        grad_norm,
        slot_first,
        slot_second,
        slot_weight,
        gain_first,
        gain_second,
        gain_new,
        bias_first,
        bias_second,
        bias_new,
        sharpness_mean_fresh,
        sharpness_variance_fresh,
        sharpness_exponent_fresh,
    )


def solution(mesh):
    wide, narrow, far, near = ("wide",), ("narrow",), ("wide",), ()
    if dict(mesh.shape) == {"wide": 8, "narrow": 4}:
        mesh = Mesh(mesh.devices.reshape(4, 2, 2, 2), ("line", "pair", "side", "core"))
        wide, narrow, far, near = ("line", "pair"), ("side", "core"), ("line",), ("pair",)
    whole, rows, blocks, heads = P(), P(wide, None), P(wide, narrow, None), P(None, narrow)
    arguments = (rows, rows, whole, whole, blocks, blocks, blocks, whole, whole, whole)
    arguments += (heads, heads, heads, whole, whole, whole)
    results = (whole, rows, rows, whole, blocks, blocks, blocks, whole, whole, whole)
    results += (heads, heads, heads, whole, whole, whole)

    def body(*arrays):
        return on_device((wide, narrow, far, near), *arrays)

    return jax.shard_map(
        body, mesh=mesh, in_specs=arguments, out_specs=results, check_vma=False
    )
```

```python
import jax
import jax.numpy as jnp
from jax import lax
from jax.experimental import pallas as pl
from jax.experimental.pallas import tpu as pltpu
from jax.sharding import Mesh
from jax.sharding import PartitionSpec as P

D = 768
FF = 3072
BUCKETS = 32
TOK_DEV = 2560
SEQS_DEV = 4
DOCLEN = 1024
CAP = 2
STEP = 10
LANE = 128
BQ = 512
BK = 512
UNIT_BLOCK = 768
REACH = DOCLEN // LANE
OFF = REACH + (BQ + BK) // LANE
SPAN = 2 * OFF + 1
LINES = 2 * REACH + 2
VMEM_LIMIT = 56 * 1024 * 1024

norm_eps = 1e-06
clip_limit = 0.01
learn_rate = 0.01
side_rate = 0.5
beta_one = 0.5
beta_two = 0.5
adam_eps = 1e-08
decay_rate = 0.01
score_scale = 0.125
masked_score = -1e30
low_type = jnp.bfloat16


def times_transposed(left_side, right_side):
    return lax.dot_general(
        left_side, right_side, (((1,), (1,)), ((), ())), preferred_element_type=jnp.float32
    )


def plain_product(left_side, right_side):
    return jnp.dot(left_side, right_side, preferred_element_type=jnp.float32)


def outer_product(left_side, right_side):
    return lax.dot_general(
        left_side, right_side, (((0,), (0,)), ((), ())), preferred_element_type=jnp.float32
    )


def rms_scale(values):
    return lax.rsqrt(jnp.mean(values * values, axis=-1, keepdims=True) + norm_eps)


def norm_backward(values, row_scale, gain_row, grad_out):
    weighted = grad_out * gain_row
    gain_grad = jnp.sum(grad_out * values * row_scale, axis=0)
    inner_mean = jnp.mean(weighted * values, axis=-1, keepdims=True)
    value_grad = row_scale * weighted - values * row_scale * row_scale * row_scale * inner_mean
    return (value_grad, gain_grad)


def decoupled_decay_step(gradient, first_moment, second_moment, weight, multiplier, step_rate):
    clipped = gradient * multiplier
    first_new = beta_one * first_moment + (1.0 - beta_one) * clipped
    second_new = beta_two * second_moment + (1.0 - beta_two) * clipped * clipped
    first_hat = first_new / (1.0 - beta_one**STEP)
    second_hat = second_new / (1.0 - beta_two**STEP)
    weight_new = weight - step_rate * (
        first_hat / (jnp.sqrt(second_hat) + adam_eps) + decay_rate * weight
    )
    return (first_new, second_new, weight_new)


def swap(values, axes, bit):
    count = lax.axis_size(axes)
    return lax.ppermute(values, axes, [(i, i ^ bit) for i in range(count)])


def sum_low(left, right):
    return (left.astype(jnp.float32) + right.astype(jnp.float32)).astype(low_type)


def narrow_bits(count):
    return [1 << s for s in range(count.bit_length() - 1)]


def peer_order(count):
    order = [0]
    for bit in reversed(narrow_bits(count)):
        order = order + [peer ^ bit for peer in order]
    return order


def join_rows(values, axes):
    for bit in reversed(narrow_bits(lax.axis_size(axes))):
        values = jnp.concatenate([values, swap(values, axes, bit)], axis=0)
    return values


def add_rows(values, axes):
    for bit in narrow_bits(lax.axis_size(axes)):
        half = values.shape[0] // 2
        came = swap(values[half:].astype(low_type), axes, bit)
        values = values[:half].astype(jnp.float32) + came.astype(jnp.float32)
    return values


def product_add_rows(left_side, right_side, axes):
    bits = narrow_bits(lax.axis_size(axes))
    half = left_side.shape[0] // 2
    sent = plain_product(left_side[half:], right_side).astype(low_type)
    came = swap(sent, axes, bits[0])
    values = plain_product(left_side[:half], right_side) + came.astype(jnp.float32)
    for bit in bits[1:]:
        half = values.shape[0] // 2
        came = swap(values[half:].astype(low_type), axes, bit)
        values = values[:half] + came.astype(jnp.float32)
    return values


def natural_rows(joined, index, count):
    order = peer_order(count)
    group = joined.shape[0] // count
    place = jnp.array([order.index(peer) for peer in range(count)], jnp.int32)
    return jnp.concatenate(
        [
            lax.dynamic_slice_in_dim(joined, place[g ^ index] * group, group, 0)
            for g in range(count)
        ],
        axis=0,
    )


def spread(values, axes):
    copies = jnp.broadcast_to(values[None], (lax.axis_size(axes),) + values.shape)
    return lax.all_to_all(copies, axes, split_axis=0, concat_axis=0, tiled=True)


def after(values, other):
    return lax.optimization_barrier((values, other))[0]


def gelu_and_slope(values):
    rate = 0.7978845608028654
    cubic = 0.044715
    squares = values * values
    turn = jnp.tanh(rate * values * (1.0 + cubic * squares))
    half = 0.5 * (1.0 + turn)
    slope = half + 0.5 * values * (1.0 - turn * turn) * (rate * (1.0 + 3.0 * cubic * squares))
    return (values * half).astype(low_type), slope.astype(low_type)


def smem():
    return pl.BlockSpec(memory_space=pltpu.SMEM)


def vmem():
    return pl.BlockSpec(memory_space=pltpu.VMEM)


def bias_kernel(chunks, tiles):
    heads = tiles.shape[0]
    tiles[...] = jnp.zeros_like(tiles)
    for h in range(heads):
        for d in range(-REACH, REACH + 1):
            left = chunks[h, REACH + 1 - d : REACH + 2 - d, :]
            right = chunks[h, REACH - d : REACH + 1 - d, :]
            line = jnp.broadcast_to(jnp.concatenate([left, right], axis=1), (LANE, 2 * LANE))
            rolled = pltpu.roll(line, 0, 1, stride=1, stride_axis=0)
            tiles[h, (d + OFF) * LANE : (d + OFF + 1) * LANE, :] = rolled[:, :LANE]


def bias_tiles(rel_chunks):
    heads = rel_chunks.shape[0]
    return pl.pallas_call(
        bias_kernel,
        out_shape=jax.ShapeDtypeStruct((heads, SPAN * LANE, LANE), jnp.float32),
        compiler_params=pltpu.CompilerParams(vmem_limit_bytes=VMEM_LIMIT),
        name="bias_tiles",
    )(rel_chunks)


def key_range(lengths, first, last):
    start = jnp.int32(0)
    low = jnp.int32(0)
    high = jnp.int32(0)
    for s in range(SEQS_DEV):
        end = start + lengths[s]
        low = jnp.where(start <= first, start, low)
        high = jnp.where(start <= last, end, high)
        start = end
    return low // BK, (high + BK - 1) // BK


def bias_part(bias, h, row):
    return jnp.concatenate(
        [
            bias[h, pl.ds(pl.multiple_of(row - b * LANE, LANE), BK), :]
            for b in range(BQ // LANE)
        ],
        axis=1,
    )


def forward_kernel(first_row, lengths, origin, qT, kn, vT, apart, bias, ctx_o, ctxT_o, lse_o, qa, acc):
    width, rows_here = qT.shape
    heads = bias.shape[0]
    size = width // heads
    qa[...] = jnp.zeros_like(qa)

    @pl.loop(0, rows_here // BQ)
    def _(i):
        q0 = pl.multiple_of(i * BQ, BQ)
        here = pl.ds(q0, BQ)
        for h in range(heads):
            qa[h * LANE : h * LANE + size, :] = qT[h * size : (h + 1) * size, here]
            qa[h * LANE + size : h * LANE + size + 16, :] = apart[:, here]
        acc[...] = jnp.zeros_like(acc)
        low, high = key_range(lengths, first_row + q0, first_row + q0 + BQ - 1)

        def step(j, carry):
            k0 = pl.multiple_of(j * BK, BK)
            row = (j * (BK // LANE) - i * (BQ // LANE) - first_row // LANE + OFF) * LANE
            out = []
            for h in range(heads):
                top, total = carry[2 * h], carry[2 * h + 1]
                own = slice(h * LANE, (h + 1) * LANE)
                rows = slice(h * size, (h + 1) * size)
                s = plain_product(kn[pl.ds(k0, BK), own], qa[own, :]) + bias_part(bias, h, row)
                new_top = jnp.maximum(top, jnp.max(s, axis=0, keepdims=True))
                fade = jnp.exp(top - new_top)
                p = jnp.exp(s - new_top)
                total = total * fade + jnp.sum(p, axis=0, keepdims=True)
                acc[rows, :] = acc[rows, :] * fade + plain_product(
                    vT[rows, pl.ds(k0, BK)], p.astype(low_type)
                )
                out += [new_top, total]
            return tuple(out)

        init = tuple(
            jnp.full((1, BQ), 2.0 * masked_score if n % 2 == 0 else 0.0, jnp.float32)
            for n in range(2 * heads)
        )
        done = lax.fori_loop(low, high, step, init)
        for h in range(heads):
            rows = slice(h * size, (h + 1) * size)
            acc[rows, :] = acc[rows, :] / done[2 * h + 1]
            lse_o[h : h + 1, here] = done[2 * h] + jnp.log(done[2 * h + 1])
        ctxT_o[:, here] = acc[...]
        turned = acc[...].T.astype(low_type)
        for b in range(BQ // LANE):
            at = pl.multiple_of(origin[i * (BQ // LANE) + b], LANE)
            ctx_o[pl.ds(at, LANE), :] = turned[b * LANE : (b + 1) * LANE, :]


def attention_forward(first_row, lengths, origin, qT, kn, vT, apart, bias):
    width, rows_here = qT.shape
    heads = bias.shape[0]

    def body(*refs):
        forward_kernel(first_row, *refs)

    return pl.pallas_call(
        body,
        out_shape=(
            jax.ShapeDtypeStruct((rows_here, width), low_type),
            jax.ShapeDtypeStruct((width, rows_here), jnp.float32),
            jax.ShapeDtypeStruct((heads, rows_here), jnp.float32),
        ),
        in_specs=[smem()] * 2 + [vmem()] * 5,
        out_specs=(vmem(),) * 3,
        scratch_shapes=[
            pltpu.VMEM((heads * LANE, BQ), low_type),
            pltpu.VMEM((width, BQ), jnp.float32),
        ],
        compiler_params=pltpu.CompilerParams(vmem_limit_bytes=VMEM_LIMIT),
        cost_estimate=pl.CostEstimate(
            flops=rows_here * width, bytes_accessed=width * TOK_DEV, transcendentals=0
        ),
        name="attention_forward",
    )(lengths, origin, qT, kn, vT, apart, bias)


def three_parts(values):
    first = values.astype(low_type).astype(jnp.float32)
    rest = values - first
    second = rest.astype(low_type).astype(jnp.float32)
    return first, second, rest - second


def backward_kernel(
    lengths, origin, qT, kn, vn, kT, dcn, ctxT, lse, apart, bias,
    dT_o, dn_o, lines_o, qa, da, dq, dk, dv, tiles,
):
    width, tokens = qT.shape
    heads = bias.shape[0]
    size = width // heads
    for ref in (qa, da, dk, dv, tiles):
        ref[...] = jnp.zeros_like(ref)
    place = lax.broadcasted_iota(jnp.int32, (16, BQ), 0) - SEQS_DEV

    def in_depth(values):
        a, b, c = three_parts(values)
        return jnp.where(place == 0, a, jnp.where(place == 1, b, jnp.where(place == 2, c, 0.0)))

    @pl.loop(0, tokens // BQ)
    def _(i):
        q0 = pl.multiple_of(i * BQ, BQ)
        here = pl.ds(q0, BQ)
        at = [pl.multiple_of(origin[i * (BQ // LANE) + b], LANE) for b in range(BQ // LANE)]
        dcT = jnp.concatenate(
            [dcn[pl.ds(at[b], LANE), :].astype(jnp.float32) for b in range(BQ // LANE)], axis=0
        ).T
        for h in range(heads):
            rows = slice(h * size, (h + 1) * size)
            top = h * LANE
            qa[top : top + size, :] = qT[rows, here]
            extra = apart[:, here].astype(jnp.float32) + in_depth(-lse[h : h + 1, here])
            qa[top + size : top + size + 16, :] = extra.astype(low_type)
            da[top : top + size, :] = dcT[rows, :].astype(low_type)
            delta = jnp.sum(dcT[rows, :] * ctxT[rows, here], axis=0, keepdims=True)
            da[top + size : top + size + 16, :] = in_depth(-delta).astype(low_type)
        dq[...] = jnp.zeros_like(dq)
        low, high = key_range(lengths, q0, q0 + BQ - 1)

        @pl.loop(low, high)
        def _(j):
            k0 = pl.multiple_of(j * BK, BK)
            there = pl.ds(k0, BK)
            row = (j * (BK // LANE) - i * (BQ // LANE) + OFF) * LANE
            for h in range(heads):
                rows = slice(h * size, (h + 1) * size)
                own = slice(h * LANE, (h + 1) * LANE)
                flat = slice(h * LANE, h * LANE + size)
                s = plain_product(kn[there, own], qa[own, :])
                p = jnp.exp(s + bias_part(bias, h, row))
                ds = p * plain_product(vn[there, own], da[own, :])
                for b in range(BQ // LANE):
                    window = pl.ds(pl.multiple_of(row - b * LANE, LANE), BK)
                    tiles[h, window, :] = (
                        tiles[h, window, :] + ds[:, b * LANE : (b + 1) * LANE]
                    )
                p_low = p.astype(low_type)
                ds_low = ds.astype(low_type)
                dv[rows, there] = dv[rows, there] + times_transposed(da[flat, :], p_low)
                dk[rows, there] = dk[rows, there] + times_transposed(qa[flat, :], ds_low)
                dq[rows, :] = dq[rows, :] + plain_product(kT[rows, there], ds_low)

        grad = dq[...] * score_scale
        dT_o[0:width, here] = grad.astype(low_type)
        turned = grad.T.astype(low_type)
        for b in range(BQ // LANE):
            dn_o[pl.ds(at[b], LANE), 0:width] = turned[b * LANE : (b + 1) * LANE, :]

    @pl.loop(0, tokens // BQ)
    def _(i):
        here = pl.ds(pl.multiple_of(i * BQ, BQ), BQ)
        both = jnp.concatenate([dk[:, here], dv[:, here]], axis=0)
        dT_o[width : 3 * width, here] = both.astype(low_type)
        turned = both.T.astype(low_type)
        for b in range(BQ // LANE):
            at = pl.multiple_of(origin[i * (BQ // LANE) + b], LANE)
            dn_o[pl.ds(at, LANE), width : 3 * width] = turned[b * LANE : (b + 1) * LANE, :]

    across = lax.broadcasted_iota(jnp.int32, (LANE, LANE), 1)
    over = across >= lax.broadcasted_iota(jnp.int32, (LANE, LANE), 0)
    sub = lax.broadcasted_iota(jnp.int32, (8, LANE), 0)
    for h in range(heads):
        for d in range(-REACH, REACH + 2):
            here = tiles[h, (d + OFF) * LANE : (d + OFF + 1) * LANE, :]
            below = tiles[h, (d + OFF - 1) * LANE : (d + OFF) * LANE, :]
            mixed = jnp.where(over, here, below)
            line = mixed[LANE - 8 :, :]
            for g in range(LANE // 8 - 2, -1, -1):
                line = mixed[8 * g : 8 * g + 8, :] + pltpu.roll(line, LANE - 8, 1)
            for bit in (1, 2, 4):
                line = jnp.where((sub & bit) != 0, pltpu.roll(line, LANE - bit, 1), line)
            lines_o[h, REACH + 1 - d : REACH + 2 - d, :] = jnp.sum(line, axis=0, keepdims=True)


def attention_backward(lengths, origin, qT, kn, vn, kT, dcn, ctxT, lse, apart, bias):
    width, tokens = qT.shape
    heads = bias.shape[0]
    return pl.pallas_call(
        backward_kernel,
        out_shape=(
            jax.ShapeDtypeStruct((3 * width, tokens), low_type),
            jax.ShapeDtypeStruct((tokens, 3 * width), low_type),
            jax.ShapeDtypeStruct((heads, LINES, LANE), jnp.float32),
        ),
        in_specs=[smem()] * 2 + [vmem()] * 9,
        out_specs=(vmem(),) * 3,
        scratch_shapes=[
            pltpu.VMEM((heads * LANE, BQ), low_type),
            pltpu.VMEM((heads * LANE, BQ), low_type),
            pltpu.VMEM((width, BQ), jnp.float32),
            pltpu.VMEM((width, tokens), jnp.float32),
            pltpu.VMEM((width, tokens), jnp.float32),
            pltpu.VMEM((heads, SPAN * LANE, LANE), jnp.float32),
        ],
        compiler_params=pltpu.CompilerParams(vmem_limit_bytes=VMEM_LIMIT),
        cost_estimate=pl.CostEstimate(
            flops=tokens * width, bytes_accessed=width * TOK_DEV, transcendentals=0
        ),
        name="attention_backward",
    )(lengths, origin, qT, kn, vn, kT, dcn, ctxT, lse, apart, bias)


def feed_forward_backward_kernel(
    grad, rows, hidden, slope, inner, outer, weight_grads, rows_grad
):
    groups, _, size, width = weight_grads.shape

    @pl.when(pl.program_id(0) == 0)
    def _():
        rows_grad[...] = jnp.zeros_like(rows_grad)

    outer_grad = outer_product(hidden[...], grad[...]).astype(low_type)
    weight_grads[:, 0] = outer_grad.reshape(groups, size, width)
    pre = (
        times_transposed(grad[...], outer[...]) * slope[...].astype(jnp.float32)
    ).astype(low_type)
    inner_grad = outer_product(pre, rows[...]).astype(low_type)
    weight_grads[:, 1] = inner_grad.reshape(groups, size, width)
    rows_grad[...] += plain_product(pre, inner[...])


def feed_forward_backward(grad, rows, hidden, slope, inner, outer, size):
    count = grad.shape[0]
    groups = UNIT_BLOCK // size
    every = pl.BlockSpec((count, D), lambda i: (0, 0))
    units = pl.BlockSpec((count, UNIT_BLOCK), lambda i: (0, i))
    weight = pl.BlockSpec((UNIT_BLOCK, D), lambda i: (i, 0))
    return pl.pallas_call(
        feed_forward_backward_kernel,
        grid=(FF // UNIT_BLOCK,),
        out_shape=(
            jax.ShapeDtypeStruct((FF // size, 2, size, D), low_type),
            jax.ShapeDtypeStruct((count, D), jnp.float32),
        ),
        in_specs=[every, every, units, units, weight, weight],
        out_specs=(pl.BlockSpec((groups, 2, size, D), lambda i: (i, 0, 0, 0)), every),
        compiler_params=pltpu.CompilerParams(vmem_limit_bytes=VMEM_LIMIT),
        cost_estimate=pl.CostEstimate(flops=FF * D, bytes_accessed=FF * D, transcendentals=0),
        name="feed_forward_backward",
    )(grad, rows, hidden, slope, inner, outer)


def loss_kernel(place, numbers, parts, proj_weight, gain, out_slope, out_low, out_row, out_gain):
    total_seqs = out_low.shape[0] // 2
    terms = parts.shape[0] // total_seqs
    exact = dict(precision=lax.Precision.HIGHEST, preferred_element_type=jnp.float32)
    seq = lax.broadcasted_iota(jnp.int32, (total_seqs, parts.shape[0]), 0)
    part = lax.broadcasted_iota(jnp.int32, (total_seqs, parts.shape[0]), 1)
    joins = jnp.logical_and(
        seq // SEQS_DEV == part // (SEQS_DEV * terms), seq % SEQS_DEV == part % SEQS_DEV
    )
    unscaled = jnp.dot(joins.astype(jnp.float32), parts[...], **exact)
    pooled_low = (unscaled * gain[...]).astype(low_type)
    projected = times_transposed(pooled_low, proj_weight[...]).astype(low_type).astype(jnp.float32)
    inverse = lax.rsqrt(jnp.sum(projected * projected, axis=1, keepdims=True) + norm_eps)
    embed_low = (projected * inverse).astype(low_type)
    sharpness_factor = jnp.exp(jnp.full((1, 1), numbers[0], jnp.float32))
    agreement = times_transposed(embed_low, embed_low)
    row = lax.broadcasted_iota(jnp.int32, (total_seqs, total_seqs), 0)
    column = lax.broadcasted_iota(jnp.int32, (total_seqs, total_seqs), 1)
    logits = jnp.where(row == column, masked_score, sharpness_factor * agreement)
    partner = (row ^ 1) == column

    def log_sum(axis):
        top = jnp.max(logits, axis=axis, keepdims=True)
        return top + jnp.log(jnp.sum(jnp.exp(logits - top), axis=axis, keepdims=True))

    log_rows = log_sum(1)
    positive = jnp.where(partner, 1.0, 0.0)
    slope = (jnp.exp(logits - log_rows) - positive) / total_seqs
    slope_turned = (jnp.exp(logits - log_sum(0)) - positive) / total_seqs
    embed_grad = sharpness_factor * jnp.dot(
        slope + slope_turned, embed_low.astype(jnp.float32), **exact
    )
    along = jnp.sum(projected * embed_grad, axis=1, keepdims=True)
    proj_grad_low = (
        inverse * embed_grad - projected * inverse * inverse * inverse * along
    ).astype(low_type)
    pooled_grad = plain_product(proj_grad_low, proj_weight[...])
    out_low[0:total_seqs, :] = proj_grad_low
    out_low[total_seqs : 2 * total_seqs, :] = pooled_low
    out_gain[...] = jnp.sum(pooled_grad * unscaled, axis=0, keepdims=True)
    loss = jnp.sum(
        log_rows - jnp.sum(positive * jnp.where(partner, logits, 0.0), axis=1, keepdims=True),
        axis=0,
        keepdims=True,
    ) / total_seqs
    temperature = sharpness_factor * jnp.sum(
        jnp.sum(slope * agreement, axis=1, keepdims=True), axis=0, keepdims=True
    )
    lane = lax.broadcasted_iota(jnp.int32, (1, LANE), 1)
    out_row[...] = jnp.where(lane == 0, loss, jnp.where(lane == 1, temperature, 0.0))
    mine = lax.broadcasted_iota(jnp.int32, (8, total_seqs), 0)
    seq_of = lax.broadcasted_iota(jnp.int32, (8, total_seqs), 1) - place[0] * SEQS_DEV
    picks = jnp.logical_and(mine == seq_of, mine < SEQS_DEV).astype(jnp.float32)
    own = jnp.dot(picks, pooled_grad, **exact)
    index = lax.broadcasted_iota(jnp.int32, (8, 1), 0)
    extent = jnp.ones((8, 1), jnp.float32)
    for s in range(SEQS_DEV):
        extent = jnp.where(index == s, place[1 + s].astype(jnp.float32), extent)
    out_slope[...] = own * gain[...] / extent


def contrastive(place, numbers, parts, proj_weight, gain, total_seqs):
    return pl.pallas_call(
        loss_kernel,
        out_shape=(
            jax.ShapeDtypeStruct((8, D), jnp.float32),
            jax.ShapeDtypeStruct((2 * total_seqs, D), low_type),
            jax.ShapeDtypeStruct((1, LANE), jnp.float32),
            jax.ShapeDtypeStruct((1, D), jnp.float32),
        ),
        in_specs=[smem()] * 2 + [vmem()] * 3,
        out_specs=(vmem(),) * 4,
        compiler_params=pltpu.CompilerParams(vmem_limit_bytes=VMEM_LIMIT),
        cost_estimate=pl.CostEstimate(
            flops=4 * total_seqs * D * D, bytes_accessed=4 * D * D, transcendentals=total_seqs
        ),
        name="contrastive",
    )(place, numbers, parts, proj_weight, gain)


def on_device(
    axes,
    layer_argument,
    document_extents,
    distance_bin_lookup,
    tile_location,
    precise_parameter_blocks,
    precise_mean_est,
    precise_variance_est,
    rescaling_coefficients,
    norm_scale_mean_est,
    norm_scale_variance_est,
    distance_bias_table,
    offset_bias_mean_est,
    offset_bias_variance_est,
    sharpness_exponent,
    sharpness_mean_est,
    sharpness_variance_est,
):
    wide, narrow, far, near = axes
    everyone = wide + narrow
    near_axes = near + narrow
    wide_count = lax.axis_size(wide)
    narrow_count = lax.axis_size(narrow)
    far_count = lax.axis_size(far)
    near_count = wide_count // far_count
    wide_index = lax.axis_index(wide)
    narrow_index = lax.axis_index(narrow)
    bits = narrow_bits(narrow_count)
    order = peer_order(narrow_count)
    place_of = jnp.array([order.index(peer) for peer in range(narrow_count)], jnp.int32)
    unit_rows = precise_parameter_blocks.shape[1]
    heads_here = distance_bias_table.shape[1]
    head_size = unit_rows // heads_here
    ffn_units = FF // D
    group = TOK_DEV // narrow_count
    own_slots = wide_index * CAP + jnp.arange(CAP, dtype=jnp.int32)

    every_slot = lax.all_gather(
        precise_parameter_blocks.astype(low_type), wide, axis=0, tiled=True
    )

    def block(u):
        return lax.dynamic_index_in_dim(every_slot, tile_location[u], 0, keepdims=False)

    qkv_weight = jnp.concatenate([block(u) for u in range(3)], axis=0)

    part_rows = D // wide_count

    def unit_order(first_unit):
        rows = jnp.concatenate([block(first_unit + k) for k in range(ffn_units)], axis=0)
        rows = rows.reshape(far_count, near_count, part_rows, D)
        return jnp.swapaxes(rows, 0, 1).reshape(near_count, far_count * part_rows, D)

    crossing = [block(3), unit_order(5), unit_order(5 + ffn_units)]
    for rows in crossing:
        qkv_weight = after(qkv_weight, rows)
    crossed = [[rows] + [swap(rows, narrow, peer) for peer in bits[1:]] for rows in crossing]

    lengths = document_extents[0]
    seq_ends = jnp.cumsum(lengths)
    positions = jnp.arange(TOK_DEV, dtype=jnp.int32)

    def segments_of(where):
        return jnp.sum((seq_ends[None, :] <= where[:, None]).astype(jnp.int32), axis=1)

    segment_ids = segments_of(positions)
    own_segments = segments_of(narrow_index * group + positions[:group])
    tile_starts = jnp.arange(TOK_DEV // LANE, dtype=jnp.int32) * LANE
    origin = place_of[(tile_starts // group) ^ narrow_index] * group + tile_starts % group

    beyond = LINES * LANE - LANE - 1 - distance_bin_lookup.shape[0]
    offsets_down = jnp.pad(distance_bin_lookup[::-1], (LANE + 1, beyond), constant_values=-1)
    bucket_onehot = (
        offsets_down[:, None] == jnp.arange(BUCKETS, dtype=jnp.int32)[None, :]
    ).astype(jnp.float32)
    rel_values = jnp.dot(bucket_onehot, distance_bias_table, precision=lax.Precision.HIGHEST).T
    tiles_bias = bias_tiles(rel_values.reshape(heads_here, LINES, LANE))

    all_rows = layer_argument.astype(jnp.float32)
    normed_one = (all_rows * rms_scale(all_rows) * rescaling_coefficients[0]).astype(low_type)
    transposed_rows = times_transposed(qkv_weight, normed_one)
    query_cols = (transposed_rows[:unit_rows] * score_scale).astype(low_type)
    key_cols = transposed_rows[unit_rows : 2 * unit_rows].astype(low_type)
    value_cols = transposed_rows[2 * unit_rows :].astype(low_type)
    spread_weight = jnp.pad(
        qkv_weight[unit_rows:].reshape(2 * heads_here, head_size, D),
        ((0, 0), (0, LANE - head_size), (0, 0)),
    ).reshape(2 * heads_here * LANE, D)
    lane_place = jnp.arange(2 * heads_here * LANE, dtype=jnp.int32) % LANE - head_size
    marks = jnp.logical_or(
        lane_place[None, :] == segment_ids[:, None],
        jnp.logical_and(lane_place >= SEQS_DEV, lane_place < SEQS_DEV + 3)[None, :],
    )
    key_value_rows = (
        times_transposed(normed_one, spread_weight) + marks.astype(jnp.float32)
    ).astype(low_type)
    key_rows = key_value_rows[:, : heads_here * LANE]
    value_rows = key_value_rows[:, heads_here * LANE :]
    row_place = jnp.arange(16, dtype=jnp.int32)[:, None]
    apart = jnp.where(
        jnp.logical_and(row_place < SEQS_DEV, row_place != segment_ids[None, :]), masked_score, 0.0
    ).astype(low_type)
    context, context_cols, log_rows = attention_forward(
        0, lengths, origin, query_cols, key_rows, value_cols, apart, tiles_bias
    )

    flat = [rows for pieces in crossed for rows in pieces[1:]]
    context, *flat = lax.optimization_barrier((context, *flat))
    evens = len(bits) - 1
    crossed = [
        [pieces[0]] + flat[n * evens : (n + 1) * evens] for n, pieces in enumerate(crossed)
    ]
    def all_peers(pieces):
        own, *even = pieces
        peers = [(0, own), (1, swap(own, narrow, 1))]
        for bit, rows in zip(bits[1:], even):
            peers += [(bit, rows), (bit + 1, swap(rows, narrow, 1))]
        return peers

    def in_unit_order(pieces):
        whole = jnp.zeros((near_count, narrow_count, far_count * part_rows, D), low_type)
        for peer, rows in all_peers(pieces):
            start = (0, narrow_index ^ peer, 0, 0)
            whole = lax.dynamic_update_slice(whole, rows[:, None], start)
        return whole.reshape(FF, D)

    out_pieces = dict(all_peers(crossed[0]))
    out_joined = jnp.concatenate([out_pieces[peer] for peer in order], axis=0)
    inner_joined = in_unit_order(crossed[1])
    outer_joined = in_unit_order(crossed[2])

    def to_peer(values, peer):
        if peer == 0:
            return values
        return swap(values, narrow, peer)

    context_own = jnp.concatenate(
        [
            to_peer(context[s * group : (s + 1) * group], peer)
            for s, peer in enumerate(order)
        ],
        axis=1,
    )
    own_rows = lax.dynamic_slice_in_dim(layer_argument, narrow_index * group, group, 0).astype(
        jnp.float32
    )
    scale_one = rms_scale(own_rows)
    residual_mid = own_rows + plain_product(context_own, out_joined)
    scale_two = rms_scale(residual_mid)
    normed_two = (residual_mid * scale_two * rescaling_coefficients[1]).astype(low_type)

    hidden_low, hidden_slope = gelu_and_slope(times_transposed(normed_two, inner_joined))
    proj_rows = after(block(4), normed_two)
    for bit in reversed(bits):
        came = after(swap(proj_rows, narrow, bit), hidden_low)
        proj_rows = jnp.concatenate([proj_rows, came], axis=0)
    proj_weight = natural_rows(proj_rows, narrow_index, narrow_count)
    result_own = residual_mid + plain_product(hidden_low, outer_joined)
    result_low = result_own.astype(low_type)
    result_even = [result_low] + [swap(result_low, narrow, peer) for peer in bits[1:]]

    scale_three = rms_scale(result_own)
    member = (
        own_segments[None, :] == jnp.arange(SEQS_DEV, dtype=jnp.int32)[:, None]
    ).astype(jnp.float32)
    length_values = lengths.astype(jnp.float32)[:, None]
    unscaled_part = (
        jnp.dot(member, result_own * scale_three, precision=lax.Precision.HIGHEST) / length_values
    )
    total_seqs = wide_count * SEQS_DEV
    own_pooled_grad, loss_low, loss_row, final_gain_grad = contrastive(
        jnp.concatenate([wide_index.reshape(1), lengths]),
        sharpness_exponent,
        spread(unscaled_part, everyone).reshape(total_seqs * narrow_count, D),
        proj_weight,
        rescaling_coefficients[2:3],
        total_seqs,
    )
    loss = loss_row[0, 0]
    sharpness_total = loss_row[0, 1:2]
    proj_grad_own = lax.dynamic_slice_in_dim(
        loss_low[:total_seqs], narrow_index * unit_rows, unit_rows, 1
    )
    proj_weight_grad = outer_product(proj_grad_own, loss_low[total_seqs:])

    weighted = own_pooled_grad[SEQS_DEV - 1]
    for s in range(SEQS_DEV - 2, -1, -1):
        weighted = jnp.where((own_segments == s)[:, None], own_pooled_grad[s], weighted)
    inner_mean = jnp.mean(weighted * result_own, axis=-1, keepdims=True)
    encoded_grad = scale_three * weighted - result_own * (
        scale_three * scale_three * scale_three * inner_mean
    )
    ffn_grad_low = encoded_grad.astype(low_type)
    group_rows = part_rows if part_rows % 16 == 0 else D
    weight_grads, normed_two_grad = feed_forward_backward(
        ffn_grad_low,
        normed_two,
        hidden_low,
        hidden_slope,
        inner_joined,
        outer_joined,
        group_rows,
    )
    near_part = lax.psum_scatter(
        weight_grads.reshape(2 * FF, D), near_axes, scatter_dimension=0, tiled=True
    )
    mid_norm_grad, ffn_gain_grad = norm_backward(
        residual_mid, scale_two, rescaling_coefficients[1], normed_two_grad
    )
    mid_grad = encoded_grad + mid_norm_grad
    attn_grad_low = mid_grad.astype(low_type)

    context_grad_own = times_transposed(attn_grad_low, out_joined).astype(low_type)
    context_grad = [
        to_peer(context_grad_own[:, s * unit_rows : (s + 1) * unit_rows], peer)
        for s, peer in enumerate(order)
    ]
    attn_grad_low = after(attn_grad_low, context_grad_own)
    out_kept = outer_product(context_own, attn_grad_low).astype(low_type)
    for bit in bits:
        half = out_kept.shape[0] // 2
        out_came = swap(out_kept[half:], narrow, bit)
        if bit == bits[-1]:
            break
        out_kept = sum_low(out_kept[:half], out_came)
    context_grad = after(jnp.concatenate(context_grad, axis=0), out_kept)
    qkv_cols, qkv_rows, bias_lines = attention_backward(
        lengths,
        origin,
        query_cols,
        key_rows,
        value_rows,
        key_cols,
        context_grad,
        context_cols,
        log_rows,
        apart,
        tiles_bias,
    )
    qkv_cols, qkv_rows, out_came, *result_even = lax.optimization_barrier(
        (qkv_cols, qkv_rows, out_came, *result_even)
    )
    out_grad = sum_low(out_kept[: out_came.shape[0]], out_came)
    offset_bias_slope = lax.dot_general(
        bucket_onehot,
        bias_lines.reshape(heads_here, LINES * LANE),
        (((0,), (1,)), ((), ())),
        precision=lax.Precision.HIGHEST,
    )

    late = jnp.concatenate(
        [plain_product(qkv_cols, normed_one).astype(low_type), out_grad], axis=0
    ).reshape(far_count, near_count, part_rows, D)
    half = qkv_rows.shape[0] // 2
    rows_sent = plain_product(qkv_rows[half:], qkv_weight).astype(low_type)
    rows_kept = plain_product(qkv_rows[:half], after(qkv_weight, rows_sent))
    near_index = wide_index % near_count
    late_sum = lax.dynamic_index_in_dim(late, near_index, 1, keepdims=False)
    for peer in range(1, near_count):
        sent = lax.dynamic_index_in_dim(late, near_index ^ peer, 1, keepdims=False)
        late_sum = sum_low(late_sum, after(swap(sent, near, peer), rows_kept))
    early = after(near_part, late).reshape(-1, 2, group_rows // part_rows, part_rows, D)
    early = jnp.swapaxes(early, 1, 2).reshape(far_count, 2, part_rows, D)
    terms = jnp.concatenate([early, late_sum[:, None]], axis=1)
    own_part = lax.psum_scatter(
        terms.reshape(far_count * 3 * part_rows, D), far, scatter_dimension=0, tiled=True
    )
    normed_one_grad = rows_kept + swap(rows_sent, narrow, bits[0]).astype(jnp.float32)
    for bit in bits[1:]:
        half = normed_one_grad.shape[0] // 2
        came = swap(normed_one_grad[half:].astype(low_type), narrow, bit)
        normed_one_grad = normed_one_grad[:half] + came.astype(jnp.float32)
    input_norm_grad, attn_gain_grad = norm_backward(
        own_rows, scale_one, rescaling_coefficients[0], normed_one_grad
    )
    input_own = mid_grad + input_norm_grad
    sums = lax.all_gather(after(own_part, input_own), wide, axis=0, tiled=True)
    input_grad = natural_rows(
        join_rows(input_own.astype(low_type), narrow), narrow_index, narrow_count
    ).astype(jnp.float32)

    result_pieces = {}
    for peer, rows in zip([0] + bits[1:], result_even):
        result_pieces[peer], result_pieces[peer + 1] = rows, swap(rows, narrow, 1)
    layer_result = natural_rows(
        jnp.concatenate([result_pieces[peer] for peer in order], axis=0),
        narrow_index,
        narrow_count,
    ).astype(jnp.float32)

    bias_size = offset_bias_slope.size
    squares = jnp.sum(jnp.square(own_part.astype(jnp.float32))) + jnp.where(
        tile_location[4] // CAP == wide_index, jnp.sum(jnp.square(proj_weight_grad)), 0.0
    )
    small = jnp.stack(
        [
            ffn_gain_grad,
            attn_gain_grad,
            jnp.pad(offset_bias_slope.reshape(bias_size), (0, D - bias_size)),
            jnp.broadcast_to(squares, (D,)),
        ]
    )
    small_all = spread(small, everyone).reshape(wide_count, narrow_count, 4, D)
    gain_sums = jnp.sum(small_all[:, :, :2], axis=(0, 1))
    gain_total = jnp.stack([gain_sums[1], gain_sums[0], final_gain_grad[0]])
    bias_all = jnp.sum(small_all[:, :, 2], axis=0)
    square_terms = small_all[:, :, 3, 0]
    bias_total = lax.dynamic_index_in_dim(bias_all, narrow_index, 0, keepdims=False)[
        :bias_size
    ].reshape(offset_bias_slope.shape)
    sums, proj_weight_grad, square_terms, *_ = lax.optimization_barrier(
        (sums, proj_weight_grad, square_terms, input_grad, layer_result, gain_total, bias_total)
    )
    sums = sums.reshape(ffn_units, wide_count // ffn_units, 3, part_rows, D)
    slot_grads = []
    for slot in range(CAP):
        here = tile_location == own_slots[slot]
        unit = jnp.sum(jnp.where(here, jnp.arange(here.shape[0], dtype=jnp.int32), 0))
        row = jnp.where(unit >= 5, (unit - 5) % ffn_units, jnp.minimum(unit, ffn_units - 1))
        column = jnp.where(unit >= 5, 1 - (unit - 5) // ffn_units, 2)
        low_sum = lax.dynamic_slice(
            sums, (row, 0, column, 0, 0), (1, wide_count // ffn_units, 1, part_rows, D)
        ).reshape(unit_rows, D)
        low_sum = jnp.where(unit == 4, proj_weight_grad, low_sum.astype(jnp.float32))
        slot_grads.append(jnp.where(jnp.any(here), low_sum, 0.0))
    slot_grads = jnp.stack(slot_grads)
    grad_norm = jnp.sqrt(
        jnp.sum(square_terms)
        + jnp.sum(gain_total * gain_total)
        + jnp.sum(bias_all * bias_all)
        + jnp.sum(sharpness_total * sharpness_total)
    )
    multiplier = jnp.minimum(1.0, clip_limit / grad_norm)
    slot_first, slot_second, slot_weight = decoupled_decay_step(
        slot_grads,
        precise_mean_est,
        precise_variance_est,
        precise_parameter_blocks,
        multiplier,
        learn_rate,
    )
    gain_first, gain_second, gain_new = decoupled_decay_step(
        gain_total,
        norm_scale_mean_est,
        norm_scale_variance_est,
        rescaling_coefficients,
        multiplier,
        side_rate,
    )
    bias_first, bias_second, bias_new = decoupled_decay_step(
        bias_total,
        offset_bias_mean_est,
        offset_bias_variance_est,
        distance_bias_table,
        multiplier,
        side_rate,
    )
    sharpness_mean_fresh, sharpness_variance_fresh, sharpness_exponent_fresh = decoupled_decay_step(
        sharpness_total,
        sharpness_mean_est,
        sharpness_variance_est,
        sharpness_exponent,
        multiplier,
        learn_rate,
    )
    return (
        loss,
        layer_result,
        input_grad,
        grad_norm,
        slot_first,
        slot_second,
        slot_weight,
        gain_first,
        gain_second,
        gain_new,
        bias_first,
        bias_second,
        bias_new,
        sharpness_mean_fresh,
        sharpness_variance_fresh,
        sharpness_exponent_fresh,
    )


def solution(mesh):
    wide, narrow, far, near = ("wide",), ("narrow",), ("wide",), ()
    if dict(mesh.shape) == {"wide": 8, "narrow": 4}:
        mesh = Mesh(mesh.devices.reshape(4, 2, 2, 2), ("line", "pair", "side", "core"))
        wide, narrow, far, near = ("line", "pair"), ("side", "core"), ("line",), ("pair",)
    whole, rows, blocks, heads = P(), P(wide, None), P(wide, narrow, None), P(None, narrow)
    arguments = (rows, rows, whole, whole, blocks, blocks, blocks, whole, whole, whole)
    arguments += (heads, heads, heads, whole, whole, whole)
    results = (whole, rows, rows, whole, blocks, blocks, blocks, whole, whole, whole)
    results += (heads, heads, heads, whole, whole, whole)

    def body(*arrays):
        return on_device((wide, narrow, far, near), *arrays)

    return jax.shard_map(
        body, mesh=mesh, in_specs=arguments, out_specs=results, check_vma=False
    )
```

```python
import jax
import jax.numpy as jnp
from jax import lax
from jax.experimental import pallas as pl
from jax.experimental.pallas import tpu as pltpu
from jax.sharding import Mesh
from jax.sharding import PartitionSpec as P

D = 768
FF = 3072
BUCKETS = 32
TOK_DEV = 2560
SEQS_DEV = 4
DOCLEN = 1024
CAP = 2
STEP = 10
LANE = 128
BQ = 512
BK = 512
UNIT_BLOCK = 768
REACH = DOCLEN // LANE
OFF = REACH + (BQ + BK) // LANE
SPAN = 2 * OFF + 1
LINES = 2 * REACH + 2
VMEM_LIMIT = 56 * 1024 * 1024

norm_eps = 1e-06
clip_limit = 0.01
learn_rate = 0.01
side_rate = 0.5
beta_one = 0.5
beta_two = 0.5
adam_eps = 1e-08
decay_rate = 0.01
score_scale = 0.125
masked_score = -1e30
low_type = jnp.bfloat16


def times_transposed(left_side, right_side):
    return lax.dot_general(
        left_side, right_side, (((1,), (1,)), ((), ())), preferred_element_type=jnp.float32
    )


def plain_product(left_side, right_side):
    return jnp.dot(left_side, right_side, preferred_element_type=jnp.float32)


def outer_product(left_side, right_side):
    return lax.dot_general(
        left_side, right_side, (((0,), (0,)), ((), ())), preferred_element_type=jnp.float32
    )


def rms_scale(values):
    return lax.rsqrt(jnp.mean(values * values, axis=-1, keepdims=True) + norm_eps)


def norm_backward(values, row_scale, gain_row, grad_out):
    weighted = grad_out * gain_row
    gain_grad = jnp.sum(grad_out * values * row_scale, axis=0)
    inner_mean = jnp.mean(weighted * values, axis=-1, keepdims=True)
    value_grad = row_scale * weighted - values * row_scale * row_scale * row_scale * inner_mean
    return (value_grad, gain_grad)


def decoupled_decay_step(gradient, first_moment, second_moment, weight, multiplier, step_rate):
    clipped = gradient * multiplier
    first_new = beta_one * first_moment + (1.0 - beta_one) * clipped
    second_new = beta_two * second_moment + (1.0 - beta_two) * clipped * clipped
    first_hat = first_new / (1.0 - beta_one**STEP)
    second_hat = second_new / (1.0 - beta_two**STEP)
    weight_new = weight - step_rate * (
        first_hat / (jnp.sqrt(second_hat) + adam_eps) + decay_rate * weight
    )
    return (first_new, second_new, weight_new)


def swap(values, axes, bit):
    count = lax.axis_size(axes)
    return lax.ppermute(values, axes, [(i, i ^ bit) for i in range(count)])


def sum_low(left, right):
    return (left.astype(jnp.float32) + right.astype(jnp.float32)).astype(low_type)


def narrow_bits(count):
    return [1 << s for s in range(count.bit_length() - 1)]


def peer_order(count):
    order = [0]
    for bit in reversed(narrow_bits(count)):
        order = order + [peer ^ bit for peer in order]
    return order


def join_rows(values, axes):
    for bit in reversed(narrow_bits(lax.axis_size(axes))):
        values = jnp.concatenate([values, swap(values, axes, bit)], axis=0)
    return values


def add_rows(values, axes):
    for bit in narrow_bits(lax.axis_size(axes)):
        half = values.shape[0] // 2
        came = swap(values[half:].astype(low_type), axes, bit)
        values = values[:half].astype(jnp.float32) + came.astype(jnp.float32)
    return values


def product_add_rows(left_side, right_side, axes):
    bits = narrow_bits(lax.axis_size(axes))
    half = left_side.shape[0] // 2
    sent = plain_product(left_side[half:], right_side).astype(low_type)
    came = swap(sent, axes, bits[0])
    values = plain_product(left_side[:half], right_side) + came.astype(jnp.float32)
    for bit in bits[1:]:
        half = values.shape[0] // 2
        came = swap(values[half:].astype(low_type), axes, bit)
        values = values[:half] + came.astype(jnp.float32)
    return values


def natural_rows(joined, places):
    group = joined.shape[0] // len(places)
    return jnp.concatenate(
        [lax.dynamic_slice_in_dim(joined, place * group, group, 0) for place in places], axis=0
    )


def spread(values, axes):
    copies = jnp.broadcast_to(values[None], (lax.axis_size(axes),) + values.shape)
    return lax.all_to_all(copies, axes, split_axis=0, concat_axis=0, tiled=True)


def after(values, other):
    return lax.optimization_barrier((values, other))[0]


def gelu_and_slope(values):
    rate = 0.7978845608028654
    cubic = 0.044715
    squares = values * values
    turn = jnp.tanh(rate * values * (1.0 + cubic * squares))
    half = 0.5 * (1.0 + turn)
    slope = half + 0.5 * values * (1.0 - turn * turn) * (rate * (1.0 + 3.0 * cubic * squares))
    return (values * half).astype(low_type), slope.astype(low_type)


def smem():
    return pl.BlockSpec(memory_space=pltpu.SMEM)


def vmem():
    return pl.BlockSpec(memory_space=pltpu.VMEM)


def bias_kernel(chunks, tiles):
    heads = tiles.shape[0]
    tiles[...] = jnp.zeros_like(tiles)
    for h in range(heads):
        for d in range(-REACH, REACH + 1):
            left = chunks[h, REACH + 1 - d : REACH + 2 - d, :]
            right = chunks[h, REACH - d : REACH + 1 - d, :]
            line = jnp.broadcast_to(jnp.concatenate([left, right], axis=1), (LANE, 2 * LANE))
            rolled = pltpu.roll(line, 0, 1, stride=1, stride_axis=0)
            tiles[h, (d + OFF) * LANE : (d + OFF + 1) * LANE, :] = rolled[:, :LANE]


def bias_tiles(rel_chunks):
    heads = rel_chunks.shape[0]
    return pl.pallas_call(
        bias_kernel,
        out_shape=jax.ShapeDtypeStruct((heads, SPAN * LANE, LANE), jnp.float32),
        compiler_params=pltpu.CompilerParams(vmem_limit_bytes=VMEM_LIMIT),
        name="bias_tiles",
    )(rel_chunks)


def key_range(lengths, first, last):
    start = jnp.int32(0)
    low = jnp.int32(0)
    high = jnp.int32(0)
    for s in range(SEQS_DEV):
        end = start + lengths[s]
        low = jnp.where(start <= first, start, low)
        high = jnp.where(start <= last, end, high)
        start = end
    return low // BK, (high + BK - 1) // BK


def bias_part(bias, h, row):
    return jnp.concatenate(
        [
            bias[h, pl.ds(pl.multiple_of(row - b * LANE, LANE), BK), :]
            for b in range(BQ // LANE)
        ],
        axis=1,
    )


def forward_kernel(first_row, lengths, origin, qT, kn, vT, apart, bias, ctx_o, ctxT_o, lse_o, qa, acc):
    width, rows_here = qT.shape
    heads = bias.shape[0]
    size = width // heads
    qa[...] = jnp.zeros_like(qa)

    @pl.loop(0, rows_here // BQ)
    def _(i):
        q0 = pl.multiple_of(i * BQ, BQ)
        here = pl.ds(q0, BQ)
        for h in range(heads):
            qa[h * LANE : h * LANE + size, :] = qT[h * size : (h + 1) * size, here]
            qa[h * LANE + size : h * LANE + size + 16, :] = apart[:, here]
        acc[...] = jnp.zeros_like(acc)
        low, high = key_range(lengths, first_row + q0, first_row + q0 + BQ - 1)

        def step(j, carry):
            k0 = pl.multiple_of(j * BK, BK)
            row = (j * (BK // LANE) - i * (BQ // LANE) - first_row // LANE + OFF) * LANE
            out = []
            for h in range(heads):
                top, total = carry[2 * h], carry[2 * h + 1]
                own = slice(h * LANE, (h + 1) * LANE)
                rows = slice(h * size, (h + 1) * size)
                s = plain_product(kn[pl.ds(k0, BK), own], qa[own, :]) + bias_part(bias, h, row)
                new_top = jnp.maximum(top, jnp.max(s, axis=0, keepdims=True))
                fade = jnp.exp(top - new_top)
                p = jnp.exp(s - new_top)
                total = total * fade + jnp.sum(p, axis=0, keepdims=True)
                acc[rows, :] = acc[rows, :] * fade + plain_product(
                    vT[rows, pl.ds(k0, BK)], p.astype(low_type)
                )
                out += [new_top, total]
            return tuple(out)

        init = tuple(
            jnp.full((1, BQ), 2.0 * masked_score if n % 2 == 0 else 0.0, jnp.float32)
            for n in range(2 * heads)
        )
        done = lax.fori_loop(low, high, step, init)
        for h in range(heads):
            rows = slice(h * size, (h + 1) * size)
            acc[rows, :] = acc[rows, :] / done[2 * h + 1]
            lse_o[h : h + 1, here] = done[2 * h] + jnp.log(done[2 * h + 1])
        ctxT_o[:, here] = acc[...]
        turned = acc[...].T.astype(low_type)
        for b in range(BQ // LANE):
            at = pl.multiple_of(origin[i * (BQ // LANE) + b], LANE)
            ctx_o[pl.ds(at, LANE), :] = turned[b * LANE : (b + 1) * LANE, :]


def attention_forward(first_row, lengths, origin, qT, kn, vT, apart, bias):
    width, rows_here = qT.shape
    heads = bias.shape[0]

    def body(*refs):
        forward_kernel(first_row, *refs)

    return pl.pallas_call(
        body,
        out_shape=(
            jax.ShapeDtypeStruct((rows_here, width), low_type),
            jax.ShapeDtypeStruct((width, rows_here), jnp.float32),
            jax.ShapeDtypeStruct((heads, rows_here), jnp.float32),
        ),
        in_specs=[smem()] * 2 + [vmem()] * 5,
        out_specs=(vmem(),) * 3,
        scratch_shapes=[
            pltpu.VMEM((heads * LANE, BQ), low_type),
            pltpu.VMEM((width, BQ), jnp.float32),
        ],
        compiler_params=pltpu.CompilerParams(vmem_limit_bytes=VMEM_LIMIT),
        cost_estimate=pl.CostEstimate(
            flops=rows_here * width, bytes_accessed=width * TOK_DEV, transcendentals=0
        ),
        name="attention_forward",
    )(lengths, origin, qT, kn, vT, apart, bias)


def three_parts(values):
    first = values.astype(low_type).astype(jnp.float32)
    rest = values - first
    second = rest.astype(low_type).astype(jnp.float32)
    return first, second, rest - second


def backward_kernel(
    lengths, origin, qT, kn, vn, kT, dcn, ctxT, lse, apart, bias,
    dT_o, dn_o, lines_o, qa, da, dq, dk, dv, tiles,
):
    width, tokens = qT.shape
    heads = bias.shape[0]
    size = width // heads
    for ref in (qa, da, dk, dv, tiles):
        ref[...] = jnp.zeros_like(ref)
    place = lax.broadcasted_iota(jnp.int32, (16, BQ), 0) - SEQS_DEV

    def in_depth(values):
        a, b, c = three_parts(values)
        return jnp.where(place == 0, a, jnp.where(place == 1, b, jnp.where(place == 2, c, 0.0)))

    @pl.loop(0, tokens // BQ)
    def _(i):
        q0 = pl.multiple_of(i * BQ, BQ)
        here = pl.ds(q0, BQ)
        at = [pl.multiple_of(origin[i * (BQ // LANE) + b], LANE) for b in range(BQ // LANE)]
        dcT = jnp.concatenate(
            [dcn[pl.ds(at[b], LANE), :].astype(jnp.float32) for b in range(BQ // LANE)], axis=0
        ).T
        for h in range(heads):
            rows = slice(h * size, (h + 1) * size)
            top = h * LANE
            qa[top : top + size, :] = qT[rows, here]
            extra = apart[:, here].astype(jnp.float32) + in_depth(-lse[h : h + 1, here])
            qa[top + size : top + size + 16, :] = extra.astype(low_type)
            da[top : top + size, :] = dcT[rows, :].astype(low_type)
            delta = jnp.sum(dcT[rows, :] * ctxT[rows, here], axis=0, keepdims=True)
            da[top + size : top + size + 16, :] = in_depth(-delta).astype(low_type)
        dq[...] = jnp.zeros_like(dq)
        low, high = key_range(lengths, q0, q0 + BQ - 1)

        @pl.loop(low, high)
        def _(j):
            k0 = pl.multiple_of(j * BK, BK)
            there = pl.ds(k0, BK)
            row = (j * (BK // LANE) - i * (BQ // LANE) + OFF) * LANE
            for h in range(heads):
                rows = slice(h * size, (h + 1) * size)
                own = slice(h * LANE, (h + 1) * LANE)
                flat = slice(h * LANE, h * LANE + size)
                s = plain_product(kn[there, own], qa[own, :])
                p = jnp.exp(s + bias_part(bias, h, row))
                ds = p * plain_product(vn[there, own], da[own, :])
                for b in range(BQ // LANE):
                    window = pl.ds(pl.multiple_of(row - b * LANE, LANE), BK)
                    tiles[h, window, :] = (
                        tiles[h, window, :] + ds[:, b * LANE : (b + 1) * LANE]
                    )
                p_low = p.astype(low_type)
                ds_low = ds.astype(low_type)
                dv[rows, there] = dv[rows, there] + times_transposed(da[flat, :], p_low)
                dk[rows, there] = dk[rows, there] + times_transposed(qa[flat, :], ds_low)
                dq[rows, :] = dq[rows, :] + plain_product(kT[rows, there], ds_low)

        grad = dq[...] * score_scale
        dT_o[0:width, here] = grad.astype(low_type)
        turned = grad.T.astype(low_type)
        for b in range(BQ // LANE):
            dn_o[pl.ds(at[b], LANE), 0:width] = turned[b * LANE : (b + 1) * LANE, :]

    @pl.loop(0, tokens // BQ)
    def _(i):
        here = pl.ds(pl.multiple_of(i * BQ, BQ), BQ)
        both = jnp.concatenate([dk[:, here], dv[:, here]], axis=0)
        dT_o[width : 3 * width, here] = both.astype(low_type)
        turned = both.T.astype(low_type)
        for b in range(BQ // LANE):
            at = pl.multiple_of(origin[i * (BQ // LANE) + b], LANE)
            dn_o[pl.ds(at, LANE), width : 3 * width] = turned[b * LANE : (b + 1) * LANE, :]

    across = lax.broadcasted_iota(jnp.int32, (LANE, LANE), 1)
    over = across >= lax.broadcasted_iota(jnp.int32, (LANE, LANE), 0)
    sub = lax.broadcasted_iota(jnp.int32, (8, LANE), 0)
    for h in range(heads):
        for d in range(-REACH, REACH + 2):
            here = tiles[h, (d + OFF) * LANE : (d + OFF + 1) * LANE, :]
            below = tiles[h, (d + OFF - 1) * LANE : (d + OFF) * LANE, :]
            mixed = jnp.where(over, here, below)
            line = mixed[LANE - 8 :, :]
            for g in range(LANE // 8 - 2, -1, -1):
                line = mixed[8 * g : 8 * g + 8, :] + pltpu.roll(line, LANE - 8, 1)
            for bit in (1, 2, 4):
                line = jnp.where((sub & bit) != 0, pltpu.roll(line, LANE - bit, 1), line)
            lines_o[h, REACH + 1 - d : REACH + 2 - d, :] = jnp.sum(line, axis=0, keepdims=True)


def attention_backward(lengths, origin, qT, kn, vn, kT, dcn, ctxT, lse, apart, bias):
    width, tokens = qT.shape
    heads = bias.shape[0]
    return pl.pallas_call(
        backward_kernel,
        out_shape=(
            jax.ShapeDtypeStruct((3 * width, tokens), low_type),
            jax.ShapeDtypeStruct((tokens, 3 * width), low_type),
            jax.ShapeDtypeStruct((heads, LINES, LANE), jnp.float32),
        ),
        in_specs=[smem()] * 2 + [vmem()] * 9,
        out_specs=(vmem(),) * 3,
        scratch_shapes=[
            pltpu.VMEM((heads * LANE, BQ), low_type),
            pltpu.VMEM((heads * LANE, BQ), low_type),
            pltpu.VMEM((width, BQ), jnp.float32),
            pltpu.VMEM((width, tokens), jnp.float32),
            pltpu.VMEM((width, tokens), jnp.float32),
            pltpu.VMEM((heads, SPAN * LANE, LANE), jnp.float32),
        ],
        compiler_params=pltpu.CompilerParams(vmem_limit_bytes=VMEM_LIMIT),
        cost_estimate=pl.CostEstimate(
            flops=tokens * width, bytes_accessed=width * TOK_DEV, transcendentals=0
        ),
        name="attention_backward",
    )(lengths, origin, qT, kn, vn, kT, dcn, ctxT, lse, apart, bias)


def feed_forward_backward_kernel(
    grad, rows, hidden, slope, inner, outer, weight_grads, rows_grad
):
    groups, _, size, width = weight_grads.shape

    @pl.when(pl.program_id(0) == 0)
    def _():
        rows_grad[...] = jnp.zeros_like(rows_grad)

    outer_grad = outer_product(hidden[...], grad[...]).astype(low_type)
    weight_grads[:, 0] = outer_grad.reshape(groups, size, width)
    pre = (
        times_transposed(grad[...], outer[...]) * slope[...].astype(jnp.float32)
    ).astype(low_type)
    inner_grad = outer_product(pre, rows[...]).astype(low_type)
    weight_grads[:, 1] = inner_grad.reshape(groups, size, width)
    rows_grad[...] += plain_product(pre, inner[...])


def feed_forward_backward(grad, rows, hidden, slope, inner, outer, size):
    count = grad.shape[0]
    groups = UNIT_BLOCK // size
    every = pl.BlockSpec((count, D), lambda i: (0, 0))
    units = pl.BlockSpec((count, UNIT_BLOCK), lambda i: (0, i))
    weight = pl.BlockSpec((UNIT_BLOCK, D), lambda i: (i, 0))
    return pl.pallas_call(
        feed_forward_backward_kernel,
        grid=(FF // UNIT_BLOCK,),
        out_shape=(
            jax.ShapeDtypeStruct((FF // size, 2, size, D), low_type),
            jax.ShapeDtypeStruct((count, D), jnp.float32),
        ),
        in_specs=[every, every, units, units, weight, weight],
        out_specs=(pl.BlockSpec((groups, 2, size, D), lambda i: (i, 0, 0, 0)), every),
        compiler_params=pltpu.CompilerParams(vmem_limit_bytes=VMEM_LIMIT),
        cost_estimate=pl.CostEstimate(flops=FF * D, bytes_accessed=FF * D, transcendentals=0),
        name="feed_forward_backward",
    )(grad, rows, hidden, slope, inner, outer)


def loss_kernel(place, numbers, parts, proj_weight, gain, out_slope, out_low, out_row, out_gain):
    total_seqs = out_low.shape[0] // 2
    terms = parts.shape[0] // total_seqs
    exact = dict(precision=lax.Precision.HIGHEST, preferred_element_type=jnp.float32)
    seq = lax.broadcasted_iota(jnp.int32, (total_seqs, parts.shape[0]), 0)
    part = lax.broadcasted_iota(jnp.int32, (total_seqs, parts.shape[0]), 1)
    joins = jnp.logical_and(
        seq // SEQS_DEV == part // (SEQS_DEV * terms), seq % SEQS_DEV == part % SEQS_DEV
    )
    unscaled = jnp.dot(joins.astype(jnp.float32), parts[...], **exact)
    pooled_low = (unscaled * gain[...]).astype(low_type)
    projected = times_transposed(pooled_low, proj_weight[...]).astype(low_type).astype(jnp.float32)
    inverse = lax.rsqrt(jnp.sum(projected * projected, axis=1, keepdims=True) + norm_eps)
    embed_low = (projected * inverse).astype(low_type)
    sharpness_factor = jnp.exp(jnp.full((1, 1), numbers[0], jnp.float32))
    agreement = times_transposed(embed_low, embed_low)
    row = lax.broadcasted_iota(jnp.int32, (total_seqs, total_seqs), 0)
    column = lax.broadcasted_iota(jnp.int32, (total_seqs, total_seqs), 1)
    logits = jnp.where(row == column, masked_score, sharpness_factor * agreement)
    partner = (row ^ 1) == column

    def log_sum(axis):
        top = jnp.max(logits, axis=axis, keepdims=True)
        return top + jnp.log(jnp.sum(jnp.exp(logits - top), axis=axis, keepdims=True))

    log_rows = log_sum(1)
    positive = jnp.where(partner, 1.0, 0.0)
    slope = (jnp.exp(logits - log_rows) - positive) / total_seqs
    slope_turned = (jnp.exp(logits - log_sum(0)) - positive) / total_seqs
    embed_grad = sharpness_factor * jnp.dot(
        slope + slope_turned, embed_low.astype(jnp.float32), **exact
    )
    along = jnp.sum(projected * embed_grad, axis=1, keepdims=True)
    proj_grad_low = (
        inverse * embed_grad - projected * inverse * inverse * inverse * along
    ).astype(low_type)
    pooled_grad = plain_product(proj_grad_low, proj_weight[...])
    out_low[0:total_seqs, :] = proj_grad_low
    out_low[total_seqs : 2 * total_seqs, :] = pooled_low
    out_gain[...] = jnp.sum(pooled_grad * unscaled, axis=0, keepdims=True)
    loss = jnp.sum(
        log_rows - jnp.sum(positive * jnp.where(partner, logits, 0.0), axis=1, keepdims=True),
        axis=0,
        keepdims=True,
    ) / total_seqs
    temperature = sharpness_factor * jnp.sum(
        jnp.sum(slope * agreement, axis=1, keepdims=True), axis=0, keepdims=True
    )
    lane = lax.broadcasted_iota(jnp.int32, (1, LANE), 1)
    out_row[...] = jnp.where(lane == 0, loss, jnp.where(lane == 1, temperature, 0.0))
    mine = lax.broadcasted_iota(jnp.int32, (8, total_seqs), 0)
    seq_of = lax.broadcasted_iota(jnp.int32, (8, total_seqs), 1) - place[0] * SEQS_DEV
    picks = jnp.logical_and(mine == seq_of, mine < SEQS_DEV).astype(jnp.float32)
    own = jnp.dot(picks, pooled_grad, **exact)
    index = lax.broadcasted_iota(jnp.int32, (8, 1), 0)
    extent = jnp.ones((8, 1), jnp.float32)
    for s in range(SEQS_DEV):
        extent = jnp.where(index == s, place[1 + s].astype(jnp.float32), extent)
    out_slope[...] = own * gain[...] / extent


def contrastive(place, numbers, parts, proj_weight, gain, total_seqs):
    return pl.pallas_call(
        loss_kernel,
        out_shape=(
            jax.ShapeDtypeStruct((8, D), jnp.float32),
            jax.ShapeDtypeStruct((2 * total_seqs, D), low_type),
            jax.ShapeDtypeStruct((1, LANE), jnp.float32),
            jax.ShapeDtypeStruct((1, D), jnp.float32),
        ),
        in_specs=[smem()] * 2 + [vmem()] * 3,
        out_specs=(vmem(),) * 4,
        compiler_params=pltpu.CompilerParams(vmem_limit_bytes=VMEM_LIMIT),
        cost_estimate=pl.CostEstimate(
            flops=4 * total_seqs * D * D, bytes_accessed=4 * D * D, transcendentals=total_seqs
        ),
        name="contrastive",
    )(place, numbers, parts, proj_weight, gain)


def on_device(
    axes,
    layer_argument,
    document_extents,
    distance_bin_lookup,
    tile_location,
    precise_parameter_blocks,
    precise_mean_est,
    precise_variance_est,
    rescaling_coefficients,
    norm_scale_mean_est,
    norm_scale_variance_est,
    distance_bias_table,
    offset_bias_mean_est,
    offset_bias_variance_est,
    sharpness_exponent,
    sharpness_mean_est,
    sharpness_variance_est,
):
    wide, narrow, far, near = axes
    everyone = wide + narrow
    near_axes = near + narrow
    wide_count = lax.axis_size(wide)
    narrow_count = lax.axis_size(narrow)
    far_count = lax.axis_size(far)
    near_count = wide_count // far_count
    wide_index = lax.axis_index(wide)
    narrow_index = lax.axis_index(narrow)
    bits = narrow_bits(narrow_count)
    order = peer_order(narrow_count)
    place_of = jnp.array([order.index(peer) for peer in range(narrow_count)], jnp.int32)
    unit_rows = precise_parameter_blocks.shape[1]
    heads_here = distance_bias_table.shape[1]
    head_size = unit_rows // heads_here
    ffn_units = FF // D
    group = TOK_DEV // narrow_count
    own_slots = wide_index * CAP + jnp.arange(CAP, dtype=jnp.int32)

    every_slot = lax.all_gather(
        precise_parameter_blocks.astype(low_type), wide, axis=0, tiled=True
    )

    def block(u):
        return lax.dynamic_index_in_dim(every_slot, tile_location[u], 0, keepdims=False)

    qkv_weight = jnp.concatenate([block(u) for u in range(3)], axis=0)

    part_rows = D // wide_count

    def unit_order(first_unit):
        rows = jnp.concatenate([block(first_unit + k) for k in range(ffn_units)], axis=0)
        rows = rows.reshape(far_count, near_count, part_rows, D)
        return jnp.swapaxes(rows, 0, 1).reshape(near_count, far_count * part_rows, D)

    crossing = [block(3), unit_order(5), unit_order(5 + ffn_units)]
    for rows in crossing:
        qkv_weight = after(qkv_weight, rows)
    crossed = [[rows] + [swap(rows, narrow, peer) for peer in bits[1:]] for rows in crossing]

    lengths = document_extents[0]
    seq_ends = jnp.cumsum(lengths)
    positions = jnp.arange(TOK_DEV, dtype=jnp.int32)

    def segments_of(where):
        return jnp.sum((seq_ends[None, :] <= where[:, None]).astype(jnp.int32), axis=1)

    segment_ids = segments_of(positions)
    own_segments = segments_of(narrow_index * group + positions[:group])
    tile_starts = jnp.arange(TOK_DEV // LANE, dtype=jnp.int32) * LANE
    origin = place_of[(tile_starts // group) ^ narrow_index] * group + tile_starts % group

    units = []
    for slot in range(CAP):
        here = tile_location == own_slots[slot]
        unit = jnp.sum(jnp.where(here, jnp.arange(1, here.shape[0] + 1, dtype=jnp.int32), 0)) - 1
        early_unit = jnp.maximum(unit - 5, 0)
        row = jnp.where(unit >= 5, early_unit % ffn_units, jnp.clip(unit, 0, ffn_units - 1))
        column = jnp.where(unit >= 5, 1 - early_unit // ffn_units, 2)
        units += [unit, row, column]
    proj_owner = (tile_location[4] // CAP == wide_index).astype(jnp.float32)
    places = [place_of[g ^ narrow_index] for g in range(narrow_count)]

    beyond = LINES * LANE - LANE - 1 - distance_bin_lookup.shape[0]
    offsets_down = jnp.pad(distance_bin_lookup[::-1], (LANE + 1, beyond), constant_values=-1)
    bucket_onehot = (
        offsets_down[:, None] == jnp.arange(BUCKETS, dtype=jnp.int32)[None, :]
    ).astype(jnp.float32)
    rel_values = jnp.dot(bucket_onehot, distance_bias_table, precision=lax.Precision.HIGHEST).T
    rel_values, origin, proj_owner, *scalars = lax.optimization_barrier(
        (rel_values, origin, proj_owner, *units, *places)
    )
    units, places = scalars[: len(units)], scalars[len(units) :]
    tiles_bias = bias_tiles(rel_values.reshape(heads_here, LINES, LANE))

    all_rows = layer_argument.astype(jnp.float32)
    normed_one = (all_rows * rms_scale(all_rows) * rescaling_coefficients[0]).astype(low_type)
    transposed_rows = times_transposed(qkv_weight, normed_one)
    query_cols = (transposed_rows[:unit_rows] * score_scale).astype(low_type)
    key_cols = transposed_rows[unit_rows : 2 * unit_rows].astype(low_type)
    value_cols = transposed_rows[2 * unit_rows :].astype(low_type)
    spread_weight = jnp.pad(
        qkv_weight[unit_rows:].reshape(2 * heads_here, head_size, D),
        ((0, 0), (0, LANE - head_size), (0, 0)),
    ).reshape(2 * heads_here * LANE, D)
    lane_place = jnp.arange(2 * heads_here * LANE, dtype=jnp.int32) % LANE - head_size
    marks = jnp.logical_or(
        lane_place[None, :] == segment_ids[:, None],
        jnp.logical_and(lane_place >= SEQS_DEV, lane_place < SEQS_DEV + 3)[None, :],
    )
    key_value_rows = (
        times_transposed(normed_one, spread_weight) + marks.astype(jnp.float32)
    ).astype(low_type)
    key_rows = key_value_rows[:, : heads_here * LANE]
    value_rows = key_value_rows[:, heads_here * LANE :]
    row_place = jnp.arange(16, dtype=jnp.int32)[:, None]
    apart = jnp.where(
        jnp.logical_and(row_place < SEQS_DEV, row_place != segment_ids[None, :]), masked_score, 0.0
    ).astype(low_type)
    context, context_cols, log_rows = attention_forward(
        0, lengths, origin, query_cols, key_rows, value_cols, apart, tiles_bias
    )

    flat = [rows for pieces in crossed for rows in pieces[1:]]
    context, *flat = lax.optimization_barrier((context, *flat))
    evens = len(bits) - 1
    crossed = [
        [pieces[0]] + flat[n * evens : (n + 1) * evens] for n, pieces in enumerate(crossed)
    ]
    def all_peers(pieces):
        own, *even = pieces
        peers = [(0, own), (1, swap(own, narrow, 1))]
        for bit, rows in zip(bits[1:], even):
            peers += [(bit, rows), (bit + 1, swap(rows, narrow, 1))]
        return peers

    def in_unit_order(pieces):
        whole = jnp.zeros((near_count, narrow_count, far_count * part_rows, D), low_type)
        for peer, rows in all_peers(pieces):
            start = (0, narrow_index ^ peer, 0, 0)
            whole = lax.dynamic_update_slice(whole, rows[:, None], start)
        return whole.reshape(FF, D)

    out_pieces = dict(all_peers(crossed[0]))
    out_joined = jnp.concatenate([out_pieces[peer] for peer in order], axis=0)
    inner_joined = in_unit_order(crossed[1])
    outer_joined = in_unit_order(crossed[2])

    def to_peer(values, peer):
        if peer == 0:
            return values
        return swap(values, narrow, peer)

    context_own = jnp.concatenate(
        [
            to_peer(context[s * group : (s + 1) * group], peer)
            for s, peer in enumerate(order)
        ],
        axis=1,
    )
    own_rows = lax.dynamic_slice_in_dim(layer_argument, narrow_index * group, group, 0).astype(
        jnp.float32
    )
    scale_one = rms_scale(own_rows)
    residual_mid = own_rows + plain_product(context_own, out_joined)
    scale_two = rms_scale(residual_mid)
    normed_two = (residual_mid * scale_two * rescaling_coefficients[1]).astype(low_type)

    hidden_low, hidden_slope = gelu_and_slope(times_transposed(normed_two, inner_joined))
    proj_rows = after(block(4), normed_two)
    for bit in reversed(bits):
        came = after(swap(proj_rows, narrow, bit), hidden_low)
        proj_rows = jnp.concatenate([proj_rows, came], axis=0)
    proj_weight = natural_rows(proj_rows, places)
    result_own = residual_mid + plain_product(hidden_low, outer_joined)
    result_low = result_own.astype(low_type)

    scale_three = rms_scale(result_own)
    member = (
        own_segments[None, :] == jnp.arange(SEQS_DEV, dtype=jnp.int32)[:, None]
    ).astype(jnp.float32)
    length_values = lengths.astype(jnp.float32)[:, None]
    unscaled_part = (
        jnp.dot(member, result_own * scale_three, precision=lax.Precision.HIGHEST) / length_values
    )
    total_seqs = wide_count * SEQS_DEV
    own_pooled_grad, loss_low, loss_row, final_gain_grad = contrastive(
        jnp.concatenate([wide_index.reshape(1), lengths]),
        sharpness_exponent,
        spread(unscaled_part, everyone).reshape(total_seqs * narrow_count, D),
        proj_weight,
        rescaling_coefficients[2:3],
        total_seqs,
    )
    loss = loss_row[0, 0]
    sharpness_total = loss_row[0, 1:2]
    proj_grad_own = lax.dynamic_slice_in_dim(
        loss_low[:total_seqs], narrow_index * unit_rows, unit_rows, 1
    )
    proj_weight_grad = outer_product(proj_grad_own, loss_low[total_seqs:])

    weighted = own_pooled_grad[SEQS_DEV - 1]
    for s in range(SEQS_DEV - 2, -1, -1):
        weighted = jnp.where((own_segments == s)[:, None], own_pooled_grad[s], weighted)
    inner_mean = jnp.mean(weighted * result_own, axis=-1, keepdims=True)
    encoded_grad = scale_three * weighted - result_own * (
        scale_three * scale_three * scale_three * inner_mean
    )
    ffn_grad_low = encoded_grad.astype(low_type)
    group_rows = part_rows if part_rows % 16 == 0 else D
    weight_grads, normed_two_grad = feed_forward_backward(
        ffn_grad_low,
        normed_two,
        hidden_low,
        hidden_slope,
        inner_joined,
        outer_joined,
        group_rows,
    )
    near_part = lax.psum_scatter(
        weight_grads.reshape(2 * FF, D), near_axes, scatter_dimension=0, tiled=True
    )
    mid_norm_grad, ffn_gain_grad = norm_backward(
        residual_mid, scale_two, rescaling_coefficients[1], normed_two_grad
    )
    mid_grad = encoded_grad + mid_norm_grad
    attn_grad_low = mid_grad.astype(low_type)

    context_grad_own = times_transposed(attn_grad_low, out_joined).astype(low_type)
    context_grad = [
        to_peer(context_grad_own[:, s * unit_rows : (s + 1) * unit_rows], peer)
        for s, peer in enumerate(order)
    ]
    attn_grad_low = after(attn_grad_low, context_grad_own)
    out_kept = outer_product(context_own, attn_grad_low).astype(low_type)
    for bit in bits:
        half = out_kept.shape[0] // 2
        out_came = swap(out_kept[half:], narrow, bit)
        if bit == bits[-1]:
            break
        out_kept = sum_low(out_kept[:half], out_came)
    context_grad = after(jnp.concatenate(context_grad, axis=0), out_kept)
    result_low = after(result_low, context_grad)
    result_even = [result_low] + [swap(result_low, narrow, peer) for peer in bits[1:]]
    qkv_cols, qkv_rows, bias_lines = attention_backward(
        lengths,
        origin,
        query_cols,
        key_rows,
        value_rows,
        key_cols,
        context_grad,
        context_cols,
        log_rows,
        apart,
        tiles_bias,
    )
    qkv_cols, qkv_rows, out_came, *result_even = lax.optimization_barrier(
        (qkv_cols, qkv_rows, out_came, *result_even)
    )
    out_grad = sum_low(out_kept[: out_came.shape[0]], out_came)
    offset_bias_slope = lax.dot_general(
        bucket_onehot,
        bias_lines.reshape(heads_here, LINES * LANE),
        (((0,), (1,)), ((), ())),
        precision=lax.Precision.HIGHEST,
    )

    late = jnp.concatenate(
        [plain_product(qkv_cols, normed_one).astype(low_type), out_grad], axis=0
    ).reshape(far_count, near_count, part_rows, D)
    half = qkv_rows.shape[0] // 2
    rows_sent = plain_product(qkv_rows[half:], qkv_weight).astype(low_type)
    rows_kept = plain_product(qkv_rows[:half], after(qkv_weight, rows_sent))
    near_index = wide_index % near_count
    late_sum = lax.dynamic_index_in_dim(late, near_index, 1, keepdims=False)
    for peer in range(1, near_count):
        sent = lax.dynamic_index_in_dim(late, near_index ^ peer, 1, keepdims=False)
        late_sum = sum_low(late_sum, after(swap(sent, near, peer), rows_kept))
    early = after(near_part, late).reshape(-1, 2, group_rows // part_rows, part_rows, D)
    early = jnp.swapaxes(early, 1, 2).reshape(far_count, 2, part_rows, D)
    terms = jnp.concatenate([early, late_sum[:, None]], axis=1)
    own_part = lax.psum_scatter(
        terms.reshape(far_count * 3 * part_rows, D), far, scatter_dimension=0, tiled=True
    )
    normed_one_grad = rows_kept + swap(rows_sent, narrow, bits[0]).astype(jnp.float32)
    for bit in bits[1:]:
        half = normed_one_grad.shape[0] // 2
        came = swap(normed_one_grad[half:].astype(low_type), narrow, bit)
        normed_one_grad = normed_one_grad[:half] + came.astype(jnp.float32)
    input_norm_grad, attn_gain_grad = norm_backward(
        own_rows, scale_one, rescaling_coefficients[0], normed_one_grad
    )
    input_own = mid_grad + input_norm_grad
    sums = lax.all_gather(after(own_part, input_own), wide, axis=0, tiled=True)
    input_grad = natural_rows(join_rows(input_own.astype(low_type), narrow), places).astype(jnp.float32)

    result_pieces = {}
    for peer, rows in zip([0] + bits[1:], result_even):
        result_pieces[peer], result_pieces[peer + 1] = rows, swap(rows, narrow, 1)
    layer_result = natural_rows(
        jnp.concatenate([result_pieces[peer] for peer in order], axis=0), places
    ).astype(jnp.float32)

    bias_size = offset_bias_slope.size
    squares = jnp.sum(jnp.square(own_part.astype(jnp.float32))) + proj_owner * jnp.sum(
        jnp.square(proj_weight_grad)
    )
    small = jnp.stack(
        [
            ffn_gain_grad,
            attn_gain_grad,
            jnp.pad(offset_bias_slope.reshape(bias_size), (0, D - bias_size)),
            jnp.broadcast_to(squares, (D,)),
        ]
    )
    small_all = spread(small, everyone).reshape(wide_count, narrow_count, 4, D)
    gain_sums = jnp.sum(small_all[:, :, :2], axis=(0, 1))
    gain_total = jnp.stack([gain_sums[1], gain_sums[0], final_gain_grad[0]])
    bias_all = jnp.sum(small_all[:, :, 2], axis=0)
    square_terms = small_all[:, :, 3, 0]
    bias_total = lax.dynamic_index_in_dim(bias_all, narrow_index, 0, keepdims=False)[
        :bias_size
    ].reshape(offset_bias_slope.shape)
    sums, proj_weight_grad, square_terms, *_ = lax.optimization_barrier(
        (sums, proj_weight_grad, square_terms, input_grad, layer_result, gain_total, bias_total)
    )
    sums = sums.reshape(ffn_units, wide_count // ffn_units, 3, part_rows, D)
    slot_grads = []
    for slot in range(CAP):
        unit, row, column = units[3 * slot : 3 * slot + 3]
        low_sum = lax.dynamic_slice(
            sums, (row, 0, column, 0, 0), (1, wide_count // ffn_units, 1, part_rows, D)
        ).reshape(unit_rows, D)
        low_sum = jnp.where(unit == 4, proj_weight_grad, low_sum.astype(jnp.float32))
        slot_grads.append(jnp.where(unit >= 0, low_sum, 0.0))
    slot_grads = jnp.stack(slot_grads)
    grad_norm = jnp.sqrt(
        jnp.sum(square_terms)
        + jnp.sum(gain_total * gain_total)
        + jnp.sum(bias_all * bias_all)
        + jnp.sum(sharpness_total * sharpness_total)
    )
    multiplier = jnp.minimum(1.0, clip_limit / grad_norm)
    slot_first, slot_second, slot_weight = decoupled_decay_step(
        slot_grads,
        precise_mean_est,
        precise_variance_est,
        precise_parameter_blocks,
        multiplier,
        learn_rate,
    )
    gain_first, gain_second, gain_new = decoupled_decay_step(
        gain_total,
        norm_scale_mean_est,
        norm_scale_variance_est,
        rescaling_coefficients,
        multiplier,
        side_rate,
    )
    bias_first, bias_second, bias_new = decoupled_decay_step(
        bias_total,
        offset_bias_mean_est,
        offset_bias_variance_est,
        distance_bias_table,
        multiplier,
        side_rate,
    )
    sharpness_mean_fresh, sharpness_variance_fresh, sharpness_exponent_fresh = decoupled_decay_step(
        sharpness_total,
        sharpness_mean_est,
        sharpness_variance_est,
        sharpness_exponent,
        multiplier,
        learn_rate,
    )
    return (
        loss,
        layer_result,
        input_grad,
        grad_norm,
        slot_first,
        slot_second,
        slot_weight,
        gain_first,
        gain_second,
        gain_new,
        bias_first,
        bias_second,
        bias_new,
        sharpness_mean_fresh,
        sharpness_variance_fresh,
        sharpness_exponent_fresh,
    )


def solution(mesh):
    wide, narrow, far, near = ("wide",), ("narrow",), ("wide",), ()
    if dict(mesh.shape) == {"wide": 8, "narrow": 4}:
        mesh = Mesh(mesh.devices.reshape(4, 2, 2, 2), ("line", "pair", "side", "core"))
        wide, narrow, far, near = ("line", "pair"), ("side", "core"), ("line",), ("pair",)
    whole, rows, blocks, heads = P(), P(wide, None), P(wide, narrow, None), P(None, narrow)
    arguments = (rows, rows, whole, whole, blocks, blocks, blocks, whole, whole, whole)
    arguments += (heads, heads, heads, whole, whole, whole)
    results = (whole, rows, rows, whole, blocks, blocks, blocks, whole, whole, whole)
    results += (heads, heads, heads, whole, whole, whole)

    def body(*arrays):
        return on_device((wide, narrow, far, near), *arrays)

    return jax.shard_map(
        body, mesh=mesh, in_specs=arguments, out_specs=results, check_vma=False
    )
```

```python
import jax
import jax.numpy as jnp
from jax import lax
from jax.experimental import pallas as pl
from jax.experimental.pallas import tpu as pltpu
from jax.sharding import Mesh
from jax.sharding import PartitionSpec as P

D = 768
FF = 3072
BUCKETS = 32
TOK_DEV = 2560
SEQS_DEV = 4
DOCLEN = 1024
CAP = 2
STEP = 10
LANE = 128
BQ = 512
BK = 512
UNIT_BLOCK = 768
REACH = DOCLEN // LANE
OFF = REACH + (BQ + BK) // LANE
SPAN = 2 * OFF + 1
LINES = 2 * REACH + 2
VMEM_LIMIT = 56 * 1024 * 1024

norm_eps = 1e-06
clip_limit = 0.01
learn_rate = 0.01
side_rate = 0.5
beta_one = 0.5
beta_two = 0.5
adam_eps = 1e-08
decay_rate = 0.01
score_scale = 0.125
masked_score = -1e30
low_type = jnp.bfloat16


def times_transposed(left_side, right_side):
    return lax.dot_general(
        left_side, right_side, (((1,), (1,)), ((), ())), preferred_element_type=jnp.float32
    )


def plain_product(left_side, right_side):
    return jnp.dot(left_side, right_side, preferred_element_type=jnp.float32)


def outer_product(left_side, right_side):
    return lax.dot_general(
        left_side, right_side, (((0,), (0,)), ((), ())), preferred_element_type=jnp.float32
    )


def rms_scale(values):
    return lax.rsqrt(jnp.mean(values * values, axis=-1, keepdims=True) + norm_eps)


def norm_backward(values, row_scale, gain_row, grad_out):
    weighted = grad_out * gain_row
    gain_grad = jnp.sum(grad_out * values * row_scale, axis=0)
    inner_mean = jnp.mean(weighted * values, axis=-1, keepdims=True)
    value_grad = row_scale * weighted - values * row_scale * row_scale * row_scale * inner_mean
    return (value_grad, gain_grad)


def decoupled_decay_step(gradient, first_moment, second_moment, weight, multiplier, step_rate):
    clipped = gradient * multiplier
    first_new = beta_one * first_moment + (1.0 - beta_one) * clipped
    second_new = beta_two * second_moment + (1.0 - beta_two) * clipped * clipped
    first_hat = first_new / (1.0 - beta_one**STEP)
    second_hat = second_new / (1.0 - beta_two**STEP)
    weight_new = weight - step_rate * (
        first_hat / (jnp.sqrt(second_hat) + adam_eps) + decay_rate * weight
    )
    return (first_new, second_new, weight_new)


def swap(values, axes, bit):
    count = lax.axis_size(axes)
    return lax.ppermute(values, axes, [(i, i ^ bit) for i in range(count)])


def sum_low(left, right):
    return (left.astype(jnp.float32) + right.astype(jnp.float32)).astype(low_type)


def narrow_bits(count):
    return [1 << s for s in range(count.bit_length() - 1)]


def peer_order(count):
    order = [0]
    for bit in reversed(narrow_bits(count)):
        order = order + [peer ^ bit for peer in order]
    return order


def join_rows(values, axes):
    for bit in reversed(narrow_bits(lax.axis_size(axes))):
        values = jnp.concatenate([values, swap(values, axes, bit)], axis=0)
    return values


def add_rows(values, axes):
    for bit in narrow_bits(lax.axis_size(axes)):
        half = values.shape[0] // 2
        came = swap(values[half:].astype(low_type), axes, bit)
        values = values[:half].astype(jnp.float32) + came.astype(jnp.float32)
    return values


def product_add_rows(left_side, right_side, axes):
    bits = narrow_bits(lax.axis_size(axes))
    half = left_side.shape[0] // 2
    sent = plain_product(left_side[half:], right_side).astype(low_type)
    came = swap(sent, axes, bits[0])
    values = plain_product(left_side[:half], right_side) + came.astype(jnp.float32)
    for bit in bits[1:]:
        half = values.shape[0] // 2
        came = swap(values[half:].astype(low_type), axes, bit)
        values = values[:half] + came.astype(jnp.float32)
    return values


def natural_rows(joined, places):
    group = joined.shape[0] // len(places)
    return jnp.concatenate(
        [lax.dynamic_slice_in_dim(joined, place * group, group, 0) for place in places], axis=0
    )


def spread(values, axes):
    copies = jnp.broadcast_to(values[None], (lax.axis_size(axes),) + values.shape)
    return lax.all_to_all(copies, axes, split_axis=0, concat_axis=0, tiled=True)


def after(values, other):
    return lax.optimization_barrier((values, other))[0]


def gelu_and_slope(values):
    rate = 0.7978845608028654
    cubic = 0.044715
    squares = values * values
    turn = jnp.tanh(rate * values * (1.0 + cubic * squares))
    half = 0.5 * (1.0 + turn)
    slope = half + 0.5 * values * (1.0 - turn * turn) * (rate * (1.0 + 3.0 * cubic * squares))
    return (values * half).astype(low_type), slope.astype(low_type)


def smem():
    return pl.BlockSpec(memory_space=pltpu.SMEM)


def vmem():
    return pl.BlockSpec(memory_space=pltpu.VMEM)


def bias_kernel(chunks, tiles):
    heads = tiles.shape[0]
    tiles[...] = jnp.zeros_like(tiles)
    for h in range(heads):
        for d in range(-REACH, REACH + 1):
            left = chunks[h, REACH + 1 - d : REACH + 2 - d, :]
            right = chunks[h, REACH - d : REACH + 1 - d, :]
            line = jnp.broadcast_to(jnp.concatenate([left, right], axis=1), (LANE, 2 * LANE))
            rolled = pltpu.roll(line, 0, 1, stride=1, stride_axis=0)
            tiles[h, (d + OFF) * LANE : (d + OFF + 1) * LANE, :] = rolled[:, :LANE]


def bias_tiles(rel_chunks):
    heads = rel_chunks.shape[0]
    return pl.pallas_call(
        bias_kernel,
        out_shape=jax.ShapeDtypeStruct((heads, SPAN * LANE, LANE), jnp.float32),
        compiler_params=pltpu.CompilerParams(vmem_limit_bytes=VMEM_LIMIT),
        name="bias_tiles",
    )(rel_chunks)


def key_range(lengths, first, last):
    start = jnp.int32(0)
    low = jnp.int32(0)
    high = jnp.int32(0)
    for s in range(SEQS_DEV):
        end = start + lengths[s]
        low = jnp.where(start <= first, start, low)
        high = jnp.where(start <= last, end, high)
        start = end
    return low // BK, (high + BK - 1) // BK


def bias_part(bias, h, row):
    return jnp.concatenate(
        [
            bias[h, pl.ds(pl.multiple_of(row - b * LANE, LANE), BK), :]
            for b in range(BQ // LANE)
        ],
        axis=1,
    )


def forward_kernel(first_row, lengths, origin, qT, kn, vT, apart, bias, ctx_o, ctxT_o, lse_o, qa, acc):
    width, rows_here = qT.shape
    heads = bias.shape[0]
    size = width // heads
    qa[...] = jnp.zeros_like(qa)

    @pl.loop(0, rows_here // BQ)
    def _(i):
        q0 = pl.multiple_of(i * BQ, BQ)
        here = pl.ds(q0, BQ)
        for h in range(heads):
            qa[h * LANE : h * LANE + size, :] = qT[h * size : (h + 1) * size, here]
            qa[h * LANE + size : h * LANE + size + 16, :] = apart[:, here]
        acc[...] = jnp.zeros_like(acc)
        low, high = key_range(lengths, first_row + q0, first_row + q0 + BQ - 1)

        def step(j, carry):
            k0 = pl.multiple_of(j * BK, BK)
            row = (j * (BK // LANE) - i * (BQ // LANE) - first_row // LANE + OFF) * LANE
            out = []
            for h in range(heads):
                top, total = carry[2 * h], carry[2 * h + 1]
                own = slice(h * LANE, (h + 1) * LANE)
                rows = slice(h * size, (h + 1) * size)
                s = plain_product(kn[pl.ds(k0, BK), own], qa[own, :]) + bias_part(bias, h, row)
                new_top = jnp.maximum(top, jnp.max(s, axis=0, keepdims=True))
                fade = jnp.exp(top - new_top)
                p = jnp.exp(s - new_top)
                total = total * fade + jnp.sum(p, axis=0, keepdims=True)
                acc[rows, :] = acc[rows, :] * fade + plain_product(
                    vT[rows, pl.ds(k0, BK)], p.astype(low_type)
                )
                out += [new_top, total]
            return tuple(out)

        init = tuple(
            jnp.full((1, BQ), 2.0 * masked_score if n % 2 == 0 else 0.0, jnp.float32)
            for n in range(2 * heads)
        )
        done = lax.fori_loop(low, high, step, init)
        for h in range(heads):
            rows = slice(h * size, (h + 1) * size)
            acc[rows, :] = acc[rows, :] / done[2 * h + 1]
            lse_o[h : h + 1, here] = done[2 * h] + jnp.log(done[2 * h + 1])
        ctxT_o[:, here] = acc[...]
        turned = acc[...].T.astype(low_type)
        for b in range(BQ // LANE):
            at = pl.multiple_of(origin[i * (BQ // LANE) + b], LANE)
            ctx_o[pl.ds(at, LANE), :] = turned[b * LANE : (b + 1) * LANE, :]


def attention_forward(first_row, lengths, origin, qT, kn, vT, apart, bias):
    width, rows_here = qT.shape
    heads = bias.shape[0]

    def body(*refs):
        forward_kernel(first_row, *refs)

    return pl.pallas_call(
        body,
        out_shape=(
            jax.ShapeDtypeStruct((rows_here, width), low_type),
            jax.ShapeDtypeStruct((width, rows_here), jnp.float32),
            jax.ShapeDtypeStruct((heads, rows_here), jnp.float32),
        ),
        in_specs=[smem()] * 2 + [vmem()] * 5,
        out_specs=(vmem(),) * 3,
        scratch_shapes=[
            pltpu.VMEM((heads * LANE, BQ), low_type),
            pltpu.VMEM((width, BQ), jnp.float32),
        ],
        compiler_params=pltpu.CompilerParams(vmem_limit_bytes=VMEM_LIMIT),
        cost_estimate=pl.CostEstimate(
            flops=rows_here * width, bytes_accessed=width * TOK_DEV, transcendentals=0
        ),
        name="attention_forward",
    )(lengths, origin, qT, kn, vT, apart, bias)


def three_parts(values):
    first = values.astype(low_type).astype(jnp.float32)
    rest = values - first
    second = rest.astype(low_type).astype(jnp.float32)
    return first, second, rest - second


def backward_kernel(
    lengths, origin, qT, kn, vn, kT, dcn, ctxT, lse, apart, bias,
    dT_o, dn_o, lines_o, qa, da, dq, dk, dv, tiles,
):
    width, tokens = qT.shape
    heads = bias.shape[0]
    size = width // heads
    for ref in (qa, da, dk, dv, tiles):
        ref[...] = jnp.zeros_like(ref)
    place = lax.broadcasted_iota(jnp.int32, (16, BQ), 0) - SEQS_DEV

    def in_depth(values):
        a, b, c = three_parts(values)
        return jnp.where(place == 0, a, jnp.where(place == 1, b, jnp.where(place == 2, c, 0.0)))

    @pl.loop(0, tokens // BQ)
    def _(i):
        q0 = pl.multiple_of(i * BQ, BQ)
        here = pl.ds(q0, BQ)
        at = [pl.multiple_of(origin[i * (BQ // LANE) + b], LANE) for b in range(BQ // LANE)]
        dcT = jnp.concatenate(
            [dcn[pl.ds(at[b], LANE), :].astype(jnp.float32) for b in range(BQ // LANE)], axis=0
        ).T
        for h in range(heads):
            rows = slice(h * size, (h + 1) * size)
            top = h * LANE
            qa[top : top + size, :] = qT[rows, here]
            extra = apart[:, here].astype(jnp.float32) + in_depth(-lse[h : h + 1, here])
            qa[top + size : top + size + 16, :] = extra.astype(low_type)
            da[top : top + size, :] = dcT[rows, :].astype(low_type)
            delta = jnp.sum(dcT[rows, :] * ctxT[rows, here], axis=0, keepdims=True)
            da[top + size : top + size + 16, :] = in_depth(-delta).astype(low_type)
        dq[...] = jnp.zeros_like(dq)
        low, high = key_range(lengths, q0, q0 + BQ - 1)

        @pl.loop(low, high)
        def _(j):
            k0 = pl.multiple_of(j * BK, BK)
            there = pl.ds(k0, BK)
            row = (j * (BK // LANE) - i * (BQ // LANE) + OFF) * LANE
            for h in range(heads):
                rows = slice(h * size, (h + 1) * size)
                own = slice(h * LANE, (h + 1) * LANE)
                flat = slice(h * LANE, h * LANE + size)
                s = plain_product(kn[there, own], qa[own, :])
                p = jnp.exp(s + bias_part(bias, h, row))
                ds = p * plain_product(vn[there, own], da[own, :])
                for b in range(BQ // LANE):
                    window = pl.ds(pl.multiple_of(row - b * LANE, LANE), BK)
                    tiles[h, window, :] = (
                        tiles[h, window, :] + ds[:, b * LANE : (b + 1) * LANE]
                    )
                p_low = p.astype(low_type)
                ds_low = ds.astype(low_type)
                dv[rows, there] = dv[rows, there] + times_transposed(da[flat, :], p_low)
                dk[rows, there] = dk[rows, there] + times_transposed(qa[flat, :], ds_low)
                dq[rows, :] = dq[rows, :] + plain_product(kT[rows, there], ds_low)

        grad = dq[...] * score_scale
        dT_o[0:width, here] = grad.astype(low_type)
        turned = grad.T.astype(low_type)
        for b in range(BQ // LANE):
            dn_o[pl.ds(at[b], LANE), 0:width] = turned[b * LANE : (b + 1) * LANE, :]

    @pl.loop(0, tokens // BQ)
    def _(i):
        here = pl.ds(pl.multiple_of(i * BQ, BQ), BQ)
        both = jnp.concatenate([dk[:, here], dv[:, here]], axis=0)
        dT_o[width : 3 * width, here] = both.astype(low_type)
        turned = both.T.astype(low_type)
        for b in range(BQ // LANE):
            at = pl.multiple_of(origin[i * (BQ // LANE) + b], LANE)
            dn_o[pl.ds(at, LANE), width : 3 * width] = turned[b * LANE : (b + 1) * LANE, :]

    across = lax.broadcasted_iota(jnp.int32, (LANE, LANE), 1)
    over = across >= lax.broadcasted_iota(jnp.int32, (LANE, LANE), 0)
    sub = lax.broadcasted_iota(jnp.int32, (8, LANE), 0)
    for h in range(heads):
        for d in range(-REACH, REACH + 2):
            here = tiles[h, (d + OFF) * LANE : (d + OFF + 1) * LANE, :]
            below = tiles[h, (d + OFF - 1) * LANE : (d + OFF) * LANE, :]
            mixed = jnp.where(over, here, below)
            line = mixed[LANE - 8 :, :]
            for g in range(LANE // 8 - 2, -1, -1):
                line = mixed[8 * g : 8 * g + 8, :] + pltpu.roll(line, LANE - 8, 1)
            for bit in (1, 2, 4):
                line = jnp.where((sub & bit) != 0, pltpu.roll(line, LANE - bit, 1), line)
            lines_o[h, REACH + 1 - d : REACH + 2 - d, :] = jnp.sum(line, axis=0, keepdims=True)


def attention_backward(lengths, origin, qT, kn, vn, kT, dcn, ctxT, lse, apart, bias):
    width, tokens = qT.shape
    heads = bias.shape[0]
    return pl.pallas_call(
        backward_kernel,
        out_shape=(
            jax.ShapeDtypeStruct((3 * width, tokens), low_type),
            jax.ShapeDtypeStruct((tokens, 3 * width), low_type),
            jax.ShapeDtypeStruct((heads, LINES, LANE), jnp.float32),
        ),
        in_specs=[smem()] * 2 + [vmem()] * 9,
        out_specs=(vmem(),) * 3,
        scratch_shapes=[
            pltpu.VMEM((heads * LANE, BQ), low_type),
            pltpu.VMEM((heads * LANE, BQ), low_type),
            pltpu.VMEM((width, BQ), jnp.float32),
            pltpu.VMEM((width, tokens), jnp.float32),
            pltpu.VMEM((width, tokens), jnp.float32),
            pltpu.VMEM((heads, SPAN * LANE, LANE), jnp.float32),
        ],
        compiler_params=pltpu.CompilerParams(vmem_limit_bytes=VMEM_LIMIT),
        cost_estimate=pl.CostEstimate(
            flops=tokens * width, bytes_accessed=width * TOK_DEV, transcendentals=0
        ),
        name="attention_backward",
    )(lengths, origin, qT, kn, vn, kT, dcn, ctxT, lse, apart, bias)


def feed_forward_backward_kernel(
    grad, rows, hidden, slope, inner, outer, weight_grads, rows_grad
):
    groups, _, size, width = weight_grads.shape

    @pl.when(pl.program_id(0) == 0)
    def _():
        rows_grad[...] = jnp.zeros_like(rows_grad)

    outer_grad = outer_product(hidden[...], grad[...]).astype(low_type)
    weight_grads[:, 0] = outer_grad.reshape(groups, size, width)
    pre = (
        times_transposed(grad[...], outer[...]) * slope[...].astype(jnp.float32)
    ).astype(low_type)
    inner_grad = outer_product(pre, rows[...]).astype(low_type)
    weight_grads[:, 1] = inner_grad.reshape(groups, size, width)
    rows_grad[...] += plain_product(pre, inner[...])


def feed_forward_backward(grad, rows, hidden, slope, inner, outer, size):
    count = grad.shape[0]
    groups = UNIT_BLOCK // size
    every = pl.BlockSpec((count, D), lambda i: (0, 0))
    units = pl.BlockSpec((count, UNIT_BLOCK), lambda i: (0, i))
    weight = pl.BlockSpec((UNIT_BLOCK, D), lambda i: (i, 0))
    return pl.pallas_call(
        feed_forward_backward_kernel,
        grid=(FF // UNIT_BLOCK,),
        out_shape=(
            jax.ShapeDtypeStruct((FF // size, 2, size, D), low_type),
            jax.ShapeDtypeStruct((count, D), jnp.float32),
        ),
        in_specs=[every, every, units, units, weight, weight],
        out_specs=(pl.BlockSpec((groups, 2, size, D), lambda i: (i, 0, 0, 0)), every),
        compiler_params=pltpu.CompilerParams(vmem_limit_bytes=VMEM_LIMIT),
        cost_estimate=pl.CostEstimate(flops=FF * D, bytes_accessed=FF * D, transcendentals=0),
        name="feed_forward_backward",
    )(grad, rows, hidden, slope, inner, outer)


def loss_kernel(place, numbers, parts, proj_weight, gain, out_slope, out_low, out_row, out_gain):
    total_seqs = out_low.shape[0] // 2
    terms = parts.shape[0] // total_seqs
    exact = dict(precision=lax.Precision.HIGHEST, preferred_element_type=jnp.float32)
    seq = lax.broadcasted_iota(jnp.int32, (total_seqs, parts.shape[0]), 0)
    part = lax.broadcasted_iota(jnp.int32, (total_seqs, parts.shape[0]), 1)
    joins = jnp.logical_and(
        seq // SEQS_DEV == part // (SEQS_DEV * terms), seq % SEQS_DEV == part % SEQS_DEV
    )
    unscaled = jnp.dot(joins.astype(jnp.float32), parts[...], **exact)
    pooled_low = (unscaled * gain[...]).astype(low_type)
    projected = times_transposed(pooled_low, proj_weight[...]).astype(low_type).astype(jnp.float32)
    inverse = lax.rsqrt(jnp.sum(projected * projected, axis=1, keepdims=True) + norm_eps)
    embed_low = (projected * inverse).astype(low_type)
    sharpness_factor = jnp.exp(jnp.full((1, 1), numbers[0], jnp.float32))
    agreement = times_transposed(embed_low, embed_low)
    row = lax.broadcasted_iota(jnp.int32, (total_seqs, total_seqs), 0)
    column = lax.broadcasted_iota(jnp.int32, (total_seqs, total_seqs), 1)
    logits = jnp.where(row == column, masked_score, sharpness_factor * agreement)
    partner = (row ^ 1) == column

    def log_sum(axis):
        top = jnp.max(logits, axis=axis, keepdims=True)
        return top + jnp.log(jnp.sum(jnp.exp(logits - top), axis=axis, keepdims=True))

    log_rows = log_sum(1)
    positive = jnp.where(partner, 1.0, 0.0)
    slope = (jnp.exp(logits - log_rows) - positive) / total_seqs
    slope_turned = (jnp.exp(logits - log_sum(0)) - positive) / total_seqs
    embed_grad = sharpness_factor * jnp.dot(
        slope + slope_turned, embed_low.astype(jnp.float32), **exact
    )
    along = jnp.sum(projected * embed_grad, axis=1, keepdims=True)
    proj_grad_low = (
        inverse * embed_grad - projected * inverse * inverse * inverse * along
    ).astype(low_type)
    pooled_grad = plain_product(proj_grad_low, proj_weight[...])
    out_low[0:total_seqs, :] = proj_grad_low
    out_low[total_seqs : 2 * total_seqs, :] = pooled_low
    out_gain[...] = jnp.sum(pooled_grad * unscaled, axis=0, keepdims=True)
    loss = jnp.sum(
        log_rows - jnp.sum(positive * jnp.where(partner, logits, 0.0), axis=1, keepdims=True),
        axis=0,
        keepdims=True,
    ) / total_seqs
    temperature = sharpness_factor * jnp.sum(
        jnp.sum(slope * agreement, axis=1, keepdims=True), axis=0, keepdims=True
    )
    lane = lax.broadcasted_iota(jnp.int32, (1, LANE), 1)
    out_row[...] = jnp.where(lane == 0, loss, jnp.where(lane == 1, temperature, 0.0))
    mine = lax.broadcasted_iota(jnp.int32, (8, total_seqs), 0)
    seq_of = lax.broadcasted_iota(jnp.int32, (8, total_seqs), 1) - place[0] * SEQS_DEV
    picks = jnp.logical_and(mine == seq_of, mine < SEQS_DEV).astype(jnp.float32)
    own = jnp.dot(picks, pooled_grad, **exact)
    index = lax.broadcasted_iota(jnp.int32, (8, 1), 0)
    extent = jnp.ones((8, 1), jnp.float32)
    for s in range(SEQS_DEV):
        extent = jnp.where(index == s, place[1 + s].astype(jnp.float32), extent)
    out_slope[...] = own * gain[...] / extent


def contrastive(place, numbers, parts, proj_weight, gain, total_seqs):
    return pl.pallas_call(
        loss_kernel,
        out_shape=(
            jax.ShapeDtypeStruct((8, D), jnp.float32),
            jax.ShapeDtypeStruct((2 * total_seqs, D), low_type),
            jax.ShapeDtypeStruct((1, LANE), jnp.float32),
            jax.ShapeDtypeStruct((1, D), jnp.float32),
        ),
        in_specs=[smem()] * 2 + [vmem()] * 3,
        out_specs=(vmem(),) * 4,
        compiler_params=pltpu.CompilerParams(vmem_limit_bytes=VMEM_LIMIT),
        cost_estimate=pl.CostEstimate(
            flops=4 * total_seqs * D * D, bytes_accessed=4 * D * D, transcendentals=total_seqs
        ),
        name="contrastive",
    )(place, numbers, parts, proj_weight, gain)


def on_device(
    axes,
    layer_argument,
    document_extents,
    distance_bin_lookup,
    tile_location,
    precise_parameter_blocks,
    precise_mean_est,
    precise_variance_est,
    rescaling_coefficients,
    norm_scale_mean_est,
    norm_scale_variance_est,
    distance_bias_table,
    offset_bias_mean_est,
    offset_bias_variance_est,
    sharpness_exponent,
    sharpness_mean_est,
    sharpness_variance_est,
):
    wide, narrow, far, near = axes
    everyone = wide + narrow
    near_axes = near + narrow
    wide_count = lax.axis_size(wide)
    narrow_count = lax.axis_size(narrow)
    far_count = lax.axis_size(far)
    near_count = wide_count // far_count
    wide_index = lax.axis_index(wide)
    narrow_index = lax.axis_index(narrow)
    bits = narrow_bits(narrow_count)
    order = peer_order(narrow_count)
    place_of = jnp.array([order.index(peer) for peer in range(narrow_count)], jnp.int32)
    unit_rows = precise_parameter_blocks.shape[1]
    heads_here = distance_bias_table.shape[1]
    head_size = unit_rows // heads_here
    ffn_units = FF // D
    group = TOK_DEV // narrow_count
    own_slots = wide_index * CAP + jnp.arange(CAP, dtype=jnp.int32)

    every_slot = lax.all_gather(
        precise_parameter_blocks.astype(low_type), wide, axis=0, tiled=True
    )

    def block(u):
        return lax.dynamic_index_in_dim(every_slot, tile_location[u], 0, keepdims=False)

    qkv_weight = jnp.concatenate([block(u) for u in range(3)], axis=0)

    part_rows = D // wide_count

    def unit_order(first_unit):
        rows = jnp.concatenate([block(first_unit + k) for k in range(ffn_units)], axis=0)
        rows = rows.reshape(far_count, near_count, part_rows, D)
        return jnp.swapaxes(rows, 0, 1).reshape(near_count, far_count * part_rows, D)

    crossing = [unit_order(5), block(3), unit_order(5 + ffn_units)]
    for rows in crossing:
        qkv_weight = after(qkv_weight, rows)

    near_index = wide_index % near_count

    def fetch(rows, peer, in_parts):
        if in_parts:
            rows = lax.dynamic_index_in_dim(rows, near_index, 0)
        return swap(rows, narrow, peer)

    evens = bits[1:]
    fetched = [
        [fetch(rows, peer, in_parts) for peer in evens]
        for rows, in_parts in zip(crossing, (True, False, True))
    ]

    def exchanged(pieces):
        return [
            [(near_index, rows)]
            + [(near_index ^ step, swap(rows, near, step)) for step in range(1, near_count)]
            for rows in pieces
        ]

    lengths = document_extents[0]
    seq_ends = jnp.cumsum(lengths)
    positions = jnp.arange(TOK_DEV, dtype=jnp.int32)

    def segments_of(where):
        return jnp.sum((seq_ends[None, :] <= where[:, None]).astype(jnp.int32), axis=1)

    segment_ids = segments_of(positions)
    own_segments = segments_of(narrow_index * group + positions[:group])
    tile_starts = jnp.arange(TOK_DEV // LANE, dtype=jnp.int32) * LANE
    origin = place_of[(tile_starts // group) ^ narrow_index] * group + tile_starts % group

    units = []
    for slot in range(CAP):
        here = tile_location == own_slots[slot]
        unit = jnp.sum(jnp.where(here, jnp.arange(1, here.shape[0] + 1, dtype=jnp.int32), 0)) - 1
        early_unit = jnp.maximum(unit - 5, 0)
        row = jnp.where(unit >= 5, early_unit % ffn_units, jnp.clip(unit, 0, ffn_units - 1))
        column = jnp.where(unit >= 5, 1 - early_unit // ffn_units, 2)
        units += [unit, row, column]
    proj_owner = (tile_location[4] // CAP == wide_index).astype(jnp.float32)
    places = [place_of[g ^ narrow_index] for g in range(narrow_count)]

    beyond = LINES * LANE - LANE - 1 - distance_bin_lookup.shape[0]
    offsets_down = jnp.pad(distance_bin_lookup[::-1], (LANE + 1, beyond), constant_values=-1)
    bucket_onehot = (
        offsets_down[:, None] == jnp.arange(BUCKETS, dtype=jnp.int32)[None, :]
    ).astype(jnp.float32)
    rel_values = jnp.dot(bucket_onehot, distance_bias_table, precision=lax.Precision.HIGHEST).T
    rel_values, origin, proj_owner, *scalars = lax.optimization_barrier(
        (rel_values, origin, proj_owner, *units, *places)
    )
    units, places = scalars[: len(units)], scalars[len(units) :]
    tiles_bias = bias_tiles(rel_values.reshape(heads_here, LINES, LANE))

    all_rows = layer_argument.astype(jnp.float32)
    normed_one = (all_rows * rms_scale(all_rows) * rescaling_coefficients[0]).astype(low_type)
    transposed_rows = times_transposed(qkv_weight, normed_one)
    query_cols = (transposed_rows[:unit_rows] * score_scale).astype(low_type)
    key_cols = transposed_rows[unit_rows : 2 * unit_rows].astype(low_type)
    value_cols = transposed_rows[2 * unit_rows :].astype(low_type)
    spread_weight = jnp.pad(
        qkv_weight[unit_rows:].reshape(2 * heads_here, head_size, D),
        ((0, 0), (0, LANE - head_size), (0, 0)),
    ).reshape(2 * heads_here * LANE, D)
    lane_place = jnp.arange(2 * heads_here * LANE, dtype=jnp.int32) % LANE - head_size
    marks = jnp.logical_or(
        lane_place[None, :] == segment_ids[:, None],
        jnp.logical_and(lane_place >= SEQS_DEV, lane_place < SEQS_DEV + 3)[None, :],
    )
    key_value_rows = (
        times_transposed(normed_one, spread_weight) + marks.astype(jnp.float32)
    ).astype(low_type)
    key_rows = key_value_rows[:, : heads_here * LANE]
    value_rows = key_value_rows[:, heads_here * LANE :]
    row_place = jnp.arange(16, dtype=jnp.int32)[:, None]
    apart = jnp.where(
        jnp.logical_and(row_place < SEQS_DEV, row_place != segment_ids[None, :]), masked_score, 0.0
    ).astype(low_type)
    inner_parts = exchanged(fetched[0])
    query_cols = after(query_cols, fetched[0][0])
    context, context_cols, log_rows = attention_forward(
        0, lengths, origin, query_cols, key_rows, value_cols, apart, tiles_bias
    )

    flat = [rows for pieces in fetched[1:] for rows in pieces]
    inner_flat = [rows for parts in inner_parts for _, rows in parts]
    context, *flat = lax.optimization_barrier((context, *flat, *inner_flat))
    inner_rows = iter(flat[2 * len(evens) :])
    inner_parts = [[(index, next(inner_rows)) for index, _ in parts] for parts in inner_parts]
    outer_parts = exchanged(flat[len(evens) : 2 * len(evens)])

    def in_unit_order(own, parts_of_peers):
        whole = jnp.zeros((near_count, narrow_count, far_count * part_rows, D), low_type)
        pieces = [(0, 0, own), (1, 0, swap(own, narrow, 1))]
        for peer, parts in zip(evens, parts_of_peers):
            for index, rows in parts:
                pieces += [(peer, index, rows), (peer + 1, index, swap(rows, narrow, 1))]
        for peer, index, rows in pieces:
            start = (index, narrow_index ^ peer, 0, 0)
            whole = lax.dynamic_update_slice(whole, rows[:, None], start)
        return whole.reshape(FF, D)

    out_pieces = {0: crossing[1], 1: swap(crossing[1], narrow, 1)}
    for peer, rows in zip(evens, flat[: len(evens)]):
        out_pieces[peer], out_pieces[peer + 1] = rows, swap(rows, narrow, 1)
    out_joined = jnp.concatenate([out_pieces[peer] for peer in order], axis=0)
    inner_joined = in_unit_order(crossing[0], inner_parts)
    outer_joined = in_unit_order(crossing[2], outer_parts)

    def to_peer(values, peer):
        if peer == 0:
            return values
        return swap(values, narrow, peer)

    context_own = jnp.concatenate(
        [
            to_peer(context[s * group : (s + 1) * group], peer)
            for s, peer in enumerate(order)
        ],
        axis=1,
    )
    own_rows = lax.dynamic_slice_in_dim(layer_argument, narrow_index * group, group, 0).astype(
        jnp.float32
    )
    scale_one = rms_scale(own_rows)
    residual_mid = own_rows + plain_product(context_own, out_joined)
    scale_two = rms_scale(residual_mid)
    normed_two = (residual_mid * scale_two * rescaling_coefficients[1]).astype(low_type)

    hidden_low, hidden_slope = gelu_and_slope(times_transposed(normed_two, inner_joined))
    proj_rows = after(block(4), normed_two)
    for bit in reversed(bits):
        came = after(swap(proj_rows, narrow, bit), hidden_low)
        proj_rows = jnp.concatenate([proj_rows, came], axis=0)
    proj_weight = natural_rows(proj_rows, places)
    result_own = residual_mid + plain_product(hidden_low, outer_joined)
    result_low = result_own.astype(low_type)

    scale_three = rms_scale(result_own)
    member = (
        own_segments[None, :] == jnp.arange(SEQS_DEV, dtype=jnp.int32)[:, None]
    ).astype(jnp.float32)
    length_values = lengths.astype(jnp.float32)[:, None]
    unscaled_part = (
        jnp.dot(member, result_own * scale_three, precision=lax.Precision.HIGHEST) / length_values
    )
    total_seqs = wide_count * SEQS_DEV
    own_pooled_grad, loss_low, loss_row, final_gain_grad = contrastive(
        jnp.concatenate([wide_index.reshape(1), lengths]),
        sharpness_exponent,
        spread(unscaled_part, everyone).reshape(total_seqs * narrow_count, D),
        proj_weight,
        rescaling_coefficients[2:3],
        total_seqs,
    )
    loss = loss_row[0, 0]
    sharpness_total = loss_row[0, 1:2]
    proj_grad_own = lax.dynamic_slice_in_dim(
        loss_low[:total_seqs], narrow_index * unit_rows, unit_rows, 1
    )
    proj_weight_grad = outer_product(proj_grad_own, loss_low[total_seqs:])

    weighted = own_pooled_grad[SEQS_DEV - 1]
    for s in range(SEQS_DEV - 2, -1, -1):
        weighted = jnp.where((own_segments == s)[:, None], own_pooled_grad[s], weighted)
    inner_mean = jnp.mean(weighted * result_own, axis=-1, keepdims=True)
    encoded_grad = scale_three * weighted - result_own * (
        scale_three * scale_three * scale_three * inner_mean
    )
    ffn_grad_low = encoded_grad.astype(low_type)
    group_rows = part_rows if part_rows % 16 == 0 else D
    weight_grads, normed_two_grad = feed_forward_backward(
        ffn_grad_low,
        normed_two,
        hidden_low,
        hidden_slope,
        inner_joined,
        outer_joined,
        group_rows,
    )
    near_part = lax.psum_scatter(
        weight_grads.reshape(2 * FF, D), near_axes, scatter_dimension=0, tiled=True
    )
    mid_norm_grad, ffn_gain_grad = norm_backward(
        residual_mid, scale_two, rescaling_coefficients[1], normed_two_grad
    )
    mid_grad = encoded_grad + mid_norm_grad
    attn_grad_low = mid_grad.astype(low_type)

    context_grad_own = times_transposed(attn_grad_low, out_joined).astype(low_type)
    context_grad = [
        to_peer(context_grad_own[:, s * unit_rows : (s + 1) * unit_rows], peer)
        for s, peer in enumerate(order)
    ]
    attn_grad_low = after(attn_grad_low, context_grad_own)
    out_kept = outer_product(context_own, attn_grad_low).astype(low_type)
    for bit in bits:
        half = out_kept.shape[0] // 2
        out_came = swap(out_kept[half:], narrow, bit)
        if bit == bits[-1]:
            break
        out_kept = sum_low(out_kept[:half], out_came)
    context_grad = after(jnp.concatenate(context_grad, axis=0), out_kept)
    qkv_cols, qkv_rows, bias_lines = attention_backward(
        lengths,
        origin,
        query_cols,
        key_rows,
        value_rows,
        key_cols,
        context_grad,
        context_cols,
        log_rows,
        apart,
        tiles_bias,
    )
    qkv_cols, qkv_rows, out_came = lax.optimization_barrier((qkv_cols, qkv_rows, out_came))
    out_grad = sum_low(out_kept[: out_came.shape[0]], out_came)
    offset_bias_slope = lax.dot_general(
        bucket_onehot,
        bias_lines.reshape(heads_here, LINES * LANE),
        (((0,), (1,)), ((), ())),
        precision=lax.Precision.HIGHEST,
    )

    late = jnp.concatenate(
        [plain_product(qkv_cols, normed_one).astype(low_type), out_grad], axis=0
    ).reshape(far_count, near_count, part_rows, D)
    half = qkv_rows.shape[0] // 2
    rows_sent = plain_product(qkv_rows[half:], qkv_weight).astype(low_type)
    rows_kept = plain_product(qkv_rows[:half], after(qkv_weight, rows_sent))
    late_sum = lax.dynamic_index_in_dim(late, near_index, 1, keepdims=False)
    for peer in range(1, near_count):
        sent = lax.dynamic_index_in_dim(late, near_index ^ peer, 1, keepdims=False)
        late_sum = sum_low(late_sum, after(swap(sent, near, peer), rows_kept))
    early = after(near_part, late).reshape(-1, 2, group_rows // part_rows, part_rows, D)
    early = jnp.swapaxes(early, 1, 2).reshape(far_count, 2, part_rows, D)
    terms = jnp.concatenate([early, late_sum[:, None]], axis=1)
    own_part = lax.psum_scatter(
        terms.reshape(far_count * 3 * part_rows, D), far, scatter_dimension=0, tiled=True
    )
    normed_one_grad = rows_kept + swap(rows_sent, narrow, bits[0]).astype(jnp.float32)
    for bit in bits[1:]:
        half = normed_one_grad.shape[0] // 2
        came = swap(normed_one_grad[half:].astype(low_type), narrow, bit)
        normed_one_grad = normed_one_grad[:half] + came.astype(jnp.float32)
    input_norm_grad, attn_gain_grad = norm_backward(
        own_rows, scale_one, rescaling_coefficients[0], normed_one_grad
    )
    input_own = mid_grad + input_norm_grad
    sums = lax.all_gather(after(own_part, input_own), wide, axis=0, tiled=True)
    bias_size = offset_bias_slope.size
    squares = jnp.sum(jnp.square(own_part.astype(jnp.float32))) + proj_owner * jnp.sum(
        jnp.square(proj_weight_grad)
    )
    small = jnp.stack(
        [
            ffn_gain_grad,
            attn_gain_grad,
            jnp.pad(offset_bias_slope.reshape(bias_size), (0, D - bias_size)),
            jnp.broadcast_to(squares, (D,)),
        ]
    )
    small_all = spread(small, everyone).reshape(wide_count, narrow_count, 4, D)
    def gathered(rows, other):
        for bit in reversed(bits):
            came = swap(rows, narrow, bit)
            if bit == bits[-1]:
                came = after(came, other)
            rows = jnp.concatenate([rows, came], axis=0)
        return natural_rows(rows, places).astype(jnp.float32)

    input_grad = gathered(input_own.astype(low_type), small_all)
    layer_result = gathered(after(result_low, input_own), small_all)
    gain_sums = jnp.sum(small_all[:, :, :2], axis=(0, 1))
    gain_total = jnp.stack([gain_sums[1], gain_sums[0], final_gain_grad[0]])
    bias_all = jnp.sum(small_all[:, :, 2], axis=0)
    square_terms = small_all[:, :, 3, 0]
    bias_total = lax.dynamic_index_in_dim(bias_all, narrow_index, 0, keepdims=False)[
        :bias_size
    ].reshape(offset_bias_slope.shape)
    sums, proj_weight_grad, square_terms, *_ = lax.optimization_barrier(
        (sums, proj_weight_grad, square_terms, input_grad, layer_result, gain_total, bias_total)
    )
    sums = sums.reshape(ffn_units, wide_count // ffn_units, 3, part_rows, D)
    slot_grads = []
    for slot in range(CAP):
        unit, row, column = units[3 * slot : 3 * slot + 3]
        low_sum = lax.dynamic_slice(
            sums, (row, 0, column, 0, 0), (1, wide_count // ffn_units, 1, part_rows, D)
        ).reshape(unit_rows, D)
        low_sum = jnp.where(unit == 4, proj_weight_grad, low_sum.astype(jnp.float32))
        slot_grads.append(jnp.where(unit >= 0, low_sum, 0.0))
    slot_grads = jnp.stack(slot_grads)
    grad_norm = jnp.sqrt(
        jnp.sum(square_terms)
        + jnp.sum(gain_total * gain_total)
        + jnp.sum(bias_all * bias_all)
        + jnp.sum(sharpness_total * sharpness_total)
    )
    multiplier = jnp.minimum(1.0, clip_limit / grad_norm)
    slot_first, slot_second, slot_weight = decoupled_decay_step(
        slot_grads,
        precise_mean_est,
        precise_variance_est,
        precise_parameter_blocks,
        multiplier,
        learn_rate,
    )
    gain_first, gain_second, gain_new = decoupled_decay_step(
        gain_total,
        norm_scale_mean_est,
        norm_scale_variance_est,
        rescaling_coefficients,
        multiplier,
        side_rate,
    )
    bias_first, bias_second, bias_new = decoupled_decay_step(
        bias_total,
        offset_bias_mean_est,
        offset_bias_variance_est,
        distance_bias_table,
        multiplier,
        side_rate,
    )
    sharpness_mean_fresh, sharpness_variance_fresh, sharpness_exponent_fresh = decoupled_decay_step(
        sharpness_total,
        sharpness_mean_est,
        sharpness_variance_est,
        sharpness_exponent,
        multiplier,
        learn_rate,
    )
    return (
        loss,
        layer_result,
        input_grad,
        grad_norm,
        slot_first,
        slot_second,
        slot_weight,
        gain_first,
        gain_second,
        gain_new,
        bias_first,
        bias_second,
        bias_new,
        sharpness_mean_fresh,
        sharpness_variance_fresh,
        sharpness_exponent_fresh,
    )


def solution(mesh):
    wide, narrow, far, near = ("wide",), ("narrow",), ("wide",), ()
    if dict(mesh.shape) == {"wide": 8, "narrow": 4}:
        mesh = Mesh(mesh.devices.reshape(4, 2, 2, 2), ("line", "pair", "side", "core"))
        wide, narrow, far, near = ("line", "pair"), ("side", "core"), ("line",), ("pair",)
    whole, rows, blocks, heads = P(), P(wide, None), P(wide, narrow, None), P(None, narrow)
    arguments = (rows, rows, whole, whole, blocks, blocks, blocks, whole, whole, whole)
    arguments += (heads, heads, heads, whole, whole, whole)
    results = (whole, rows, rows, whole, blocks, blocks, blocks, whole, whole, whole)
    results += (heads, heads, heads, whole, whole, whole)

    def body(*arrays):
        return on_device((wide, narrow, far, near), *arrays)

    return jax.shard_map(
        body, mesh=mesh, in_specs=arguments, out_specs=results, check_vma=False
    )
```

```python
import jax
import jax.numpy as jnp
from jax import lax
from jax.experimental import pallas as pl
from jax.experimental.pallas import tpu as pltpu
from jax.sharding import Mesh
from jax.sharding import PartitionSpec as P

D = 768
FF = 3072
BUCKETS = 32
TOK_DEV = 2560
SEQS_DEV = 4
DOCLEN = 1024
CAP = 2
STEP = 10
LANE = 128
BQ = 512
BK = 512
UNIT_BLOCK = 768
REACH = DOCLEN // LANE
OFF = REACH + (BQ + BK) // LANE
SPAN = 2 * OFF + 1
LINES = 2 * REACH + 2
VMEM_LIMIT = 56 * 1024 * 1024

norm_eps = 1e-06
clip_limit = 0.01
learn_rate = 0.01
side_rate = 0.5
beta_one = 0.5
beta_two = 0.5
adam_eps = 1e-08
decay_rate = 0.01
score_scale = 0.125
masked_score = -1e30
low_type = jnp.bfloat16


def times_transposed(left_side, right_side):
    return lax.dot_general(
        left_side, right_side, (((1,), (1,)), ((), ())), preferred_element_type=jnp.float32
    )


def plain_product(left_side, right_side):
    return jnp.dot(left_side, right_side, preferred_element_type=jnp.float32)


def outer_product(left_side, right_side):
    return lax.dot_general(
        left_side, right_side, (((0,), (0,)), ((), ())), preferred_element_type=jnp.float32
    )


def rms_scale(values):
    return lax.rsqrt(jnp.mean(values * values, axis=-1, keepdims=True) + norm_eps)


def norm_backward(values, row_scale, gain_row, grad_out):
    weighted = grad_out * gain_row
    gain_grad = jnp.sum(grad_out * values * row_scale, axis=0)
    inner_mean = jnp.mean(weighted * values, axis=-1, keepdims=True)
    value_grad = row_scale * weighted - values * row_scale * row_scale * row_scale * inner_mean
    return (value_grad, gain_grad)


def decoupled_decay_step(gradient, first_moment, second_moment, weight, multiplier, step_rate):
    clipped = gradient * multiplier
    first_new = beta_one * first_moment + (1.0 - beta_one) * clipped
    second_new = beta_two * second_moment + (1.0 - beta_two) * clipped * clipped
    first_hat = first_new / (1.0 - beta_one**STEP)
    second_hat = second_new / (1.0 - beta_two**STEP)
    weight_new = weight - step_rate * (
        first_hat / (jnp.sqrt(second_hat) + adam_eps) + decay_rate * weight
    )
    return (first_new, second_new, weight_new)


def swap(values, axes, bit):
    count = lax.axis_size(axes)
    return lax.ppermute(values, axes, [(i, i ^ bit) for i in range(count)])


def sum_low(left, right):
    return (left.astype(jnp.float32) + right.astype(jnp.float32)).astype(low_type)


def narrow_bits(count):
    return [1 << s for s in range(count.bit_length() - 1)]


def peer_order(count):
    order = [0]
    for bit in reversed(narrow_bits(count)):
        order = order + [peer ^ bit for peer in order]
    return order


def join_rows(values, axes):
    for bit in reversed(narrow_bits(lax.axis_size(axes))):
        values = jnp.concatenate([values, swap(values, axes, bit)], axis=0)
    return values


def add_rows(values, axes):
    for bit in narrow_bits(lax.axis_size(axes)):
        half = values.shape[0] // 2
        came = swap(values[half:].astype(low_type), axes, bit)
        values = values[:half].astype(jnp.float32) + came.astype(jnp.float32)
    return values


def product_add_rows(left_side, right_side, axes):
    bits = narrow_bits(lax.axis_size(axes))
    half = left_side.shape[0] // 2
    sent = plain_product(left_side[half:], right_side).astype(low_type)
    came = swap(sent, axes, bits[0])
    values = plain_product(left_side[:half], right_side) + came.astype(jnp.float32)
    for bit in bits[1:]:
        half = values.shape[0] // 2
        came = swap(values[half:].astype(low_type), axes, bit)
        values = values[:half] + came.astype(jnp.float32)
    return values


def natural_rows(joined, places):
    group = joined.shape[0] // len(places)
    return jnp.concatenate(
        [lax.dynamic_slice_in_dim(joined, place * group, group, 0) for place in places], axis=0
    )


def spread(values, axes):
    copies = jnp.broadcast_to(values[None], (lax.axis_size(axes),) + values.shape)
    return lax.all_to_all(copies, axes, split_axis=0, concat_axis=0, tiled=True)


def after(values, other):
    return lax.optimization_barrier((values, other))[0]


def gelu_and_slope(values):
    rate = 0.7978845608028654
    cubic = 0.044715
    squares = values * values
    turn = jnp.tanh(rate * values * (1.0 + cubic * squares))
    half = 0.5 * (1.0 + turn)
    slope = half + 0.5 * values * (1.0 - turn * turn) * (rate * (1.0 + 3.0 * cubic * squares))
    return (values * half).astype(low_type), slope.astype(low_type)


def smem():
    return pl.BlockSpec(memory_space=pltpu.SMEM)


def vmem():
    return pl.BlockSpec(memory_space=pltpu.VMEM)


def bias_kernel(chunks, tiles):
    heads = tiles.shape[0]
    tiles[...] = jnp.zeros_like(tiles)
    for h in range(heads):
        for d in range(-REACH, REACH + 1):
            left = chunks[h, REACH + 1 - d : REACH + 2 - d, :]
            right = chunks[h, REACH - d : REACH + 1 - d, :]
            line = jnp.broadcast_to(jnp.concatenate([left, right], axis=1), (LANE, 2 * LANE))
            rolled = pltpu.roll(line, 0, 1, stride=1, stride_axis=0)
            tiles[h, (d + OFF) * LANE : (d + OFF + 1) * LANE, :] = rolled[:, :LANE]


def bias_tiles(rel_chunks):
    heads = rel_chunks.shape[0]
    return pl.pallas_call(
        bias_kernel,
        out_shape=jax.ShapeDtypeStruct((heads, SPAN * LANE, LANE), jnp.float32),
        compiler_params=pltpu.CompilerParams(vmem_limit_bytes=VMEM_LIMIT),
        name="bias_tiles",
    )(rel_chunks)


def key_range(lengths, first, last):
    start = jnp.int32(0)
    low = jnp.int32(0)
    high = jnp.int32(0)
    for s in range(SEQS_DEV):
        end = start + lengths[s]
        low = jnp.where(start <= first, start, low)
        high = jnp.where(start <= last, end, high)
        start = end
    return low // BK, (high + BK - 1) // BK


def bias_part(bias, h, row):
    return jnp.concatenate(
        [
            bias[h, pl.ds(pl.multiple_of(row - b * LANE, LANE), BK), :]
            for b in range(BQ // LANE)
        ],
        axis=1,
    )


def forward_kernel(
    lengths, origin, cols, rows_in, apart, bias, ctx_o, ctxT_o, lse_o, qa, acc
):
    width, rows_here = cols.shape[0] // 3, cols.shape[1]
    heads = bias.shape[0]
    size = width // heads
    first_row = 0
    qa[...] = jnp.zeros_like(qa)

    @pl.loop(0, rows_here // BQ)
    def _(i):
        q0 = pl.multiple_of(i * BQ, BQ)
        here = pl.ds(q0, BQ)
        for h in range(heads):
            scaled = cols[h * size : (h + 1) * size, here].astype(jnp.float32) * score_scale
            qa[h * LANE : h * LANE + size, :] = scaled.astype(low_type)
            qa[h * LANE + size : h * LANE + size + 16, :] = apart[:, here]
        acc[...] = jnp.zeros_like(acc)
        low, high = key_range(lengths, first_row + q0, first_row + q0 + BQ - 1)

        def step(j, carry):
            k0 = pl.multiple_of(j * BK, BK)
            row = (j * (BK // LANE) - i * (BQ // LANE) - first_row // LANE + OFF) * LANE
            out = []
            for h in range(heads):
                top, total = carry[2 * h], carry[2 * h + 1]
                own = slice(h * LANE, (h + 1) * LANE)
                rows = slice(h * size, (h + 1) * size)
                s = plain_product(rows_in[pl.ds(k0, BK), own], qa[own, :])
                s = s + bias_part(bias, h, row)
                new_top = jnp.maximum(top, jnp.max(s, axis=0, keepdims=True))
                fade = jnp.exp(top - new_top)
                p = jnp.exp(s - new_top)
                total = total * fade + jnp.sum(p, axis=0, keepdims=True)
                acc[rows, :] = acc[rows, :] * fade + plain_product(
                    cols[2 * width + h * size : 2 * width + (h + 1) * size, pl.ds(k0, BK)],
                    p.astype(low_type),
                )
                out += [new_top, total]
            return tuple(out)

        init = tuple(
            jnp.full((1, BQ), 2.0 * masked_score if n % 2 == 0 else 0.0, jnp.float32)
            for n in range(2 * heads)
        )
        done = lax.fori_loop(low, high, step, init)
        for h in range(heads):
            rows = slice(h * size, (h + 1) * size)
            acc[rows, :] = acc[rows, :] / done[2 * h + 1]
            lse_o[h : h + 1, here] = done[2 * h] + jnp.log(done[2 * h + 1])
        ctxT_o[:, here] = acc[...]
        turned = acc[...].T.astype(low_type)
        for b in range(BQ // LANE):
            at = pl.multiple_of(origin[i * (BQ // LANE) + b], LANE)
            ctx_o[pl.ds(at, LANE), :] = turned[b * LANE : (b + 1) * LANE, :]


def attention_forward(lengths, origin, cols, rows_in, apart, bias):
    width, rows_here = cols.shape[0] // 3, cols.shape[1]
    heads = bias.shape[0]
    return pl.pallas_call(
        forward_kernel,
        out_shape=(
            jax.ShapeDtypeStruct((rows_here, width), low_type),
            jax.ShapeDtypeStruct((width, rows_here), jnp.float32),
            jax.ShapeDtypeStruct((heads, rows_here), jnp.float32),
        ),
        in_specs=[smem()] * 2 + [vmem()] * 4,
        out_specs=(vmem(),) * 3,
        scratch_shapes=[
            pltpu.VMEM((heads * LANE, BQ), low_type),
            pltpu.VMEM((width, BQ), jnp.float32),
        ],
        compiler_params=pltpu.CompilerParams(vmem_limit_bytes=VMEM_LIMIT),
        cost_estimate=pl.CostEstimate(
            flops=rows_here * width, bytes_accessed=width * TOK_DEV, transcendentals=0
        ),
        name="attention_forward",
    )(lengths, origin, cols, rows_in, apart, bias)


def three_parts(values):
    first = values.astype(low_type).astype(jnp.float32)
    rest = values - first
    second = rest.astype(low_type).astype(jnp.float32)
    return first, second, rest - second


def backward_kernel(
    lengths, origin, cols, rows_in, dcn, ctxT, lse, apart, bias,
    dT_o, dn_o, lines_o, qa, da, dq, dk, dv, tiles,
):
    width, tokens = cols.shape[0] // 3, cols.shape[1]
    heads = bias.shape[0]
    size = width // heads
    for ref in (qa, da, dk, dv, tiles):
        ref[...] = jnp.zeros_like(ref)
    place = lax.broadcasted_iota(jnp.int32, (16, BQ), 0) - SEQS_DEV

    def in_depth(values):
        a, b, c = three_parts(values)
        return jnp.where(place == 0, a, jnp.where(place == 1, b, jnp.where(place == 2, c, 0.0)))

    @pl.loop(0, tokens // BQ)
    def _(i):
        q0 = pl.multiple_of(i * BQ, BQ)
        here = pl.ds(q0, BQ)
        at = [pl.multiple_of(origin[i * (BQ // LANE) + b], LANE) for b in range(BQ // LANE)]
        dcT = jnp.concatenate(
            [dcn[pl.ds(at[b], LANE), :].astype(jnp.float32) for b in range(BQ // LANE)], axis=0
        ).T
        for h in range(heads):
            rows = slice(h * size, (h + 1) * size)
            top = h * LANE
            scaled = cols[rows, here].astype(jnp.float32) * score_scale
            qa[top : top + size, :] = scaled.astype(low_type)
            extra = apart[:, here].astype(jnp.float32) + in_depth(-lse[h : h + 1, here])
            qa[top + size : top + size + 16, :] = extra.astype(low_type)
            da[top : top + size, :] = dcT[rows, :].astype(low_type)
            delta = jnp.sum(dcT[rows, :] * ctxT[rows, here], axis=0, keepdims=True)
            da[top + size : top + size + 16, :] = in_depth(-delta).astype(low_type)
        dq[...] = jnp.zeros_like(dq)
        low, high = key_range(lengths, q0, q0 + BQ - 1)

        @pl.loop(low, high)
        def _(j):
            k0 = pl.multiple_of(j * BK, BK)
            there = pl.ds(k0, BK)
            row = (j * (BK // LANE) - i * (BQ // LANE) + OFF) * LANE
            for h in range(heads):
                rows = slice(h * size, (h + 1) * size)
                own = slice(h * LANE, (h + 1) * LANE)
                flat = slice(h * LANE, h * LANE + size)
                values = slice((heads + h) * LANE, (heads + h + 1) * LANE)
                keys = slice(width + h * size, width + (h + 1) * size)
                s = plain_product(rows_in[there, own], qa[own, :])
                p = jnp.exp(s + bias_part(bias, h, row))
                ds = p * plain_product(rows_in[there, values], da[own, :])
                for b in range(BQ // LANE):
                    window = pl.ds(pl.multiple_of(row - b * LANE, LANE), BK)
                    tiles[h, window, :] = (
                        tiles[h, window, :] + ds[:, b * LANE : (b + 1) * LANE]
                    )
                p_low = p.astype(low_type)
                ds_low = ds.astype(low_type)
                dv[rows, there] = dv[rows, there] + times_transposed(da[flat, :], p_low)
                dk[rows, there] = dk[rows, there] + times_transposed(qa[flat, :], ds_low)
                dq[rows, :] = dq[rows, :] + plain_product(cols[keys, there], ds_low)

        grad = dq[...] * score_scale
        dT_o[0:width, here] = grad.astype(low_type)
        turned = grad.T.astype(low_type)
        for b in range(BQ // LANE):
            dn_o[pl.ds(at[b], LANE), 0:width] = turned[b * LANE : (b + 1) * LANE, :]

    @pl.loop(0, tokens // BQ)
    def _(i):
        here = pl.ds(pl.multiple_of(i * BQ, BQ), BQ)
        both = jnp.concatenate([dk[:, here], dv[:, here]], axis=0)
        dT_o[width : 3 * width, here] = both.astype(low_type)
        turned = both.T.astype(low_type)
        for b in range(BQ // LANE):
            at = pl.multiple_of(origin[i * (BQ // LANE) + b], LANE)
            dn_o[pl.ds(at, LANE), width : 3 * width] = turned[b * LANE : (b + 1) * LANE, :]

    across = lax.broadcasted_iota(jnp.int32, (LANE, LANE), 1)
    over = across >= lax.broadcasted_iota(jnp.int32, (LANE, LANE), 0)
    sub = lax.broadcasted_iota(jnp.int32, (8, LANE), 0)
    for h in range(heads):
        for d in range(-REACH, REACH + 2):
            here = tiles[h, (d + OFF) * LANE : (d + OFF + 1) * LANE, :]
            below = tiles[h, (d + OFF - 1) * LANE : (d + OFF) * LANE, :]
            mixed = jnp.where(over, here, below)
            line = mixed[LANE - 8 :, :]
            for g in range(LANE // 8 - 2, -1, -1):
                line = mixed[8 * g : 8 * g + 8, :] + pltpu.roll(line, LANE - 8, 1)
            for bit in (1, 2, 4):
                line = jnp.where((sub & bit) != 0, pltpu.roll(line, LANE - bit, 1), line)
            lines_o[h, REACH + 1 - d : REACH + 2 - d, :] = jnp.sum(line, axis=0, keepdims=True)


def attention_backward(lengths, origin, cols, rows_in, dcn, ctxT, lse, apart, bias):
    width, tokens = cols.shape[0] // 3, cols.shape[1]
    heads = bias.shape[0]
    return pl.pallas_call(
        backward_kernel,
        out_shape=(
            jax.ShapeDtypeStruct((3 * width, tokens), low_type),
            jax.ShapeDtypeStruct((tokens, 3 * width), low_type),
            jax.ShapeDtypeStruct((heads, LINES, LANE), jnp.float32),
        ),
        in_specs=[smem()] * 2 + [vmem()] * 7,
        out_specs=(vmem(),) * 3,
        scratch_shapes=[
            pltpu.VMEM((heads * LANE, BQ), low_type),
            pltpu.VMEM((heads * LANE, BQ), low_type),
            pltpu.VMEM((width, BQ), jnp.float32),
            pltpu.VMEM((width, tokens), jnp.float32),
            pltpu.VMEM((width, tokens), jnp.float32),
            pltpu.VMEM((heads, SPAN * LANE, LANE), jnp.float32),
        ],
        compiler_params=pltpu.CompilerParams(vmem_limit_bytes=VMEM_LIMIT),
        cost_estimate=pl.CostEstimate(
            flops=tokens * width, bytes_accessed=width * TOK_DEV, transcendentals=0
        ),
        name="attention_backward",
    )(lengths, origin, cols, rows_in, dcn, ctxT, lse, apart, bias)


def feed_forward_backward_kernel(
    grad, rows, hidden, slope, inner, outer, weight_grads, rows_grad
):
    groups, _, size, width = weight_grads.shape

    @pl.when(pl.program_id(0) == 0)
    def _():
        rows_grad[...] = jnp.zeros_like(rows_grad)

    outer_grad = outer_product(hidden[...], grad[...]).astype(low_type)
    weight_grads[:, 0] = outer_grad.reshape(groups, size, width)
    pre = (
        times_transposed(grad[...], outer[...]) * slope[...].astype(jnp.float32)
    ).astype(low_type)
    inner_grad = outer_product(pre, rows[...]).astype(low_type)
    weight_grads[:, 1] = inner_grad.reshape(groups, size, width)
    rows_grad[...] += plain_product(pre, inner[...])


def feed_forward_backward(grad, rows, hidden, slope, inner, outer, size):
    count = grad.shape[0]
    groups = UNIT_BLOCK // size
    every = pl.BlockSpec((count, D), lambda i: (0, 0))
    units = pl.BlockSpec((count, UNIT_BLOCK), lambda i: (0, i))
    weight = pl.BlockSpec((UNIT_BLOCK, D), lambda i: (i, 0))
    return pl.pallas_call(
        feed_forward_backward_kernel,
        grid=(FF // UNIT_BLOCK,),
        out_shape=(
            jax.ShapeDtypeStruct((FF // size, 2, size, D), low_type),
            jax.ShapeDtypeStruct((count, D), jnp.float32),
        ),
        in_specs=[every, every, units, units, weight, weight],
        out_specs=(pl.BlockSpec((groups, 2, size, D), lambda i: (i, 0, 0, 0)), every),
        compiler_params=pltpu.CompilerParams(vmem_limit_bytes=VMEM_LIMIT),
        cost_estimate=pl.CostEstimate(flops=FF * D, bytes_accessed=FF * D, transcendentals=0),
        name="feed_forward_backward",
    )(grad, rows, hidden, slope, inner, outer)


def assemble(places, pieces):
    group = pieces[0].shape[0]

    def body(places_in, *refs):
        for s, piece in enumerate(refs[:-1]):

            @pl.when(places_in[pl.program_id(0)] == s)
            def _(piece=piece):
                refs[-1][...] = piece[...].astype(jnp.float32)

    return pl.pallas_call(
        body,
        grid=(len(pieces),),
        out_shape=jax.ShapeDtypeStruct((len(pieces) * group, D), jnp.float32),
        in_specs=[smem()] + [pl.BlockSpec((group, D), lambda g: (0, 0))] * len(pieces),
        out_specs=pl.BlockSpec((group, D), lambda g: (g, 0)),
        compiler_params=pltpu.CompilerParams(vmem_limit_bytes=VMEM_LIMIT),
        cost_estimate=pl.CostEstimate(flops=D, bytes_accessed=group * D, transcendentals=0),
        name="assemble",
    )(places, *pieces)


def loss_kernel(place, numbers, parts, proj_weight, gain, out_slope, out_low, out_row, out_gain):
    total_seqs = out_low.shape[0] // 2
    terms = parts.shape[0] // total_seqs
    exact = dict(precision=lax.Precision.HIGHEST, preferred_element_type=jnp.float32)
    seq = lax.broadcasted_iota(jnp.int32, (total_seqs, parts.shape[0]), 0)
    part = lax.broadcasted_iota(jnp.int32, (total_seqs, parts.shape[0]), 1)
    joins = jnp.logical_and(
        seq // SEQS_DEV == part // (SEQS_DEV * terms), seq % SEQS_DEV == part % SEQS_DEV
    )
    unscaled = jnp.dot(joins.astype(jnp.float32), parts[...], **exact)
    pooled_low = (unscaled * gain[...]).astype(low_type)
    projected = times_transposed(pooled_low, proj_weight[...]).astype(low_type).astype(jnp.float32)
    inverse = lax.rsqrt(jnp.sum(projected * projected, axis=1, keepdims=True) + norm_eps)
    embed_low = (projected * inverse).astype(low_type)
    sharpness_factor = jnp.exp(jnp.full((1, 1), numbers[0], jnp.float32))
    agreement = times_transposed(embed_low, embed_low)
    row = lax.broadcasted_iota(jnp.int32, (total_seqs, total_seqs), 0)
    column = lax.broadcasted_iota(jnp.int32, (total_seqs, total_seqs), 1)
    logits = jnp.where(row == column, masked_score, sharpness_factor * agreement)
    partner = (row ^ 1) == column

    def log_sum(axis):
        top = jnp.max(logits, axis=axis, keepdims=True)
        return top + jnp.log(jnp.sum(jnp.exp(logits - top), axis=axis, keepdims=True))

    log_rows = log_sum(1)
    positive = jnp.where(partner, 1.0, 0.0)
    slope = (jnp.exp(logits - log_rows) - positive) / total_seqs
    slope_turned = (jnp.exp(logits - log_sum(0)) - positive) / total_seqs
    embed_grad = sharpness_factor * jnp.dot(
        slope + slope_turned, embed_low.astype(jnp.float32), **exact
    )
    along = jnp.sum(projected * embed_grad, axis=1, keepdims=True)
    proj_grad_low = (
        inverse * embed_grad - projected * inverse * inverse * inverse * along
    ).astype(low_type)
    pooled_grad = plain_product(proj_grad_low, proj_weight[...])
    out_low[0:total_seqs, :] = proj_grad_low
    out_low[total_seqs : 2 * total_seqs, :] = pooled_low
    out_gain[...] = jnp.sum(pooled_grad * unscaled, axis=0, keepdims=True)
    loss = jnp.sum(
        log_rows - jnp.sum(positive * jnp.where(partner, logits, 0.0), axis=1, keepdims=True),
        axis=0,
        keepdims=True,
    ) / total_seqs
    temperature = sharpness_factor * jnp.sum(
        jnp.sum(slope * agreement, axis=1, keepdims=True), axis=0, keepdims=True
    )
    lane = lax.broadcasted_iota(jnp.int32, (1, LANE), 1)
    out_row[...] = jnp.where(lane == 0, loss, jnp.where(lane == 1, temperature, 0.0))
    mine = lax.broadcasted_iota(jnp.int32, (8, total_seqs), 0)
    seq_of = lax.broadcasted_iota(jnp.int32, (8, total_seqs), 1) - place[0] * SEQS_DEV
    picks = jnp.logical_and(mine == seq_of, mine < SEQS_DEV).astype(jnp.float32)
    own = jnp.dot(picks, pooled_grad, **exact)
    index = lax.broadcasted_iota(jnp.int32, (8, 1), 0)
    extent = jnp.ones((8, 1), jnp.float32)
    for s in range(SEQS_DEV):
        extent = jnp.where(index == s, place[1 + s].astype(jnp.float32), extent)
    out_slope[...] = own * gain[...] / extent


def contrastive(place, numbers, parts, proj_weight, gain, total_seqs):
    return pl.pallas_call(
        loss_kernel,
        out_shape=(
            jax.ShapeDtypeStruct((8, D), jnp.float32),
            jax.ShapeDtypeStruct((2 * total_seqs, D), low_type),
            jax.ShapeDtypeStruct((1, LANE), jnp.float32),
            jax.ShapeDtypeStruct((1, D), jnp.float32),
        ),
        in_specs=[smem()] * 2 + [vmem()] * 3,
        out_specs=(vmem(),) * 4,
        compiler_params=pltpu.CompilerParams(vmem_limit_bytes=VMEM_LIMIT),
        cost_estimate=pl.CostEstimate(
            flops=4 * total_seqs * D * D, bytes_accessed=4 * D * D, transcendentals=total_seqs
        ),
        name="contrastive",
    )(place, numbers, parts, proj_weight, gain)


def on_device(
    axes,
    layer_argument,
    document_extents,
    distance_bin_lookup,
    tile_location,
    precise_parameter_blocks,
    precise_mean_est,
    precise_variance_est,
    rescaling_coefficients,
    norm_scale_mean_est,
    norm_scale_variance_est,
    distance_bias_table,
    offset_bias_mean_est,
    offset_bias_variance_est,
    sharpness_exponent,
    sharpness_mean_est,
    sharpness_variance_est,
):
    wide, narrow, far, near = axes
    everyone = wide + narrow
    near_axes = near + narrow
    wide_count = lax.axis_size(wide)
    narrow_count = lax.axis_size(narrow)
    far_count = lax.axis_size(far)
    near_count = wide_count // far_count
    wide_index = lax.axis_index(wide)
    narrow_index = lax.axis_index(narrow)
    bits = narrow_bits(narrow_count)
    order = peer_order(narrow_count)
    place_of = jnp.array([order.index(peer) for peer in range(narrow_count)], jnp.int32)
    unit_rows = precise_parameter_blocks.shape[1]
    heads_here = distance_bias_table.shape[1]
    head_size = unit_rows // heads_here
    ffn_units = FF // D
    group = TOK_DEV // narrow_count
    own_slots = wide_index * CAP + jnp.arange(CAP, dtype=jnp.int32)

    every_slot = lax.all_gather(
        precise_parameter_blocks.astype(low_type), wide, axis=0, tiled=True
    )

    def block(u):
        return lax.dynamic_index_in_dim(every_slot, tile_location[u], 0, keepdims=False)

    qkv_weight = jnp.concatenate([block(u) for u in range(3)], axis=0)

    part_rows = D // wide_count

    def unit_order(first_unit):
        rows = jnp.concatenate([block(first_unit + k) for k in range(ffn_units)], axis=0)
        rows = rows.reshape(far_count, near_count, part_rows, D)
        return jnp.swapaxes(rows, 0, 1).reshape(near_count, far_count * part_rows, D)

    crossing = [unit_order(5), block(3), unit_order(5 + ffn_units)]
    for rows in crossing:
        qkv_weight = after(qkv_weight, rows)

    near_index = wide_index % near_count

    def fetch(rows, peer, in_parts):
        if in_parts:
            rows = lax.dynamic_index_in_dim(rows, near_index, 0)
        return swap(rows, narrow, peer)

    evens = bits[1:]
    def exchanged(pieces):
        return [
            [(near_index, rows)]
            + [(near_index ^ step, swap(rows, near, step)) for step in range(1, near_count)]
            for rows in pieces
        ]

    lengths = document_extents[0]
    seq_ends = jnp.cumsum(lengths)
    positions = jnp.arange(TOK_DEV, dtype=jnp.int32)

    def segments_of(where):
        return jnp.sum((seq_ends[None, :] <= where[:, None]).astype(jnp.int32), axis=1)

    segment_ids = segments_of(positions)
    own_segments = segments_of(narrow_index * group + positions[:group])
    tile_starts = jnp.arange(TOK_DEV // LANE, dtype=jnp.int32) * LANE
    origin = place_of[(tile_starts // group) ^ narrow_index] * group + tile_starts % group

    units = []
    for slot in range(CAP):
        here = tile_location == own_slots[slot]
        unit = jnp.sum(jnp.where(here, jnp.arange(1, here.shape[0] + 1, dtype=jnp.int32), 0)) - 1
        early_unit = jnp.maximum(unit - 5, 0)
        row = jnp.where(unit >= 5, early_unit % ffn_units, jnp.clip(unit, 0, ffn_units - 1))
        column = jnp.where(unit >= 5, 1 - early_unit // ffn_units, 2)
        units += [unit, row, column]
    proj_owner = (tile_location[4] // CAP == wide_index).astype(jnp.float32)
    places = [place_of[g ^ narrow_index] for g in range(narrow_count)]

    beyond = LINES * LANE - LANE - 1 - distance_bin_lookup.shape[0]
    offsets_down = jnp.pad(distance_bin_lookup[::-1], (LANE + 1, beyond), constant_values=-1)
    bucket_onehot = (
        offsets_down[:, None] == jnp.arange(BUCKETS, dtype=jnp.int32)[None, :]
    ).astype(jnp.float32)
    rel_values = jnp.dot(bucket_onehot, distance_bias_table, precision=lax.Precision.HIGHEST).T
    rel_values, origin, proj_owner, *scalars = lax.optimization_barrier(
        (rel_values, origin, proj_owner, *units, *places)
    )
    units, places = scalars[: len(units)], scalars[len(units) :]
    tiles_bias = bias_tiles(rel_values.reshape(heads_here, LINES, LANE))

    all_rows = layer_argument.astype(jnp.float32)
    normed_one = (all_rows * rms_scale(all_rows) * rescaling_coefficients[0]).astype(low_type)
    qkv_turned = times_transposed(qkv_weight, normed_one).astype(low_type)
    spread_weight = jnp.pad(
        qkv_weight[unit_rows:].reshape(2 * heads_here, head_size, D),
        ((0, 0), (0, LANE - head_size), (0, 0)),
    ).reshape(2 * heads_here * LANE, D)
    lane_place = jnp.arange(2 * heads_here * LANE, dtype=jnp.int32) % LANE - head_size
    marks = jnp.logical_or(
        lane_place[None, :] == segment_ids[:, None],
        jnp.logical_and(lane_place >= SEQS_DEV, lane_place < SEQS_DEV + 3)[None, :],
    )
    key_value_rows = (
        times_transposed(normed_one, spread_weight) + marks.astype(jnp.float32)
    ).astype(low_type)
    row_place = jnp.arange(16, dtype=jnp.int32)[:, None]
    apart = jnp.where(
        jnp.logical_and(row_place < SEQS_DEV, row_place != segment_ids[None, :]), masked_score, 0.0
    ).astype(low_type)
    crossing[1] = after(crossing[1], key_value_rows)
    fetched = [
        [fetch(rows, peer, in_parts) for peer in evens]
        for rows, in_parts in zip(crossing, (True, False, True))
    ]
    inner_parts = exchanged(fetched[0])
    apart = after(apart, fetched[0][0])
    context, context_cols, log_rows = attention_forward(
        lengths, origin, qkv_turned, key_value_rows, apart, tiles_bias
    )

    flat = [rows for pieces in fetched[1:] for rows in pieces]
    inner_flat = [rows for parts in inner_parts for _, rows in parts]
    context, *flat = lax.optimization_barrier((context, *flat, *inner_flat))
    inner_rows = iter(flat[2 * len(evens) :])
    inner_parts = [[(index, next(inner_rows)) for index, _ in parts] for parts in inner_parts]
    outer_parts = exchanged(flat[len(evens) : 2 * len(evens)])

    def in_unit_order(own, parts_of_peers):
        whole = jnp.zeros((near_count, narrow_count, far_count * part_rows, D), low_type)
        pieces = [(0, 0, own), (1, 0, swap(own, narrow, 1))]
        for peer, parts in zip(evens, parts_of_peers):
            for index, rows in parts:
                pieces += [(peer, index, rows), (peer + 1, index, swap(rows, narrow, 1))]
        for peer, index, rows in pieces:
            start = (index, narrow_index ^ peer, 0, 0)
            whole = lax.dynamic_update_slice(whole, rows[:, None], start)
        return whole.reshape(FF, D)

    out_pieces = {0: crossing[1], 1: swap(crossing[1], narrow, 1)}
    for peer, rows in zip(evens, flat[: len(evens)]):
        out_pieces[peer], out_pieces[peer + 1] = rows, swap(rows, narrow, 1)
    out_joined = jnp.concatenate([out_pieces[peer] for peer in order], axis=0)
    inner_joined = in_unit_order(crossing[0], inner_parts)
    outer_joined = in_unit_order(crossing[2], outer_parts)

    def to_peer(values, peer):
        if peer == 0:
            return values
        return swap(values, narrow, peer)

    context_own = jnp.concatenate(
        [
            to_peer(context[s * group : (s + 1) * group], peer)
            for s, peer in enumerate(order)
        ],
        axis=1,
    )
    own_rows = lax.dynamic_slice_in_dim(layer_argument, narrow_index * group, group, 0).astype(
        jnp.float32
    )
    scale_one = rms_scale(own_rows)
    residual_mid = own_rows + plain_product(context_own, out_joined)
    scale_two = rms_scale(residual_mid)
    normed_two = (residual_mid * scale_two * rescaling_coefficients[1]).astype(low_type)

    hidden_low, hidden_slope = gelu_and_slope(times_transposed(normed_two, inner_joined))
    proj_rows = after(block(4), normed_two)
    for bit in reversed(bits):
        came = after(swap(proj_rows, narrow, bit), hidden_low)
        proj_rows = jnp.concatenate([proj_rows, came], axis=0)
    proj_weight = natural_rows(proj_rows, places)
    result_own = residual_mid + plain_product(hidden_low, outer_joined)
    result_low = result_own.astype(low_type)

    scale_three = rms_scale(result_own)
    member = (
        own_segments[None, :] == jnp.arange(SEQS_DEV, dtype=jnp.int32)[:, None]
    ).astype(jnp.float32)
    length_values = lengths.astype(jnp.float32)[:, None]
    unscaled_part = (
        jnp.dot(member, result_own * scale_three, precision=lax.Precision.HIGHEST) / length_values
    )
    total_seqs = wide_count * SEQS_DEV
    own_pooled_grad, loss_low, loss_row, final_gain_grad = contrastive(
        jnp.concatenate([wide_index.reshape(1), lengths]),
        sharpness_exponent,
        spread(unscaled_part, everyone).reshape(total_seqs * narrow_count, D),
        proj_weight,
        rescaling_coefficients[2:3],
        total_seqs,
    )
    loss = loss_row[0, 0]
    sharpness_total = loss_row[0, 1:2]
    proj_grad_own = lax.dynamic_slice_in_dim(
        loss_low[:total_seqs], narrow_index * unit_rows, unit_rows, 1
    )
    proj_weight_grad = outer_product(proj_grad_own, loss_low[total_seqs:])

    weighted = own_pooled_grad[SEQS_DEV - 1]
    for s in range(SEQS_DEV - 2, -1, -1):
        weighted = jnp.where((own_segments == s)[:, None], own_pooled_grad[s], weighted)
    inner_mean = jnp.mean(weighted * result_own, axis=-1, keepdims=True)
    encoded_grad = scale_three * weighted - result_own * (
        scale_three * scale_three * scale_three * inner_mean
    )
    ffn_grad_low = encoded_grad.astype(low_type)
    group_rows = part_rows if part_rows % 16 == 0 else D
    weight_grads, normed_two_grad = feed_forward_backward(
        ffn_grad_low,
        normed_two,
        hidden_low,
        hidden_slope,
        inner_joined,
        outer_joined,
        group_rows,
    )
    near_part = lax.psum_scatter(
        weight_grads.reshape(2 * FF, D), near_axes, scatter_dimension=0, tiled=True
    )
    mid_norm_grad, ffn_gain_grad = norm_backward(
        residual_mid, scale_two, rescaling_coefficients[1], normed_two_grad
    )
    mid_grad = encoded_grad + mid_norm_grad
    attn_grad_low = mid_grad.astype(low_type)

    context_grad_own = times_transposed(attn_grad_low, out_joined).astype(low_type)
    context_grad = [
        to_peer(context_grad_own[:, s * unit_rows : (s + 1) * unit_rows], peer)
        for s, peer in enumerate(order)
    ]
    attn_grad_low = after(attn_grad_low, context_grad_own)
    out_kept = outer_product(context_own, attn_grad_low).astype(low_type)
    for bit in bits:
        half = out_kept.shape[0] // 2
        out_came = swap(out_kept[half:], narrow, bit)
        if bit == bits[-1]:
            break
        out_kept = sum_low(out_kept[:half], out_came)
    context_grad = after(jnp.concatenate(context_grad, axis=0), out_kept)
    qkv_cols, qkv_rows, bias_lines = attention_backward(
        lengths,
        origin,
        qkv_turned,
        key_value_rows,
        context_grad,
        context_cols,
        log_rows,
        apart,
        tiles_bias,
    )
    qkv_cols, qkv_rows, out_came = lax.optimization_barrier((qkv_cols, qkv_rows, out_came))
    out_grad = sum_low(out_kept[: out_came.shape[0]], out_came)
    offset_bias_slope = lax.dot_general(
        bucket_onehot,
        bias_lines.reshape(heads_here, LINES * LANE),
        (((0,), (1,)), ((), ())),
        precision=lax.Precision.HIGHEST,
    )

    late = jnp.concatenate(
        [plain_product(qkv_cols, normed_one).astype(low_type), out_grad], axis=0
    ).reshape(far_count, near_count, part_rows, D)
    qkv_rows = after(qkv_rows, late)
    half = qkv_rows.shape[0] // 2
    rows_sent = plain_product(qkv_rows[half:], qkv_weight).astype(low_type)
    normed_one_grad = plain_product(qkv_rows[:half], after(qkv_weight, rows_sent)) + swap(
        rows_sent, narrow, bits[0]
    ).astype(jnp.float32)
    for bit in bits[1:]:
        half = normed_one_grad.shape[0] // 2
        rows_sent = normed_one_grad[half:].astype(low_type)
        normed_one_grad = normed_one_grad[:half] + swap(rows_sent, narrow, bit).astype(
            jnp.float32
        )
    late_sum = lax.dynamic_index_in_dim(late, near_index, 1, keepdims=False)
    for peer in range(1, near_count):
        sent = lax.dynamic_index_in_dim(late, near_index ^ peer, 1, keepdims=False)
        late_sum = sum_low(late_sum, after(swap(sent, near, peer), rows_sent))
    early = after(near_part, late).reshape(-1, 2, group_rows // part_rows, part_rows, D)
    early = jnp.swapaxes(early, 1, 2).reshape(far_count, 2, part_rows, D)
    terms = jnp.concatenate([early, late_sum[:, None]], axis=1)
    own_part = lax.psum_scatter(
        terms.reshape(far_count * 3 * part_rows, D), far, scatter_dimension=0, tiled=True
    )
    input_norm_grad, attn_gain_grad = norm_backward(
        own_rows, scale_one, rescaling_coefficients[0], normed_one_grad
    )
    input_own = mid_grad + input_norm_grad
    sums = lax.all_gather(after(own_part, input_own), wide, axis=0, tiled=True)
    bias_size = offset_bias_slope.size
    squares = jnp.sum(jnp.square(own_part.astype(jnp.float32))) + proj_owner * jnp.sum(
        jnp.square(proj_weight_grad)
    )
    small = jnp.stack(
        [
            ffn_gain_grad,
            attn_gain_grad,
            jnp.pad(offset_bias_slope.reshape(bias_size), (0, D - bias_size)),
            jnp.broadcast_to(squares, (D,)),
        ]
    )
    small_all = spread(small, everyone).reshape(wide_count, narrow_count, 4, D)
    def gathered(own):
        pieces = {0: own, 1: swap(own, narrow, 1)}
        for peer in evens:
            rows = after(swap(own, narrow, peer), small_all)
            pieces[peer], pieces[peer + 1] = rows, swap(rows, narrow, 1)
        return assemble(jnp.stack(places), [pieces[peer] for peer in order])

    input_grad = gathered(input_own.astype(low_type))
    layer_result = gathered(after(result_low, input_own))
    gain_sums = jnp.sum(small_all[:, :, :2], axis=(0, 1))
    gain_total = jnp.stack([gain_sums[1], gain_sums[0], final_gain_grad[0]])
    bias_all = jnp.sum(small_all[:, :, 2], axis=0)
    square_terms = small_all[:, :, 3, 0]
    bias_total = lax.dynamic_index_in_dim(bias_all, narrow_index, 0, keepdims=False)[
        :bias_size
    ].reshape(offset_bias_slope.shape)
    sums, proj_weight_grad, square_terms, *_ = lax.optimization_barrier(
        (sums, proj_weight_grad, square_terms, input_grad, layer_result, gain_total, bias_total)
    )
    sums = sums.reshape(ffn_units, wide_count // ffn_units, 3, part_rows, D)
    slot_grads = []
    for slot in range(CAP):
        unit, row, column = units[3 * slot : 3 * slot + 3]
        low_sum = lax.dynamic_slice(
            sums, (row, 0, column, 0, 0), (1, wide_count // ffn_units, 1, part_rows, D)
        ).reshape(unit_rows, D)
        low_sum = jnp.where(unit == 4, proj_weight_grad, low_sum.astype(jnp.float32))
        slot_grads.append(jnp.where(unit >= 0, low_sum, 0.0))
    slot_grads = jnp.stack(slot_grads)
    grad_norm = jnp.sqrt(
        jnp.sum(square_terms)
        + jnp.sum(gain_total * gain_total)
        + jnp.sum(bias_all * bias_all)
        + jnp.sum(sharpness_total * sharpness_total)
    )
    multiplier = jnp.minimum(1.0, clip_limit / grad_norm)
    slot_first, slot_second, slot_weight = decoupled_decay_step(
        slot_grads,
        precise_mean_est,
        precise_variance_est,
        precise_parameter_blocks,
        multiplier,
        learn_rate,
    )
    gain_first, gain_second, gain_new = decoupled_decay_step(
        gain_total,
        norm_scale_mean_est,
        norm_scale_variance_est,
        rescaling_coefficients,
        multiplier,
        side_rate,
    )
    bias_first, bias_second, bias_new = decoupled_decay_step(
        bias_total,
        offset_bias_mean_est,
        offset_bias_variance_est,
        distance_bias_table,
        multiplier,
        side_rate,
    )
    sharpness_mean_fresh, sharpness_variance_fresh, sharpness_exponent_fresh = decoupled_decay_step(
        sharpness_total,
        sharpness_mean_est,
        sharpness_variance_est,
        sharpness_exponent,
        multiplier,
        learn_rate,
    )
    return (
        loss,
        layer_result,
        input_grad,
        grad_norm,
        slot_first,
        slot_second,
        slot_weight,
        gain_first,
        gain_second,
        gain_new,
        bias_first,
        bias_second,
        bias_new,
        sharpness_mean_fresh,
        sharpness_variance_fresh,
        sharpness_exponent_fresh,
    )


def solution(mesh):
    wide, narrow, far, near = ("wide",), ("narrow",), ("wide",), ()
    if dict(mesh.shape) == {"wide": 8, "narrow": 4}:
        mesh = Mesh(mesh.devices.reshape(4, 2, 2, 2), ("line", "pair", "side", "core"))
        wide, narrow, far, near = ("line", "pair"), ("side", "core"), ("line",), ("pair",)
    whole, rows, blocks, heads = P(), P(wide, None), P(wide, narrow, None), P(None, narrow)
    arguments = (rows, rows, whole, whole, blocks, blocks, blocks, whole, whole, whole)
    arguments += (heads, heads, heads, whole, whole, whole)
    results = (whole, rows, rows, whole, blocks, blocks, blocks, whole, whole, whole)
    results += (heads, heads, heads, whole, whole, whole)

    def body(*arrays):
        return on_device((wide, narrow, far, near), *arrays)

    return jax.shard_map(
        body, mesh=mesh, in_specs=arguments, out_specs=results, check_vma=False
    )
```

```python
import jax
import jax.numpy as jnp
from jax import lax
from jax.experimental import pallas as pl
from jax.experimental.pallas import tpu as pltpu
from jax.sharding import Mesh
from jax.sharding import PartitionSpec as P

D = 768
FF = 3072
BUCKETS = 32
TOK_DEV = 2560
SEQS_DEV = 4
DOCLEN = 1024
CAP = 2
STEP = 10
LANE = 128
BQ = 512
BK = 256
UNIT_BLOCK = 768
REACH = DOCLEN // LANE
OFF = REACH + (BQ + 2 * BK) // LANE
SPAN = 2 * OFF + 1
LINES = 2 * REACH + 2
MIB = 1024 * 1024
SMALL_VMEM = 20 * MIB
FORWARD_VMEM = 26 * MIB
BACKWARD_VMEM = 40 * MIB
LAYER_VMEM = 36 * MIB

norm_eps = 1e-06
clip_limit = 0.01
learn_rate = 0.01
side_rate = 0.5
beta_one = 0.5
beta_two = 0.5
adam_eps = 1e-08
decay_rate = 0.01
score_scale = 0.125
masked_score = -1e30
low_type = jnp.bfloat16


def times_transposed(left_side, right_side):
    return lax.dot_general(
        left_side, right_side, (((1,), (1,)), ((), ())), preferred_element_type=jnp.float32
    )


def plain_product(left_side, right_side):
    return jnp.dot(left_side, right_side, preferred_element_type=jnp.float32)


def outer_product(left_side, right_side):
    return lax.dot_general(
        left_side, right_side, (((0,), (0,)), ((), ())), preferred_element_type=jnp.float32
    )


def rms_scale(values):
    return lax.rsqrt(jnp.mean(values * values, axis=-1, keepdims=True) + norm_eps)


def norm_backward(values, row_scale, gain_row, grad_out):
    weighted = grad_out * gain_row
    gain_grad = jnp.sum(grad_out * values * row_scale, axis=0)
    inner_mean = jnp.mean(weighted * values, axis=-1, keepdims=True)
    value_grad = row_scale * weighted - values * row_scale * row_scale * row_scale * inner_mean
    return (value_grad, gain_grad)


def decoupled_decay_step(gradient, first_moment, second_moment, weight, multiplier, step_rate):
    clipped = gradient * multiplier
    first_new = beta_one * first_moment + (1.0 - beta_one) * clipped
    second_new = beta_two * second_moment + (1.0 - beta_two) * clipped * clipped
    first_hat = first_new / (1.0 - beta_one**STEP)
    second_hat = second_new / (1.0 - beta_two**STEP)
    weight_new = weight - step_rate * (
        first_hat / (jnp.sqrt(second_hat) + adam_eps) + decay_rate * weight
    )
    return (first_new, second_new, weight_new)


def swap(values, axes, bit):
    count = lax.axis_size(axes)
    return lax.ppermute(values, axes, [(i, i ^ bit) for i in range(count)])


def sum_low(left, right):
    return (left.astype(jnp.float32) + right.astype(jnp.float32)).astype(low_type)


def narrow_bits(count):
    return [1 << s for s in range(count.bit_length() - 1)]


def peer_order(count):
    order = [0]
    for bit in reversed(narrow_bits(count)):
        order = order + [peer ^ bit for peer in order]
    return order


def join_rows(values, axes):
    for bit in reversed(narrow_bits(lax.axis_size(axes))):
        values = jnp.concatenate([values, swap(values, axes, bit)], axis=0)
    return values


def add_rows(values, axes):
    for bit in narrow_bits(lax.axis_size(axes)):
        half = values.shape[0] // 2
        came = swap(values[half:].astype(low_type), axes, bit)
        values = values[:half].astype(jnp.float32) + came.astype(jnp.float32)
    return values


def product_add_rows(left_side, right_side, axes):
    bits = narrow_bits(lax.axis_size(axes))
    half = left_side.shape[0] // 2
    sent = plain_product(left_side[half:], right_side).astype(low_type)
    came = swap(sent, axes, bits[0])
    values = plain_product(left_side[:half], right_side) + came.astype(jnp.float32)
    for bit in bits[1:]:
        half = values.shape[0] // 2
        came = swap(values[half:].astype(low_type), axes, bit)
        values = values[:half] + came.astype(jnp.float32)
    return values


def natural_rows(joined, places):
    group = joined.shape[0] // len(places)
    return jnp.concatenate(
        [lax.dynamic_slice_in_dim(joined, place * group, group, 0) for place in places], axis=0
    )


def spread(values, axes):
    copies = jnp.broadcast_to(values[None], (lax.axis_size(axes),) + values.shape)
    return lax.all_to_all(copies, axes, split_axis=0, concat_axis=0, tiled=True)


def after(values, other):
    return lax.optimization_barrier((values, other))[0]


def gelu_and_slope(values):
    rate = 0.7978845608028654
    cubic = 0.044715
    squares = values * values
    turn = jnp.tanh(rate * values * (1.0 + cubic * squares))
    half = 0.5 * (1.0 + turn)
    slope = half + 0.5 * values * (1.0 - turn * turn) * (rate * (1.0 + 3.0 * cubic * squares))
    return (values * half).astype(low_type), slope.astype(low_type)


def smem():
    return pl.BlockSpec(memory_space=pltpu.SMEM)


def vmem():
    return pl.BlockSpec(memory_space=pltpu.VMEM)


def bias_kernel(chunks, tiles):
    heads = tiles.shape[0]
    tiles[...] = jnp.zeros_like(tiles)
    for h in range(heads):
        for d in range(-REACH, REACH + 1):
            left = chunks[h, REACH + 1 - d : REACH + 2 - d, :]
            right = chunks[h, REACH - d : REACH + 1 - d, :]
            line = jnp.broadcast_to(jnp.concatenate([left, right], axis=1), (LANE, 2 * LANE))
            rolled = pltpu.roll(line, 0, 1, stride=1, stride_axis=0)
            tiles[h, (d + OFF) * LANE : (d + OFF + 1) * LANE, :] = rolled[:, :LANE]


def bias_tiles(rel_chunks):
    heads = rel_chunks.shape[0]
    return pl.pallas_call(
        bias_kernel,
        out_shape=jax.ShapeDtypeStruct((heads, SPAN * LANE, LANE), jnp.float32),
        compiler_params=pltpu.CompilerParams(vmem_limit_bytes=SMALL_VMEM),
        name="bias_tiles",
    )(rel_chunks)


def key_range(lengths, first, last):
    start = jnp.int32(0)
    low = jnp.int32(0)
    high = jnp.int32(0)
    for s in range(SEQS_DEV):
        end = start + lengths[s]
        low = jnp.where(start <= first, start, low)
        high = jnp.where(start <= last, end, high)
        start = end
    return low // BK, (high + BK - 1) // BK


def bias_part(bias, h, row, size):
    return jnp.concatenate(
        [
            bias[h, pl.ds(pl.multiple_of(row - b * LANE, LANE), size), :]
            for b in range(BQ // LANE)
        ],
        axis=1,
    )


def forward_kernel(
    lengths, origin, cols, rows_in, apart, bias, ctx_o, ctxT_o, lse_o, qa, acc
):
    width, rows_here = cols.shape[0] // 3, cols.shape[1]
    heads = bias.shape[0]
    size = width // heads
    qa[...] = jnp.zeros_like(qa)

    @pl.loop(0, rows_here // BQ)
    def _(i):
        q0 = pl.multiple_of(i * BQ, BQ)
        here = pl.ds(q0, BQ)
        for h in range(heads):
            scaled = cols[h * size : (h + 1) * size, here].astype(jnp.float32) * score_scale
            qa[h * LANE : h * LANE + size, :] = scaled.astype(low_type)
            qa[h * LANE + size : h * LANE + size + 16, :] = apart[:, here]
        acc[...] = jnp.zeros_like(acc)
        low, high = key_range(lengths, q0, q0 + BQ - 1)

        def step(j, count, carry):
            k0 = pl.multiple_of(j * BK, BK)
            there = pl.ds(k0, count * BK)
            row = (j * (BK // LANE) - i * (BQ // LANE) + OFF) * LANE
            out = []
            for h in range(heads):
                top, total = carry[2 * h], carry[2 * h + 1]
                own = slice(h * LANE, (h + 1) * LANE)
                rows = slice(h * size, (h + 1) * size)
                s = plain_product(rows_in[there, own], qa[own, :])
                s = s + bias_part(bias, h, row, count * BK)
                new_top = jnp.maximum(top, jnp.max(s, axis=0, keepdims=True))
                fade = jnp.exp(top - new_top)
                p = jnp.exp(s - new_top)
                total = total * fade + jnp.sum(p, axis=0, keepdims=True)
                acc[rows, :] = acc[rows, :] * fade + plain_product(
                    cols[2 * width + h * size : 2 * width + (h + 1) * size, there],
                    p.astype(low_type),
                )
                out += [new_top, total]
            return tuple(out)

        init = tuple(
            jnp.full((1, BQ), 2.0 * masked_score if n % 2 == 0 else 0.0, jnp.float32)
            for n in range(2 * heads)
        )
        pairs = (high - low) // 2
        done = lax.fori_loop(0, pairs, lambda n, carry: step(low + 2 * n, 2, carry), init)
        done = lax.fori_loop(low + 2 * pairs, high, lambda j, carry: step(j, 1, carry), done)
        for h in range(heads):
            rows = slice(h * size, (h + 1) * size)
            acc[rows, :] = acc[rows, :] / done[2 * h + 1]
            lse_o[h : h + 1, here] = done[2 * h] + jnp.log(done[2 * h + 1])
        ctxT_o[:, here] = acc[...]
        turned = acc[...].T.astype(low_type)
        for b in range(BQ // LANE):
            at = pl.multiple_of(origin[i * (BQ // LANE) + b], LANE)
            ctx_o[pl.ds(at, LANE), :] = turned[b * LANE : (b + 1) * LANE, :]


def attention_forward(lengths, origin, cols, rows_in, apart, bias):
    width, rows_here = cols.shape[0] // 3, cols.shape[1]
    heads = bias.shape[0]
    return pl.pallas_call(
        forward_kernel,
        out_shape=(
            jax.ShapeDtypeStruct((rows_here, width), low_type),
            jax.ShapeDtypeStruct((width, rows_here), jnp.float32),
            jax.ShapeDtypeStruct((heads, rows_here), jnp.float32),
        ),
        in_specs=[smem()] * 2 + [vmem()] * 4,
        out_specs=(vmem(),) * 3,
        scratch_shapes=[
            pltpu.VMEM((heads * LANE, BQ), low_type),
            pltpu.VMEM((width, BQ), jnp.float32),
        ],
        compiler_params=pltpu.CompilerParams(vmem_limit_bytes=FORWARD_VMEM),
        cost_estimate=pl.CostEstimate(
            flops=rows_here * width, bytes_accessed=width * TOK_DEV, transcendentals=0
        ),
        name="attention_forward",
    )(lengths, origin, cols, rows_in, apart, bias)


def three_parts(values):
    first = values.astype(low_type).astype(jnp.float32)
    rest = values - first
    second = rest.astype(low_type).astype(jnp.float32)
    return first, second, rest - second


def backward_kernel(
    lengths, origin, cols, rows_in, dcn, ctxT, lse, apart, bias,
    dT_o, dn_o, lines_o, qa, da, dq, dk, dv, tiles,
):
    width, tokens = cols.shape[0] // 3, cols.shape[1]
    heads = bias.shape[0]
    size = width // heads
    for ref in (qa, da, dk, dv, tiles):
        ref[...] = jnp.zeros_like(ref)
    place = lax.broadcasted_iota(jnp.int32, (16, BQ), 0) - SEQS_DEV

    def in_depth(values):
        a, b, c = three_parts(values)
        return jnp.where(place == 0, a, jnp.where(place == 1, b, jnp.where(place == 2, c, 0.0)))

    @pl.loop(0, tokens // BQ)
    def _(i):
        q0 = pl.multiple_of(i * BQ, BQ)
        here = pl.ds(q0, BQ)
        at = [pl.multiple_of(origin[i * (BQ // LANE) + b], LANE) for b in range(BQ // LANE)]
        dcT = jnp.concatenate(
            [dcn[pl.ds(at[b], LANE), :].astype(jnp.float32) for b in range(BQ // LANE)], axis=0
        ).T
        for h in range(heads):
            rows = slice(h * size, (h + 1) * size)
            top = h * LANE
            scaled = cols[rows, here].astype(jnp.float32) * score_scale
            qa[top : top + size, :] = scaled.astype(low_type)
            extra = apart[:, here].astype(jnp.float32) + in_depth(-lse[h : h + 1, here])
            qa[top + size : top + size + 16, :] = extra.astype(low_type)
            da[top : top + size, :] = dcT[rows, :].astype(low_type)
            delta = jnp.sum(dcT[rows, :] * ctxT[rows, here], axis=0, keepdims=True)
            da[top + size : top + size + 16, :] = in_depth(-delta).astype(low_type)
        dq[...] = jnp.zeros_like(dq)
        low, high = key_range(lengths, q0, q0 + BQ - 1)

        def step(j, count):
            k0 = pl.multiple_of(j * BK, BK)
            there = pl.ds(k0, count * BK)
            row = (j * (BK // LANE) - i * (BQ // LANE) + OFF) * LANE
            for h in range(heads):
                rows = slice(h * size, (h + 1) * size)
                own = slice(h * LANE, (h + 1) * LANE)
                flat = slice(h * LANE, h * LANE + size)
                values = slice((heads + h) * LANE, (heads + h + 1) * LANE)
                keys = slice(width + h * size, width + (h + 1) * size)
                s = plain_product(rows_in[there, own], qa[own, :])
                p = jnp.exp(s + bias_part(bias, h, row, count * BK))
                ds = p * plain_product(rows_in[there, values], da[own, :])
                for b in range(BQ // LANE):
                    window = pl.ds(pl.multiple_of(row - b * LANE, LANE), count * BK)
                    tiles[h, window, :] = (
                        tiles[h, window, :] + ds[:, b * LANE : (b + 1) * LANE]
                    )
                p_low = p.astype(low_type)
                ds_low = ds.astype(low_type)
                dv[rows, there] = dv[rows, there] + times_transposed(da[flat, :], p_low)
                dk[rows, there] = dk[rows, there] + times_transposed(qa[flat, :], ds_low)
                dq[rows, :] = dq[rows, :] + plain_product(cols[keys, there], ds_low)

        pairs = (high - low) // 2

        @pl.loop(0, pairs)
        def _(n):
            step(low + 2 * n, 2)

        @pl.loop(low + 2 * pairs, high)
        def _(j):
            step(j, 1)

        grad = dq[...] * score_scale
        dT_o[0:width, here] = grad.astype(low_type)
        turned = grad.T.astype(low_type)
        for b in range(BQ // LANE):
            dn_o[pl.ds(at[b], LANE), 0:width] = turned[b * LANE : (b + 1) * LANE, :]

    @pl.loop(0, tokens // BQ)
    def _(i):
        here = pl.ds(pl.multiple_of(i * BQ, BQ), BQ)
        both = jnp.concatenate([dk[:, here], dv[:, here]], axis=0)
        dT_o[width : 3 * width, here] = both.astype(low_type)
        turned = both.T.astype(low_type)
        for b in range(BQ // LANE):
            at = pl.multiple_of(origin[i * (BQ // LANE) + b], LANE)
            dn_o[pl.ds(at, LANE), width : 3 * width] = turned[b * LANE : (b + 1) * LANE, :]

    across = lax.broadcasted_iota(jnp.int32, (LANE, LANE), 1)
    over = across >= lax.broadcasted_iota(jnp.int32, (LANE, LANE), 0)
    sub = lax.broadcasted_iota(jnp.int32, (8, LANE), 0)
    for h in range(heads):
        for d in range(-REACH, REACH + 2):
            here = tiles[h, (d + OFF) * LANE : (d + OFF + 1) * LANE, :]
            below = tiles[h, (d + OFF - 1) * LANE : (d + OFF) * LANE, :]
            mixed = jnp.where(over, here, below)
            line = mixed[LANE - 8 :, :]
            for g in range(LANE // 8 - 2, -1, -1):
                line = mixed[8 * g : 8 * g + 8, :] + pltpu.roll(line, LANE - 8, 1)
            for bit in (1, 2, 4):
                line = jnp.where((sub & bit) != 0, pltpu.roll(line, LANE - bit, 1), line)
            lines_o[h, REACH + 1 - d : REACH + 2 - d, :] = jnp.sum(line, axis=0, keepdims=True)


def attention_backward(lengths, origin, cols, rows_in, dcn, ctxT, lse, apart, bias):
    width, tokens = cols.shape[0] // 3, cols.shape[1]
    heads = bias.shape[0]
    return pl.pallas_call(
        backward_kernel,
        out_shape=(
            jax.ShapeDtypeStruct((3 * width, tokens), low_type),
            jax.ShapeDtypeStruct((tokens, 3 * width), low_type),
            jax.ShapeDtypeStruct((heads, LINES, LANE), jnp.float32),
        ),
        in_specs=[smem()] * 2 + [vmem()] * 7,
        out_specs=(vmem(),) * 3,
        scratch_shapes=[
            pltpu.VMEM((heads * LANE, BQ), low_type),
            pltpu.VMEM((heads * LANE, BQ), low_type),
            pltpu.VMEM((width, BQ), jnp.float32),
            pltpu.VMEM((width, tokens), jnp.float32),
            pltpu.VMEM((width, tokens), jnp.float32),
            pltpu.VMEM((heads, SPAN * LANE, LANE), jnp.float32),
        ],
        compiler_params=pltpu.CompilerParams(vmem_limit_bytes=BACKWARD_VMEM),
        cost_estimate=pl.CostEstimate(
            flops=tokens * width, bytes_accessed=width * TOK_DEV, transcendentals=0
        ),
        name="attention_backward",
    )(lengths, origin, cols, rows_in, dcn, ctxT, lse, apart, bias)


def layer_backward_kernel(
    result, middle, segments, pooled, gain, rows, out_map, hidden, slope, inner, outer,
    weight_grads, mid_grad, attn_grad, context_grad, gain_grad, encoded, grad, rows_grad,
):
    groups, _, size, width = weight_grads.shape
    exact = dict(precision=lax.Precision.HIGHEST, preferred_element_type=jnp.float32)

    @pl.when(pl.program_id(0) == 0)
    def _():
        values = result[...]
        lane = lax.broadcasted_iota(jnp.int32, (values.shape[0], pooled.shape[0]), 1)
        member = (segments[...] == lane).astype(jnp.float32)
        weighted = jnp.dot(member, pooled[...], **exact)
        row_scale = rms_scale(values)
        inner_mean = jnp.mean(weighted * values, axis=-1, keepdims=True)
        value_grad = row_scale * weighted - values * (
            row_scale * row_scale * row_scale * inner_mean
        )
        encoded[...] = value_grad
        grad[...] = value_grad.astype(low_type)
        rows_grad[...] = jnp.zeros_like(rows_grad)

    outer_grad = outer_product(hidden[...], grad[...]).astype(low_type)
    weight_grads[:, 0] = outer_grad.reshape(groups, size, width)
    pre = (
        times_transposed(grad[...], outer[...]) * slope[...].astype(jnp.float32)
    ).astype(low_type)
    inner_grad = outer_product(pre, rows[...]).astype(low_type)
    weight_grads[:, 1] = inner_grad.reshape(groups, size, width)
    rows_grad[...] += plain_product(pre, inner[...])

    @pl.when(pl.program_id(0) == pl.num_programs(0) - 1)
    def _():
        values = middle[...]
        grad_out = rows_grad[...]
        row_scale = rms_scale(values)
        value_grad, gain_sum = norm_backward(values, row_scale, gain[...], grad_out)
        total = encoded[...] + value_grad
        mid_grad[...] = total
        attn_grad[...] = total.astype(low_type)
        context_grad[...] = times_transposed(attn_grad[...], out_map[...]).astype(low_type)
        gain_grad[...] = gain_sum[None, :]


def layer_backward(
    result, middle, segments, pooled, gain, rows, out_map, hidden, slope, inner, outer, size
):
    count = result.shape[0]
    groups = UNIT_BLOCK // size

    def every(array):
        return pl.BlockSpec(array.shape, lambda i: (0, 0), pipeline_mode=pl.Buffered(1))

    whole = pl.BlockSpec((count, D), lambda i: (0, 0))
    units = pl.BlockSpec((count, UNIT_BLOCK), lambda i: (0, i))
    weight = pl.BlockSpec((UNIT_BLOCK, D), lambda i: (i, 0))
    constant = (result, middle, segments, pooled, gain, rows, out_map)
    return pl.pallas_call(
        layer_backward_kernel,
        grid=(FF // UNIT_BLOCK,),
        out_shape=(
            jax.ShapeDtypeStruct((FF // size, 2, size, D), low_type),
            jax.ShapeDtypeStruct((count, D), jnp.float32),
            jax.ShapeDtypeStruct((count, D), low_type),
            jax.ShapeDtypeStruct((count, D), low_type),
            jax.ShapeDtypeStruct((1, D), jnp.float32),
        ),
        in_specs=[every(array) for array in constant] + [units, units, weight, weight],
        out_specs=(
            pl.BlockSpec((groups, 2, size, D), lambda i: (i, 0, 0, 0)),
            whole,
            whole,
            whole,
            pl.BlockSpec((1, D), lambda i: (0, 0)),
        ),
        scratch_shapes=[
            pltpu.VMEM((count, D), jnp.float32),
            pltpu.VMEM((count, D), low_type),
            pltpu.VMEM((count, D), jnp.float32),
        ],
        compiler_params=pltpu.CompilerParams(vmem_limit_bytes=LAYER_VMEM),
        cost_estimate=pl.CostEstimate(flops=FF * D, bytes_accessed=FF * D, transcendentals=0),
        name="layer_backward",
    )(*constant, hidden, slope, inner, outer)


def assemble(places, pieces):
    group = pieces[0].shape[0]

    def body(places_in, *refs):
        for s, piece in enumerate(refs[:-1]):

            @pl.when(places_in[pl.program_id(0)] == s)
            def _(piece=piece):
                refs[-1][...] = piece[...].astype(jnp.float32)

    return pl.pallas_call(
        body,
        grid=(len(pieces),),
        out_shape=jax.ShapeDtypeStruct((len(pieces) * group, D), jnp.float32),
        in_specs=[smem()] + [pl.BlockSpec((group, D), lambda g: (0, 0))] * len(pieces),
        out_specs=pl.BlockSpec((group, D), lambda g: (g, 0)),
        compiler_params=pltpu.CompilerParams(vmem_limit_bytes=SMALL_VMEM),
        cost_estimate=pl.CostEstimate(flops=D, bytes_accessed=group * D, transcendentals=0),
        name="assemble",
    )(places, *pieces)


def loss_kernel(place, numbers, parts, proj_weight, gain, out_slope, out_low, out_row, out_gain):
    total_seqs = out_low.shape[0] // 2
    terms = parts.shape[0] // total_seqs
    exact = dict(precision=lax.Precision.HIGHEST, preferred_element_type=jnp.float32)
    seq = lax.broadcasted_iota(jnp.int32, (total_seqs, parts.shape[0]), 0)
    part = lax.broadcasted_iota(jnp.int32, (total_seqs, parts.shape[0]), 1)
    joins = jnp.logical_and(
        seq // SEQS_DEV == part // (SEQS_DEV * terms), seq % SEQS_DEV == part % SEQS_DEV
    )
    unscaled = jnp.dot(joins.astype(jnp.float32), parts[...], **exact)
    pooled_low = (unscaled * gain[...]).astype(low_type)
    projected = times_transposed(pooled_low, proj_weight[...]).astype(low_type).astype(jnp.float32)
    inverse = lax.rsqrt(jnp.sum(projected * projected, axis=1, keepdims=True) + norm_eps)
    embed_low = (projected * inverse).astype(low_type)
    sharpness_factor = jnp.exp(jnp.full((1, 1), numbers[0], jnp.float32))
    agreement = times_transposed(embed_low, embed_low)
    row = lax.broadcasted_iota(jnp.int32, (total_seqs, total_seqs), 0)
    column = lax.broadcasted_iota(jnp.int32, (total_seqs, total_seqs), 1)
    logits = jnp.where(row == column, masked_score, sharpness_factor * agreement)
    partner = (row ^ 1) == column

    def log_sum(axis):
        top = jnp.max(logits, axis=axis, keepdims=True)
        return top + jnp.log(jnp.sum(jnp.exp(logits - top), axis=axis, keepdims=True))

    log_rows = log_sum(1)
    positive = jnp.where(partner, 1.0, 0.0)
    slope = (jnp.exp(logits - log_rows) - positive) / total_seqs
    slope_turned = (jnp.exp(logits - log_sum(0)) - positive) / total_seqs
    embed_grad = sharpness_factor * jnp.dot(
        slope + slope_turned, embed_low.astype(jnp.float32), **exact
    )
    along = jnp.sum(projected * embed_grad, axis=1, keepdims=True)
    proj_grad_low = (
        inverse * embed_grad - projected * inverse * inverse * inverse * along
    ).astype(low_type)
    pooled_grad = plain_product(proj_grad_low, proj_weight[...])
    out_low[0:total_seqs, :] = proj_grad_low
    out_low[total_seqs : 2 * total_seqs, :] = pooled_low
    out_gain[...] = jnp.sum(pooled_grad * unscaled, axis=0, keepdims=True)
    loss = jnp.sum(
        log_rows - jnp.sum(positive * jnp.where(partner, logits, 0.0), axis=1, keepdims=True),
        axis=0,
        keepdims=True,
    ) / total_seqs
    temperature = sharpness_factor * jnp.sum(
        jnp.sum(slope * agreement, axis=1, keepdims=True), axis=0, keepdims=True
    )
    lane = lax.broadcasted_iota(jnp.int32, (1, LANE), 1)
    out_row[...] = jnp.where(lane == 0, loss, jnp.where(lane == 1, temperature, 0.0))
    mine = lax.broadcasted_iota(jnp.int32, (8, total_seqs), 0)
    seq_of = lax.broadcasted_iota(jnp.int32, (8, total_seqs), 1) - place[0] * SEQS_DEV
    picks = jnp.logical_and(mine == seq_of, mine < SEQS_DEV).astype(jnp.float32)
    own = jnp.dot(picks, pooled_grad, **exact)
    index = lax.broadcasted_iota(jnp.int32, (8, 1), 0)
    extent = jnp.ones((8, 1), jnp.float32)
    for s in range(SEQS_DEV):
        extent = jnp.where(index == s, place[1 + s].astype(jnp.float32), extent)
    out_slope[...] = own * gain[...] / extent


def contrastive(place, numbers, parts, proj_weight, gain, total_seqs):
    return pl.pallas_call(
        loss_kernel,
        out_shape=(
            jax.ShapeDtypeStruct((8, D), jnp.float32),
            jax.ShapeDtypeStruct((2 * total_seqs, D), low_type),
            jax.ShapeDtypeStruct((1, LANE), jnp.float32),
            jax.ShapeDtypeStruct((1, D), jnp.float32),
        ),
        in_specs=[smem()] * 2 + [vmem()] * 3,
        out_specs=(vmem(),) * 4,
        compiler_params=pltpu.CompilerParams(vmem_limit_bytes=SMALL_VMEM),
        cost_estimate=pl.CostEstimate(
            flops=4 * total_seqs * D * D, bytes_accessed=4 * D * D, transcendentals=total_seqs
        ),
        name="contrastive",
    )(place, numbers, parts, proj_weight, gain)


def on_device(
    axes,
    layer_argument,
    document_extents,
    distance_bin_lookup,
    tile_location,
    precise_parameter_blocks,
    precise_mean_est,
    precise_variance_est,
    rescaling_coefficients,
    norm_scale_mean_est,
    norm_scale_variance_est,
    distance_bias_table,
    offset_bias_mean_est,
    offset_bias_variance_est,
    sharpness_exponent,
    sharpness_mean_est,
    sharpness_variance_est,
):
    wide, narrow, far, near = axes
    everyone = wide + narrow
    near_axes = near + narrow
    wide_count = lax.axis_size(wide)
    narrow_count = lax.axis_size(narrow)
    far_count = lax.axis_size(far)
    near_count = wide_count // far_count
    wide_index = lax.axis_index(wide)
    narrow_index = lax.axis_index(narrow)
    bits = narrow_bits(narrow_count)
    order = peer_order(narrow_count)
    place_of = jnp.array([order.index(peer) for peer in range(narrow_count)], jnp.int32)
    unit_rows = precise_parameter_blocks.shape[1]
    heads_here = distance_bias_table.shape[1]
    head_size = unit_rows // heads_here
    ffn_units = FF // D
    group = TOK_DEV // narrow_count
    own_slots = wide_index * CAP + jnp.arange(CAP, dtype=jnp.int32)

    every_slot = lax.all_gather(
        precise_parameter_blocks.astype(low_type), wide, axis=0, tiled=True
    )

    def block(u):
        return lax.dynamic_index_in_dim(every_slot, tile_location[u], 0, keepdims=False)

    qkv_weight = jnp.concatenate([block(u) for u in range(3)], axis=0)

    part_rows = D // wide_count

    def unit_order(first_unit):
        rows = jnp.concatenate([block(first_unit + k) for k in range(ffn_units)], axis=0)
        rows = rows.reshape(far_count, near_count, part_rows, D)
        return jnp.swapaxes(rows, 0, 1).reshape(near_count, far_count * part_rows, D)

    crossing = [unit_order(5), block(3), unit_order(5 + ffn_units)]
    for rows in crossing:
        qkv_weight = after(qkv_weight, rows)

    near_index = wide_index % near_count

    def fetch(rows, peer, in_parts):
        if in_parts:
            rows = lax.dynamic_index_in_dim(rows, near_index, 0)
        return swap(rows, narrow, peer)

    evens = bits[1:]
    def exchanged(pieces):
        return [
            [(near_index, rows)]
            + [(near_index ^ step, swap(rows, near, step)) for step in range(1, near_count)]
            for rows in pieces
        ]

    lengths = document_extents[0]
    seq_ends = jnp.cumsum(lengths)
    positions = jnp.arange(TOK_DEV, dtype=jnp.int32)

    def segments_of(where):
        return jnp.sum((seq_ends[None, :] <= where[:, None]).astype(jnp.int32), axis=1)

    segment_ids = segments_of(positions)
    own_segments = segments_of(narrow_index * group + positions[:group])
    tile_starts = jnp.arange(TOK_DEV // LANE, dtype=jnp.int32) * LANE
    origin = place_of[(tile_starts // group) ^ narrow_index] * group + tile_starts % group

    units = []
    for slot in range(CAP):
        here = tile_location == own_slots[slot]
        unit = jnp.sum(jnp.where(here, jnp.arange(1, here.shape[0] + 1, dtype=jnp.int32), 0)) - 1
        early_unit = jnp.maximum(unit - 5, 0)
        row = jnp.where(unit >= 5, early_unit % ffn_units, jnp.clip(unit, 0, ffn_units - 1))
        column = jnp.where(unit >= 5, 1 - early_unit // ffn_units, 2)
        units += [unit, row, column]
    proj_owner = (tile_location[4] // CAP == wide_index).astype(jnp.float32)
    places = [place_of[g ^ narrow_index] for g in range(narrow_count)]

    beyond = LINES * LANE - LANE - 1 - distance_bin_lookup.shape[0]
    offsets_down = jnp.pad(distance_bin_lookup[::-1], (LANE + 1, beyond), constant_values=-1)
    bucket_onehot = (
        offsets_down[:, None] == jnp.arange(BUCKETS, dtype=jnp.int32)[None, :]
    ).astype(jnp.float32)
    rel_values = jnp.dot(bucket_onehot, distance_bias_table, precision=lax.Precision.HIGHEST).T
    rel_values, origin, proj_owner, *scalars = lax.optimization_barrier(
        (rel_values, origin, proj_owner, *units, *places)
    )
    units, places = scalars[: len(units)], scalars[len(units) :]
    tiles_bias = bias_tiles(rel_values.reshape(heads_here, LINES, LANE))

    all_rows = layer_argument.astype(jnp.float32)
    normed_one = (all_rows * rms_scale(all_rows) * rescaling_coefficients[0]).astype(low_type)
    spread_weight = jnp.pad(
        qkv_weight[unit_rows:].reshape(2 * heads_here, head_size, D),
        ((0, 0), (0, LANE - head_size), (0, 0)),
    ).reshape(2 * heads_here * LANE, D)
    lane_place = jnp.arange(2 * heads_here * LANE, dtype=jnp.int32) % LANE - head_size
    marks = jnp.logical_or(
        lane_place[None, :] == segment_ids[:, None],
        jnp.logical_and(lane_place >= SEQS_DEV, lane_place < SEQS_DEV + 3)[None, :],
    )
    key_value_rows = (
        times_transposed(normed_one, spread_weight) + marks.astype(jnp.float32)
    ).astype(low_type)
    crossing[1] = after(crossing[1], key_value_rows)
    fetched = [
        [fetch(rows, peer, in_parts) for peer in evens]
        for rows, in_parts in zip(crossing, (True, False, True))
    ]
    inner_parts = exchanged(fetched[0])
    qkv_turned = times_transposed(after(qkv_weight, fetched[0][0]), normed_one).astype(low_type)
    row_place = jnp.arange(16, dtype=jnp.int32)[:, None]
    apart = jnp.where(
        jnp.logical_and(row_place < SEQS_DEV, row_place != segment_ids[None, :]), masked_score, 0.0
    ).astype(low_type)
    context, context_cols, log_rows = attention_forward(
        lengths, origin, qkv_turned, key_value_rows, apart, tiles_bias
    )

    flat = [rows for pieces in fetched[1:] for rows in pieces]
    inner_flat = [rows for parts in inner_parts for _, rows in parts]
    context, *flat = lax.optimization_barrier((context, *flat, *inner_flat))
    inner_rows = iter(flat[2 * len(evens) :])
    inner_parts = [[(index, next(inner_rows)) for index, _ in parts] for parts in inner_parts]
    context_parts = [context[s * group : (s + 1) * group] for s in range(narrow_count)]
    context_parts = list(lax.optimization_barrier(tuple(context_parts)))
    outer_parts = exchanged(flat[len(evens) : 2 * len(evens)])

    def in_unit_order(own, parts_of_peers):
        whole = jnp.zeros((near_count, narrow_count, far_count * part_rows, D), low_type)
        own = after(own, context_parts[0])
        pieces = [(0, 0, own), (1, 0, swap(own, narrow, 1))]
        for peer, parts in zip(evens, parts_of_peers):
            for index, rows in parts:
                pieces += [(peer, index, rows), (peer + 1, index, swap(rows, narrow, 1))]
        for peer, index, rows in pieces:
            start = (index, narrow_index ^ peer, 0, 0)
            whole = lax.dynamic_update_slice(whole, rows[:, None], start)
        return whole.reshape(FF, D)

    out_pieces = {0: crossing[1], 1: swap(crossing[1], narrow, 1)}
    for peer, rows in zip(evens, flat[: len(evens)]):
        out_pieces[peer], out_pieces[peer + 1] = rows, swap(rows, narrow, 1)
    out_joined = jnp.concatenate([out_pieces[peer] for peer in order], axis=0)
    inner_joined = in_unit_order(crossing[0], inner_parts)
    outer_joined = in_unit_order(crossing[2], outer_parts)

    def to_peer(values, peer):
        if peer == 0:
            return values
        return swap(values, narrow, peer)

    context_own = jnp.concatenate(
        [
            to_peer(context_parts[s], peer)
            for s, peer in enumerate(order)
        ],
        axis=1,
    )
    own_rows = lax.dynamic_slice_in_dim(layer_argument, narrow_index * group, group, 0).astype(
        jnp.float32
    )
    scale_one = rms_scale(own_rows)
    residual_mid = own_rows + plain_product(context_own, out_joined)
    scale_two = rms_scale(residual_mid)
    normed_two = (residual_mid * scale_two * rescaling_coefficients[1]).astype(low_type)

    hidden_low, hidden_slope = gelu_and_slope(times_transposed(normed_two, inner_joined))
    proj_rows = after(block(4), normed_two)
    for bit in reversed(bits):
        came = after(swap(proj_rows, narrow, bit), hidden_low)
        proj_rows = jnp.concatenate([proj_rows, came], axis=0)
    proj_weight = natural_rows(proj_rows, places)
    result_own = residual_mid + plain_product(hidden_low, outer_joined)
    result_low = result_own.astype(low_type)

    scale_three = rms_scale(result_own)
    member = (
        own_segments[None, :] == jnp.arange(SEQS_DEV, dtype=jnp.int32)[:, None]
    ).astype(jnp.float32)
    length_values = lengths.astype(jnp.float32)[:, None]
    unscaled_part = (
        jnp.dot(member, result_own * scale_three, precision=lax.Precision.HIGHEST) / length_values
    )
    total_seqs = wide_count * SEQS_DEV
    own_pooled_grad, loss_low, loss_row, final_gain_grad = contrastive(
        jnp.concatenate([wide_index.reshape(1), lengths]),
        sharpness_exponent,
        spread(unscaled_part, everyone).reshape(total_seqs * narrow_count, D),
        proj_weight,
        rescaling_coefficients[2:3],
        total_seqs,
    )
    loss = loss_row[0, 0]
    sharpness_total = loss_row[0, 1:2]
    proj_grad_own = lax.dynamic_slice_in_dim(
        loss_low[:total_seqs], narrow_index * unit_rows, unit_rows, 1
    )
    proj_weight_grad = outer_product(proj_grad_own, loss_low[total_seqs:])

    group_rows = part_rows if part_rows % 16 == 0 else D
    weight_grads, mid_grad, attn_grad_low, context_grad_own, ffn_gain_grad = layer_backward(
        result_own,
        residual_mid,
        own_segments[:, None],
        own_pooled_grad,
        rescaling_coefficients[1:2],
        normed_two,
        out_joined,
        hidden_low,
        hidden_slope,
        inner_joined,
        outer_joined,
        group_rows,
    )
    near_part = lax.psum_scatter(
        weight_grads.reshape(2 * FF, D), near_axes, scatter_dimension=0, tiled=True
    )
    ffn_gain_grad = ffn_gain_grad[0]

    context_grad = [
        to_peer(context_grad_own[:, s * unit_rows : (s + 1) * unit_rows], peer)
        for s, peer in enumerate(order)
    ]
    attn_grad_low = after(attn_grad_low, context_grad_own)
    out_kept = outer_product(context_own, attn_grad_low).astype(low_type)
    for bit in bits:
        half = out_kept.shape[0] // 2
        out_came = swap(out_kept[half:], narrow, bit)
        if bit == bits[-1]:
            break
        out_kept = sum_low(out_kept[:half], out_came)
    context_grad = after(jnp.concatenate(context_grad, axis=0), out_kept)
    qkv_cols, qkv_rows, bias_lines = attention_backward(
        lengths,
        origin,
        qkv_turned,
        key_value_rows,
        context_grad,
        context_cols,
        log_rows,
        apart,
        tiles_bias,
    )
    qkv_cols, qkv_rows, out_came = lax.optimization_barrier((qkv_cols, qkv_rows, out_came))
    out_grad = sum_low(out_kept[: out_came.shape[0]], out_came)
    offset_bias_slope = lax.dot_general(
        bucket_onehot,
        bias_lines.reshape(heads_here, LINES * LANE),
        (((0,), (1,)), ((), ())),
        precision=lax.Precision.HIGHEST,
    )

    late = jnp.concatenate(
        [plain_product(qkv_cols, normed_one).astype(low_type), out_grad], axis=0
    ).reshape(far_count, near_count, part_rows, D)
    qkv_rows = after(qkv_rows, late)
    half = qkv_rows.shape[0] // 2
    rows_sent = plain_product(qkv_rows[half:], qkv_weight).astype(low_type)
    normed_one_grad = plain_product(qkv_rows[:half], after(qkv_weight, rows_sent)) + swap(
        rows_sent, narrow, bits[0]
    ).astype(jnp.float32)
    for bit in bits[1:]:
        half = normed_one_grad.shape[0] // 2
        rows_sent = normed_one_grad[half:].astype(low_type)
        normed_one_grad = normed_one_grad[:half] + swap(rows_sent, narrow, bit).astype(
            jnp.float32
        )
    late_sum = lax.dynamic_index_in_dim(late, near_index, 1, keepdims=False)
    for peer in range(1, near_count):
        sent = lax.dynamic_index_in_dim(late, near_index ^ peer, 1, keepdims=False)
        late_sum = sum_low(late_sum, after(swap(sent, near, peer), rows_sent))
    early = after(near_part, late).reshape(-1, 2, group_rows // part_rows, part_rows, D)
    early = jnp.swapaxes(early, 1, 2).reshape(far_count * 2 * part_rows, D)
    early_part = lax.psum_scatter(early, far, scatter_dimension=0, tiled=True)
    late_terms = lax.all_to_all(late_sum, far, split_axis=0, concat_axis=0, tiled=True)
    late_part = jnp.sum(late_terms.astype(jnp.float32), axis=0).astype(low_type)
    own_part = jnp.concatenate([early_part, late_part], axis=0)
    input_norm_grad, attn_gain_grad = norm_backward(
        own_rows, scale_one, rescaling_coefficients[0], normed_one_grad
    )
    input_own = mid_grad + input_norm_grad
    sums = lax.all_gather(after(own_part, input_own), wide, axis=0, tiled=True)
    bias_size = offset_bias_slope.size
    squares = jnp.sum(jnp.square(own_part.astype(jnp.float32))) + proj_owner * jnp.sum(
        jnp.square(proj_weight_grad)
    )
    small = jnp.stack(
        [
            ffn_gain_grad,
            attn_gain_grad,
            jnp.pad(offset_bias_slope.reshape(bias_size), (0, D - bias_size)),
            jnp.broadcast_to(squares, (D,)),
        ]
    )
    small_all = spread(small, everyone).reshape(wide_count, narrow_count, 4, D)
    def gathered(own):
        pieces = {0: own, 1: swap(own, narrow, 1)}
        for peer in evens:
            rows = after(swap(own, narrow, peer), small_all)
            pieces[peer], pieces[peer + 1] = rows, swap(rows, narrow, 1)
        return assemble(jnp.stack(places), [pieces[peer] for peer in order])

    input_grad = gathered(input_own.astype(low_type))
    layer_result = gathered(after(result_low, input_own))
    gain_sums = jnp.sum(small_all[:, :, :2], axis=(0, 1))
    gain_total = jnp.stack([gain_sums[1], gain_sums[0], final_gain_grad[0]])
    bias_all = jnp.sum(small_all[:, :, 2], axis=0)
    square_terms = small_all[:, :, 3, 0]
    bias_total = lax.dynamic_index_in_dim(bias_all, narrow_index, 0, keepdims=False)[
        :bias_size
    ].reshape(offset_bias_slope.shape)
    sums, proj_weight_grad, square_terms, *_ = lax.optimization_barrier(
        (sums, proj_weight_grad, square_terms, input_grad, layer_result, gain_total, bias_total)
    )
    sums = sums.reshape(ffn_units, wide_count // ffn_units, 3, part_rows, D)
    slot_grads = []
    for slot in range(CAP):
        unit, row, column = units[3 * slot : 3 * slot + 3]
        low_sum = lax.dynamic_slice(
            sums, (row, 0, column, 0, 0), (1, wide_count // ffn_units, 1, part_rows, D)
        ).reshape(unit_rows, D)
        low_sum = jnp.where(unit == 4, proj_weight_grad, low_sum.astype(jnp.float32))
        slot_grads.append(jnp.where(unit >= 0, low_sum, 0.0))
    slot_grads = jnp.stack(slot_grads)
    grad_norm = jnp.sqrt(
        jnp.sum(square_terms)
        + jnp.sum(gain_total * gain_total)
        + jnp.sum(bias_all * bias_all)
        + jnp.sum(sharpness_total * sharpness_total)
    )
    multiplier = jnp.minimum(1.0, clip_limit / grad_norm)
    slot_first, slot_second, slot_weight = decoupled_decay_step(
        slot_grads,
        precise_mean_est,
        precise_variance_est,
        precise_parameter_blocks,
        multiplier,
        learn_rate,
    )
    gain_first, gain_second, gain_new = decoupled_decay_step(
        gain_total,
        norm_scale_mean_est,
        norm_scale_variance_est,
        rescaling_coefficients,
        multiplier,
        side_rate,
    )
    bias_first, bias_second, bias_new = decoupled_decay_step(
        bias_total,
        offset_bias_mean_est,
        offset_bias_variance_est,
        distance_bias_table,
        multiplier,
        side_rate,
    )
    sharpness_mean_fresh, sharpness_variance_fresh, sharpness_exponent_fresh = decoupled_decay_step(
        sharpness_total,
        sharpness_mean_est,
        sharpness_variance_est,
        sharpness_exponent,
        multiplier,
        learn_rate,
    )
    return (
        loss,
        layer_result,
        input_grad,
        grad_norm,
        slot_first,
        slot_second,
        slot_weight,
        gain_first,
        gain_second,
        gain_new,
        bias_first,
        bias_second,
        bias_new,
        sharpness_mean_fresh,
        sharpness_variance_fresh,
        sharpness_exponent_fresh,
    )


def solution(mesh):
    wide, narrow, far, near = ("wide",), ("narrow",), ("wide",), ()
    if dict(mesh.shape) == {"wide": 8, "narrow": 4}:
        mesh = Mesh(mesh.devices.reshape(4, 2, 2, 2), ("line", "pair", "side", "core"))
        wide, narrow, far, near = ("line", "pair"), ("side", "core"), ("line",), ("pair",)
    whole, rows, blocks, heads = P(), P(wide, None), P(wide, narrow, None), P(None, narrow)
    arguments = (rows, rows, whole, whole, blocks, blocks, blocks, whole, whole, whole)
    arguments += (heads, heads, heads, whole, whole, whole)
    results = (whole, rows, rows, whole, blocks, blocks, blocks, whole, whole, whole)
    results += (heads, heads, heads, whole, whole, whole)

    def body(*arrays):
        return on_device((wide, narrow, far, near), *arrays)

    return jax.shard_map(
        body, mesh=mesh, in_specs=arguments, out_specs=results, check_vma=False
    )
```
